32 devices in a mesh: section: 8 (over z, core), expert: 4 (over y, x).
Axes of the slice: x: 2, y: 2, z: 4, core: 2. Of those that a mesh axis runs over, the one named last changes fastest.
Arguments:
- fwd_prev: bfloat16 [8, 512, 2048], P('section', 'expert'), may hold values from -24 to 24
- bwd_prev: bfloat16 [8, 512, 2048], P('section', 'expert'), may hold values from -6 to 6
- bwd_saved: bfloat16 [8, 512, 2048], P('section', 'expert'), may hold values from -24 to 24
- fwd_routes: int32 [8, 512, 2], P('section', 'expert'), may hold values from 0 to 3, all different within a row; in each aligned block of 128 rows (0 to 127, 128 to 255, ..., all dimensions but the last counted through in order) at most 96 rows name the same one
- fwd_gates: float32 [8, 512, 2], P('section', 'expert'), may hold values from 0.2 to 1
- bwd_routes: int32 [8, 512, 2], P('section', 'expert'), may hold values from 0 to 3, all different within a row; in each aligned block of 128 rows (0 to 127, 128 to 255, ..., all dimensions but the last counted through in order) at most 96 rows name the same one
- bwd_gates: float32 [8, 512, 2], P('section', 'expert'), may hold values from 0.2 to 1
- norm_gain: float32 [8, 2048], P('section'), may hold values from 0.25 to 1.75
- w_in: bfloat16 [8, 4, 2048, 1536], P('section', 'expert'), may hold values from -0.125 to 0.125
- w_out: bfloat16 [8, 4, 768, 2048], P('section', 'expert'), may hold values from -0.21875 to 0.21875
Outputs:
- fwd_out: bfloat16 [8, 512, 2048], P('section', 'expert')
- bwd_out: bfloat16 [8, 512, 2048], P('section', 'expert')
The draws below stay inside these ranges and needn't reach their ends.
Inputs may be any that keep to these rules, and one draw needn't show every extreme that they name: `fwd_routes`: each row names 2 different experts; within the 128 rows of one device in one section no expert is named by more than 96 rows. `bwd_routes`: each row names 2 different experts; within the 128 rows of one device in one section no expert is named by more than 96 rows.
All inputs are finite; a program needn't handle non-finite values.
Results may differ from the reference program's by a relative error of at most 0.006.
Values may be sent and summed in bfloat16 or wider, within the bound.
No kernel may reach another device: no remote copies, remote signals or barrier semaphores. Data moves between devices by JAX's collectives and lax.ppermute only.
A program may use at most 64 MiB of HBM per device.

```python
import math
import jax
import jax.numpy as jnp
import numpy as np
from jax import lax

D = 2048
H = 768
TOK_DEV = 128
TOPK = 2
EXPERTS = 4
CAP = 96
TOKENS = 512
N_SECTION = 8
N_EXPERT = 4


def rows_with_scales(key, shape):
    key_base, key_scale = jax.random.split(key, 2)
    scale = jnp.exp(jax.random.uniform(key_scale, shape[:-1] + (1,), jnp.float32, math.log(0.3), math.log(3.0)))
    base = jax.random.normal(key_base, shape, jnp.float32)
    return jnp.clip(base * scale, -24.0, 24.0)


def draw_fwd_prev(key, part):
    return rows_with_scales(jax.random.fold_in(key, 11), (N_SECTION, TOKENS, D)).astype(jnp.bfloat16)


def draw_bwd_saved(key, part):
    return rows_with_scales(jax.random.fold_in(key, 12), (N_SECTION, TOKENS, D)).astype(jnp.bfloat16)


def steps_of(stream_key, dims, cuts, least, largest):
    level = 1.0
    for dim, blocks in cuts:
        heights = jax.random.uniform(jax.random.fold_in(jax.random.fold_in(stream_key, 6), dim), (blocks,), jnp.float32, least / len(cuts), largest / len(cuts))
        level = level * jnp.repeat(jnp.exp(heights), dims[dim] // blocks).reshape((-1,) + (1,) * (len(dims) - 1 - dim))
    return level


def shared_out(stream_key, own, number, rows, amount, top, reach, skew):
    order = jax.random.permutation(stream_key, amount)
    crowded, ordinary = shares(amount, rows * top, reach, skew, True), shares(amount, rows * top, reach, skew, False)
    places = jnp.arange(amount)

    def named(tallies, offset_by):
        used = int((tallies > 0).sum())
        fixed = max(1, used // 4)
        moved = fixed + (places - fixed + offset_by * (used - fixed)) % max(1, amount - fixed)
        return jnp.zeros((amount,), jnp.int32).at[order[jnp.where(places < fixed, places, moved)]].set(jnp.asarray(tallies, jnp.int32))

    tallies = jnp.where(number % 4 == 0, named(crowded, number // 4), named(ordinary, number - number // 4 - 1))
    mixed = jax.random.permutation(jax.random.fold_in(own, 3), amount)
    source_of, taker = mixed[0:amount // 2 * 2:2], mixed[1:amount // 2 * 2:2]
    slack = jnp.minimum(tallies[source_of] - 1, reach - tallies[taker]) // 2
    slack = jnp.where((source_of == order[0]) | (taker == order[0]) | (tallies[taker] == 0), 0, jnp.maximum(slack, 0))
    moved = jax.random.randint(jax.random.fold_in(own, 4), (amount // 2,), 0, 1 << 20) % (slack + 1)
    tallies = tallies.at[source_of].add(-moved).at[taker].add(moved)
    items = jnp.searchsorted(jnp.cumsum(tallies), jnp.arange(rows * top), side="right").astype(jnp.int32)
    grid = items.reshape(top, rows).T
    grid = grid[jax.random.permutation(jax.random.fold_in(own, 1), rows)]
    offset_by = jax.random.randint(jax.random.fold_in(own, 2), (rows, 1), 0, top)
    return jnp.take_along_axis(grid, (jnp.arange(top)[None, :] + offset_by) % top, axis=1)


def shares(amount, total, bound, slope, full):
    weights = [(1 << 20) // math.isqrt(standing ** slope) + 1 for standing in range(1, amount + 1)]
    largest = bound if full else min(bound, max(-(-total // amount), total * weights[0] // sum(weights)))
    least = 1 if total - largest >= amount - 1 else 0
    given, surplus = [largest] + [least] * (amount - 1), total - largest - least * (amount - 1)
    while surplus > 0:
        candidates = [i for i in range(1, amount) if given[i] < largest] or [i for i in range(1, amount) if given[i] < bound]
        pool, left = sum([weights[i] for i in candidates]), surplus
        for i in candidates:
            addition = min(bound - given[i], max(1, left * weights[i] // pool), surplus)
            given[i] = given[i] + addition
            surplus = surplus - addition
    return np.array(given)


def normal_values(key, dims, scale, most, pieces=(), held_as=jnp.bfloat16):
    entries = scale * jax.random.normal(key, dims, jnp.float32)
    if pieces:
        entries = entries * steps_of(key, dims, pieces, -0.22, 0.18)
    return jnp.clip(entries, -most, most).astype(held_as)


def setup_inputs(seed: int = 0) -> dict:
    splits = jax.random.split(jax.random.key(seed), 11)
    fwd_prev = draw_fwd_prev(jax.random.fold_in(splits[10], 71), 0)
    bwd_prev = normal_values(splits[1], (N_SECTION, TOKENS, D), 1.0, 6.0, ((0, 8), (1, 4)))
    bwd_saved = draw_bwd_saved(jax.random.fold_in(splits[10], 71), 0)
    fwd_routes_keys = jax.random.split(jax.random.fold_in(splits[3], 1), N_SECTION * TOKENS // TOK_DEV)
    fwd_routes_turns = jax.random.permutation(jax.random.fold_in(splits[3], 3), N_SECTION * TOKENS // TOK_DEV)
    fwd_routes = jax.vmap(lambda own, number: shared_out(jax.random.fold_in(splits[3], 2), own, number, TOK_DEV, EXPERTS, TOPK, CAP, 2))(fwd_routes_keys, fwd_routes_turns).reshape((N_SECTION, TOKENS, TOPK))
    fwd_gates = jnp.clip(0.2 + 0.8 * jax.random.uniform(splits[4], (N_SECTION, TOKENS, TOPK), jnp.float32) ** steps_of(splits[4], (N_SECTION, TOKENS, TOPK), ((0, 8), (1, 4)), -0.2, 0.2), 0.2, 1.0)
    bwd_routes_keys = jax.random.split(jax.random.fold_in(splits[5], 1), N_SECTION * TOKENS // TOK_DEV)
    bwd_routes_turns = jax.random.permutation(jax.random.fold_in(splits[5], 3), N_SECTION * TOKENS // TOK_DEV)
    bwd_routes = jax.vmap(lambda own, number: shared_out(jax.random.fold_in(splits[5], 2), own, number, TOK_DEV, EXPERTS, TOPK, CAP, 2))(bwd_routes_keys, bwd_routes_turns).reshape((N_SECTION, TOKENS, TOPK))
    bwd_gates = jnp.clip(0.2 + 0.8 * jax.random.uniform(splits[6], (N_SECTION, TOKENS, TOPK), jnp.float32) ** steps_of(splits[6], (N_SECTION, TOKENS, TOPK), ((0, 8), (1, 4)), -0.2, 0.2), 0.2, 1.0)
    norm_gain = jnp.clip(1.0 + 0.15 * jax.random.normal(splits[7], (N_SECTION, D), jnp.float32), 0.25, 1.75)
    w_in = normal_values(splits[8], (N_SECTION, EXPERTS, D, 2 * H), D ** -0.5, 0.125, ((0, 8), (1, 4)))
    w_out = normal_values(splits[9], (N_SECTION, EXPERTS, H, D), H ** -0.5, 0.21875, ((0, 8), (1, 4)))
    return {"fwd_prev": fwd_prev, "bwd_prev": bwd_prev, "bwd_saved": bwd_saved, "fwd_routes": fwd_routes, "fwd_gates": fwd_gates, "bwd_routes": bwd_routes, "bwd_gates": bwd_gates, "norm_gain": norm_gain, "w_in": w_in, "w_out": w_out}


EPS = 1e-06

def pair_places(routes):
    blocks = routes.reshape(N_EXPERT, TOK_DEV * TOPK).astype(jnp.int32)
    onehot = (blocks[:, :, None] == jnp.arange(EXPERTS, dtype=jnp.int32)[None, None, :]).astype(jnp.int32)
    earlier = (jnp.cumsum(onehot, axis=1) - onehot).astype(jnp.int32)
    slot_index = lax.optimization_barrier(jnp.sum(earlier * onehot, axis=2)).astype(jnp.int32)
    source = jnp.arange(N_EXPERT, dtype=jnp.int32)[:, None]
    row_index = (source * CAP + slot_index).astype(jnp.int32)
    return (blocks.reshape(-1), row_index.reshape(-1))

def normalize(values, gain_row):
    wide = values.astype(jnp.float32)
    inv_rms = lax.rsqrt(lax.optimization_barrier(jnp.mean(wide * wide, axis=-1, keepdims=True)) + EPS)
    return (wide, inv_rms, (wide * inv_rms * gain_row).astype(jnp.bfloat16))

def expert_buffer(values, experts, row_index):
    buffer = jnp.zeros((EXPERTS, N_EXPERT * CAP, values.shape[-1]), jnp.bfloat16)
    return buffer.at[experts, row_index].set(values)

def expert_forward(in_rows, weight_in, weight_out):
    projected = jnp.dot(in_rows, weight_in, preferred_element_type=jnp.float32)
    hidden = (jax.nn.silu(projected[:, :H]) * projected[:, H:]).astype(jnp.bfloat16)
    return jnp.dot(hidden, weight_out, preferred_element_type=jnp.float32).astype(jnp.bfloat16)

def expert_backward(in_rows, grad_rows, weight_in, weight_out):
    projected = jnp.dot(in_rows, weight_in, preferred_element_type=jnp.float32)
    gate_pre = projected[:, :H]
    up_pre = projected[:, H:]
    d_hidden = lax.dot_general(grad_rows, weight_out, (((1,), (1,)), ((), ())), preferred_element_type=jnp.float32)
    sigmoid_gate = 1.0 / (1.0 + jnp.exp(-gate_pre))
    d_gate = (d_hidden * up_pre * sigmoid_gate * (1.0 + gate_pre * (1.0 - sigmoid_gate))).astype(jnp.bfloat16)
    d_up = (d_hidden * gate_pre * sigmoid_gate).astype(jnp.bfloat16)
    d_both = jnp.concatenate([d_gate, d_up], axis=1)
    return lax.dot_general(d_both, weight_in, (((1,), (1,)), ((), ())), preferred_element_type=jnp.float32).astype(jnp.bfloat16)

def one_section(section_args):
    layer_in, grad_in, saved, f_routes, f_gates, b_routes, b_gates, gain_row, weight_in, weight_out = section_args
    layer_wide, inv_fwd, normed_fwd = normalize(layer_in, gain_row)
    f_experts, f_rows = pair_places(f_routes)
    in_fwd = expert_buffer(jnp.repeat(normed_fwd, TOPK, axis=0), f_experts, f_rows)
    out_rows = lax.map(lambda item: expert_forward(item[0], item[1], item[2]), (in_fwd, weight_in, weight_out))
    picked = out_rows[f_experts, f_rows].reshape(TOKENS, TOPK, D).astype(jnp.float32)
    fwd_block = (layer_wide + lax.optimization_barrier(jnp.sum(f_gates[:, :, None] * picked, axis=1))).astype(jnp.bfloat16)
    saved_wide, inv_bwd, normed_bwd = normalize(saved, gain_row)
    b_experts, b_rows = pair_places(b_routes)
    grad_pair = (b_gates[:, :, None] * grad_in.astype(jnp.float32)[:, None, :]).astype(jnp.bfloat16).reshape(TOKENS * TOPK, D)
    in_bwd = expert_buffer(jnp.repeat(normed_bwd, TOPK, axis=0), b_experts, b_rows)
    grad_bwd = expert_buffer(grad_pair, b_experts, b_rows)
    d_rows = lax.map(lambda item: expert_backward(item[0], item[1], item[2], item[3]), (in_bwd, grad_bwd, weight_in, weight_out))
    d_normed = lax.optimization_barrier(jnp.sum(d_rows[b_experts, b_rows].reshape(TOKENS, TOPK, D).astype(jnp.float32), axis=1))
    scaled = d_normed * gain_row
    cubed = inv_bwd * inv_bwd * inv_bwd
    d_input = inv_bwd * scaled - cubed / D * saved_wide * lax.optimization_barrier(jnp.sum(scaled * saved_wide, axis=-1, keepdims=True))
    bwd_block = (grad_in.astype(jnp.float32) + d_input).astype(jnp.bfloat16)
    return (fwd_block, bwd_block)

def reference(fwd_prev, bwd_prev, bwd_saved, fwd_routes, fwd_gates, bwd_routes, bwd_gates, norm_gain, w_in, w_out):
    layer_inputs = jnp.roll(fwd_prev, 1, axis=0)
    grad_inputs = jnp.roll(bwd_prev, -1, axis=0)
    fwd_out, bwd_out = lax.map(one_section, (layer_inputs, grad_inputs, bwd_saved, fwd_routes, fwd_gates, bwd_routes, bwd_gates, norm_gain, w_in, w_out))
    return (fwd_out, bwd_out)
```

```python
import functools

import jax
import jax.numpy as jnp
from jax import lax
from jax.experimental import pallas as pl
from jax.experimental.pallas import tpu as pltpu
from jax.sharding import PartitionSpec as P

EPS = 1e-06
VMEM_LIMIT = 48 * 1024 * 1024


def passed_along(value, axis, steps):
    count = lax.axis_size(axis)
    pairs = [(source, (source + steps) % count) for source in range(count)]
    return lax.ppermute(value, axis, pairs)


def swapped(value, axis, offset):
    count = lax.axis_size(axis)
    pairs = [(source, source ^ offset) for source in range(count)]
    return lax.ppermute(value, axis, pairs)


def exchanged(blocks, axis):
    return [blocks[0]] + [swapped(blocks[d], axis, d) for d in range(1, len(blocks))]


def slot_table(routes, expert_count):
    top_count, tok_rows = routes.shape
    experts = max(8, expert_count)
    wanted = lax.broadcasted_iota(jnp.int32, (experts, tok_rows), 0)
    member = routes[0:1, :] == wanted
    for k in range(1, top_count):
        member = jnp.logical_or(member, routes[k : k + 1, :] == wanted)
    before = lax.broadcasted_iota(jnp.int32, (tok_rows, tok_rows), 0) < lax.broadcasted_iota(
        jnp.int32, (tok_rows, tok_rows), 1
    )
    slots = jnp.dot(
        member.astype(jnp.bfloat16),
        before.astype(jnp.bfloat16),
        preferred_element_type=jnp.float32,
    )
    return jnp.where(member, slots, -1.0)


def placement(slots, expert, capacity):
    tok_rows = slots.shape[1]
    row = lax.broadcasted_iota(jnp.int32, (capacity, tok_rows), 0).astype(jnp.float32)
    return slots[expert : expert + 1, :] == row


def gate_row(routes, gates, expert):
    total = jnp.zeros((1, routes.shape[1]), jnp.float32)
    for k in range(routes.shape[0]):
        total = total + jnp.where(routes[k : k + 1, :] == expert, gates[k : k + 1, :], 0.0)
    return total


def halves(weights):
    high = weights.astype(jnp.bfloat16)
    low = (weights - high.astype(jnp.float32)).astype(jnp.bfloat16)
    return high, low


def normed_kernel(values_ref, routes_ref, gain_ref, *out_refs):
    expert_count = len(out_refs)
    capacity = out_refs[0].shape[0]
    wide = values_ref[...].astype(jnp.float32)
    inv_rms = lax.rsqrt(jnp.mean(wide * wide, axis=-1, keepdims=True) + EPS)
    normed = (wide * inv_rms * gain_ref[...]).astype(jnp.bfloat16)
    slots = slot_table(routes_ref[...], expert_count)
    for e in range(expert_count):
        place = placement(slots, e, capacity).astype(jnp.bfloat16)
        out_refs[e][...] = jnp.dot(place, normed, preferred_element_type=jnp.float32).astype(
            jnp.bfloat16
        )


def grads_kernel(grads_ref, routes_ref, gates_ref, *out_refs):
    expert_count = len(out_refs)
    capacity = out_refs[0].shape[0]
    grads = grads_ref[...]
    routes = routes_ref[...]
    slots = slot_table(routes, expert_count)
    for e in range(expert_count):
        place = placement(slots, e, capacity)
        high, low = halves(jnp.where(place, gate_row(routes, gates_ref[...], e), 0.0))
        out_refs[e][...] = (
            jnp.dot(high, grads, preferred_element_type=jnp.float32)
            + jnp.dot(low, grads, preferred_element_type=jnp.float32)
        ).astype(jnp.bfloat16)


def rows_dot(weights, rows):
    return lax.dot_general(
        weights, rows, (((0,), (0,)), ((), ())), preferred_element_type=jnp.float32
    )


def fwd_end_kernel(layer_ref, routes_ref, gates_ref, *refs):
    row_refs, out_ref = refs[:-1], refs[-1]
    expert_count = len(row_refs)
    capacity = row_refs[0].shape[0]
    routes = routes_ref[...]
    slots = slot_table(routes, expert_count)
    total = layer_ref[...].astype(jnp.float32)
    for e in range(expert_count):
        place = placement(slots, e, capacity)
        high, low = halves(jnp.where(place, gate_row(routes, gates_ref[...], e), 0.0))
        rows = row_refs[e][...]
        total = total + (rows_dot(high, rows) + rows_dot(low, rows))
    out_ref[...] = total.astype(jnp.bfloat16)


def bwd_end_kernel(grads_ref, saved_ref, gain_ref, routes_ref, *refs):
    row_refs, out_ref = refs[:-1], refs[-1]
    expert_count = len(row_refs)
    capacity = row_refs[0].shape[0]
    features = saved_ref.shape[1]
    slots = slot_table(routes_ref[...], expert_count)
    d_normed = None
    for e in range(expert_count):
        place = placement(slots, e, capacity).astype(jnp.bfloat16)
        part = rows_dot(place, row_refs[e][...])
        d_normed = part if d_normed is None else d_normed + part
    wide = saved_ref[...].astype(jnp.float32)
    inv_rms = lax.rsqrt(jnp.mean(wide * wide, axis=-1, keepdims=True) + EPS)
    scaled = d_normed * gain_ref[...]
    cubed = inv_rms * inv_rms * inv_rms
    inner = jnp.sum(scaled * wide, axis=-1, keepdims=True)
    out_ref[...] = (
        grads_ref[...].astype(jnp.float32) + inv_rms * scaled - cubed / features * wide * inner
    ).astype(jnp.bfloat16)


def local_call(kernel, out_shapes, flops, moved):
    return pl.pallas_call(
        kernel,
        out_shape=out_shapes,
        compiler_params=pltpu.CompilerParams(vmem_limit_bytes=VMEM_LIMIT),
        cost_estimate=pl.CostEstimate(flops=flops, bytes_accessed=moved, transcendentals=0),
    )


def expert_forward(in_rows, weight_in, weight_out, hidden_units):
    projected = jnp.dot(in_rows, weight_in, preferred_element_type=jnp.float32)
    hidden = (jax.nn.silu(projected[:, :hidden_units]) * projected[:, hidden_units:]).astype(
        jnp.bfloat16
    )
    return jnp.dot(hidden, weight_out, preferred_element_type=jnp.float32).astype(jnp.bfloat16)


def expert_backward(in_rows, grad_rows, weight_in, weight_out, hidden_units):
    projected = jnp.dot(in_rows, weight_in, preferred_element_type=jnp.float32)
    gate_pre = projected[:, :hidden_units]
    up_pre = projected[:, hidden_units:]
    d_hidden = lax.dot_general(
        grad_rows, weight_out, (((1,), (1,)), ((), ())), preferred_element_type=jnp.float32
    )
    sigmoid_gate = 1.0 / (1.0 + jnp.exp(-gate_pre))
    d_gate = (d_hidden * up_pre * sigmoid_gate * (1.0 + gate_pre * (1.0 - sigmoid_gate))).astype(
        jnp.bfloat16
    )
    d_up = (d_hidden * gate_pre * sigmoid_gate).astype(jnp.bfloat16)
    d_both = jnp.concatenate([d_gate, d_up], axis=1)
    return lax.dot_general(
        d_both, weight_in, (((1,), (1,)), ((), ())), preferred_element_type=jnp.float32
    ).astype(jnp.bfloat16)


def per_device(
    fwd_prev,
    bwd_prev,
    bwd_saved,
    fwd_routes,
    fwd_gates,
    bwd_routes,
    bwd_gates,
    norm_gain,
    w_in,
    w_out,
):
    expert_count = lax.axis_size("expert")
    tok_rows = fwd_prev.shape[1]
    features = fwd_prev.shape[2]
    top_count = fwd_routes.shape[2]
    hidden_units = w_in.shape[3] // 2
    capacity = 3 * tok_rows * top_count // (2 * expert_count)
    gain_row = norm_gain
    weight_in = w_in[0, 0]
    weight_out = w_out[0, 0]
    me = lax.axis_index("expert")
    f_routes = (fwd_routes[0] ^ me).T
    b_routes = (bwd_routes[0] ^ me).T
    f_gates = fwd_gates[0].T
    b_gates = bwd_gates[0].T
    saved = bwd_saved[0]
    layer_in = passed_along(fwd_prev[0], "section", 1)
    grad_in = passed_along(bwd_prev[0], "section", -1)

    block = jax.ShapeDtypeStruct((capacity, features), jnp.bfloat16)
    whole = jax.ShapeDtypeStruct((tok_rows, features), jnp.bfloat16)
    one_dot = 2 * expert_count * capacity * tok_rows * features
    moved = 2 * features * (tok_rows + expert_count * capacity)
    normed_call = local_call(normed_kernel, [block] * expert_count, one_dot, moved)
    grads_call = local_call(grads_kernel, [block] * expert_count, 2 * one_dot, moved)
    fwd_end = local_call(fwd_end_kernel, whole, 2 * one_dot, moved)
    bwd_end = local_call(bwd_end_kernel, whole, one_dot, moved)

    b_rows = exchanged(normed_call(saved, b_routes, gain_row), "expert")
    f_rows = exchanged(normed_call(layer_in, f_routes, gain_row), "expert")
    g_rows = exchanged(grads_call(grad_in, b_routes, b_gates), "expert")

    def cut(rows):
        return [rows[d * capacity : (d + 1) * capacity] for d in range(expert_count)]

    f_done = expert_forward(jnp.concatenate(f_rows), weight_in, weight_out, hidden_units)
    f_back = exchanged(cut(f_done), "expert")
    b_done = expert_backward(
        jnp.concatenate(b_rows), jnp.concatenate(g_rows), weight_in, weight_out, hidden_units
    )
    b_back = exchanged(cut(b_done), "expert")
    fwd_block = fwd_end(layer_in, f_routes, f_gates, *f_back)
    bwd_block = bwd_end(grad_in, saved, gain_row, b_routes, *b_back)
    return (fwd_block[None], bwd_block[None])


def solution(mesh):
    in_specs = (
        P("section", "expert", None),
        P("section", "expert", None),
        P("section", "expert", None),
        P("section", "expert", None),
        P("section", "expert", None),
        P("section", "expert", None),
        P("section", "expert", None),
        P("section", None),
        P("section", "expert", None, None),
        P("section", "expert", None, None),
    )
    out_specs = (P("section", "expert", None), P("section", "expert", None))
    return jax.shard_map(
        per_device, mesh=mesh, in_specs=in_specs, out_specs=out_specs, check_vma=False
    )
```

```python
import functools

import jax
import jax.numpy as jnp
from jax import lax
from jax.experimental import pallas as pl
from jax.experimental.pallas import tpu as pltpu
from jax.sharding import PartitionSpec as P

EPS = 1e-06
VMEM_LIMIT = 32 * 1024 * 1024


def passed_along(value, axis, steps):
    count = lax.axis_size(axis)
    pairs = [(source, (source + steps) % count) for source in range(count)]
    return lax.ppermute(value, axis, pairs)


def swapped(value, axis, offset):
    count = lax.axis_size(axis)
    pairs = [(source, source ^ offset) for source in range(count)]
    return lax.ppermute(value, axis, pairs)


def exchanged(blocks, axis):
    return [blocks[0]] + [swapped(blocks[d], axis, d) for d in range(1, len(blocks))]


def slot_table(routes, expert_count):
    top_count, tok_rows = routes.shape
    experts = max(8, expert_count)
    wanted = lax.broadcasted_iota(jnp.int32, (experts, tok_rows), 0)
    member = routes[0:1, :] == wanted
    for k in range(1, top_count):
        member = jnp.logical_or(member, routes[k : k + 1, :] == wanted)
    before = lax.broadcasted_iota(jnp.int32, (tok_rows, tok_rows), 0) < lax.broadcasted_iota(
        jnp.int32, (tok_rows, tok_rows), 1
    )
    slots = jnp.dot(
        member.astype(jnp.bfloat16),
        before.astype(jnp.bfloat16),
        preferred_element_type=jnp.float32,
    )
    return jnp.where(member, slots, -1.0)


def placement(slots, expert, capacity):
    tok_rows = slots.shape[1]
    row = lax.broadcasted_iota(jnp.int32, (capacity, tok_rows), 0).astype(jnp.float32)
    return slots[expert : expert + 1, :] == row


def gate_row(routes, gates, expert):
    total = jnp.zeros((1, routes.shape[1]), jnp.float32)
    for k in range(routes.shape[0]):
        total = total + jnp.where(routes[k : k + 1, :] == expert, gates[k : k + 1, :], 0.0)
    return total


def halves(weights):
    high = weights.astype(jnp.bfloat16)
    low = (weights - high.astype(jnp.float32)).astype(jnp.bfloat16)
    return high, low


def rows_dot(weights, rows):
    return lax.dot_general(
        weights, rows, (((0,), (0,)), ((), ())), preferred_element_type=jnp.float32
    )


def fwd_end_kernel(layer_ref, routes_ref, gates_ref, *refs):
    row_refs, out_ref = refs[:-1], refs[-1]
    expert_count = len(row_refs)
    capacity = row_refs[0].shape[0]
    routes = routes_ref[...]
    slots = slot_table(routes, expert_count)
    total = layer_ref[...].astype(jnp.float32)
    for e in range(expert_count):
        place = placement(slots, e, capacity)
        high, low = halves(jnp.where(place, gate_row(routes, gates_ref[...], e), 0.0))
        rows = row_refs[e][...]
        total = total + (rows_dot(high, rows) + rows_dot(low, rows))
    out_ref[...] = total.astype(jnp.bfloat16)


def bwd_end_kernel(grads_ref, saved_ref, gain_ref, routes_ref, *refs):
    row_refs, out_ref = refs[:-1], refs[-1]
    expert_count = len(row_refs)
    capacity = row_refs[0].shape[0]
    features = saved_ref.shape[1]
    slots = slot_table(routes_ref[...], expert_count)
    d_normed = None
    for e in range(expert_count):
        place = placement(slots, e, capacity).astype(jnp.bfloat16)
        part = rows_dot(place, row_refs[e][...])
        d_normed = part if d_normed is None else d_normed + part
    wide = saved_ref[...].astype(jnp.float32)
    inv_rms = lax.rsqrt(jnp.mean(wide * wide, axis=-1, keepdims=True) + EPS)
    scaled = d_normed * gain_ref[...]
    cubed = inv_rms * inv_rms * inv_rms
    inner = jnp.sum(scaled * wide, axis=-1, keepdims=True)
    out_ref[...] = (
        grads_ref[...].astype(jnp.float32) + inv_rms * scaled - cubed / features * wide * inner
    ).astype(jnp.bfloat16)


def tiles(size, step):
    return [(start, min(step, size - start)) for start in range(0, size, step)]


def named_here(table_ref, source, first, top_count, expert):
    rows = table_ref[source]
    routes = rows[first : first + top_count]
    gates = rows[first + top_count : first + 2 * top_count]
    member = routes == expert
    tok_rows = routes.shape[1]
    held = jnp.sum(member.astype(jnp.float32), axis=0, keepdims=True)
    gate = jnp.sum(jnp.where(member, gates, 0.0), axis=0, keepdims=True)
    before = lax.broadcasted_iota(jnp.int32, (tok_rows, tok_rows), 0) < lax.broadcasted_iota(
        jnp.int32, (tok_rows, tok_rows), 1
    )
    slots = jnp.dot(
        jnp.broadcast_to(held, (8, tok_rows)).astype(jnp.bfloat16),
        before.astype(jnp.bfloat16),
        preferred_element_type=jnp.float32,
    )[0:1]
    return jnp.where(held > 0.0, slots, -1.0), gate


def placed_normed(values_ref, table_ref, gain_ref, rows_ref, me, first, top_count):
    expert_count, _, tok_rows = table_ref.shape
    capacity = rows_ref.shape[0] // expert_count
    for d in range(expert_count):
        source = me ^ d
        slots, _ = named_here(table_ref, source, first, top_count, me.astype(jnp.float32))
        wide = values_ref[pl.ds(pl.multiple_of(source * tok_rows, tok_rows), tok_rows), :].astype(
            jnp.float32
        )
        inv_rms = lax.rsqrt(jnp.mean(wide * wide, axis=-1, keepdims=True) + EPS)
        normed = (wide * inv_rms * gain_ref[...]).astype(jnp.bfloat16)
        place = placement(slots, 0, capacity).astype(jnp.bfloat16)
        rows_ref[d * capacity : (d + 1) * capacity, :] = jnp.dot(
            place, normed, preferred_element_type=jnp.float32
        ).astype(jnp.bfloat16)


def placed_grads(grads_ref, table_ref, rows_ref, me, first, top_count):
    expert_count, _, tok_rows = table_ref.shape
    capacity = rows_ref.shape[0] // expert_count
    for d in range(expert_count):
        source = me ^ d
        slots, gate = named_here(table_ref, source, first, top_count, me.astype(jnp.float32))
        grads = grads_ref[pl.ds(pl.multiple_of(source * tok_rows, tok_rows), tok_rows), :]
        high, low = halves(jnp.where(placement(slots, 0, capacity), gate, 0.0))
        rows_ref[d * capacity : (d + 1) * capacity, :] = (
            jnp.dot(high, grads, preferred_element_type=jnp.float32)
            + jnp.dot(low, grads, preferred_element_type=jnp.float32)
        ).astype(jnp.bfloat16)


def expert_fwd_kernel(
    top_count, me_ref, values_ref, table_ref, gain_ref, weight_in, weight_out, *refs
):
    out_refs = refs[:-2]
    rows_ref, hidden_ref = refs[-2:]
    capacity = out_refs[0].shape[0]
    hidden_units, features = weight_out.shape
    placed_normed(values_ref, table_ref, gain_ref, rows_ref, me_ref[0], 0, top_count)
    for start, size in tiles(hidden_units, 256):
        gate = jnp.dot(
            rows_ref[...], weight_in[:, start : start + size], preferred_element_type=jnp.float32
        )
        up = jnp.dot(
            rows_ref[...],
            weight_in[:, hidden_units + start : hidden_units + start + size],
            preferred_element_type=jnp.float32,
        )
        hidden_ref[:, start : start + size] = (gate / (1.0 + jnp.exp(-gate)) * up).astype(
            jnp.bfloat16
        )
    for start, size in tiles(features, 512):
        out = jnp.dot(
            hidden_ref[...], weight_out[:, start : start + size], preferred_element_type=jnp.float32
        )
        for d in range(len(out_refs)):
            out_refs[d][:, start : start + size] = out[d * capacity : (d + 1) * capacity].astype(
                jnp.bfloat16
            )


def expert_bwd_kernel(
    top_count, me_ref, values_ref, grad_in_ref, table_ref, gain_ref, weight_in, weight_out, *refs
):
    out_refs = refs[:-3]
    rows_ref, grads_ref, both_ref = refs[-3:]
    capacity = out_refs[0].shape[0]
    hidden_units, features = weight_out.shape
    first = 2 * top_count
    placed_normed(values_ref, table_ref, gain_ref, rows_ref, me_ref[0], first, top_count)
    placed_grads(grad_in_ref, table_ref, grads_ref, me_ref[0], first, top_count)
    for start, size in tiles(hidden_units, 256):
        gate = jnp.dot(
            rows_ref[...], weight_in[:, start : start + size], preferred_element_type=jnp.float32
        )
        up = jnp.dot(
            rows_ref[...],
            weight_in[:, hidden_units + start : hidden_units + start + size],
            preferred_element_type=jnp.float32,
        )
        d_hidden = lax.dot_general(
            grads_ref[...],
            weight_out[start : start + size, :],
            (((1,), (1,)), ((), ())),
            preferred_element_type=jnp.float32,
        )
        sig = 1.0 / (1.0 + jnp.exp(-gate))
        both_ref[:, start : start + size] = (
            d_hidden * up * sig * (1.0 + gate * (1.0 - sig))
        ).astype(jnp.bfloat16)
        both_ref[:, hidden_units + start : hidden_units + start + size] = (
            d_hidden * gate * sig
        ).astype(jnp.bfloat16)
    for start, size in tiles(features, 512):
        out = lax.dot_general(
            both_ref[...],
            weight_in[start : start + size, :],
            (((1,), (1,)), ((), ())),
            preferred_element_type=jnp.float32,
        )
        for d in range(len(out_refs)):
            out_refs[d][:, start : start + size] = out[d * capacity : (d + 1) * capacity].astype(
                jnp.bfloat16
            )


def local_call(kernel, out_shapes, inputs, flops, moved, scratch=(), scalars=0):
    specs = [pl.BlockSpec(memory_space=pltpu.SMEM)] * scalars
    specs += [pl.BlockSpec(memory_space=pltpu.VMEM)] * (len(inputs) - scalars)
    return pl.pallas_call(
        kernel,
        out_shape=out_shapes,
        in_specs=specs,
        scratch_shapes=list(scratch),
        compiler_params=pltpu.CompilerParams(vmem_limit_bytes=VMEM_LIMIT),
        cost_estimate=pl.CostEstimate(flops=flops, bytes_accessed=moved, transcendentals=0),
    )(*inputs)


def per_device(
    fwd_prev,
    bwd_prev,
    bwd_saved,
    fwd_routes,
    fwd_gates,
    bwd_routes,
    bwd_gates,
    norm_gain,
    w_in,
    w_out,
):
    expert_count = lax.axis_size("expert")
    tok_rows = fwd_prev.shape[1]
    features = fwd_prev.shape[2]
    top_count = fwd_routes.shape[2]
    hidden_units = w_in.shape[3] // 2
    capacity = 3 * tok_rows * top_count // (2 * expert_count)
    gain_row = norm_gain
    weight_in = w_in[0, 0]
    weight_out = w_out[0, 0]
    me = lax.axis_index("expert")
    f_routes = fwd_routes[0].T
    b_routes = bwd_routes[0].T
    f_gates = fwd_gates[0].T
    b_gates = bwd_gates[0].T
    saved = bwd_saved[0]

    def gathered(value):
        return lax.all_gather(value, "expert", axis=0, tiled=True)

    table = lax.all_gather(
        jnp.concatenate(
            [f_routes.astype(jnp.float32), f_gates, b_routes.astype(jnp.float32), b_gates]
        ),
        "expert",
        axis=0,
    )
    all_saved = gathered(saved)
    layer_in = passed_along(fwd_prev[0], "section", 1)
    grad_in = passed_along(bwd_prev[0], "section", -1)
    all_layer = gathered(layer_in)
    all_grads = gathered(grad_in)

    block = jax.ShapeDtypeStruct((capacity, features), jnp.bfloat16)
    whole = jax.ShapeDtypeStruct((tok_rows, features), jnp.bfloat16)
    blocks = [block] * expert_count
    slot_total = expert_count * capacity
    one_dot = 2 * slot_total * tok_rows * features
    moved = 2 * features * (tok_rows + slot_total)
    expert_flops = 2 * slot_total * features * hidden_units
    expert_moved = 2 * features * (3 * hidden_units + 3 * slot_total)
    rows_scratch = pltpu.VMEM((slot_total, features), jnp.bfloat16)
    here = me.astype(jnp.int32).reshape(1)

    f_done = local_call(
        functools.partial(expert_fwd_kernel, top_count),
        blocks,
        (here, all_layer, table, gain_row, weight_in, weight_out),
        3 * expert_flops,
        expert_moved,
        scratch=(rows_scratch, pltpu.VMEM((slot_total, hidden_units), jnp.bfloat16)),
        scalars=1,
    )
    f_back = exchanged(f_done, "expert")
    b_done = local_call(
        functools.partial(expert_bwd_kernel, top_count),
        blocks,
        (here, all_saved, all_grads, table, gain_row, weight_in, weight_out),
        5 * expert_flops,
        expert_moved,
        scratch=(
            rows_scratch,
            rows_scratch,
            pltpu.VMEM((slot_total, 2 * hidden_units), jnp.bfloat16),
        ),
        scalars=1,
    )
    b_back = exchanged(b_done, "expert")
    fwd_block = local_call(
        fwd_end_kernel, whole, (layer_in, f_routes ^ me, f_gates, *f_back), 2 * one_dot, moved
    )
    bwd_block = local_call(
        bwd_end_kernel, whole, (grad_in, saved, gain_row, b_routes ^ me, *b_back), one_dot, moved
    )
    return (fwd_block[None], bwd_block[None])


def solution(mesh):
    in_specs = (
        P("section", "expert", None),
        P("section", "expert", None),
        P("section", "expert", None),
        P("section", "expert", None),
        P("section", "expert", None),
        P("section", "expert", None),
        P("section", "expert", None),
        P("section", None),
        P("section", "expert", None, None),
        P("section", "expert", None, None),
    )
    out_specs = (P("section", "expert", None), P("section", "expert", None))
    return jax.shard_map(
        per_device, mesh=mesh, in_specs=in_specs, out_specs=out_specs, check_vma=False
    )
```

```python
import functools

import jax
import jax.numpy as jnp
from jax import lax
from jax.experimental import pallas as pl
from jax.experimental.pallas import tpu as pltpu
from jax.sharding import PartitionSpec as P

EPS = 1e-06
VMEM_LIMIT = 32 * 1024 * 1024


def passed_along(value, axis, steps):
    count = lax.axis_size(axis)
    pairs = [(source, (source + steps) % count) for source in range(count)]
    return lax.ppermute(value, axis, pairs)


def swapped(value, axis, offset):
    count = lax.axis_size(axis)
    pairs = [(source, source ^ offset) for source in range(count)]
    return lax.ppermute(value, axis, pairs)


def exchanged(blocks, axis):
    return [blocks[0]] + [swapped(blocks[d], axis, d) for d in range(1, len(blocks))]


def slot_table(routes, expert_count):
    top_count, tok_rows = routes.shape
    experts = max(8, expert_count)
    wanted = lax.broadcasted_iota(jnp.int32, (experts, tok_rows), 0)
    member = routes[0:1, :] == wanted
    for k in range(1, top_count):
        member = jnp.logical_or(member, routes[k : k + 1, :] == wanted)
    before = lax.broadcasted_iota(jnp.int32, (tok_rows, tok_rows), 0) < lax.broadcasted_iota(
        jnp.int32, (tok_rows, tok_rows), 1
    )
    slots = jnp.dot(
        member.astype(jnp.bfloat16),
        before.astype(jnp.bfloat16),
        preferred_element_type=jnp.float32,
    )
    return jnp.where(member, slots, -1.0)


def placement(slots, expert, capacity):
    tok_rows = slots.shape[1]
    row = lax.broadcasted_iota(jnp.int32, (capacity, tok_rows), 0).astype(jnp.float32)
    return slots[expert : expert + 1, :] == row


def gate_row(routes, gates, expert):
    total = jnp.zeros((1, routes.shape[1]), jnp.float32)
    for k in range(routes.shape[0]):
        total = total + jnp.where(routes[k : k + 1, :] == expert, gates[k : k + 1, :], 0.0)
    return total


def halves(weights):
    high = weights.astype(jnp.bfloat16)
    low = (weights - high.astype(jnp.float32)).astype(jnp.bfloat16)
    return high, low


def normed_kernel(values_ref, routes_ref, gain_ref, *out_refs):
    expert_count = len(out_refs)
    capacity = out_refs[0].shape[0]
    wide = values_ref[...].astype(jnp.float32)
    inv_rms = lax.rsqrt(jnp.mean(wide * wide, axis=-1, keepdims=True) + EPS)
    normed = (wide * inv_rms * gain_ref[...]).astype(jnp.bfloat16)
    slots = slot_table(routes_ref[...], expert_count)
    for e in range(expert_count):
        place = placement(slots, e, capacity).astype(jnp.bfloat16)
        out_refs[e][...] = jnp.dot(place, normed, preferred_element_type=jnp.float32).astype(
            jnp.bfloat16
        )


def grads_kernel(grads_ref, routes_ref, gates_ref, *out_refs):
    expert_count = len(out_refs)
    capacity = out_refs[0].shape[0]
    grads = grads_ref[...]
    routes = routes_ref[...]
    slots = slot_table(routes, expert_count)
    for e in range(expert_count):
        place = placement(slots, e, capacity)
        high, low = halves(jnp.where(place, gate_row(routes, gates_ref[...], e), 0.0))
        out_refs[e][...] = (
            jnp.dot(high, grads, preferred_element_type=jnp.float32)
            + jnp.dot(low, grads, preferred_element_type=jnp.float32)
        ).astype(jnp.bfloat16)


def rows_dot(weights, rows):
    return lax.dot_general(
        weights, rows, (((0,), (0,)), ((), ())), preferred_element_type=jnp.float32
    )


def fwd_end_kernel(layer_ref, routes_ref, gates_ref, *refs):
    row_refs, out_ref = refs[:-1], refs[-1]
    expert_count = len(row_refs)
    capacity = row_refs[0].shape[0]
    routes = routes_ref[...]
    slots = slot_table(routes, expert_count)
    total = layer_ref[...].astype(jnp.float32)
    for e in range(expert_count):
        place = placement(slots, e, capacity)
        high, low = halves(jnp.where(place, gate_row(routes, gates_ref[...], e), 0.0))
        rows = row_refs[e][...]
        total = total + (rows_dot(high, rows) + rows_dot(low, rows))
    out_ref[...] = total.astype(jnp.bfloat16)


def bwd_end_kernel(grads_ref, saved_ref, gain_ref, routes_ref, *refs):
    row_refs, out_ref = refs[:-1], refs[-1]
    expert_count = len(row_refs)
    capacity = row_refs[0].shape[0]
    features = saved_ref.shape[1]
    slots = slot_table(routes_ref[...], expert_count)
    d_normed = None
    for e in range(expert_count):
        place = placement(slots, e, capacity).astype(jnp.bfloat16)
        part = rows_dot(place, row_refs[e][...])
        d_normed = part if d_normed is None else d_normed + part
    wide = saved_ref[...].astype(jnp.float32)
    inv_rms = lax.rsqrt(jnp.mean(wide * wide, axis=-1, keepdims=True) + EPS)
    scaled = d_normed * gain_ref[...]
    cubed = inv_rms * inv_rms * inv_rms
    inner = jnp.sum(scaled * wide, axis=-1, keepdims=True)
    out_ref[...] = (
        grads_ref[...].astype(jnp.float32) + inv_rms * scaled - cubed / features * wide * inner
    ).astype(jnp.bfloat16)


def joined(refs):
    rows = [ref[...] for ref in refs]
    if rows[0].shape[0] % 16 == 0:
        return jnp.concatenate(rows, axis=0)
    return jnp.concatenate([r.astype(jnp.float32) for r in rows], axis=0).astype(jnp.bfloat16)


def tiles(size, step):
    return [(start, min(step, size - start)) for start in range(0, size, step)]


def expert_fwd_kernel(*refs):
    expert_count = (len(refs) - 4) // 2
    row_refs = refs[:expert_count]
    weight_in, weight_out = refs[expert_count : expert_count + 2]
    out_refs = refs[expert_count + 2 : 2 * expert_count + 2]
    rows_ref, hidden_ref = refs[-2:]
    capacity = row_refs[0].shape[0]
    hidden_units, features = weight_out.shape
    rows_ref[...] = joined(row_refs)
    for start, size in tiles(hidden_units, 256):
        gate = jnp.dot(
            rows_ref[...], weight_in[:, start : start + size], preferred_element_type=jnp.float32
        )
        up = jnp.dot(
            rows_ref[...],
            weight_in[:, hidden_units + start : hidden_units + start + size],
            preferred_element_type=jnp.float32,
        )
        hidden_ref[:, start : start + size] = (gate / (1.0 + jnp.exp(-gate)) * up).astype(
            jnp.bfloat16
        )
    for start, size in tiles(features, 512):
        out = jnp.dot(
            hidden_ref[...], weight_out[:, start : start + size], preferred_element_type=jnp.float32
        )
        for d in range(expert_count):
            out_refs[d][:, start : start + size] = out[d * capacity : (d + 1) * capacity].astype(
                jnp.bfloat16
            )


def expert_again_kernel(*refs):
    expert_count = len(refs) - 4
    row_refs = refs[:expert_count]
    weight_in, gate_ref, up_ref, rows_ref = refs[expert_count:]
    hidden_units = gate_ref.shape[1]
    rows_ref[...] = joined(row_refs)
    for start, size in tiles(hidden_units, 256):
        gate_ref[:, start : start + size] = jnp.dot(
            rows_ref[...], weight_in[:, start : start + size], preferred_element_type=jnp.float32
        )
        up_ref[:, start : start + size] = jnp.dot(
            rows_ref[...],
            weight_in[:, hidden_units + start : hidden_units + start + size],
            preferred_element_type=jnp.float32,
        )


def expert_bwd_kernel(*refs):
    expert_count = (len(refs) - 6) // 2
    grad_refs = refs[:expert_count]
    gate_ref, up_ref, weight_in, weight_out = refs[expert_count : expert_count + 4]
    out_refs = refs[expert_count + 4 : 2 * expert_count + 4]
    grads_ref, both_ref = refs[-2:]
    capacity = grad_refs[0].shape[0]
    hidden_units, features = weight_out.shape
    grads_ref[...] = joined(grad_refs)
    for start, size in tiles(hidden_units, 256):
        gate = gate_ref[:, start : start + size]
        up = up_ref[:, start : start + size]
        d_hidden = lax.dot_general(
            grads_ref[...],
            weight_out[start : start + size, :],
            (((1,), (1,)), ((), ())),
            preferred_element_type=jnp.float32,
        )
        sig = 1.0 / (1.0 + jnp.exp(-gate))
        both_ref[:, start : start + size] = (
            d_hidden * up * sig * (1.0 + gate * (1.0 - sig))
        ).astype(jnp.bfloat16)
        both_ref[:, hidden_units + start : hidden_units + start + size] = (
            d_hidden * gate * sig
        ).astype(jnp.bfloat16)
    for start, size in tiles(features, 512):
        out = lax.dot_general(
            both_ref[...],
            weight_in[start : start + size, :],
            (((1,), (1,)), ((), ())),
            preferred_element_type=jnp.float32,
        )
        for d in range(expert_count):
            out_refs[d][:, start : start + size] = out[d * capacity : (d + 1) * capacity].astype(
                jnp.bfloat16
            )


def local_call(kernel, out_shapes, inputs, flops, moved, scratch=(), after=()):
    in_specs = [pl.BlockSpec(memory_space=pltpu.VMEM)] * len(inputs)
    held = len(inputs)

    def body(*refs):
        kernel(*refs[:held], *refs[held + len(after) :])

    return pl.pallas_call(
        body if after else kernel,
        out_shape=out_shapes,
        in_specs=in_specs + [pl.BlockSpec(memory_space=pl.ANY)] * len(after),
        scratch_shapes=list(scratch),
        compiler_params=pltpu.CompilerParams(vmem_limit_bytes=VMEM_LIMIT),
        cost_estimate=pl.CostEstimate(flops=flops, bytes_accessed=moved, transcendentals=0),
    )(*inputs, *after)


def per_device(
    fwd_prev,
    bwd_prev,
    bwd_saved,
    fwd_routes,
    fwd_gates,
    bwd_routes,
    bwd_gates,
    norm_gain,
    w_in,
    w_out,
):
    expert_count = lax.axis_size("expert")
    tok_rows = fwd_prev.shape[1]
    features = fwd_prev.shape[2]
    top_count = fwd_routes.shape[2]
    hidden_units = w_in.shape[3] // 2
    capacity = 3 * tok_rows * top_count // (2 * expert_count)
    gain_row = norm_gain
    weight_in = w_in[0, 0]
    weight_out = w_out[0, 0]
    me = lax.axis_index("expert")
    f_routes = (fwd_routes[0] ^ me).T
    b_routes = (bwd_routes[0] ^ me).T
    f_gates = fwd_gates[0].T
    b_gates = bwd_gates[0].T
    saved = bwd_saved[0]
    layer_in = passed_along(fwd_prev[0], "section", 1)
    grad_in = passed_along(bwd_prev[0], "section", -1)

    block = jax.ShapeDtypeStruct((capacity, features), jnp.bfloat16)
    whole = jax.ShapeDtypeStruct((tok_rows, features), jnp.bfloat16)
    one_dot = 2 * expert_count * capacity * tok_rows * features
    moved = 2 * features * (tok_rows + expert_count * capacity)
    slot_total = expert_count * capacity
    blocks = [block] * expert_count
    expert_flops = 2 * slot_total * features * hidden_units
    expert_moved = 2 * features * (3 * hidden_units + 3 * slot_total)
    rows_scratch = pltpu.VMEM((slot_total, features), jnp.bfloat16)

    b_sent = local_call(normed_kernel, blocks, (saved, b_routes, gain_row), one_dot, moved)
    b_rows = exchanged(b_sent, "expert")
    f_sent = local_call(
        normed_kernel, blocks, (layer_in, f_routes, gain_row), one_dot, moved, after=(b_sent[0],)
    )
    f_rows = exchanged(f_sent, "expert")
    g_sent = local_call(
        grads_kernel, blocks, (grad_in, b_routes, b_gates), 2 * one_dot, moved, after=(f_sent[0],)
    )
    g_rows = exchanged(g_sent, "expert")
    projected = jax.ShapeDtypeStruct((slot_total, hidden_units), jnp.float32)
    gate_pre, up_pre = local_call(
        expert_again_kernel,
        [projected, projected],
        (*b_rows, weight_in),
        2 * expert_flops,
        expert_moved,
        scratch=(rows_scratch,),
        after=(g_sent[0],),
    )
    f_done = local_call(
        expert_fwd_kernel,
        blocks,
        (*f_rows, weight_in, weight_out),
        3 * expert_flops,
        expert_moved,
        scratch=(rows_scratch, pltpu.VMEM((slot_total, hidden_units), jnp.bfloat16)),
        after=(gate_pre,),
    )
    f_back = exchanged(f_done, "expert")
    b_done = local_call(
        expert_bwd_kernel,
        blocks,
        (*g_rows, gate_pre, up_pre, weight_in, weight_out),
        3 * expert_flops,
        expert_moved,
        scratch=(rows_scratch, pltpu.VMEM((slot_total, 2 * hidden_units), jnp.bfloat16)),
        after=(f_back[1],),
    )
    b_back = exchanged(b_done, "expert")
    fwd_block = local_call(
        fwd_end_kernel,
        whole,
        (layer_in, f_routes, f_gates, *f_back),
        2 * one_dot,
        moved,
        after=(b_done[0],),
    )
    bwd_block = local_call(
        bwd_end_kernel,
        whole,
        (grad_in, saved, gain_row, b_routes, *b_back),
        one_dot,
        moved,
    )
    return (fwd_block[None], bwd_block[None])


def solution(mesh):
    in_specs = (
        P("section", "expert", None),
        P("section", "expert", None),
        P("section", "expert", None),
        P("section", "expert", None),
        P("section", "expert", None),
        P("section", "expert", None),
        P("section", "expert", None),
        P("section", None),
        P("section", "expert", None, None),
        P("section", "expert", None, None),
    )
    out_specs = (P("section", "expert", None), P("section", "expert", None))
    return jax.shard_map(
        per_device, mesh=mesh, in_specs=in_specs, out_specs=out_specs, check_vma=False
    )
```

```python
import functools

import jax
import jax.numpy as jnp
from jax import lax
from jax.experimental import pallas as pl
from jax.experimental.pallas import tpu as pltpu
from jax.sharding import PartitionSpec as P

EPS = 1e-06
VMEM_LIMIT = 32 * 1024 * 1024


def passed_along(value, axis, steps):
    count = lax.axis_size(axis)
    pairs = [(source, (source + steps) % count) for source in range(count)]
    return lax.ppermute(value, axis, pairs)


def swapped(value, axis, offset):
    count = lax.axis_size(axis)
    pairs = [(source, source ^ offset) for source in range(count)]
    return lax.ppermute(value, axis, pairs)


def exchanged(blocks, axis):
    return [blocks[0]] + [swapped(blocks[d], axis, d) for d in range(1, len(blocks))]


def slot_table(routes, expert_count):
    top_count, tok_rows = routes.shape
    experts = max(8, expert_count)
    wanted = lax.broadcasted_iota(jnp.int32, (experts, tok_rows), 0)
    member = routes[0:1, :] == wanted
    for k in range(1, top_count):
        member = jnp.logical_or(member, routes[k : k + 1, :] == wanted)
    before = lax.broadcasted_iota(jnp.int32, (tok_rows, tok_rows), 0) < lax.broadcasted_iota(
        jnp.int32, (tok_rows, tok_rows), 1
    )
    slots = jnp.dot(
        member.astype(jnp.bfloat16),
        before.astype(jnp.bfloat16),
        preferred_element_type=jnp.float32,
    )
    return jnp.where(member, slots, -1.0)


def placement(slots, expert, capacity):
    tok_rows = slots.shape[1]
    row = lax.broadcasted_iota(jnp.int32, (capacity, tok_rows), 0).astype(jnp.float32)
    return slots[expert : expert + 1, :] == row


def gate_row(routes, gates, expert):
    total = jnp.zeros((1, routes.shape[1]), jnp.float32)
    for k in range(routes.shape[0]):
        total = total + jnp.where(routes[k : k + 1, :] == expert, gates[k : k + 1, :], 0.0)
    return total


def halves(weights):
    high = weights.astype(jnp.bfloat16)
    low = (weights - high.astype(jnp.float32)).astype(jnp.bfloat16)
    return high, low


def normed_kernel(values_ref, routes_ref, gain_ref, *out_refs):
    expert_count = len(out_refs)
    capacity = out_refs[0].shape[0]
    wide = values_ref[...].astype(jnp.float32)
    inv_rms = lax.rsqrt(jnp.mean(wide * wide, axis=-1, keepdims=True) + EPS)
    normed = (wide * inv_rms * gain_ref[...]).astype(jnp.bfloat16)
    slots = slot_table(routes_ref[...], expert_count)
    for e in range(expert_count):
        place = placement(slots, e, capacity).astype(jnp.bfloat16)
        out_refs[e][...] = jnp.dot(place, normed, preferred_element_type=jnp.float32).astype(
            jnp.bfloat16
        )


def grads_kernel(grads_ref, routes_ref, gates_ref, *out_refs):
    expert_count = len(out_refs)
    capacity = out_refs[0].shape[0]
    grads = grads_ref[...]
    routes = routes_ref[...]
    slots = slot_table(routes, expert_count)
    for e in range(expert_count):
        place = placement(slots, e, capacity)
        high, low = halves(jnp.where(place, gate_row(routes, gates_ref[...], e), 0.0))
        out_refs[e][...] = (
            jnp.dot(high, grads, preferred_element_type=jnp.float32)
            + jnp.dot(low, grads, preferred_element_type=jnp.float32)
        ).astype(jnp.bfloat16)


def rows_dot(weights, rows):
    return lax.dot_general(
        weights, rows, (((0,), (0,)), ((), ())), preferred_element_type=jnp.float32
    )


def fwd_end_kernel(layer_ref, routes_ref, gates_ref, *refs):
    row_refs, out_ref = refs[:-1], refs[-1]
    expert_count = len(row_refs)
    capacity = row_refs[0].shape[0]
    routes = routes_ref[...]
    slots = slot_table(routes, expert_count)
    total = layer_ref[...].astype(jnp.float32)
    for e in range(expert_count):
        place = placement(slots, e, capacity)
        high, low = halves(jnp.where(place, gate_row(routes, gates_ref[...], e), 0.0))
        rows = row_refs[e][...]
        total = total + (rows_dot(high, rows) + rows_dot(low, rows))
    out_ref[...] = total.astype(jnp.bfloat16)


def bwd_end_kernel(grads_ref, saved_ref, gain_ref, routes_ref, *refs):
    row_refs, out_ref = refs[:-1], refs[-1]
    expert_count = len(row_refs)
    capacity = row_refs[0].shape[0]
    features = saved_ref.shape[1]
    slots = slot_table(routes_ref[...], expert_count)
    d_normed = None
    for e in range(expert_count):
        place = placement(slots, e, capacity).astype(jnp.bfloat16)
        part = rows_dot(place, row_refs[e][...])
        d_normed = part if d_normed is None else d_normed + part
    wide = saved_ref[...].astype(jnp.float32)
    inv_rms = lax.rsqrt(jnp.mean(wide * wide, axis=-1, keepdims=True) + EPS)
    scaled = d_normed * gain_ref[...]
    cubed = inv_rms * inv_rms * inv_rms
    inner = jnp.sum(scaled * wide, axis=-1, keepdims=True)
    out_ref[...] = (
        grads_ref[...].astype(jnp.float32) + inv_rms * scaled - cubed / features * wide * inner
    ).astype(jnp.bfloat16)


def joined(refs):
    rows = [ref[...] for ref in refs]
    if rows[0].shape[0] % 16 == 0:
        return jnp.concatenate(rows, axis=0)
    return jnp.concatenate([r.astype(jnp.float32) for r in rows], axis=0).astype(jnp.bfloat16)


def tiles(size, step):
    return [(start, min(step, size - start)) for start in range(0, size, step)]


def expert_fwd_kernel(*refs):
    expert_count = (len(refs) - 4) // 2
    row_refs = refs[:expert_count]
    weight_in, weight_out = refs[expert_count : expert_count + 2]
    out_refs = refs[expert_count + 2 : 2 * expert_count + 2]
    rows_ref, hidden_ref = refs[-2:]
    capacity = row_refs[0].shape[0]
    hidden_units, features = weight_out.shape
    rows_ref[...] = joined(row_refs)
    for start, size in tiles(hidden_units, 256):
        gate = jnp.dot(
            rows_ref[...], weight_in[:, start : start + size], preferred_element_type=jnp.float32
        )
        up = jnp.dot(
            rows_ref[...],
            weight_in[:, hidden_units + start : hidden_units + start + size],
            preferred_element_type=jnp.float32,
        )
        hidden_ref[:, start : start + size] = (gate / (1.0 + jnp.exp(-gate)) * up).astype(
            jnp.bfloat16
        )
    for start, size in tiles(features, 512):
        out = jnp.dot(
            hidden_ref[...], weight_out[:, start : start + size], preferred_element_type=jnp.float32
        )
        for d in range(expert_count):
            out_refs[d][:, start : start + size] = out[d * capacity : (d + 1) * capacity].astype(
                jnp.bfloat16
            )


def expert_again_kernel(*refs):
    expert_count = len(refs) - 4
    row_refs = refs[:expert_count]
    weight_in, gate_ref, up_ref, rows_ref = refs[expert_count:]
    hidden_units = gate_ref.shape[1]
    rows_ref[...] = joined(row_refs)
    for start, size in tiles(hidden_units, 256):
        gate_ref[:, start : start + size] = jnp.dot(
            rows_ref[...], weight_in[:, start : start + size], preferred_element_type=jnp.float32
        )
        up_ref[:, start : start + size] = jnp.dot(
            rows_ref[...],
            weight_in[:, hidden_units + start : hidden_units + start + size],
            preferred_element_type=jnp.float32,
        )


def expert_bwd_kernel(*refs):
    expert_count = (len(refs) - 6) // 2
    grad_refs = refs[:expert_count]
    gate_ref, up_ref, weight_in, weight_out = refs[expert_count : expert_count + 4]
    out_refs = refs[expert_count + 4 : 2 * expert_count + 4]
    grads_ref, both_ref = refs[-2:]
    capacity = grad_refs[0].shape[0]
    hidden_units, features = weight_out.shape
    grads_ref[...] = joined(grad_refs)
    for start, size in tiles(hidden_units, 256):
        gate = gate_ref[:, start : start + size]
        up = up_ref[:, start : start + size]
        d_hidden = lax.dot_general(
            grads_ref[...],
            weight_out[start : start + size, :],
            (((1,), (1,)), ((), ())),
            preferred_element_type=jnp.float32,
        )
        sig = 1.0 / (1.0 + jnp.exp(-gate))
        both_ref[:, start : start + size] = (
            d_hidden * up * sig * (1.0 + gate * (1.0 - sig))
        ).astype(jnp.bfloat16)
        both_ref[:, hidden_units + start : hidden_units + start + size] = (
            d_hidden * gate * sig
        ).astype(jnp.bfloat16)
    for start, size in tiles(features, 512):
        out = lax.dot_general(
            both_ref[...],
            weight_in[start : start + size, :],
            (((1,), (1,)), ((), ())),
            preferred_element_type=jnp.float32,
        )
        for d in range(expert_count):
            out_refs[d][:, start : start + size] = out[d * capacity : (d + 1) * capacity].astype(
                jnp.bfloat16
            )


def local_call(kernel, out_shapes, inputs, flops, moved, scratch=(), after=()):
    in_specs = [pl.BlockSpec(memory_space=pltpu.VMEM)] * len(inputs)
    held = len(inputs)

    def body(*refs):
        kernel(*refs[:held], *refs[held + len(after) :])

    return pl.pallas_call(
        body if after else kernel,
        out_shape=out_shapes,
        in_specs=in_specs + [pl.BlockSpec(memory_space=pl.ANY)] * len(after),
        scratch_shapes=list(scratch),
        compiler_params=pltpu.CompilerParams(vmem_limit_bytes=VMEM_LIMIT),
        cost_estimate=pl.CostEstimate(flops=flops, bytes_accessed=moved, transcendentals=0),
    )(*inputs, *after)


def per_device_direct(
    fwd_prev,
    bwd_prev,
    bwd_saved,
    fwd_routes,
    fwd_gates,
    bwd_routes,
    bwd_gates,
    norm_gain,
    w_in,
    w_out,
):
    expert_count = lax.axis_size("expert")
    tok_rows = fwd_prev.shape[1]
    features = fwd_prev.shape[2]
    top_count = fwd_routes.shape[2]
    hidden_units = w_in.shape[3] // 2
    capacity = 3 * tok_rows * top_count // (2 * expert_count)
    gain_row = norm_gain
    weight_in = w_in[0, 0]
    weight_out = w_out[0, 0]
    me = lax.axis_index("expert")
    f_routes = (fwd_routes[0] ^ me).T
    b_routes = (bwd_routes[0] ^ me).T
    f_gates = fwd_gates[0].T
    b_gates = bwd_gates[0].T
    saved = bwd_saved[0]
    layer_in = passed_along(fwd_prev[0], "section", 1)
    grad_in = passed_along(bwd_prev[0], "section", -1)

    block = jax.ShapeDtypeStruct((capacity, features), jnp.bfloat16)
    whole = jax.ShapeDtypeStruct((tok_rows, features), jnp.bfloat16)
    one_dot = 2 * expert_count * capacity * tok_rows * features
    moved = 2 * features * (tok_rows + expert_count * capacity)
    slot_total = expert_count * capacity
    blocks = [block] * expert_count
    expert_flops = 2 * slot_total * features * hidden_units
    expert_moved = 2 * features * (3 * hidden_units + 3 * slot_total)
    rows_scratch = pltpu.VMEM((slot_total, features), jnp.bfloat16)

    b_sent = local_call(normed_kernel, blocks, (saved, b_routes, gain_row), one_dot, moved)
    b_rows = exchanged(b_sent, "expert")
    f_sent = local_call(
        normed_kernel, blocks, (layer_in, f_routes, gain_row), one_dot, moved, after=(b_sent[0],)
    )
    f_rows = exchanged(f_sent, "expert")
    g_sent = local_call(
        grads_kernel, blocks, (grad_in, b_routes, b_gates), 2 * one_dot, moved, after=(f_sent[0],)
    )
    g_rows = exchanged(g_sent, "expert")
    projected = jax.ShapeDtypeStruct((slot_total, hidden_units), jnp.float32)
    gate_pre, up_pre = local_call(
        expert_again_kernel,
        [projected, projected],
        (*b_rows, weight_in),
        2 * expert_flops,
        expert_moved,
        scratch=(rows_scratch,),
        after=(g_sent[0],),
    )
    f_done = local_call(
        expert_fwd_kernel,
        blocks,
        (*f_rows, weight_in, weight_out),
        3 * expert_flops,
        expert_moved,
        scratch=(rows_scratch, pltpu.VMEM((slot_total, hidden_units), jnp.bfloat16)),
        after=(gate_pre,),
    )
    f_back = exchanged(f_done, "expert")
    b_done = local_call(
        expert_bwd_kernel,
        blocks,
        (*g_rows, gate_pre, up_pre, weight_in, weight_out),
        3 * expert_flops,
        expert_moved,
        scratch=(rows_scratch, pltpu.VMEM((slot_total, 2 * hidden_units), jnp.bfloat16)),
        after=(f_back[1],),
    )
    b_back = exchanged(b_done, "expert")
    fwd_block = local_call(
        fwd_end_kernel,
        whole,
        (layer_in, f_routes, f_gates, *f_back),
        2 * one_dot,
        moved,
        after=(b_done[0],),
    )
    bwd_block = local_call(
        bwd_end_kernel,
        whole,
        (grad_in, saved, gain_row, b_routes, *b_back),
        one_dot,
        moved,
    )
    return (fwd_block[None], bwd_block[None])


def pick(table, expert, capacity, kind, top_count):
    first = 0 if kind[0] == "f" else 2 * top_count
    routes = table[first : first + top_count]
    gates = table[first + top_count : first + 2 * top_count]
    tok_rows = table.shape[1]
    member = routes == float(expert)
    held = jnp.sum(member.astype(jnp.float32), axis=0, keepdims=True)
    before = lax.broadcasted_iota(jnp.int32, (tok_rows, tok_rows), 0) < lax.broadcasted_iota(
        jnp.int32, (tok_rows, tok_rows), 1
    )
    slots = jnp.dot(
        jnp.broadcast_to(held, (8, tok_rows)).astype(jnp.bfloat16),
        before.astype(jnp.bfloat16),
        preferred_element_type=jnp.float32,
    )[0:1]
    place = placement(jnp.where(held > 0.0, slots, -1.0), 0, capacity)
    if len(kind) == 1:
        return (place.astype(jnp.bfloat16),)
    gate = jnp.sum(jnp.where(member, gates, 0.0), axis=0, keepdims=True)
    return halves(jnp.where(place, gate, 0.0))


def to_slots(weights, values):
    total = None
    for part in weights:
        term = jnp.dot(part, values, preferred_element_type=jnp.float32)
        total = term if total is None else total + term
    return total.astype(jnp.bfloat16)


def to_tokens(weights, rows):
    total = None
    for part in weights:
        term = rows_dot(part, rows)
        total = term if total is None else total + term
    return total


def three_parts(values):
    high = values.astype(jnp.bfloat16)
    rest = values - high.astype(jnp.float32)
    mid = rest.astype(jnp.bfloat16)
    low = (rest - mid.astype(jnp.float32)).astype(jnp.bfloat16)
    return high, mid, low


def normed_halves(wide, gain):
    inv_rms = lax.rsqrt(jnp.mean(wide * wide, axis=-1, keepdims=True) + EPS)
    return (wide * inv_rms * gain).astype(jnp.bfloat16)


def first_kernel(top_count, me_ref, *refs):
    sources, refs = refs[:6], refs[6:]
    (left_ref, right_ref, table_ref), refs = refs[:3], refs[3:]
    held, sems = refs[:6], refs[6]
    copies = [pltpu.make_async_copy(sources[i], held[i], sems.at[i]) for i in range(6)]
    for copy in copies:
        copy.start()
    for copy in copies[1:]:
        copy.wait()
    saved, gain, f_routes, f_gates, b_routes, b_gates = held
    me = me_ref[0]
    fr = (f_routes[...] ^ me).astype(jnp.float32)
    br = (b_routes[...] ^ me).astype(jnp.float32)
    fg = f_gates[...]
    bg = b_gates[...]
    table_ref[...] = jnp.concatenate([fr, fg, br, bg], axis=0)
    packed = [fr.astype(jnp.bfloat16), br.astype(jnp.bfloat16), *three_parts(fg), *three_parts(bg)]
    packed = jnp.concatenate([part.astype(jnp.float32) for part in packed], axis=0)
    tok_rows, features = saved.shape
    half = features // 2
    copies[0].wait()
    normed = normed_halves(saved[...].astype(jnp.float32), gain[...])
    for half_ref, start in ((left_ref, 0), (right_ref, half)):
        half_ref[:tok_rows, :] = normed[:, start : start + half]
        half_ref[tok_rows:, :] = jnp.zeros((half_ref.shape[0] - tok_rows, half), jnp.bfloat16)
        half_ref[tok_rows:, :tok_rows] = packed.astype(jnp.bfloat16)


def unpacked(block, tok_rows, top_count):
    rows = block[tok_rows:, :tok_rows].astype(jnp.float32)
    k = top_count
    fr, br = rows[0:k], rows[k : 2 * k]
    fg = (rows[2 * k : 3 * k] + rows[3 * k : 4 * k]) + rows[4 * k : 5 * k]
    bg = (rows[5 * k : 6 * k] + rows[6 * k : 7 * k]) + rows[7 * k : 8 * k]
    return jnp.concatenate([fr, fg, br, bg], axis=0)


def normed_kernel_halves(values_ref, gain_ref, left_ref, right_ref):
    half = left_ref.shape[1]
    normed = normed_halves(values_ref[...].astype(jnp.float32), gain_ref[...])
    left_ref[...] = normed[:, :half]
    right_ref[...] = normed[:, half:]


def split_kernel(values_ref, left_ref, right_ref):
    half = left_ref.shape[1]
    left_ref[...] = values_ref[:, :half]
    right_ref[...] = values_ref[:, half:]


def tables_kernel(top_count, from_x, from_y, x_table, y_table):
    tok_rows = x_table.shape[1]
    x_table[...] = unpacked(from_x[...], tok_rows, top_count)
    y_table[...] = unpacked(from_y[...], tok_rows, top_count)


def hop_kernel(kind, top_count, own, x_tab, y_tab, left, right, from_x, from_y, to_y, to_x):
    capacity = to_y.shape[0] // 2
    tok_rows = own.shape[1]
    to_y[:capacity, :] = to_slots(pick(own[...], 2, capacity, kind, top_count), left[:tok_rows, :])
    to_y[capacity:, :] = to_slots(
        pick(x_tab[...], 3, capacity, kind, top_count), from_x[:tok_rows, :]
    )
    to_x[:capacity, :] = to_slots(pick(own[...], 1, capacity, kind, top_count), right[:tok_rows, :])
    to_x[capacity:, :] = to_slots(
        pick(y_tab[...], 3, capacity, kind, top_count), from_y[:tok_rows, :]
    )


def assemble(kind, top_count, own, x_tab, y_tab, left, right, from_x, from_y, got_y, got_x, rows):
    capacity = got_y.shape[0] // 2
    half = got_y.shape[1]
    tok_rows = own.shape[1]
    mine = pick(own[...], 0, capacity, kind, top_count)
    rows[:capacity, :half] = to_slots(mine, left[:tok_rows, :])
    rows[:capacity, half:] = to_slots(mine, right[:tok_rows, :])
    rows[capacity : 2 * capacity, :half] = to_slots(
        pick(x_tab[...], 1, capacity, kind, top_count), from_x[:tok_rows, :]
    )
    rows[capacity : 2 * capacity, half:] = got_x[:capacity, :]
    rows[2 * capacity : 3 * capacity, :half] = got_y[:capacity, :]
    rows[2 * capacity : 3 * capacity, half:] = to_slots(
        pick(y_tab[...], 2, capacity, kind, top_count), from_y[:tok_rows, :]
    )
    rows[3 * capacity :, :half] = got_y[capacity:, :]
    rows[3 * capacity :, half:] = got_x[capacity:, :]


def hand_out(out, start, capacity, half, keep, x_left, y_right, to_y, to_x):
    size = out.shape[1]
    rows = out.astype(jnp.bfloat16)
    parts = [rows[d * capacity : (d + 1) * capacity] for d in range(4)]
    keep[:, start : start + size] = parts[0]
    if start < half:
        x_left[:, start : start + size] = parts[1]
        to_y[:capacity, start : start + size] = parts[2]
        to_y[capacity:, start : start + size] = parts[3]
    else:
        at = start - half
        to_x[:capacity, at : at + size] = parts[1]
        y_right[:, at : at + size] = parts[2]
        to_x[capacity:, at : at + size] = parts[3]


def hop_again_kernel(top_count, *refs):
    dispatch, (weight_in, gate_ref, up_ref, rows_ref) = refs[:9], refs[9:]
    assemble("b", top_count, *dispatch, rows_ref)
    hidden_units = gate_ref.shape[1]
    for start, size in tiles(hidden_units, 256):
        gate_ref[:, start : start + size] = jnp.dot(
            rows_ref[...], weight_in[:, start : start + size], preferred_element_type=jnp.float32
        )
        up_ref[:, start : start + size] = jnp.dot(
            rows_ref[...],
            weight_in[:, hidden_units + start : hidden_units + start + size],
            preferred_element_type=jnp.float32,
        )


def hop_fwd_kernel(top_count, *refs):
    dispatch, refs = refs[:9], refs[9:]
    weight_in, weight_out = refs[:2]
    outs, (rows_ref, hidden_ref) = refs[2:7], refs[7:]
    capacity = outs[0].shape[0]
    hidden_units, features = weight_out.shape
    assemble("f", top_count, *dispatch, rows_ref)
    for start, size in tiles(hidden_units, 256):
        gate = jnp.dot(
            rows_ref[...], weight_in[:, start : start + size], preferred_element_type=jnp.float32
        )
        up = jnp.dot(
            rows_ref[...],
            weight_in[:, hidden_units + start : hidden_units + start + size],
            preferred_element_type=jnp.float32,
        )
        hidden_ref[:, start : start + size] = (gate / (1.0 + jnp.exp(-gate)) * up).astype(
            jnp.bfloat16
        )
    for start, size in tiles(features, features // 4):
        out = jnp.dot(
            hidden_ref[...], weight_out[:, start : start + size], preferred_element_type=jnp.float32
        )
        hand_out(out, start, capacity, features // 2, *outs)


def hop_bwd_kernel(top_count, *refs):
    dispatch, refs = refs[:9], refs[9:]
    gate_ref, up_ref, weight_in, weight_out = refs[:4]
    outs, (grads_ref, both_ref) = refs[4:9], refs[9:]
    capacity = outs[0].shape[0]
    hidden_units, features = weight_out.shape
    assemble("bg", top_count, *dispatch, grads_ref)
    for start, size in tiles(hidden_units, 256):
        gate = gate_ref[:, start : start + size]
        up = up_ref[:, start : start + size]
        d_hidden = lax.dot_general(
            grads_ref[...],
            weight_out[start : start + size, :],
            (((1,), (1,)), ((), ())),
            preferred_element_type=jnp.float32,
        )
        sig = 1.0 / (1.0 + jnp.exp(-gate))
        both_ref[:, start : start + size] = (
            d_hidden * up * sig * (1.0 + gate * (1.0 - sig))
        ).astype(jnp.bfloat16)
        both_ref[:, hidden_units + start : hidden_units + start + size] = (
            d_hidden * gate * sig
        ).astype(jnp.bfloat16)
    for start, size in tiles(features, features // 4):
        out = lax.dot_general(
            both_ref[...],
            weight_in[start : start + size, :],
            (((1,), (1,)), ((), ())),
            preferred_element_type=jnp.float32,
        )
        hand_out(out, start, capacity, features // 2, *outs)


def sums_kernel(kind, top_count, x_tab, y_tab, x_left, y_right, got_y, got_x, sum_x, sum_y):
    capacity = x_left.shape[0]
    for table, near, far, out in (
        ((x_tab, 1), x_left, got_y, sum_x),
        ((y_tab, 2), y_right, got_x, sum_y),
    ):
        tab = table[0][...]
        out[...] = (
            to_tokens(pick(tab, table[1], capacity, kind, top_count), near[...])
            + to_tokens(pick(tab, 3, capacity, kind, top_count), far[capacity:, :])
        ).astype(jnp.bfloat16)


def summed(kind, top_count, own, keep, got_y, got_x, sum_x, sum_y):
    capacity, features = keep.shape
    half = features // 2
    mine = pick(own[...], 0, capacity, kind, top_count)
    near_y = pick(own[...], 2, capacity, kind, top_count)
    near_x = pick(own[...], 1, capacity, kind, top_count)
    left = to_tokens(mine, keep[:, :half]) + to_tokens(near_y, got_y[:capacity, :])
    right = to_tokens(mine, keep[:, half:]) + to_tokens(near_x, got_x[:capacity, :])
    return left + sum_x[...].astype(jnp.float32), right + sum_y[...].astype(jnp.float32)


def hop_fwd_end_kernel(top_count, layer_ref, own, keep, got_y, got_x, sum_x, sum_y, out_ref):
    half = got_y.shape[1]
    left, right = summed("fg", top_count, own, keep, got_y, got_x, sum_x, sum_y)
    out_ref[:, :half] = (layer_ref[:, :half].astype(jnp.float32) + left).astype(jnp.bfloat16)
    out_ref[:, half:] = (layer_ref[:, half:].astype(jnp.float32) + right).astype(jnp.bfloat16)


def hop_bwd_end_kernel(
    top_count, grads_ref, saved_ref, gain_ref, own, keep, got_y, got_x, sum_x, sum_y, out_ref
):
    features = saved_ref.shape[1]
    left, right = summed("b", top_count, own, keep, got_y, got_x, sum_x, sum_y)
    wide = saved_ref[...].astype(jnp.float32)
    inv_rms = lax.rsqrt(jnp.mean(wide * wide, axis=-1, keepdims=True) + EPS)
    scaled = jnp.concatenate([left, right], axis=1) * gain_ref[...]
    cubed = inv_rms * inv_rms * inv_rms
    inner = jnp.sum(scaled * wide, axis=-1, keepdims=True)
    out_ref[...] = (
        grads_ref[...].astype(jnp.float32) + inv_rms * scaled - cubed / features * wide * inner
    ).astype(jnp.bfloat16)


def per_device_hops(
    fwd_prev,
    bwd_prev,
    bwd_saved,
    fwd_routes,
    fwd_gates,
    bwd_routes,
    bwd_gates,
    norm_gain,
    w_in,
    w_out,
):
    tok_rows, features = fwd_prev.shape[1:]
    top_count = fwd_routes.shape[2]
    hidden_units = w_in.shape[3] // 2
    capacity = 3 * tok_rows * top_count // 8
    half = features // 2
    gain_row = norm_gain
    weight_in = w_in[0, 0]
    weight_out = w_out[0, 0]
    me = lax.axis_index("expert").astype(jnp.int32).reshape(1)
    saved = bwd_saved[0]
    layer_in = passed_along(fwd_prev[0], "section", 1)
    grad_in = passed_along(bwd_prev[0], "section", -1)

    def shaped(rows, columns, dtype=jnp.bfloat16):
        return jax.ShapeDtypeStruct((rows, columns), dtype)

    def crossed(left, right):
        return swapped(left, "expert", 1), swapped(right, "expert", 2)

    slot_total = 4 * capacity
    table_rows = 4 * top_count
    one_hop = moved = 1024
    expert_flops = 2 * slot_total * features * hidden_units
    expert_moved = 2 * features * (3 * hidden_units + 3 * slot_total)
    rows_scratch = pltpu.VMEM((slot_total, features), jnp.bfloat16)
    halves_out = [shaped(tok_rows, half)] * 2
    hop_out = [shaped(2 * capacity, half)] * 2
    expert_out = [shaped(capacity, features), shaped(capacity, half), shaped(capacity, half)] + hop_out
    table_shape = shaped(table_rows, tok_rows, jnp.float32)
    first_rows = tok_rows + 8 * top_count

    b_left, b_right, own = pl.pallas_call(
        functools.partial(first_kernel, top_count),
        out_shape=[shaped(first_rows, half), shaped(first_rows, half), table_shape],
        in_specs=[pl.BlockSpec(memory_space=pltpu.SMEM)]
        + [pl.BlockSpec(memory_space=pltpu.HBM)] * 6,
        scratch_shapes=[
            pltpu.VMEM((tok_rows, features), jnp.bfloat16),
            pltpu.VMEM((1, features), jnp.float32),
            pltpu.VMEM((top_count, tok_rows), jnp.int32),
            pltpu.VMEM((top_count, tok_rows), jnp.float32),
            pltpu.VMEM((top_count, tok_rows), jnp.int32),
            pltpu.VMEM((top_count, tok_rows), jnp.float32),
            pltpu.SemaphoreType.DMA((6,)),
        ],
        compiler_params=pltpu.CompilerParams(vmem_limit_bytes=VMEM_LIMIT),
        cost_estimate=pl.CostEstimate(flops=one_hop, bytes_accessed=moved, transcendentals=0),
    )(
        me,
        *[
            pltpu.with_memory_space_constraint(value, pltpu.HBM)
            for value in (
                saved,
                gain_row,
                fwd_routes[0].T,
                fwd_gates[0].T,
                bwd_routes[0].T,
                bwd_gates[0].T,
            )
        ],
    )
    b_from_x, b_from_y = crossed(b_left, b_right)
    x_tab, y_tab = local_call(
        functools.partial(tables_kernel, top_count),
        [table_shape] * 2,
        (b_from_x, b_from_y),
        1024,
        1024,
    )
    tabs = (own, x_tab, y_tab)

    def onward(kind, sent, got, after):
        to_y, to_x = local_call(
            functools.partial(hop_kernel, kind, top_count),
            hop_out,
            (*tabs, *sent, *got),
            one_hop,
            moved,
            after=after,
        )
        return swapped(to_y, "expert", 2), swapped(to_x, "expert", 1), to_y

    b_got_y, b_got_x, b_to_y = onward("b", (b_left, b_right), (b_from_x, b_from_y), ())
    f_left, f_right = local_call(
        normed_kernel_halves, halves_out, (layer_in, gain_row), one_hop, moved, after=(b_to_y,)
    )
    f_from_x, f_from_y = crossed(f_left, f_right)
    g_left, g_right = local_call(split_kernel, halves_out, (grad_in,), 1024, moved, after=(f_left,))
    g_from_x, g_from_y = crossed(g_left, g_right)
    f_got_y, f_got_x, f_to_y = onward("f", (f_left, f_right), (f_from_x, f_from_y), (g_left,))
    gate_pre, up_pre = local_call(
        functools.partial(hop_again_kernel, top_count),
        [shaped(slot_total, hidden_units, jnp.float32)] * 2,
        (*tabs, b_left, b_right, b_from_x, b_from_y, b_got_y, b_got_x, weight_in),
        2 * expert_flops,
        expert_moved,
        scratch=(rows_scratch,),
        after=(f_to_y,),
    )
    g_got_y, g_got_x, g_to_y = onward("bg", (g_left, g_right), (g_from_x, g_from_y), (gate_pre,))
    f_keep, f_x_left, f_y_right, f_to_y, f_to_x = local_call(
        functools.partial(hop_fwd_kernel, top_count),
        expert_out,
        (*tabs, f_left, f_right, f_from_x, f_from_y, f_got_y, f_got_x, weight_in, weight_out),
        3 * expert_flops,
        expert_moved,
        scratch=(rows_scratch, pltpu.VMEM((slot_total, hidden_units), jnp.bfloat16)),
        after=(g_to_y,),
    )
    f_ret_y, f_ret_x = swapped(f_to_y, "expert", 2), swapped(f_to_x, "expert", 1)
    b_keep, b_x_left, b_y_right, b_to_y, b_to_x = local_call(
        functools.partial(hop_bwd_kernel, top_count),
        expert_out,
        (
            *tabs,
            g_left,
            g_right,
            g_from_x,
            g_from_y,
            g_got_y,
            g_got_x,
            gate_pre,
            up_pre,
            weight_in,
            weight_out,
        ),
        3 * expert_flops,
        expert_moved,
        scratch=(rows_scratch, pltpu.VMEM((slot_total, 2 * hidden_units), jnp.bfloat16)),
        after=(f_keep,),
    )
    b_ret_y, b_ret_x = swapped(b_to_y, "expert", 2), swapped(b_to_x, "expert", 1)

    def summed_call(kind, x_left, y_right, ret_y, ret_x, after):
        sums = local_call(
            functools.partial(sums_kernel, kind, top_count),
            halves_out,
            (x_tab, y_tab, x_left, y_right, ret_y, ret_x),
            one_hop,
            moved,
            after=after,
        )
        return (*crossed(*sums), sums[0])

    f_sum_x, f_sum_y, f_sum = summed_call("fg", f_x_left, f_y_right, f_ret_y, f_ret_x, (b_keep,))
    b_sum_x, b_sum_y, b_sum = summed_call("b", b_x_left, b_y_right, b_ret_y, b_ret_x, (f_sum,))
    fwd_block = local_call(
        functools.partial(hop_fwd_end_kernel, top_count),
        shaped(tok_rows, features),
        (layer_in, own, f_keep, f_ret_y, f_ret_x, f_sum_x, f_sum_y),
        one_hop,
        moved,
        after=(b_sum,),
    )
    bwd_block = local_call(
        functools.partial(hop_bwd_end_kernel, top_count),
        shaped(tok_rows, features),
        (grad_in, saved, gain_row, own, b_keep, b_ret_y, b_ret_x, b_sum_x, b_sum_y),
        one_hop,
        moved,
    )
    return (fwd_block[None], bwd_block[None])


def per_device(*arrays):
    if lax.axis_size("expert") == 4:
        return per_device_hops(*arrays)
    return per_device_direct(*arrays)


def solution(mesh):
    in_specs = (
        P("section", "expert", None),
        P("section", "expert", None),
        P("section", "expert", None),
        P("section", "expert", None),
        P("section", "expert", None),
        P("section", "expert", None),
        P("section", "expert", None),
        P("section", None),
        P("section", "expert", None, None),
        P("section", "expert", None, None),
    )
    out_specs = (P("section", "expert", None), P("section", "expert", None))
    return jax.shard_map(
        per_device, mesh=mesh, in_specs=in_specs, out_specs=out_specs, check_vma=False
    )
```

```python
import functools

import jax
import jax.numpy as jnp
from jax import lax
from jax.experimental import pallas as pl
from jax.experimental.pallas import tpu as pltpu
from jax.sharding import PartitionSpec as P

EPS = 1e-06
VMEM_LIMIT = 32 * 1024 * 1024


def passed_along(value, axis, steps):
    count = lax.axis_size(axis)
    pairs = [(source, (source + steps) % count) for source in range(count)]
    return lax.ppermute(value, axis, pairs)


def swapped(value, axis, offset):
    count = lax.axis_size(axis)
    pairs = [(source, source ^ offset) for source in range(count)]
    return lax.ppermute(value, axis, pairs)


def exchanged(blocks, axis):
    return [blocks[0]] + [swapped(blocks[d], axis, d) for d in range(1, len(blocks))]


def slot_table(routes, expert_count):
    top_count, tok_rows = routes.shape
    experts = max(8, expert_count)
    wanted = lax.broadcasted_iota(jnp.int32, (experts, tok_rows), 0)
    member = routes[0:1, :] == wanted
    for k in range(1, top_count):
        member = jnp.logical_or(member, routes[k : k + 1, :] == wanted)
    before = lax.broadcasted_iota(jnp.int32, (tok_rows, tok_rows), 0) < lax.broadcasted_iota(
        jnp.int32, (tok_rows, tok_rows), 1
    )
    slots = jnp.dot(
        member.astype(jnp.bfloat16),
        before.astype(jnp.bfloat16),
        preferred_element_type=jnp.float32,
    )
    return jnp.where(member, slots, -1.0)


def placement(slots, expert, capacity):
    tok_rows = slots.shape[1]
    row = lax.broadcasted_iota(jnp.int32, (capacity, tok_rows), 0).astype(jnp.float32)
    return slots[expert : expert + 1, :] == row


def gate_row(routes, gates, expert):
    total = jnp.zeros((1, routes.shape[1]), jnp.float32)
    for k in range(routes.shape[0]):
        total = total + jnp.where(routes[k : k + 1, :] == expert, gates[k : k + 1, :], 0.0)
    return total


def halves(weights):
    high = weights.astype(jnp.bfloat16)
    low = (weights - high.astype(jnp.float32)).astype(jnp.bfloat16)
    return high, low


def normed_kernel(values_ref, routes_ref, gain_ref, *out_refs):
    expert_count = len(out_refs)
    capacity = out_refs[0].shape[0]
    wide = values_ref[...].astype(jnp.float32)
    inv_rms = lax.rsqrt(jnp.mean(wide * wide, axis=-1, keepdims=True) + EPS)
    normed = (wide * inv_rms * gain_ref[...]).astype(jnp.bfloat16)
    slots = slot_table(routes_ref[...], expert_count)
    for e in range(expert_count):
        place = placement(slots, e, capacity).astype(jnp.bfloat16)
        out_refs[e][...] = jnp.dot(place, normed, preferred_element_type=jnp.float32).astype(
            jnp.bfloat16
        )


def grads_kernel(grads_ref, routes_ref, gates_ref, *out_refs):
    expert_count = len(out_refs)
    capacity = out_refs[0].shape[0]
    grads = grads_ref[...]
    routes = routes_ref[...]
    slots = slot_table(routes, expert_count)
    for e in range(expert_count):
        place = placement(slots, e, capacity)
        high, low = halves(jnp.where(place, gate_row(routes, gates_ref[...], e), 0.0))
        out_refs[e][...] = (
            jnp.dot(high, grads, preferred_element_type=jnp.float32)
            + jnp.dot(low, grads, preferred_element_type=jnp.float32)
        ).astype(jnp.bfloat16)


def rows_dot(weights, rows):
    return lax.dot_general(
        weights, rows, (((0,), (0,)), ((), ())), preferred_element_type=jnp.float32
    )


def fwd_end_kernel(layer_ref, routes_ref, gates_ref, *refs):
    row_refs, out_ref = refs[:-1], refs[-1]
    expert_count = len(row_refs)
    capacity = row_refs[0].shape[0]
    routes = routes_ref[...]
    slots = slot_table(routes, expert_count)
    total = layer_ref[...].astype(jnp.float32)
    for e in range(expert_count):
        place = placement(slots, e, capacity)
        high, low = halves(jnp.where(place, gate_row(routes, gates_ref[...], e), 0.0))
        rows = row_refs[e][...]
        total = total + (rows_dot(high, rows) + rows_dot(low, rows))
    out_ref[...] = total.astype(jnp.bfloat16)


def bwd_end_kernel(grads_ref, saved_ref, gain_ref, routes_ref, *refs):
    row_refs, out_ref = refs[:-1], refs[-1]
    expert_count = len(row_refs)
    capacity = row_refs[0].shape[0]
    features = saved_ref.shape[1]
    slots = slot_table(routes_ref[...], expert_count)
    d_normed = None
    for e in range(expert_count):
        place = placement(slots, e, capacity).astype(jnp.bfloat16)
        part = rows_dot(place, row_refs[e][...])
        d_normed = part if d_normed is None else d_normed + part
    wide = saved_ref[...].astype(jnp.float32)
    inv_rms = lax.rsqrt(jnp.mean(wide * wide, axis=-1, keepdims=True) + EPS)
    scaled = d_normed * gain_ref[...]
    cubed = inv_rms * inv_rms * inv_rms
    inner = jnp.sum(scaled * wide, axis=-1, keepdims=True)
    out_ref[...] = (
        grads_ref[...].astype(jnp.float32) + inv_rms * scaled - cubed / features * wide * inner
    ).astype(jnp.bfloat16)


def joined(refs):
    rows = [ref[...] for ref in refs]
    if rows[0].shape[0] % 16 == 0:
        return jnp.concatenate(rows, axis=0)
    return jnp.concatenate([r.astype(jnp.float32) for r in rows], axis=0).astype(jnp.bfloat16)


def tiles(size, step):
    return [(start, min(step, size - start)) for start in range(0, size, step)]


def expert_fwd_kernel(*refs):
    expert_count = (len(refs) - 4) // 2
    row_refs = refs[:expert_count]
    weight_in, weight_out = refs[expert_count : expert_count + 2]
    out_refs = refs[expert_count + 2 : 2 * expert_count + 2]
    rows_ref, hidden_ref = refs[-2:]
    capacity = row_refs[0].shape[0]
    hidden_units, features = weight_out.shape
    rows_ref[...] = joined(row_refs)
    for start, size in tiles(hidden_units, 256):
        gate = jnp.dot(
            rows_ref[...], weight_in[:, start : start + size], preferred_element_type=jnp.float32
        )
        up = jnp.dot(
            rows_ref[...],
            weight_in[:, hidden_units + start : hidden_units + start + size],
            preferred_element_type=jnp.float32,
        )
        hidden_ref[:, start : start + size] = (gate / (1.0 + jnp.exp(-gate)) * up).astype(
            jnp.bfloat16
        )
    for start, size in tiles(features, 512):
        out = jnp.dot(
            hidden_ref[...], weight_out[:, start : start + size], preferred_element_type=jnp.float32
        )
        for d in range(expert_count):
            out_refs[d][:, start : start + size] = out[d * capacity : (d + 1) * capacity].astype(
                jnp.bfloat16
            )


def expert_again_kernel(*refs):
    expert_count = len(refs) - 4
    row_refs = refs[:expert_count]
    weight_in, gate_ref, up_ref, rows_ref = refs[expert_count:]
    hidden_units = gate_ref.shape[1]
    rows_ref[...] = joined(row_refs)
    for start, size in tiles(hidden_units, 256):
        gate_ref[:, start : start + size] = jnp.dot(
            rows_ref[...], weight_in[:, start : start + size], preferred_element_type=jnp.float32
        )
        up_ref[:, start : start + size] = jnp.dot(
            rows_ref[...],
            weight_in[:, hidden_units + start : hidden_units + start + size],
            preferred_element_type=jnp.float32,
        )


def expert_bwd_kernel(*refs):
    expert_count = (len(refs) - 6) // 2
    grad_refs = refs[:expert_count]
    gate_ref, up_ref, weight_in, weight_out = refs[expert_count : expert_count + 4]
    out_refs = refs[expert_count + 4 : 2 * expert_count + 4]
    grads_ref, both_ref = refs[-2:]
    capacity = grad_refs[0].shape[0]
    hidden_units, features = weight_out.shape
    grads_ref[...] = joined(grad_refs)
    for start, size in tiles(hidden_units, 256):
        gate = gate_ref[:, start : start + size]
        up = up_ref[:, start : start + size]
        d_hidden = lax.dot_general(
            grads_ref[...],
            weight_out[start : start + size, :],
            (((1,), (1,)), ((), ())),
            preferred_element_type=jnp.float32,
        )
        sig = 1.0 / (1.0 + jnp.exp(-gate))
        both_ref[:, start : start + size] = (
            d_hidden * up * sig * (1.0 + gate * (1.0 - sig))
        ).astype(jnp.bfloat16)
        both_ref[:, hidden_units + start : hidden_units + start + size] = (
            d_hidden * gate * sig
        ).astype(jnp.bfloat16)
    for start, size in tiles(features, 512):
        out = lax.dot_general(
            both_ref[...],
            weight_in[start : start + size, :],
            (((1,), (1,)), ((), ())),
            preferred_element_type=jnp.float32,
        )
        for d in range(expert_count):
            out_refs[d][:, start : start + size] = out[d * capacity : (d + 1) * capacity].astype(
                jnp.bfloat16
            )


def local_call(kernel, out_shapes, inputs, flops, moved, scratch=(), after=()):
    in_specs = [pl.BlockSpec(memory_space=pltpu.VMEM)] * len(inputs)
    held = len(inputs)

    def body(*refs):
        kernel(*refs[:held], *refs[held + len(after) :])

    return pl.pallas_call(
        body if after else kernel,
        out_shape=out_shapes,
        in_specs=in_specs + [pl.BlockSpec(memory_space=pl.ANY)] * len(after),
        scratch_shapes=list(scratch),
        compiler_params=pltpu.CompilerParams(vmem_limit_bytes=VMEM_LIMIT),
        cost_estimate=pl.CostEstimate(flops=flops, bytes_accessed=moved, transcendentals=0),
    )(*inputs, *after)


def per_device_direct(
    fwd_prev,
    bwd_prev,
    bwd_saved,
    fwd_routes,
    fwd_gates,
    bwd_routes,
    bwd_gates,
    norm_gain,
    w_in,
    w_out,
):
    expert_count = lax.axis_size("expert")
    tok_rows = fwd_prev.shape[1]
    features = fwd_prev.shape[2]
    top_count = fwd_routes.shape[2]
    hidden_units = w_in.shape[3] // 2
    capacity = 3 * tok_rows * top_count // (2 * expert_count)
    gain_row = norm_gain
    weight_in = w_in[0, 0]
    weight_out = w_out[0, 0]
    me = lax.axis_index("expert")
    f_routes = (fwd_routes[0] ^ me).T
    b_routes = (bwd_routes[0] ^ me).T
    f_gates = fwd_gates[0].T
    b_gates = bwd_gates[0].T
    saved = bwd_saved[0]
    layer_in = passed_along(fwd_prev[0], "section", 1)
    grad_in = passed_along(bwd_prev[0], "section", -1)

    block = jax.ShapeDtypeStruct((capacity, features), jnp.bfloat16)
    whole = jax.ShapeDtypeStruct((tok_rows, features), jnp.bfloat16)
    one_dot = 2 * expert_count * capacity * tok_rows * features
    moved = 2 * features * (tok_rows + expert_count * capacity)
    slot_total = expert_count * capacity
    blocks = [block] * expert_count
    expert_flops = 2 * slot_total * features * hidden_units
    expert_moved = 2 * features * (3 * hidden_units + 3 * slot_total)
    rows_scratch = pltpu.VMEM((slot_total, features), jnp.bfloat16)

    b_sent = local_call(normed_kernel, blocks, (saved, b_routes, gain_row), one_dot, moved)
    b_rows = exchanged(b_sent, "expert")
    f_sent = local_call(
        normed_kernel, blocks, (layer_in, f_routes, gain_row), one_dot, moved, after=(b_sent[0],)
    )
    f_rows = exchanged(f_sent, "expert")
    g_sent = local_call(
        grads_kernel, blocks, (grad_in, b_routes, b_gates), 2 * one_dot, moved, after=(f_sent[0],)
    )
    g_rows = exchanged(g_sent, "expert")
    projected = jax.ShapeDtypeStruct((slot_total, hidden_units), jnp.float32)
    gate_pre, up_pre = local_call(
        expert_again_kernel,
        [projected, projected],
        (*b_rows, weight_in),
        2 * expert_flops,
        expert_moved,
        scratch=(rows_scratch,),
        after=(g_sent[0],),
    )
    f_done = local_call(
        expert_fwd_kernel,
        blocks,
        (*f_rows, weight_in, weight_out),
        3 * expert_flops,
        expert_moved,
        scratch=(rows_scratch, pltpu.VMEM((slot_total, hidden_units), jnp.bfloat16)),
        after=(gate_pre,),
    )
    f_back = exchanged(f_done, "expert")
    b_done = local_call(
        expert_bwd_kernel,
        blocks,
        (*g_rows, gate_pre, up_pre, weight_in, weight_out),
        3 * expert_flops,
        expert_moved,
        scratch=(rows_scratch, pltpu.VMEM((slot_total, 2 * hidden_units), jnp.bfloat16)),
        after=(f_back[1],),
    )
    b_back = exchanged(b_done, "expert")
    fwd_block = local_call(
        fwd_end_kernel,
        whole,
        (layer_in, f_routes, f_gates, *f_back),
        2 * one_dot,
        moved,
        after=(b_done[0],),
    )
    bwd_block = local_call(
        bwd_end_kernel,
        whole,
        (grad_in, saved, gain_row, b_routes, *b_back),
        one_dot,
        moved,
    )
    return (fwd_block[None], bwd_block[None])


def pick(table, expert, capacity, kind, top_count):
    first = 0 if kind[0] == "f" else 2 * top_count
    routes = table[first : first + top_count]
    gates = table[first + top_count : first + 2 * top_count]
    tok_rows = table.shape[1]
    member = routes == float(expert)
    held = jnp.sum(member.astype(jnp.float32), axis=0, keepdims=True)
    before = lax.broadcasted_iota(jnp.int32, (tok_rows, tok_rows), 0) < lax.broadcasted_iota(
        jnp.int32, (tok_rows, tok_rows), 1
    )
    slots = jnp.dot(
        jnp.broadcast_to(held, (8, tok_rows)).astype(jnp.bfloat16),
        before.astype(jnp.bfloat16),
        preferred_element_type=jnp.float32,
    )[0:1]
    place = placement(jnp.where(held > 0.0, slots, -1.0), 0, capacity)
    if len(kind) == 1:
        return (place.astype(jnp.bfloat16),)
    gate = jnp.sum(jnp.where(member, gates, 0.0), axis=0, keepdims=True)
    return halves(jnp.where(place, gate, 0.0))


def to_slots(weights, values):
    total = None
    for part in weights:
        term = jnp.dot(part, values, preferred_element_type=jnp.float32)
        total = term if total is None else total + term
    return total.astype(jnp.bfloat16)


def to_tokens(weights, rows):
    total = None
    for part in weights:
        term = rows_dot(part, rows)
        total = term if total is None else total + term
    return total


def three_parts(values):
    high = values.astype(jnp.bfloat16)
    rest = values - high.astype(jnp.float32)
    mid = rest.astype(jnp.bfloat16)
    low = (rest - mid.astype(jnp.float32)).astype(jnp.bfloat16)
    return high, mid, low


def normed_halves(wide, gain):
    inv_rms = lax.rsqrt(jnp.mean(wide * wide, axis=-1, keepdims=True) + EPS)
    return (wide * inv_rms * gain).astype(jnp.bfloat16)


def first_kernel(top_count, me_ref, *refs):
    sources, refs = refs[:6], refs[6:]
    (left_ref, right_ref, table_ref, gain_out), refs = refs[:4], refs[4:]
    held, sems = refs[:6], refs[6]
    copies = [pltpu.make_async_copy(sources[i], held[i], sems.at[i]) for i in range(6)]
    for copy in copies:
        copy.start()
    for copy in copies[1:]:
        copy.wait()
    saved, gain, f_routes, f_gates, b_routes, b_gates = held
    me = me_ref[0]
    fr = (f_routes[...] ^ me).astype(jnp.float32)
    br = (b_routes[...] ^ me).astype(jnp.float32)
    fg = f_gates[...]
    bg = b_gates[...]
    table_ref[...] = jnp.concatenate([fr, fg, br, bg], axis=0)
    packed = [fr.astype(jnp.bfloat16), br.astype(jnp.bfloat16), *three_parts(fg), *three_parts(bg)]
    packed = jnp.concatenate([part.astype(jnp.float32) for part in packed], axis=0)
    gain_out[...] = gain[...]
    tok_rows, features = saved.shape
    half = features // 2
    copies[0].wait()
    normed = normed_halves(saved[...].astype(jnp.float32), gain[...])
    for half_ref, start in ((left_ref, 0), (right_ref, half)):
        half_ref[:tok_rows, :] = normed[:, start : start + half]
        half_ref[tok_rows:, :] = jnp.zeros((half_ref.shape[0] - tok_rows, half), jnp.bfloat16)
        half_ref[tok_rows:, :tok_rows] = packed.astype(jnp.bfloat16)


def unpacked(block, tok_rows, top_count):
    rows = block[tok_rows:, :tok_rows].astype(jnp.float32)
    k = top_count
    fr, br = rows[0:k], rows[k : 2 * k]
    fg = (rows[2 * k : 3 * k] + rows[3 * k : 4 * k]) + rows[4 * k : 5 * k]
    bg = (rows[5 * k : 6 * k] + rows[6 * k : 7 * k]) + rows[7 * k : 8 * k]
    return jnp.concatenate([fr, fg, br, bg], axis=0)


def normed_kernel_halves(values_ref, gain_ref, left_ref, right_ref):
    half = left_ref.shape[1]
    normed = normed_halves(values_ref[...].astype(jnp.float32), gain_ref[...])
    left_ref[...] = normed[:, :half]
    right_ref[...] = normed[:, half:]


def split_kernel(values_ref, left_ref, right_ref):
    half = left_ref.shape[1]
    left_ref[...] = values_ref[:, :half]
    right_ref[...] = values_ref[:, half:]


def tables_kernel(top_count, from_x, from_y, x_table, y_table):
    tok_rows = x_table.shape[1]
    x_table[...] = unpacked(from_x[...], tok_rows, top_count)
    y_table[...] = unpacked(from_y[...], tok_rows, top_count)


def hop_kernel(kind, top_count, own, x_tab, y_tab, left, right, from_x, from_y, to_y, to_x):
    capacity = to_y.shape[0] // 2
    tok_rows = own.shape[1]
    to_y[:capacity, :] = to_slots(pick(own[...], 2, capacity, kind, top_count), left[:tok_rows, :])
    to_y[capacity:, :] = to_slots(
        pick(x_tab[...], 3, capacity, kind, top_count), from_x[:tok_rows, :]
    )
    to_x[:capacity, :] = to_slots(pick(own[...], 1, capacity, kind, top_count), right[:tok_rows, :])
    to_x[capacity:, :] = to_slots(
        pick(y_tab[...], 3, capacity, kind, top_count), from_y[:tok_rows, :]
    )


def assemble(kind, top_count, own, x_tab, y_tab, left, right, from_x, from_y, got_y, got_x, rows):
    capacity = got_y.shape[0] // 2
    half = got_y.shape[1]
    tok_rows = own.shape[1]
    mine = pick(own[...], 0, capacity, kind, top_count)
    rows[:capacity, :half] = to_slots(mine, left[:tok_rows, :])
    rows[:capacity, half:] = to_slots(mine, right[:tok_rows, :])
    rows[capacity : 2 * capacity, :half] = to_slots(
        pick(x_tab[...], 1, capacity, kind, top_count), from_x[:tok_rows, :]
    )
    rows[capacity : 2 * capacity, half:] = got_x[:capacity, :]
    rows[2 * capacity : 3 * capacity, :half] = got_y[:capacity, :]
    rows[2 * capacity : 3 * capacity, half:] = to_slots(
        pick(y_tab[...], 2, capacity, kind, top_count), from_y[:tok_rows, :]
    )
    rows[3 * capacity :, :half] = got_y[capacity:, :]
    rows[3 * capacity :, half:] = got_x[capacity:, :]


def hand_out(out, at, capacity, to_left, keep, near, onward):
    size = out.shape[1]
    rows = out.astype(jnp.bfloat16)
    mine, from_x, from_y, far = [rows[d * capacity : (d + 1) * capacity] for d in range(4)]
    keep[:, at : at + size] = mine
    near[:, at : at + size] = from_x if to_left else from_y
    onward[:capacity, at : at + size] = from_y if to_left else from_x
    onward[capacity:, at : at + size] = far


def fwd_half(hidden_ref, weight_out, to_left, keep, near, onward):
    capacity, half = keep.shape
    first = 0 if to_left else half
    for at, size in tiles(half, 512):
        out = jnp.dot(
            hidden_ref[...],
            weight_out[:, first + at : first + at + size],
            preferred_element_type=jnp.float32,
        )
        hand_out(out, at, capacity, to_left, keep, near, onward)


def bwd_half(both_ref, weight_in, to_left, keep, near, onward):
    capacity, half = keep.shape
    first = 0 if to_left else half
    for at, size in tiles(half, 512):
        out = lax.dot_general(
            both_ref[...],
            weight_in[first + at : first + at + size, :],
            (((1,), (1,)), ((), ())),
            preferred_element_type=jnp.float32,
        )
        hand_out(out, at, capacity, to_left, keep, near, onward)


def fwd_right_kernel(hidden_ref, weight_out, keep, near, onward):
    fwd_half(hidden_ref, weight_out, False, keep, near, onward)


def bwd_right_kernel(both_ref, weight_in, keep, near, onward):
    bwd_half(both_ref, weight_in, False, keep, near, onward)


def hop_again_kernel(top_count, *refs):
    dispatch, (weight_in, gate_ref, up_ref, rows_ref) = refs[:9], refs[9:]
    assemble("b", top_count, *dispatch, rows_ref)
    hidden_units = gate_ref.shape[1]
    for start, size in tiles(hidden_units, 256):
        gate_ref[:, start : start + size] = jnp.dot(
            rows_ref[...], weight_in[:, start : start + size], preferred_element_type=jnp.float32
        )
        up_ref[:, start : start + size] = jnp.dot(
            rows_ref[...],
            weight_in[:, hidden_units + start : hidden_units + start + size],
            preferred_element_type=jnp.float32,
        )


def hop_fwd_kernel(top_count, *refs):
    dispatch, refs = refs[:9], refs[9:]
    weight_in, weight_out = refs[:2]
    outs, hidden_ref, rows_ref = refs[2:5], refs[5], refs[6]
    hidden_units = weight_out.shape[0]
    assemble("f", top_count, *dispatch, rows_ref)
    for start, size in tiles(hidden_units, 256):
        gate = jnp.dot(
            rows_ref[...], weight_in[:, start : start + size], preferred_element_type=jnp.float32
        )
        up = jnp.dot(
            rows_ref[...],
            weight_in[:, hidden_units + start : hidden_units + start + size],
            preferred_element_type=jnp.float32,
        )
        hidden_ref[:, start : start + size] = (gate / (1.0 + jnp.exp(-gate)) * up).astype(
            jnp.bfloat16
        )
    fwd_half(hidden_ref, weight_out, True, *outs)


def hop_bwd_kernel(top_count, *refs):
    dispatch, refs = refs[:9], refs[9:]
    gate_ref, up_ref, weight_in, weight_out = refs[:4]
    outs, both_ref, grads_ref = refs[4:7], refs[7], refs[8]
    hidden_units = weight_out.shape[0]
    assemble("bg", top_count, *dispatch, grads_ref)
    for start, size in tiles(hidden_units, 256):
        gate = gate_ref[:, start : start + size]
        up = up_ref[:, start : start + size]
        d_hidden = lax.dot_general(
            grads_ref[...],
            weight_out[start : start + size, :],
            (((1,), (1,)), ((), ())),
            preferred_element_type=jnp.float32,
        )
        sig = 1.0 / (1.0 + jnp.exp(-gate))
        both_ref[:, start : start + size] = (
            d_hidden * up * sig * (1.0 + gate * (1.0 - sig))
        ).astype(jnp.bfloat16)
        both_ref[:, hidden_units + start : hidden_units + start + size] = (
            d_hidden * gate * sig
        ).astype(jnp.bfloat16)
    bwd_half(both_ref, weight_in, True, *outs)


def sums_kernel(kind, top_count, here, table_ref, near, far, out):
    capacity = near.shape[0]
    table = table_ref[...]
    out[...] = (
        to_tokens(pick(table, here, capacity, kind, top_count), near[...])
        + to_tokens(pick(table, 3, capacity, kind, top_count), far[capacity:, :])
    ).astype(jnp.bfloat16)


def summed(kind, top_count, own, keep_left, keep_right, got_y, got_x, sum_x, sum_y):
    capacity = keep_left.shape[0]
    mine = pick(own[...], 0, capacity, kind, top_count)
    near_y = pick(own[...], 2, capacity, kind, top_count)
    near_x = pick(own[...], 1, capacity, kind, top_count)
    left = to_tokens(mine, keep_left[...]) + to_tokens(near_y, got_y[:capacity, :])
    right = to_tokens(mine, keep_right[...]) + to_tokens(near_x, got_x[:capacity, :])
    return left + sum_x[...].astype(jnp.float32), right + sum_y[...].astype(jnp.float32)


def hop_fwd_end_kernel(top_count, layer_ref, *refs):
    out_ref = refs[-1]
    half = layer_ref.shape[1] // 2
    left, right = summed("fg", top_count, *refs[:-1])
    out_ref[:, :half] = (layer_ref[:, :half].astype(jnp.float32) + left).astype(jnp.bfloat16)
    out_ref[:, half:] = (layer_ref[:, half:].astype(jnp.float32) + right).astype(jnp.bfloat16)


def hop_bwd_end_kernel(top_count, grads_ref, saved_ref, gain_ref, *refs):
    out_ref = refs[-1]
    features = saved_ref.shape[1]
    left, right = summed("b", top_count, *refs[:-1])
    wide = saved_ref[...].astype(jnp.float32)
    inv_rms = lax.rsqrt(jnp.mean(wide * wide, axis=-1, keepdims=True) + EPS)
    scaled = jnp.concatenate([left, right], axis=1) * gain_ref[...]
    cubed = inv_rms * inv_rms * inv_rms
    inner = jnp.sum(scaled * wide, axis=-1, keepdims=True)
    out_ref[...] = (
        grads_ref[...].astype(jnp.float32) + inv_rms * scaled - cubed / features * wide * inner
    ).astype(jnp.bfloat16)


def per_device_hops(
    fwd_prev,
    bwd_prev,
    bwd_saved,
    fwd_routes,
    fwd_gates,
    bwd_routes,
    bwd_gates,
    norm_gain,
    w_in,
    w_out,
):
    tok_rows, features = fwd_prev.shape[1:]
    top_count = fwd_routes.shape[2]
    hidden_units = w_in.shape[3] // 2
    capacity = 3 * tok_rows * top_count // 8
    half = features // 2
    gain_row = norm_gain
    weight_in = w_in[0, 0]
    weight_out = w_out[0, 0]
    me = lax.axis_index("expert").astype(jnp.int32).reshape(1)
    saved = bwd_saved[0]
    layer_in = passed_along(fwd_prev[0], "section", 1)
    grad_in = passed_along(bwd_prev[0], "section", -1)

    def shaped(rows, columns, dtype=jnp.bfloat16):
        return jax.ShapeDtypeStruct((rows, columns), dtype)

    def crossed(left, right):
        return swapped(left, "expert", 1), swapped(right, "expert", 2)

    slot_total = 4 * capacity
    table_rows = 4 * top_count
    one_hop = moved = 1024
    expert_flops = 2 * slot_total * features * hidden_units
    expert_moved = 2 * features * (3 * hidden_units + 3 * slot_total)
    rows_scratch = pltpu.VMEM((slot_total, features), jnp.bfloat16)
    halves_out = [shaped(tok_rows, half)] * 2
    hop_out = [shaped(2 * capacity, half)] * 2
    half_out = [shaped(capacity, half), shaped(capacity, half), shaped(2 * capacity, half)]
    hidden_shape = shaped(slot_total, hidden_units)
    both_shape = shaped(slot_total, 2 * hidden_units)
    table_shape = shaped(table_rows, tok_rows, jnp.float32)
    first_rows = tok_rows + 8 * top_count

    b_left, b_right, own, gain_here = pl.pallas_call(
        functools.partial(first_kernel, top_count),
        out_shape=[
            shaped(first_rows, half),
            shaped(first_rows, half),
            table_shape,
            shaped(1, features, jnp.float32),
        ],
        in_specs=[pl.BlockSpec(memory_space=pltpu.SMEM)]
        + [pl.BlockSpec(memory_space=pltpu.HBM)] * 6,
        scratch_shapes=[
            pltpu.VMEM((tok_rows, features), jnp.bfloat16),
            pltpu.VMEM((1, features), jnp.float32),
            pltpu.VMEM((top_count, tok_rows), jnp.int32),
            pltpu.VMEM((top_count, tok_rows), jnp.float32),
            pltpu.VMEM((top_count, tok_rows), jnp.int32),
            pltpu.VMEM((top_count, tok_rows), jnp.float32),
            pltpu.SemaphoreType.DMA((6,)),
        ],
        compiler_params=pltpu.CompilerParams(vmem_limit_bytes=VMEM_LIMIT),
        cost_estimate=pl.CostEstimate(flops=one_hop, bytes_accessed=moved, transcendentals=0),
    )(
        me,
        *[
            pltpu.with_memory_space_constraint(value, pltpu.HBM)
            for value in (
                saved,
                gain_row,
                fwd_routes[0].T,
                fwd_gates[0].T,
                bwd_routes[0].T,
                bwd_gates[0].T,
            )
        ],
    )
    b_from_x, b_from_y = crossed(b_left, b_right)
    x_tab, y_tab = local_call(
        functools.partial(tables_kernel, top_count),
        [table_shape] * 2,
        (b_from_x, b_from_y),
        1024,
        1024,
    )
    tabs = (own, x_tab, y_tab)

    def onward(kind, sent, got, after):
        to_y, to_x = local_call(
            functools.partial(hop_kernel, kind, top_count),
            hop_out,
            (*tabs, *sent, *got),
            one_hop,
            moved,
            after=after,
        )
        return swapped(to_y, "expert", 2), swapped(to_x, "expert", 1), to_y

    b_got_y, b_got_x, b_to_y = onward("b", (b_left, b_right), (b_from_x, b_from_y), ())
    f_left, f_right = local_call(
        normed_kernel_halves, halves_out, (layer_in, gain_here), one_hop, moved, after=(b_to_y,)
    )
    f_from_x, f_from_y = crossed(f_left, f_right)
    g_left, g_right = local_call(split_kernel, halves_out, (grad_in,), 1024, moved, after=(f_left,))
    g_from_x, g_from_y = crossed(g_left, g_right)
    f_got_y, f_got_x, f_to_y = onward("f", (f_left, f_right), (f_from_x, f_from_y), (g_left,))
    g_got_y, g_got_x, g_to_y = onward("bg", (g_left, g_right), (g_from_x, g_from_y), (f_to_y,))
    gate_pre, up_pre = local_call(
        functools.partial(hop_again_kernel, top_count),
        [shaped(slot_total, hidden_units, jnp.float32)] * 2,
        (*tabs, b_left, b_right, b_from_x, b_from_y, b_got_y, b_got_x, weight_in),
        2 * expert_flops,
        expert_moved,
        scratch=(rows_scratch,),
        after=(g_to_y,),
    )
    f_keep_l, f_near_l, f_on_l, hidden = local_call(
        functools.partial(hop_fwd_kernel, top_count),
        half_out + [hidden_shape],
        (*tabs, f_left, f_right, f_from_x, f_from_y, f_got_y, f_got_x, weight_in, weight_out),
        5 * expert_flops // 2,
        expert_moved,
        scratch=(rows_scratch,),
        after=(gate_pre,),
    )
    f_ret_y = swapped(f_on_l, "expert", 2)
    f_keep_r, f_near_r, f_on_r = local_call(
        fwd_right_kernel, half_out, (hidden, weight_out), 1024, 1024
    )
    f_ret_x = swapped(f_on_r, "expert", 1)
    b_keep_l, b_near_l, b_on_l, both = local_call(
        functools.partial(hop_bwd_kernel, top_count),
        half_out + [both_shape],
        (
            *tabs,
            g_left,
            g_right,
            g_from_x,
            g_from_y,
            g_got_y,
            g_got_x,
            gate_pre,
            up_pre,
            weight_in,
            weight_out,
        ),
        2 * expert_flops,
        expert_moved,
        scratch=(rows_scratch,),
        after=(f_keep_r,),
    )
    b_ret_y = swapped(b_on_l, "expert", 2)
    b_keep_r, b_near_r, b_on_r = local_call(
        bwd_right_kernel, half_out, (both, weight_in), 1024, 1024
    )
    b_ret_x = swapped(b_on_r, "expert", 1)

    def summed_call(kind, here, table, near, far, after):
        part = local_call(
            functools.partial(sums_kernel, kind, top_count, here),
            shaped(tok_rows, half),
            (table, near, far),
            one_hop,
            moved,
            after=after,
        )
        return swapped(part, "expert", here), part

    f_sum_x, last = summed_call("fg", 1, x_tab, f_near_l, f_ret_y, (b_keep_r,))
    f_sum_y, last = summed_call("fg", 2, y_tab, f_near_r, f_ret_x, (last,))
    b_sum_x, last = summed_call("b", 1, x_tab, b_near_l, b_ret_y, (last,))
    b_sum_y, last = summed_call("b", 2, y_tab, b_near_r, b_ret_x, (last,))
    f_keep = (f_keep_l, f_keep_r)
    b_keep = (b_keep_l, b_keep_r)
    fwd_block = local_call(
        functools.partial(hop_fwd_end_kernel, top_count),
        shaped(tok_rows, features),
        (layer_in, own, *f_keep, f_ret_y, f_ret_x, f_sum_x, f_sum_y),
        one_hop,
        moved,
        after=(last,),
    )
    bwd_block = local_call(
        functools.partial(hop_bwd_end_kernel, top_count),
        shaped(tok_rows, features),
        (grad_in, saved, gain_here, own, *b_keep, b_ret_y, b_ret_x, b_sum_x, b_sum_y),
        one_hop,
        moved,
    )
    return (fwd_block[None], bwd_block[None])


def per_device(*arrays):
    if lax.axis_size("expert") == 4:
        return per_device_hops(*arrays)
    return per_device_direct(*arrays)


def solution(mesh):
    in_specs = (
        P("section", "expert", None),
        P("section", "expert", None),
        P("section", "expert", None),
        P("section", "expert", None),
        P("section", "expert", None),
        P("section", "expert", None),
        P("section", "expert", None),
        P("section", None),
        P("section", "expert", None, None),
        P("section", "expert", None, None),
    )
    out_specs = (P("section", "expert", None), P("section", "expert", None))
    return jax.shard_map(
        per_device, mesh=mesh, in_specs=in_specs, out_specs=out_specs, check_vma=False
    )
```

```python
import functools

import jax
import jax.numpy as jnp
from jax import lax
from jax.experimental import pallas as pl
from jax.experimental.pallas import tpu as pltpu
from jax.sharding import PartitionSpec as P

EPS = 1e-06
VMEM_LIMIT = 32 * 1024 * 1024


def passed_along(value, axis, steps):
    count = lax.axis_size(axis)
    pairs = [(source, (source + steps) % count) for source in range(count)]
    return lax.ppermute(value, axis, pairs)


def swapped(value, axis, offset):
    count = lax.axis_size(axis)
    pairs = [(source, source ^ offset) for source in range(count)]
    return lax.ppermute(value, axis, pairs)


def exchanged(blocks, axis):
    return [blocks[0]] + [swapped(blocks[d], axis, d) for d in range(1, len(blocks))]


def slot_table(routes, expert_count):
    top_count, tok_rows = routes.shape
    experts = max(8, expert_count)
    wanted = lax.broadcasted_iota(jnp.int32, (experts, tok_rows), 0)
    member = routes[0:1, :] == wanted
    for k in range(1, top_count):
        member = jnp.logical_or(member, routes[k : k + 1, :] == wanted)
    before = lax.broadcasted_iota(jnp.int32, (tok_rows, tok_rows), 0) < lax.broadcasted_iota(
        jnp.int32, (tok_rows, tok_rows), 1
    )
    slots = jnp.dot(
        member.astype(jnp.bfloat16),
        before.astype(jnp.bfloat16),
        preferred_element_type=jnp.float32,
    )
    return jnp.where(member, slots, -1.0)


def placement(slots, expert, capacity):
    tok_rows = slots.shape[1]
    row = lax.broadcasted_iota(jnp.int32, (capacity, tok_rows), 0).astype(jnp.float32)
    return slots[expert : expert + 1, :] == row


def gate_row(routes, gates, expert):
    total = jnp.zeros((1, routes.shape[1]), jnp.float32)
    for k in range(routes.shape[0]):
        total = total + jnp.where(routes[k : k + 1, :] == expert, gates[k : k + 1, :], 0.0)
    return total


def halves(weights):
    high = weights.astype(jnp.bfloat16)
    low = (weights - high.astype(jnp.float32)).astype(jnp.bfloat16)
    return high, low


def normed_kernel(values_ref, routes_ref, gain_ref, *out_refs):
    expert_count = len(out_refs)
    capacity = out_refs[0].shape[0]
    wide = values_ref[...].astype(jnp.float32)
    inv_rms = lax.rsqrt(jnp.mean(wide * wide, axis=-1, keepdims=True) + EPS)
    normed = (wide * inv_rms * gain_ref[...]).astype(jnp.bfloat16)
    slots = slot_table(routes_ref[...], expert_count)
    for e in range(expert_count):
        place = placement(slots, e, capacity).astype(jnp.bfloat16)
        out_refs[e][...] = jnp.dot(place, normed, preferred_element_type=jnp.float32).astype(
            jnp.bfloat16
        )


def grads_kernel(grads_ref, routes_ref, gates_ref, *out_refs):
    expert_count = len(out_refs)
    capacity = out_refs[0].shape[0]
    grads = grads_ref[...]
    routes = routes_ref[...]
    slots = slot_table(routes, expert_count)
    for e in range(expert_count):
        place = placement(slots, e, capacity)
        high, low = halves(jnp.where(place, gate_row(routes, gates_ref[...], e), 0.0))
        out_refs[e][...] = (
            jnp.dot(high, grads, preferred_element_type=jnp.float32)
            + jnp.dot(low, grads, preferred_element_type=jnp.float32)
        ).astype(jnp.bfloat16)


def rows_dot(weights, rows):
    return lax.dot_general(
        weights, rows, (((0,), (0,)), ((), ())), preferred_element_type=jnp.float32
    )


def fwd_end_kernel(layer_ref, routes_ref, gates_ref, *refs):
    row_refs, out_ref = refs[:-1], refs[-1]
    expert_count = len(row_refs)
    capacity = row_refs[0].shape[0]
    routes = routes_ref[...]
    slots = slot_table(routes, expert_count)
    total = layer_ref[...].astype(jnp.float32)
    for e in range(expert_count):
        place = placement(slots, e, capacity)
        high, low = halves(jnp.where(place, gate_row(routes, gates_ref[...], e), 0.0))
        rows = row_refs[e][...]
        total = total + (rows_dot(high, rows) + rows_dot(low, rows))
    out_ref[...] = total.astype(jnp.bfloat16)


def bwd_end_kernel(grads_ref, saved_ref, gain_ref, routes_ref, *refs):
    row_refs, out_ref = refs[:-1], refs[-1]
    expert_count = len(row_refs)
    capacity = row_refs[0].shape[0]
    features = saved_ref.shape[1]
    slots = slot_table(routes_ref[...], expert_count)
    d_normed = None
    for e in range(expert_count):
        place = placement(slots, e, capacity).astype(jnp.bfloat16)
        part = rows_dot(place, row_refs[e][...])
        d_normed = part if d_normed is None else d_normed + part
    wide = saved_ref[...].astype(jnp.float32)
    inv_rms = lax.rsqrt(jnp.mean(wide * wide, axis=-1, keepdims=True) + EPS)
    scaled = d_normed * gain_ref[...]
    cubed = inv_rms * inv_rms * inv_rms
    inner = jnp.sum(scaled * wide, axis=-1, keepdims=True)
    out_ref[...] = (
        grads_ref[...].astype(jnp.float32) + inv_rms * scaled - cubed / features * wide * inner
    ).astype(jnp.bfloat16)


def joined(refs):
    rows = [ref[...] for ref in refs]
    if rows[0].shape[0] % 16 == 0:
        return jnp.concatenate(rows, axis=0)
    return jnp.concatenate([r.astype(jnp.float32) for r in rows], axis=0).astype(jnp.bfloat16)


def tiles(size, step):
    return [(start, min(step, size - start)) for start in range(0, size, step)]


def expert_fwd_kernel(*refs):
    expert_count = (len(refs) - 4) // 2
    row_refs = refs[:expert_count]
    weight_in, weight_out = refs[expert_count : expert_count + 2]
    out_refs = refs[expert_count + 2 : 2 * expert_count + 2]
    rows_ref, hidden_ref = refs[-2:]
    capacity = row_refs[0].shape[0]
    hidden_units, features = weight_out.shape
    rows_ref[...] = joined(row_refs)
    for start, size in tiles(hidden_units, 256):
        gate = jnp.dot(
            rows_ref[...], weight_in[:, start : start + size], preferred_element_type=jnp.float32
        )
        up = jnp.dot(
            rows_ref[...],
            weight_in[:, hidden_units + start : hidden_units + start + size],
            preferred_element_type=jnp.float32,
        )
        hidden_ref[:, start : start + size] = (gate / (1.0 + jnp.exp(-gate)) * up).astype(
            jnp.bfloat16
        )
    for start, size in tiles(features, 512):
        out = jnp.dot(
            hidden_ref[...], weight_out[:, start : start + size], preferred_element_type=jnp.float32
        )
        for d in range(expert_count):
            out_refs[d][:, start : start + size] = out[d * capacity : (d + 1) * capacity].astype(
                jnp.bfloat16
            )


def expert_again_kernel(*refs):
    expert_count = len(refs) - 4
    row_refs = refs[:expert_count]
    weight_in, gate_ref, up_ref, rows_ref = refs[expert_count:]
    hidden_units = gate_ref.shape[1]
    rows_ref[...] = joined(row_refs)
    for start, size in tiles(hidden_units, 256):
        gate_ref[:, start : start + size] = jnp.dot(
            rows_ref[...], weight_in[:, start : start + size], preferred_element_type=jnp.float32
        )
        up_ref[:, start : start + size] = jnp.dot(
            rows_ref[...],
            weight_in[:, hidden_units + start : hidden_units + start + size],
            preferred_element_type=jnp.float32,
        )


def expert_bwd_kernel(*refs):
    expert_count = (len(refs) - 6) // 2
    grad_refs = refs[:expert_count]
    gate_ref, up_ref, weight_in, weight_out = refs[expert_count : expert_count + 4]
    out_refs = refs[expert_count + 4 : 2 * expert_count + 4]
    grads_ref, both_ref = refs[-2:]
    capacity = grad_refs[0].shape[0]
    hidden_units, features = weight_out.shape
    grads_ref[...] = joined(grad_refs)
    for start, size in tiles(hidden_units, 256):
        gate = gate_ref[:, start : start + size]
        up = up_ref[:, start : start + size]
        d_hidden = lax.dot_general(
            grads_ref[...],
            weight_out[start : start + size, :],
            (((1,), (1,)), ((), ())),
            preferred_element_type=jnp.float32,
        )
        sig = 1.0 / (1.0 + jnp.exp(-gate))
        both_ref[:, start : start + size] = (
            d_hidden * up * sig * (1.0 + gate * (1.0 - sig))
        ).astype(jnp.bfloat16)
        both_ref[:, hidden_units + start : hidden_units + start + size] = (
            d_hidden * gate * sig
        ).astype(jnp.bfloat16)
    for start, size in tiles(features, 512):
        out = lax.dot_general(
            both_ref[...],
            weight_in[start : start + size, :],
            (((1,), (1,)), ((), ())),
            preferred_element_type=jnp.float32,
        )
        for d in range(expert_count):
            out_refs[d][:, start : start + size] = out[d * capacity : (d + 1) * capacity].astype(
                jnp.bfloat16
            )


def local_call(kernel, out_shapes, inputs, flops, moved, scratch=(), after=()):
    in_specs = [pl.BlockSpec(memory_space=pltpu.VMEM)] * len(inputs)
    held = len(inputs)

    def body(*refs):
        kernel(*refs[:held], *refs[held + len(after) :])

    return pl.pallas_call(
        body if after else kernel,
        out_shape=out_shapes,
        in_specs=in_specs + [pl.BlockSpec(memory_space=pl.ANY)] * len(after),
        scratch_shapes=list(scratch),
        compiler_params=pltpu.CompilerParams(vmem_limit_bytes=VMEM_LIMIT),
        cost_estimate=pl.CostEstimate(flops=flops, bytes_accessed=moved, transcendentals=0),
    )(*inputs, *after)


def per_device_direct(
    fwd_prev,
    bwd_prev,
    bwd_saved,
    fwd_routes,
    fwd_gates,
    bwd_routes,
    bwd_gates,
    norm_gain,
    w_in,
    w_out,
):
    expert_count = lax.axis_size("expert")
    tok_rows = fwd_prev.shape[1]
    features = fwd_prev.shape[2]
    top_count = fwd_routes.shape[2]
    hidden_units = w_in.shape[3] // 2
    capacity = 3 * tok_rows * top_count // (2 * expert_count)
    gain_row = norm_gain
    weight_in = w_in[0, 0]
    weight_out = w_out[0, 0]
    me = lax.axis_index("expert")
    f_routes = (fwd_routes[0] ^ me).T
    b_routes = (bwd_routes[0] ^ me).T
    f_gates = fwd_gates[0].T
    b_gates = bwd_gates[0].T
    saved = bwd_saved[0]
    layer_in = passed_along(fwd_prev[0], "section", 1)
    grad_in = passed_along(bwd_prev[0], "section", -1)

    block = jax.ShapeDtypeStruct((capacity, features), jnp.bfloat16)
    whole = jax.ShapeDtypeStruct((tok_rows, features), jnp.bfloat16)
    one_dot = 2 * expert_count * capacity * tok_rows * features
    moved = 2 * features * (tok_rows + expert_count * capacity)
    slot_total = expert_count * capacity
    blocks = [block] * expert_count
    expert_flops = 2 * slot_total * features * hidden_units
    expert_moved = 2 * features * (3 * hidden_units + 3 * slot_total)
    rows_scratch = pltpu.VMEM((slot_total, features), jnp.bfloat16)

    b_sent = local_call(normed_kernel, blocks, (saved, b_routes, gain_row), one_dot, moved)
    b_rows = exchanged(b_sent, "expert")
    f_sent = local_call(
        normed_kernel, blocks, (layer_in, f_routes, gain_row), one_dot, moved, after=(b_sent[0],)
    )
    f_rows = exchanged(f_sent, "expert")
    g_sent = local_call(
        grads_kernel, blocks, (grad_in, b_routes, b_gates), 2 * one_dot, moved, after=(f_sent[0],)
    )
    g_rows = exchanged(g_sent, "expert")
    projected = jax.ShapeDtypeStruct((slot_total, hidden_units), jnp.float32)
    gate_pre, up_pre = local_call(
        expert_again_kernel,
        [projected, projected],
        (*b_rows, weight_in),
        2 * expert_flops,
        expert_moved,
        scratch=(rows_scratch,),
        after=(g_sent[0],),
    )
    f_done = local_call(
        expert_fwd_kernel,
        blocks,
        (*f_rows, weight_in, weight_out),
        3 * expert_flops,
        expert_moved,
        scratch=(rows_scratch, pltpu.VMEM((slot_total, hidden_units), jnp.bfloat16)),
        after=(gate_pre,),
    )
    f_back = exchanged(f_done, "expert")
    b_done = local_call(
        expert_bwd_kernel,
        blocks,
        (*g_rows, gate_pre, up_pre, weight_in, weight_out),
        3 * expert_flops,
        expert_moved,
        scratch=(rows_scratch, pltpu.VMEM((slot_total, 2 * hidden_units), jnp.bfloat16)),
        after=(f_back[1],),
    )
    b_back = exchanged(b_done, "expert")
    fwd_block = local_call(
        fwd_end_kernel,
        whole,
        (layer_in, f_routes, f_gates, *f_back),
        2 * one_dot,
        moved,
        after=(b_done[0],),
    )
    bwd_block = local_call(
        bwd_end_kernel,
        whole,
        (grad_in, saved, gain_row, b_routes, *b_back),
        one_dot,
        moved,
    )
    return (fwd_block[None], bwd_block[None])


def pick(table, expert, capacity, kind, top_count):
    first = 0 if kind[0] == "f" else 2 * top_count
    routes = table[first : first + top_count]
    gates = table[first + top_count : first + 2 * top_count]
    tok_rows = table.shape[1]
    member = routes == float(expert)
    held = jnp.sum(member.astype(jnp.float32), axis=0, keepdims=True)
    before = lax.broadcasted_iota(jnp.int32, (tok_rows, tok_rows), 0) < lax.broadcasted_iota(
        jnp.int32, (tok_rows, tok_rows), 1
    )
    slots = jnp.dot(
        jnp.broadcast_to(held, (8, tok_rows)).astype(jnp.bfloat16),
        before.astype(jnp.bfloat16),
        preferred_element_type=jnp.float32,
    )[0:1]
    place = placement(jnp.where(held > 0.0, slots, -1.0), 0, capacity)
    if len(kind) == 1:
        return (place.astype(jnp.bfloat16),)
    gate = jnp.sum(jnp.where(member, gates, 0.0), axis=0, keepdims=True)
    return halves(jnp.where(place, gate, 0.0))


def to_slots(weights, values):
    total = None
    for part in weights:
        term = jnp.dot(part, values, preferred_element_type=jnp.float32)
        total = term if total is None else total + term
    return total.astype(jnp.bfloat16)


def to_tokens(weights, rows):
    total = None
    for part in weights:
        term = rows_dot(part, rows)
        total = term if total is None else total + term
    return total


def three_parts(values):
    high = values.astype(jnp.bfloat16)
    rest = values - high.astype(jnp.float32)
    mid = rest.astype(jnp.bfloat16)
    low = (rest - mid.astype(jnp.float32)).astype(jnp.bfloat16)
    return high, mid, low


def normed_halves(wide, gain):
    inv_rms = lax.rsqrt(jnp.mean(wide * wide, axis=-1, keepdims=True) + EPS)
    return (wide * inv_rms * gain).astype(jnp.bfloat16)


def first_kernel(top_count, me_ref, *refs):
    sources, refs = refs[:8], refs[8:]
    (left_ref, right_ref, table_ref, gain_out, fwd_out, bwd_out), refs = refs[:6], refs[6:]
    sems = refs[6]
    held = (*refs[:6], fwd_out, bwd_out)
    copies = [pltpu.make_async_copy(sources[i], held[i], sems.at[i]) for i in range(8)]
    for copy in copies:
        copy.start()
    for copy in copies[1:6]:
        copy.wait()
    saved, gain, f_routes, f_gates, b_routes, b_gates = held[:6]
    me = me_ref[0]
    fr = (f_routes[...] ^ me).astype(jnp.float32)
    br = (b_routes[...] ^ me).astype(jnp.float32)
    fg = f_gates[...]
    bg = b_gates[...]
    table_ref[...] = jnp.concatenate([fr, fg, br, bg], axis=0)
    packed = [fr.astype(jnp.bfloat16), br.astype(jnp.bfloat16), *three_parts(fg), *three_parts(bg)]
    packed = jnp.concatenate([part.astype(jnp.float32) for part in packed], axis=0)
    gain_out[...] = gain[...]
    tok_rows, features = saved.shape
    half = features // 2
    copies[0].wait()
    normed = normed_halves(saved[...].astype(jnp.float32), gain[...])
    for half_ref, start in ((left_ref, 0), (right_ref, half)):
        half_ref[:tok_rows, :] = normed[:, start : start + half]
        half_ref[tok_rows:, :] = jnp.zeros((half_ref.shape[0] - tok_rows, half), jnp.bfloat16)
        half_ref[tok_rows:, :tok_rows] = packed.astype(jnp.bfloat16)
    for copy in copies[6:]:
        copy.wait()


def unpacked(block, tok_rows, top_count):
    rows = block[tok_rows:, :tok_rows].astype(jnp.float32)
    k = top_count
    fr, br = rows[0:k], rows[k : 2 * k]
    fg = (rows[2 * k : 3 * k] + rows[3 * k : 4 * k]) + rows[4 * k : 5 * k]
    bg = (rows[5 * k : 6 * k] + rows[6 * k : 7 * k]) + rows[7 * k : 8 * k]
    return jnp.concatenate([fr, fg, br, bg], axis=0)


def normed_kernel_halves(values_ref, gain_ref, left_ref, right_ref):
    half = left_ref.shape[1]
    normed = normed_halves(values_ref[...].astype(jnp.float32), gain_ref[...])
    left_ref[...] = normed[:, :half]
    right_ref[...] = normed[:, half:]


def split_kernel(values_ref, left_ref, right_ref):
    half = left_ref.shape[1]
    left_ref[...] = values_ref[:, :half]
    right_ref[...] = values_ref[:, half:]


def tables_kernel(top_count, from_x, from_y, x_table, y_table):
    tok_rows = x_table.shape[1]
    x_table[...] = unpacked(from_x[...], tok_rows, top_count)
    y_table[...] = unpacked(from_y[...], tok_rows, top_count)


def hop_kernel(kind, top_count, own, x_tab, y_tab, left, right, from_x, from_y, to_y, to_x):
    capacity = to_y.shape[0] // 2
    tok_rows = own.shape[1]
    to_y[:capacity, :] = to_slots(pick(own[...], 2, capacity, kind, top_count), left[:tok_rows, :])
    to_y[capacity:, :] = to_slots(
        pick(x_tab[...], 3, capacity, kind, top_count), from_x[:tok_rows, :]
    )
    to_x[:capacity, :] = to_slots(pick(own[...], 1, capacity, kind, top_count), right[:tok_rows, :])
    to_x[capacity:, :] = to_slots(
        pick(y_tab[...], 3, capacity, kind, top_count), from_y[:tok_rows, :]
    )


def assemble(kind, top_count, own, x_tab, y_tab, left, right, from_x, from_y, got_y, got_x, rows):
    capacity = got_y.shape[0] // 2
    half = got_y.shape[1]
    tok_rows = own.shape[1]
    mine = pick(own[...], 0, capacity, kind, top_count)
    rows[:capacity, :half] = to_slots(mine, left[:tok_rows, :])
    rows[:capacity, half:] = to_slots(mine, right[:tok_rows, :])
    rows[capacity : 2 * capacity, :half] = to_slots(
        pick(x_tab[...], 1, capacity, kind, top_count), from_x[:tok_rows, :]
    )
    rows[capacity : 2 * capacity, half:] = got_x[:capacity, :]
    rows[2 * capacity : 3 * capacity, :half] = got_y[:capacity, :]
    rows[2 * capacity : 3 * capacity, half:] = to_slots(
        pick(y_tab[...], 2, capacity, kind, top_count), from_y[:tok_rows, :]
    )
    rows[3 * capacity :, :half] = got_y[capacity:, :]
    rows[3 * capacity :, half:] = got_x[capacity:, :]


def hand_out(out, at, capacity, to_left, keep, near, onward):
    size = out.shape[1]
    rows = out.astype(jnp.bfloat16)
    mine, from_x, from_y, far = [rows[d * capacity : (d + 1) * capacity] for d in range(4)]
    keep[:, at : at + size] = mine
    near[:, at : at + size] = from_x if to_left else from_y
    onward[:capacity, at : at + size] = from_y if to_left else from_x
    onward[capacity:, at : at + size] = far


def fwd_half(hidden_ref, weight_out, to_left, keep, near, onward):
    capacity, half = keep.shape
    first = 0 if to_left else half
    for at, size in tiles(half, 512):
        out = jnp.dot(
            hidden_ref[...],
            weight_out[:, first + at : first + at + size],
            preferred_element_type=jnp.float32,
        )
        hand_out(out, at, capacity, to_left, keep, near, onward)


def bwd_half(both_ref, weight_in, to_left, keep, near, onward):
    capacity, half = keep.shape
    first = 0 if to_left else half
    for at, size in tiles(half, 512):
        out = lax.dot_general(
            both_ref[...],
            weight_in[first + at : first + at + size, :],
            (((1,), (1,)), ((), ())),
            preferred_element_type=jnp.float32,
        )
        hand_out(out, at, capacity, to_left, keep, near, onward)


def fwd_right_kernel(hidden_ref, weight_out, keep, near, onward):
    fwd_half(hidden_ref, weight_out, False, keep, near, onward)


def bwd_right_kernel(both_ref, weight_in, keep, near, onward):
    bwd_half(both_ref, weight_in, False, keep, near, onward)


def hop_again_kernel(top_count, *refs):
    dispatch, (weight_in, gate_ref, up_ref, rows_ref) = refs[:9], refs[9:]
    assemble("b", top_count, *dispatch, rows_ref)
    hidden_units = gate_ref.shape[1]
    for start, size in tiles(hidden_units, 256):
        gate_ref[:, start : start + size] = jnp.dot(
            rows_ref[...], weight_in[:, start : start + size], preferred_element_type=jnp.float32
        )
        up_ref[:, start : start + size] = jnp.dot(
            rows_ref[...],
            weight_in[:, hidden_units + start : hidden_units + start + size],
            preferred_element_type=jnp.float32,
        )


def hop_fwd_kernel(top_count, *refs):
    dispatch, refs = refs[:9], refs[9:]
    weight_in, weight_out = refs[:2]
    outs, hidden_ref, rows_ref = refs[2:5], refs[5], refs[6]
    hidden_units = weight_out.shape[0]
    assemble("f", top_count, *dispatch, rows_ref)
    for start, size in tiles(hidden_units, 256):
        gate = jnp.dot(
            rows_ref[...], weight_in[:, start : start + size], preferred_element_type=jnp.float32
        )
        up = jnp.dot(
            rows_ref[...],
            weight_in[:, hidden_units + start : hidden_units + start + size],
            preferred_element_type=jnp.float32,
        )
        hidden_ref[:, start : start + size] = (gate / (1.0 + jnp.exp(-gate)) * up).astype(
            jnp.bfloat16
        )
    fwd_half(hidden_ref, weight_out, True, *outs)


def hop_bwd_kernel(top_count, *refs):
    dispatch, refs = refs[:9], refs[9:]
    gate_ref, up_ref, weight_in, weight_out = refs[:4]
    outs, both_ref, grads_ref = refs[4:7], refs[7], refs[8]
    hidden_units = weight_out.shape[0]
    assemble("bg", top_count, *dispatch, grads_ref)
    for start, size in tiles(hidden_units, 256):
        gate = gate_ref[:, start : start + size]
        up = up_ref[:, start : start + size]
        d_hidden = lax.dot_general(
            grads_ref[...],
            weight_out[start : start + size, :],
            (((1,), (1,)), ((), ())),
            preferred_element_type=jnp.float32,
        )
        sig = 1.0 / (1.0 + jnp.exp(-gate))
        both_ref[:, start : start + size] = (
            d_hidden * up * sig * (1.0 + gate * (1.0 - sig))
        ).astype(jnp.bfloat16)
        both_ref[:, hidden_units + start : hidden_units + start + size] = (
            d_hidden * gate * sig
        ).astype(jnp.bfloat16)
    bwd_half(both_ref, weight_in, True, *outs)


def sums_kernel(kind, top_count, here, table_ref, near, far, out):
    capacity = near.shape[0]
    table = table_ref[...]
    out[...] = (
        to_tokens(pick(table, here, capacity, kind, top_count), near[...])
        + to_tokens(pick(table, 3, capacity, kind, top_count), far[capacity:, :])
    ).astype(jnp.bfloat16)


def summed(kind, top_count, own, keep_left, keep_right, got_y, got_x, sum_x, sum_y):
    capacity = keep_left.shape[0]
    mine = pick(own[...], 0, capacity, kind, top_count)
    near_y = pick(own[...], 2, capacity, kind, top_count)
    near_x = pick(own[...], 1, capacity, kind, top_count)
    left = to_tokens(mine, keep_left[...]) + to_tokens(near_y, got_y[:capacity, :])
    right = to_tokens(mine, keep_right[...]) + to_tokens(near_x, got_x[:capacity, :])
    return left + sum_x[...].astype(jnp.float32), right + sum_y[...].astype(jnp.float32)


def hop_fwd_end_kernel(top_count, layer_ref, *refs):
    out_ref = refs[-1]
    half = layer_ref.shape[1] // 2
    left, right = summed("fg", top_count, *refs[:-1])
    out_ref[:, :half] = (layer_ref[:, :half].astype(jnp.float32) + left).astype(jnp.bfloat16)
    out_ref[:, half:] = (layer_ref[:, half:].astype(jnp.float32) + right).astype(jnp.bfloat16)


def hop_bwd_end_kernel(top_count, grads_ref, saved_ref, gain_ref, *refs):
    out_ref = refs[-1]
    features = saved_ref.shape[1]
    left, right = summed("b", top_count, *refs[:-1])
    wide = saved_ref[...].astype(jnp.float32)
    inv_rms = lax.rsqrt(jnp.mean(wide * wide, axis=-1, keepdims=True) + EPS)
    scaled = jnp.concatenate([left, right], axis=1) * gain_ref[...]
    cubed = inv_rms * inv_rms * inv_rms
    inner = jnp.sum(scaled * wide, axis=-1, keepdims=True)
    out_ref[...] = (
        grads_ref[...].astype(jnp.float32) + inv_rms * scaled - cubed / features * wide * inner
    ).astype(jnp.bfloat16)


def per_device_hops(
    fwd_prev,
    bwd_prev,
    bwd_saved,
    fwd_routes,
    fwd_gates,
    bwd_routes,
    bwd_gates,
    norm_gain,
    w_in,
    w_out,
):
    tok_rows, features = fwd_prev.shape[1:]
    top_count = fwd_routes.shape[2]
    hidden_units = w_in.shape[3] // 2
    capacity = 3 * tok_rows * top_count // 8
    half = features // 2
    gain_row = norm_gain
    weight_in = w_in[0, 0]
    weight_out = w_out[0, 0]
    me = lax.axis_index("expert").astype(jnp.int32).reshape(1)
    saved = bwd_saved[0]

    def shaped(rows, columns, dtype=jnp.bfloat16):
        return jax.ShapeDtypeStruct((rows, columns), dtype)

    def crossed(left, right):
        return swapped(left, "expert", 1), swapped(right, "expert", 2)

    slot_total = 4 * capacity
    table_rows = 4 * top_count
    one_hop = moved = 1024
    expert_flops = 2 * slot_total * features * hidden_units
    expert_moved = 2 * features * (3 * hidden_units + 3 * slot_total)
    rows_scratch = pltpu.VMEM((slot_total, features), jnp.bfloat16)
    halves_out = [shaped(tok_rows, half)] * 2
    hop_out = [shaped(2 * capacity, half)] * 2
    half_out = [shaped(capacity, half), shaped(capacity, half), shaped(2 * capacity, half)]
    hidden_shape = shaped(slot_total, hidden_units)
    both_shape = shaped(slot_total, 2 * hidden_units)
    table_shape = shaped(table_rows, tok_rows, jnp.float32)
    first_rows = tok_rows + 8 * top_count

    b_left, b_right, own, gain_here, fwd_here, bwd_here = pl.pallas_call(
        functools.partial(first_kernel, top_count),
        out_shape=[
            shaped(first_rows, half),
            shaped(first_rows, half),
            table_shape,
            shaped(1, features, jnp.float32),
            shaped(tok_rows, features),
            shaped(tok_rows, features),
        ],
        in_specs=[pl.BlockSpec(memory_space=pltpu.SMEM)]
        + [pl.BlockSpec(memory_space=pltpu.HBM)] * 8,
        scratch_shapes=[
            pltpu.VMEM((tok_rows, features), jnp.bfloat16),
            pltpu.VMEM((1, features), jnp.float32),
            pltpu.VMEM((top_count, tok_rows), jnp.int32),
            pltpu.VMEM((top_count, tok_rows), jnp.float32),
            pltpu.VMEM((top_count, tok_rows), jnp.int32),
            pltpu.VMEM((top_count, tok_rows), jnp.float32),
            pltpu.SemaphoreType.DMA((8,)),
        ],
        compiler_params=pltpu.CompilerParams(vmem_limit_bytes=VMEM_LIMIT),
        cost_estimate=pl.CostEstimate(flops=one_hop, bytes_accessed=moved, transcendentals=0),
    )(
        me,
        *[
            pltpu.with_memory_space_constraint(value, pltpu.HBM)
            for value in (
                saved,
                gain_row,
                fwd_routes[0].T,
                fwd_gates[0].T,
                bwd_routes[0].T,
                bwd_gates[0].T,
                fwd_prev[0],
                bwd_prev[0],
            )
        ],
    )
    layer_in = passed_along(fwd_here, "section", 1)
    grad_in = passed_along(bwd_here, "section", -1)
    b_from_x, b_from_y = crossed(b_left, b_right)
    f_left, f_right = local_call(
        normed_kernel_halves, halves_out, (layer_in, gain_here), one_hop, moved, after=(b_left,)
    )
    f_from_x, f_from_y = crossed(f_left, f_right)
    g_left, g_right = local_call(split_kernel, halves_out, (grad_in,), 1024, moved, after=(f_left,))
    g_from_x, g_from_y = crossed(g_left, g_right)
    x_tab, y_tab = local_call(
        functools.partial(tables_kernel, top_count),
        [table_shape] * 2,
        (b_from_x, b_from_y),
        1024,
        1024,
        after=(g_left,),
    )
    tabs = (own, x_tab, y_tab)

    def onward(kind, sent, got, after):
        to_y, to_x = local_call(
            functools.partial(hop_kernel, kind, top_count),
            hop_out,
            (*tabs, *sent, *got),
            one_hop,
            moved,
            after=after,
        )
        return swapped(to_y, "expert", 2), swapped(to_x, "expert", 1), to_y

    b_got_y, b_got_x, b_to_y = onward("b", (b_left, b_right), (b_from_x, b_from_y), (g_left,))
    f_got_y, f_got_x, f_to_y = onward("f", (f_left, f_right), (f_from_x, f_from_y), (b_to_y,))
    g_got_y, g_got_x, g_to_y = onward("bg", (g_left, g_right), (g_from_x, g_from_y), (f_to_y,))
    gate_pre, up_pre = local_call(
        functools.partial(hop_again_kernel, top_count),
        [shaped(slot_total, hidden_units, jnp.float32)] * 2,
        (*tabs, b_left, b_right, b_from_x, b_from_y, b_got_y, b_got_x, weight_in),
        2 * expert_flops,
        expert_moved,
        scratch=(rows_scratch,),
        after=(g_to_y,),
    )
    f_keep_l, f_near_l, f_on_l, hidden = local_call(
        functools.partial(hop_fwd_kernel, top_count),
        half_out + [hidden_shape],
        (*tabs, f_left, f_right, f_from_x, f_from_y, f_got_y, f_got_x, weight_in, weight_out),
        5 * expert_flops // 2,
        expert_moved,
        scratch=(rows_scratch,),
        after=(gate_pre,),
    )
    f_ret_y = swapped(f_on_l, "expert", 2)
    f_keep_r, f_near_r, f_on_r = local_call(
        fwd_right_kernel, half_out, (hidden, weight_out), 1024, 1024
    )
    f_ret_x = swapped(f_on_r, "expert", 1)
    b_keep_l, b_near_l, b_on_l, both = local_call(
        functools.partial(hop_bwd_kernel, top_count),
        half_out + [both_shape],
        (
            *tabs,
            g_left,
            g_right,
            g_from_x,
            g_from_y,
            g_got_y,
            g_got_x,
            gate_pre,
            up_pre,
            weight_in,
            weight_out,
        ),
        2 * expert_flops,
        expert_moved,
        scratch=(rows_scratch,),
        after=(f_keep_r,),
    )
    b_ret_y = swapped(b_on_l, "expert", 2)
    b_keep_r, b_near_r, b_on_r = local_call(
        bwd_right_kernel, half_out, (both, weight_in), 1024, 1024
    )
    b_ret_x = swapped(b_on_r, "expert", 1)

    def summed_call(kind, here, table, near, far, after):
        part = local_call(
            functools.partial(sums_kernel, kind, top_count, here),
            shaped(tok_rows, half),
            (table, near, far),
            one_hop,
            moved,
            after=after,
        )
        return swapped(part, "expert", here), part

    f_sum_x, last = summed_call("fg", 1, x_tab, f_near_l, f_ret_y, (b_keep_r,))
    f_sum_y, last = summed_call("fg", 2, y_tab, f_near_r, f_ret_x, (last,))
    b_sum_x, last = summed_call("b", 1, x_tab, b_near_l, b_ret_y, (last,))
    b_sum_y, last = summed_call("b", 2, y_tab, b_near_r, b_ret_x, (last,))
    f_keep = (f_keep_l, f_keep_r)
    b_keep = (b_keep_l, b_keep_r)
    fwd_block = local_call(
        functools.partial(hop_fwd_end_kernel, top_count),
        shaped(tok_rows, features),
        (layer_in, own, *f_keep, f_ret_y, f_ret_x, f_sum_x, f_sum_y),
        one_hop,
        moved,
        after=(last,),
    )
    bwd_block = local_call(
        functools.partial(hop_bwd_end_kernel, top_count),
        shaped(tok_rows, features),
        (grad_in, saved, gain_here, own, *b_keep, b_ret_y, b_ret_x, b_sum_x, b_sum_y),
        one_hop,
        moved,
    )
    return (fwd_block[None], bwd_block[None])


def per_device(*arrays):
    if lax.axis_size("expert") == 4:
        return per_device_hops(*arrays)
    return per_device_direct(*arrays)


def solution(mesh):
    in_specs = (
        P("section", "expert", None),
        P("section", "expert", None),
        P("section", "expert", None),
        P("section", "expert", None),
        P("section", "expert", None),
        P("section", "expert", None),
        P("section", "expert", None),
        P("section", None),
        P("section", "expert", None, None),
        P("section", "expert", None, None),
    )
    out_specs = (P("section", "expert", None), P("section", "expert", None))
    return jax.shard_map(
        per_device, mesh=mesh, in_specs=in_specs, out_specs=out_specs, check_vma=False
    )
```

```python
import functools

import jax
import jax.numpy as jnp
from jax import lax
from jax.experimental import pallas as pl
from jax.experimental.pallas import tpu as pltpu
from jax.sharding import PartitionSpec as P

EPS = 1e-06
VMEM_LIMIT = 32 * 1024 * 1024


def passed_along(value, axis, steps):
    count = lax.axis_size(axis)
    pairs = [(source, (source + steps) % count) for source in range(count)]
    return lax.ppermute(value, axis, pairs)


def swapped(value, axis, offset):
    count = lax.axis_size(axis)
    pairs = [(source, source ^ offset) for source in range(count)]
    return lax.ppermute(value, axis, pairs)


def exchanged(blocks, axis):
    return [blocks[0]] + [swapped(blocks[d], axis, d) for d in range(1, len(blocks))]


def slot_table(routes, expert_count):
    top_count, tok_rows = routes.shape
    experts = max(8, expert_count)
    wanted = lax.broadcasted_iota(jnp.int32, (experts, tok_rows), 0)
    member = routes[0:1, :] == wanted
    for k in range(1, top_count):
        member = jnp.logical_or(member, routes[k : k + 1, :] == wanted)
    before = lax.broadcasted_iota(jnp.int32, (tok_rows, tok_rows), 0) < lax.broadcasted_iota(
        jnp.int32, (tok_rows, tok_rows), 1
    )
    slots = jnp.dot(
        member.astype(jnp.bfloat16),
        before.astype(jnp.bfloat16),
        preferred_element_type=jnp.float32,
    )
    return jnp.where(member, slots, -1.0)


def placement(slots, expert, capacity):
    tok_rows = slots.shape[1]
    row = lax.broadcasted_iota(jnp.int32, (capacity, tok_rows), 0).astype(jnp.float32)
    return slots[expert : expert + 1, :] == row


def gate_row(routes, gates, expert):
    total = jnp.zeros((1, routes.shape[1]), jnp.float32)
    for k in range(routes.shape[0]):
        total = total + jnp.where(routes[k : k + 1, :] == expert, gates[k : k + 1, :], 0.0)
    return total


def halves(weights):
    high = weights.astype(jnp.bfloat16)
    low = (weights - high.astype(jnp.float32)).astype(jnp.bfloat16)
    return high, low


def normed_kernel(values_ref, routes_ref, gain_ref, *out_refs):
    expert_count = len(out_refs)
    capacity = out_refs[0].shape[0]
    wide = values_ref[...].astype(jnp.float32)
    inv_rms = lax.rsqrt(jnp.mean(wide * wide, axis=-1, keepdims=True) + EPS)
    normed = (wide * inv_rms * gain_ref[...]).astype(jnp.bfloat16)
    slots = slot_table(routes_ref[...], expert_count)
    for e in range(expert_count):
        place = placement(slots, e, capacity).astype(jnp.bfloat16)
        out_refs[e][...] = jnp.dot(place, normed, preferred_element_type=jnp.float32).astype(
            jnp.bfloat16
        )


def grads_kernel(grads_ref, routes_ref, gates_ref, *out_refs):
    expert_count = len(out_refs)
    capacity = out_refs[0].shape[0]
    grads = grads_ref[...]
    routes = routes_ref[...]
    slots = slot_table(routes, expert_count)
    for e in range(expert_count):
        place = placement(slots, e, capacity)
        high, low = halves(jnp.where(place, gate_row(routes, gates_ref[...], e), 0.0))
        out_refs[e][...] = (
            jnp.dot(high, grads, preferred_element_type=jnp.float32)
            + jnp.dot(low, grads, preferred_element_type=jnp.float32)
        ).astype(jnp.bfloat16)


def rows_dot(weights, rows):
    return lax.dot_general(
        weights, rows, (((0,), (0,)), ((), ())), preferred_element_type=jnp.float32
    )


def fwd_end_kernel(layer_ref, routes_ref, gates_ref, *refs):
    row_refs, out_ref = refs[:-1], refs[-1]
    expert_count = len(row_refs)
    capacity = row_refs[0].shape[0]
    routes = routes_ref[...]
    slots = slot_table(routes, expert_count)
    total = layer_ref[...].astype(jnp.float32)
    for e in range(expert_count):
        place = placement(slots, e, capacity)
        high, low = halves(jnp.where(place, gate_row(routes, gates_ref[...], e), 0.0))
        rows = row_refs[e][...]
        total = total + (rows_dot(high, rows) + rows_dot(low, rows))
    out_ref[...] = total.astype(jnp.bfloat16)


def bwd_end_kernel(grads_ref, saved_ref, gain_ref, routes_ref, *refs):
    row_refs, out_ref = refs[:-1], refs[-1]
    expert_count = len(row_refs)
    capacity = row_refs[0].shape[0]
    features = saved_ref.shape[1]
    slots = slot_table(routes_ref[...], expert_count)
    d_normed = None
    for e in range(expert_count):
        place = placement(slots, e, capacity).astype(jnp.bfloat16)
        part = rows_dot(place, row_refs[e][...])
        d_normed = part if d_normed is None else d_normed + part
    wide = saved_ref[...].astype(jnp.float32)
    inv_rms = lax.rsqrt(jnp.mean(wide * wide, axis=-1, keepdims=True) + EPS)
    scaled = d_normed * gain_ref[...]
    cubed = inv_rms * inv_rms * inv_rms
    inner = jnp.sum(scaled * wide, axis=-1, keepdims=True)
    out_ref[...] = (
        grads_ref[...].astype(jnp.float32) + inv_rms * scaled - cubed / features * wide * inner
    ).astype(jnp.bfloat16)


def joined(refs):
    rows = [ref[...] for ref in refs]
    if rows[0].shape[0] % 16 == 0:
        return jnp.concatenate(rows, axis=0)
    return jnp.concatenate([r.astype(jnp.float32) for r in rows], axis=0).astype(jnp.bfloat16)


def tiles(size, step):
    return [(start, min(step, size - start)) for start in range(0, size, step)]


def expert_fwd_kernel(*refs):
    expert_count = (len(refs) - 4) // 2
    row_refs = refs[:expert_count]
    weight_in, weight_out = refs[expert_count : expert_count + 2]
    out_refs = refs[expert_count + 2 : 2 * expert_count + 2]
    rows_ref, hidden_ref = refs[-2:]
    capacity = row_refs[0].shape[0]
    hidden_units, features = weight_out.shape
    rows_ref[...] = joined(row_refs)
    for start, size in tiles(hidden_units, 256):
        gate = jnp.dot(
            rows_ref[...], weight_in[:, start : start + size], preferred_element_type=jnp.float32
        )
        up = jnp.dot(
            rows_ref[...],
            weight_in[:, hidden_units + start : hidden_units + start + size],
            preferred_element_type=jnp.float32,
        )
        hidden_ref[:, start : start + size] = (gate / (1.0 + jnp.exp(-gate)) * up).astype(
            jnp.bfloat16
        )
    for start, size in tiles(features, 512):
        out = jnp.dot(
            hidden_ref[...], weight_out[:, start : start + size], preferred_element_type=jnp.float32
        )
        for d in range(expert_count):
            out_refs[d][:, start : start + size] = out[d * capacity : (d + 1) * capacity].astype(
                jnp.bfloat16
            )


def expert_again_kernel(*refs):
    expert_count = len(refs) - 4
    row_refs = refs[:expert_count]
    weight_in, gate_ref, up_ref, rows_ref = refs[expert_count:]
    hidden_units = gate_ref.shape[1]
    rows_ref[...] = joined(row_refs)
    for start, size in tiles(hidden_units, 256):
        gate_ref[:, start : start + size] = jnp.dot(
            rows_ref[...], weight_in[:, start : start + size], preferred_element_type=jnp.float32
        )
        up_ref[:, start : start + size] = jnp.dot(
            rows_ref[...],
            weight_in[:, hidden_units + start : hidden_units + start + size],
            preferred_element_type=jnp.float32,
        )


def expert_bwd_kernel(*refs):
    expert_count = (len(refs) - 6) // 2
    grad_refs = refs[:expert_count]
    gate_ref, up_ref, weight_in, weight_out = refs[expert_count : expert_count + 4]
    out_refs = refs[expert_count + 4 : 2 * expert_count + 4]
    grads_ref, both_ref = refs[-2:]
    capacity = grad_refs[0].shape[0]
    hidden_units, features = weight_out.shape
    grads_ref[...] = joined(grad_refs)
    for start, size in tiles(hidden_units, 256):
        gate = gate_ref[:, start : start + size]
        up = up_ref[:, start : start + size]
        d_hidden = lax.dot_general(
            grads_ref[...],
            weight_out[start : start + size, :],
            (((1,), (1,)), ((), ())),
            preferred_element_type=jnp.float32,
        )
        sig = 1.0 / (1.0 + jnp.exp(-gate))
        both_ref[:, start : start + size] = (
            d_hidden * up * sig * (1.0 + gate * (1.0 - sig))
        ).astype(jnp.bfloat16)
        both_ref[:, hidden_units + start : hidden_units + start + size] = (
            d_hidden * gate * sig
        ).astype(jnp.bfloat16)
    for start, size in tiles(features, 512):
        out = lax.dot_general(
            both_ref[...],
            weight_in[start : start + size, :],
            (((1,), (1,)), ((), ())),
            preferred_element_type=jnp.float32,
        )
        for d in range(expert_count):
            out_refs[d][:, start : start + size] = out[d * capacity : (d + 1) * capacity].astype(
                jnp.bfloat16
            )


def local_call(kernel, out_shapes, inputs, flops, moved, scratch=(), after=()):
    in_specs = [pl.BlockSpec(memory_space=pltpu.VMEM)] * len(inputs)
    held = len(inputs)

    def body(*refs):
        kernel(*refs[:held], *refs[held + len(after) :])

    return pl.pallas_call(
        body if after else kernel,
        out_shape=out_shapes,
        in_specs=in_specs + [pl.BlockSpec(memory_space=pl.ANY)] * len(after),
        scratch_shapes=list(scratch),
        compiler_params=pltpu.CompilerParams(vmem_limit_bytes=VMEM_LIMIT),
        cost_estimate=pl.CostEstimate(flops=flops, bytes_accessed=moved, transcendentals=0),
    )(*inputs, *after)


def per_device_direct(
    fwd_prev,
    bwd_prev,
    bwd_saved,
    fwd_routes,
    fwd_gates,
    bwd_routes,
    bwd_gates,
    norm_gain,
    w_in,
    w_out,
):
    expert_count = lax.axis_size("expert")
    tok_rows = fwd_prev.shape[1]
    features = fwd_prev.shape[2]
    top_count = fwd_routes.shape[2]
    hidden_units = w_in.shape[3] // 2
    capacity = 3 * tok_rows * top_count // (2 * expert_count)
    gain_row = norm_gain
    weight_in = w_in[0, 0]
    weight_out = w_out[0, 0]
    me = lax.axis_index("expert")
    f_routes = (fwd_routes[0] ^ me).T
    b_routes = (bwd_routes[0] ^ me).T
    f_gates = fwd_gates[0].T
    b_gates = bwd_gates[0].T
    saved = bwd_saved[0]
    layer_in = passed_along(fwd_prev[0], "section", 1)
    grad_in = passed_along(bwd_prev[0], "section", -1)

    block = jax.ShapeDtypeStruct((capacity, features), jnp.bfloat16)
    whole = jax.ShapeDtypeStruct((tok_rows, features), jnp.bfloat16)
    one_dot = 2 * expert_count * capacity * tok_rows * features
    moved = 2 * features * (tok_rows + expert_count * capacity)
    slot_total = expert_count * capacity
    blocks = [block] * expert_count
    expert_flops = 2 * slot_total * features * hidden_units
    expert_moved = 2 * features * (3 * hidden_units + 3 * slot_total)
    rows_scratch = pltpu.VMEM((slot_total, features), jnp.bfloat16)

    b_sent = local_call(normed_kernel, blocks, (saved, b_routes, gain_row), one_dot, moved)
    b_rows = exchanged(b_sent, "expert")
    f_sent = local_call(
        normed_kernel, blocks, (layer_in, f_routes, gain_row), one_dot, moved, after=(b_sent[0],)
    )
    f_rows = exchanged(f_sent, "expert")
    g_sent = local_call(
        grads_kernel, blocks, (grad_in, b_routes, b_gates), 2 * one_dot, moved, after=(f_sent[0],)
    )
    g_rows = exchanged(g_sent, "expert")
    projected = jax.ShapeDtypeStruct((slot_total, hidden_units), jnp.float32)
    gate_pre, up_pre = local_call(
        expert_again_kernel,
        [projected, projected],
        (*b_rows, weight_in),
        2 * expert_flops,
        expert_moved,
        scratch=(rows_scratch,),
        after=(g_sent[0],),
    )
    f_done = local_call(
        expert_fwd_kernel,
        blocks,
        (*f_rows, weight_in, weight_out),
        3 * expert_flops,
        expert_moved,
        scratch=(rows_scratch, pltpu.VMEM((slot_total, hidden_units), jnp.bfloat16)),
        after=(gate_pre,),
    )
    f_back = exchanged(f_done, "expert")
    b_done = local_call(
        expert_bwd_kernel,
        blocks,
        (*g_rows, gate_pre, up_pre, weight_in, weight_out),
        3 * expert_flops,
        expert_moved,
        scratch=(rows_scratch, pltpu.VMEM((slot_total, 2 * hidden_units), jnp.bfloat16)),
        after=(f_back[1],),
    )
    b_back = exchanged(b_done, "expert")
    fwd_block = local_call(
        fwd_end_kernel,
        whole,
        (layer_in, f_routes, f_gates, *f_back),
        2 * one_dot,
        moved,
        after=(b_done[0],),
    )
    bwd_block = local_call(
        bwd_end_kernel,
        whole,
        (grad_in, saved, gain_row, b_routes, *b_back),
        one_dot,
        moved,
    )
    return (fwd_block[None], bwd_block[None])


def pick(table, expert, capacity, kind, top_count):
    first = 0 if kind[0] == "f" else 2 * top_count
    routes = table[first : first + top_count]
    gates = table[first + top_count : first + 2 * top_count]
    tok_rows = table.shape[1]
    member = routes == float(expert)
    held = jnp.sum(member.astype(jnp.float32), axis=0, keepdims=True)
    before = lax.broadcasted_iota(jnp.int32, (tok_rows, tok_rows), 0) < lax.broadcasted_iota(
        jnp.int32, (tok_rows, tok_rows), 1
    )
    slots = jnp.dot(
        jnp.broadcast_to(held, (8, tok_rows)).astype(jnp.bfloat16),
        before.astype(jnp.bfloat16),
        preferred_element_type=jnp.float32,
    )[0:1]
    place = placement(jnp.where(held > 0.0, slots, -1.0), 0, capacity)
    if len(kind) == 1:
        return (place.astype(jnp.bfloat16),)
    gate = jnp.sum(jnp.where(member, gates, 0.0), axis=0, keepdims=True)
    return halves(jnp.where(place, gate, 0.0))


def to_slots(weights, values):
    total = None
    for part in weights:
        term = jnp.dot(part, values, preferred_element_type=jnp.float32)
        total = term if total is None else total + term
    return total.astype(jnp.bfloat16)


def to_tokens(weights, rows):
    total = None
    for part in weights:
        term = rows_dot(part, rows)
        total = term if total is None else total + term
    return total


def three_parts(values):
    high = values.astype(jnp.bfloat16)
    rest = values - high.astype(jnp.float32)
    mid = rest.astype(jnp.bfloat16)
    low = (rest - mid.astype(jnp.float32)).astype(jnp.bfloat16)
    return high, mid, low


def normed_halves(wide, gain):
    inv_rms = lax.rsqrt(jnp.mean(wide * wide, axis=-1, keepdims=True) + EPS)
    return (wide * inv_rms * gain).astype(jnp.bfloat16)


def first_kernel(top_count, me_ref, *refs):
    sources, refs = refs[:6], refs[6:]
    (left_ref, right_ref, table_ref, gain_out), refs = refs[:4], refs[4:]
    held, sems = refs[:6], refs[6]
    copies = [pltpu.make_async_copy(sources[i], held[i], sems.at[i]) for i in range(6)]
    for copy in copies:
        copy.start()
    for copy in copies[1:]:
        copy.wait()
    saved, gain, f_routes, f_gates, b_routes, b_gates = held
    me = me_ref[0]
    fr = (f_routes[...] ^ me).astype(jnp.float32)
    br = (b_routes[...] ^ me).astype(jnp.float32)
    fg = f_gates[...]
    bg = b_gates[...]
    table_ref[...] = jnp.concatenate([fr, fg, br, bg], axis=0)
    packed = [fr.astype(jnp.bfloat16), br.astype(jnp.bfloat16), *three_parts(fg), *three_parts(bg)]
    packed = jnp.concatenate([part.astype(jnp.float32) for part in packed], axis=0)
    gain_out[...] = gain[...]
    tok_rows, features = saved.shape
    half = features // 2
    copies[0].wait()
    normed = normed_halves(saved[...].astype(jnp.float32), gain[...])
    for half_ref, start in ((left_ref, 0), (right_ref, half)):
        half_ref[:tok_rows, :] = normed[:, start : start + half]
        half_ref[tok_rows:, :] = jnp.zeros((half_ref.shape[0] - tok_rows, half), jnp.bfloat16)
        half_ref[tok_rows:, :tok_rows] = packed.astype(jnp.bfloat16)


def unpacked(block, tok_rows, top_count):
    rows = block[tok_rows:, :tok_rows].astype(jnp.float32)
    k = top_count
    fr, br = rows[0:k], rows[k : 2 * k]
    fg = (rows[2 * k : 3 * k] + rows[3 * k : 4 * k]) + rows[4 * k : 5 * k]
    bg = (rows[5 * k : 6 * k] + rows[6 * k : 7 * k]) + rows[7 * k : 8 * k]
    return jnp.concatenate([fr, fg, br, bg], axis=0)


def normed_kernel_halves(values_ref, gain_ref, left_ref, right_ref):
    half = left_ref.shape[1]
    normed = normed_halves(values_ref[...].astype(jnp.float32), gain_ref[...])
    left_ref[...] = normed[:, :half]
    right_ref[...] = normed[:, half:]


def split_kernel(values_ref, left_ref, right_ref):
    half = left_ref.shape[1]
    left_ref[...] = values_ref[:, :half]
    right_ref[...] = values_ref[:, half:]


def tables_kernel(top_count, from_x, from_y, kept_ref, x_table, y_table, handed_ref, sem):
    copy = pltpu.make_async_copy(kept_ref, handed_ref, sem)
    copy.start()
    tok_rows = x_table.shape[1]
    x_table[...] = unpacked(from_x[...], tok_rows, top_count)
    y_table[...] = unpacked(from_y[...], tok_rows, top_count)
    copy.wait()


def hop_kernel(kind, top_count, own, x_tab, y_tab, left, right, from_x, from_y, to_y, to_x):
    capacity = to_y.shape[0] // 2
    tok_rows = own.shape[1]
    to_y[:capacity, :] = to_slots(pick(own[...], 2, capacity, kind, top_count), left[:tok_rows, :])
    to_y[capacity:, :] = to_slots(
        pick(x_tab[...], 3, capacity, kind, top_count), from_x[:tok_rows, :]
    )
    to_x[:capacity, :] = to_slots(pick(own[...], 1, capacity, kind, top_count), right[:tok_rows, :])
    to_x[capacity:, :] = to_slots(
        pick(y_tab[...], 3, capacity, kind, top_count), from_y[:tok_rows, :]
    )


def assemble(kind, top_count, own, x_tab, y_tab, left, right, from_x, from_y, got_y, got_x, rows):
    capacity = got_y.shape[0] // 2
    half = got_y.shape[1]
    tok_rows = own.shape[1]
    mine = pick(own[...], 0, capacity, kind, top_count)
    rows[:capacity, :half] = to_slots(mine, left[:tok_rows, :])
    rows[:capacity, half:] = to_slots(mine, right[:tok_rows, :])
    rows[capacity : 2 * capacity, :half] = to_slots(
        pick(x_tab[...], 1, capacity, kind, top_count), from_x[:tok_rows, :]
    )
    rows[capacity : 2 * capacity, half:] = got_x[:capacity, :]
    rows[2 * capacity : 3 * capacity, :half] = got_y[:capacity, :]
    rows[2 * capacity : 3 * capacity, half:] = to_slots(
        pick(y_tab[...], 2, capacity, kind, top_count), from_y[:tok_rows, :]
    )
    rows[3 * capacity :, :half] = got_y[capacity:, :]
    rows[3 * capacity :, half:] = got_x[capacity:, :]


def hand_out(out, at, capacity, to_left, keep, near, onward):
    size = out.shape[1]
    rows = out.astype(jnp.bfloat16)
    mine, from_x, from_y, far = [rows[d * capacity : (d + 1) * capacity] for d in range(4)]
    keep[:, at : at + size] = mine
    near[:, at : at + size] = from_x if to_left else from_y
    onward[:capacity, at : at + size] = from_y if to_left else from_x
    onward[capacity:, at : at + size] = far


def fwd_half(hidden_ref, weight_out, to_left, keep, near, onward):
    capacity, half = keep.shape
    first = 0 if to_left else half
    for at, size in tiles(half, 512):
        out = jnp.dot(
            hidden_ref[...],
            weight_out[:, first + at : first + at + size],
            preferred_element_type=jnp.float32,
        )
        hand_out(out, at, capacity, to_left, keep, near, onward)


def bwd_half(both_ref, weight_in, to_left, keep, near, onward):
    capacity, half = keep.shape
    first = 0 if to_left else half
    for at, size in tiles(half, 512):
        out = lax.dot_general(
            both_ref[...],
            weight_in[first + at : first + at + size, :],
            (((1,), (1,)), ((), ())),
            preferred_element_type=jnp.float32,
        )
        hand_out(out, at, capacity, to_left, keep, near, onward)


def fwd_right_kernel(hidden_ref, weight_out, keep, near, onward):
    fwd_half(hidden_ref, weight_out, False, keep, near, onward)


def bwd_right_kernel(both_ref, weight_in, keep, near, onward):
    bwd_half(both_ref, weight_in, False, keep, near, onward)


def hop_again_kernel(top_count, *refs):
    dispatch, (weight_in, gate_ref, up_ref, rows_ref) = refs[:9], refs[9:]
    assemble("b", top_count, *dispatch, rows_ref)
    hidden_units = gate_ref.shape[1]
    for start, size in tiles(hidden_units, 256):
        gate_ref[:, start : start + size] = jnp.dot(
            rows_ref[...], weight_in[:, start : start + size], preferred_element_type=jnp.float32
        )
        up_ref[:, start : start + size] = jnp.dot(
            rows_ref[...],
            weight_in[:, hidden_units + start : hidden_units + start + size],
            preferred_element_type=jnp.float32,
        )


def hop_fwd_kernel(top_count, *refs):
    dispatch, refs = refs[:9], refs[9:]
    weight_in, weight_out = refs[:2]
    outs, hidden_ref, rows_ref = refs[2:5], refs[5], refs[6]
    hidden_units = weight_out.shape[0]
    assemble("f", top_count, *dispatch, rows_ref)
    for start, size in tiles(hidden_units, 256):
        gate = jnp.dot(
            rows_ref[...], weight_in[:, start : start + size], preferred_element_type=jnp.float32
        )
        up = jnp.dot(
            rows_ref[...],
            weight_in[:, hidden_units + start : hidden_units + start + size],
            preferred_element_type=jnp.float32,
        )
        hidden_ref[:, start : start + size] = (gate / (1.0 + jnp.exp(-gate)) * up).astype(
            jnp.bfloat16
        )
    fwd_half(hidden_ref, weight_out, True, *outs)


def hop_bwd_kernel(top_count, *refs):
    dispatch, refs = refs[:9], refs[9:]
    gate_ref, up_ref, weight_in, weight_out = refs[:4]
    outs, both_ref, grads_ref = refs[4:7], refs[7], refs[8]
    hidden_units = weight_out.shape[0]
    assemble("bg", top_count, *dispatch, grads_ref)
    for start, size in tiles(hidden_units, 256):
        gate = gate_ref[:, start : start + size]
        up = up_ref[:, start : start + size]
        d_hidden = lax.dot_general(
            grads_ref[...],
            weight_out[start : start + size, :],
            (((1,), (1,)), ((), ())),
            preferred_element_type=jnp.float32,
        )
        sig = 1.0 / (1.0 + jnp.exp(-gate))
        both_ref[:, start : start + size] = (
            d_hidden * up * sig * (1.0 + gate * (1.0 - sig))
        ).astype(jnp.bfloat16)
        both_ref[:, hidden_units + start : hidden_units + start + size] = (
            d_hidden * gate * sig
        ).astype(jnp.bfloat16)
    bwd_half(both_ref, weight_in, True, *outs)


def sums_kernel(kind, top_count, here, table_ref, near, far, out):
    capacity = near.shape[0]
    table = table_ref[...]
    out[...] = (
        to_tokens(pick(table, here, capacity, kind, top_count), near[...])
        + to_tokens(pick(table, 3, capacity, kind, top_count), far[capacity:, :])
    ).astype(jnp.bfloat16)


def summed(kind, top_count, own, keep_left, keep_right, got_y, got_x, sum_x, sum_y):
    capacity = keep_left.shape[0]
    mine = pick(own[...], 0, capacity, kind, top_count)
    near_y = pick(own[...], 2, capacity, kind, top_count)
    near_x = pick(own[...], 1, capacity, kind, top_count)
    left = to_tokens(mine, keep_left[...]) + to_tokens(near_y, got_y[:capacity, :])
    right = to_tokens(mine, keep_right[...]) + to_tokens(near_x, got_x[:capacity, :])
    return left + sum_x[...].astype(jnp.float32), right + sum_y[...].astype(jnp.float32)


def hop_fwd_end_kernel(top_count, layer_ref, *refs):
    out_ref = refs[-1]
    half = layer_ref.shape[1] // 2
    left, right = summed("fg", top_count, *refs[:-1])
    out_ref[:, :half] = (layer_ref[:, :half].astype(jnp.float32) + left).astype(jnp.bfloat16)
    out_ref[:, half:] = (layer_ref[:, half:].astype(jnp.float32) + right).astype(jnp.bfloat16)


def hop_bwd_end_kernel(top_count, grads_ref, saved_ref, gain_ref, *refs):
    out_ref = refs[-1]
    features = saved_ref.shape[1]
    left, right = summed("b", top_count, *refs[:-1])
    wide = saved_ref[...].astype(jnp.float32)
    inv_rms = lax.rsqrt(jnp.mean(wide * wide, axis=-1, keepdims=True) + EPS)
    scaled = jnp.concatenate([left, right], axis=1) * gain_ref[...]
    cubed = inv_rms * inv_rms * inv_rms
    inner = jnp.sum(scaled * wide, axis=-1, keepdims=True)
    out_ref[...] = (
        grads_ref[...].astype(jnp.float32) + inv_rms * scaled - cubed / features * wide * inner
    ).astype(jnp.bfloat16)


def per_device_hops(
    fwd_prev,
    bwd_prev,
    bwd_saved,
    fwd_routes,
    fwd_gates,
    bwd_routes,
    bwd_gates,
    norm_gain,
    w_in,
    w_out,
):
    tok_rows, features = fwd_prev.shape[1:]
    top_count = fwd_routes.shape[2]
    hidden_units = w_in.shape[3] // 2
    capacity = 3 * tok_rows * top_count // 8
    half = features // 2
    gain_row = norm_gain
    weight_in = w_in[0, 0]
    weight_out = w_out[0, 0]
    me = lax.axis_index("expert").astype(jnp.int32).reshape(1)
    saved = bwd_saved[0]
    layer_in = passed_along(fwd_prev[0], "section", 1)

    def shaped(rows, columns, dtype=jnp.bfloat16):
        return jax.ShapeDtypeStruct((rows, columns), dtype)

    def crossed(left, right):
        return swapped(left, "expert", 1), swapped(right, "expert", 2)

    slot_total = 4 * capacity
    table_rows = 4 * top_count
    one_hop = moved = 1024
    expert_flops = 2 * slot_total * features * hidden_units
    expert_moved = 2 * features * (3 * hidden_units + 3 * slot_total)
    rows_scratch = pltpu.VMEM((slot_total, features), jnp.bfloat16)
    halves_out = [shaped(tok_rows, half)] * 2
    hop_out = [shaped(2 * capacity, half)] * 2
    half_out = [shaped(capacity, half), shaped(capacity, half), shaped(2 * capacity, half)]
    hidden_shape = shaped(slot_total, hidden_units)
    both_shape = shaped(slot_total, 2 * hidden_units)
    table_shape = shaped(table_rows, tok_rows, jnp.float32)
    first_rows = tok_rows + 8 * top_count

    b_left, b_right, own, gain_here = pl.pallas_call(
        functools.partial(first_kernel, top_count),
        out_shape=[
            shaped(first_rows, half),
            shaped(first_rows, half),
            table_shape,
            shaped(1, features, jnp.float32),
        ],
        in_specs=[pl.BlockSpec(memory_space=pltpu.SMEM)]
        + [pl.BlockSpec(memory_space=pltpu.HBM)] * 6,
        scratch_shapes=[
            pltpu.VMEM((tok_rows, features), jnp.bfloat16),
            pltpu.VMEM((1, features), jnp.float32),
            pltpu.VMEM((top_count, tok_rows), jnp.int32),
            pltpu.VMEM((top_count, tok_rows), jnp.float32),
            pltpu.VMEM((top_count, tok_rows), jnp.int32),
            pltpu.VMEM((top_count, tok_rows), jnp.float32),
            pltpu.SemaphoreType.DMA((6,)),
        ],
        compiler_params=pltpu.CompilerParams(vmem_limit_bytes=VMEM_LIMIT),
        cost_estimate=pl.CostEstimate(flops=one_hop, bytes_accessed=moved, transcendentals=0),
    )(
        me,
        *[
            pltpu.with_memory_space_constraint(value, pltpu.HBM)
            for value in (
                saved,
                gain_row,
                fwd_routes[0].T,
                fwd_gates[0].T,
                bwd_routes[0].T,
                bwd_gates[0].T,
            )
        ],
    )
    b_from_x, b_from_y = crossed(b_left, b_right)
    x_tab, y_tab, bwd_here = pl.pallas_call(
        functools.partial(tables_kernel, top_count),
        out_shape=[table_shape, table_shape, shaped(tok_rows, features)],
        in_specs=[pl.BlockSpec(memory_space=pltpu.VMEM)] * 2
        + [pl.BlockSpec(memory_space=pltpu.HBM)],
        scratch_shapes=[pltpu.SemaphoreType.DMA(())],
        compiler_params=pltpu.CompilerParams(vmem_limit_bytes=VMEM_LIMIT),
        cost_estimate=pl.CostEstimate(flops=one_hop, bytes_accessed=moved, transcendentals=0),
    )(b_from_x, b_from_y, pltpu.with_memory_space_constraint(bwd_prev[0], pltpu.HBM))
    grad_in = passed_along(bwd_here, "section", -1)
    tabs = (own, x_tab, y_tab)

    def onward(kind, sent, got, after):
        to_y, to_x = local_call(
            functools.partial(hop_kernel, kind, top_count),
            hop_out,
            (*tabs, *sent, *got),
            one_hop,
            moved,
            after=after,
        )
        return swapped(to_y, "expert", 2), swapped(to_x, "expert", 1), to_y

    b_got_y, b_got_x, b_to_y = onward("b", (b_left, b_right), (b_from_x, b_from_y), ())
    f_left, f_right = local_call(
        normed_kernel_halves, halves_out, (layer_in, gain_here), one_hop, moved, after=(b_to_y,)
    )
    f_from_x, f_from_y = crossed(f_left, f_right)
    g_left, g_right = local_call(split_kernel, halves_out, (grad_in,), 1024, moved, after=(f_left,))
    g_from_x, g_from_y = crossed(g_left, g_right)
    f_got_y, f_got_x, f_to_y = onward("f", (f_left, f_right), (f_from_x, f_from_y), (g_left,))
    g_got_y, g_got_x, g_to_y = onward("bg", (g_left, g_right), (g_from_x, g_from_y), (f_to_y,))
    gate_pre, up_pre = local_call(
        functools.partial(hop_again_kernel, top_count),
        [shaped(slot_total, hidden_units, jnp.float32)] * 2,
        (*tabs, b_left, b_right, b_from_x, b_from_y, b_got_y, b_got_x, weight_in),
        2 * expert_flops,
        expert_moved,
        scratch=(rows_scratch,),
        after=(g_to_y,),
    )
    f_keep_l, f_near_l, f_on_l, hidden = local_call(
        functools.partial(hop_fwd_kernel, top_count),
        half_out + [hidden_shape],
        (*tabs, f_left, f_right, f_from_x, f_from_y, f_got_y, f_got_x, weight_in, weight_out),
        5 * expert_flops // 2,
        expert_moved,
        scratch=(rows_scratch,),
        after=(gate_pre,),
    )
    f_ret_y = swapped(f_on_l, "expert", 2)
    f_keep_r, f_near_r, f_on_r = local_call(
        fwd_right_kernel, half_out, (hidden, weight_out), 1024, 1024
    )
    f_ret_x = swapped(f_on_r, "expert", 1)
    b_keep_l, b_near_l, b_on_l, both = local_call(
        functools.partial(hop_bwd_kernel, top_count),
        half_out + [both_shape],
        (
            *tabs,
            g_left,
            g_right,
            g_from_x,
            g_from_y,
            g_got_y,
            g_got_x,
            gate_pre,
            up_pre,
            weight_in,
            weight_out,
        ),
        2 * expert_flops,
        expert_moved,
        scratch=(rows_scratch,),
        after=(f_keep_r,),
    )
    b_ret_y = swapped(b_on_l, "expert", 2)
    b_keep_r, b_near_r, b_on_r = local_call(
        bwd_right_kernel, half_out, (both, weight_in), 1024, 1024
    )
    b_ret_x = swapped(b_on_r, "expert", 1)

    def summed_call(kind, here, table, near, far, after):
        part = local_call(
            functools.partial(sums_kernel, kind, top_count, here),
            shaped(tok_rows, half),
            (table, near, far),
            one_hop,
            moved,
            after=after,
        )
        return swapped(part, "expert", here), part

    f_sum_x, last = summed_call("fg", 1, x_tab, f_near_l, f_ret_y, (b_keep_r,))
    f_sum_y, last = summed_call("fg", 2, y_tab, f_near_r, f_ret_x, (last,))
    b_sum_x, last = summed_call("b", 1, x_tab, b_near_l, b_ret_y, (last,))
    b_sum_y, last = summed_call("b", 2, y_tab, b_near_r, b_ret_x, (last,))
    f_keep = (f_keep_l, f_keep_r)
    b_keep = (b_keep_l, b_keep_r)
    fwd_block = local_call(
        functools.partial(hop_fwd_end_kernel, top_count),
        shaped(tok_rows, features),
        (layer_in, own, *f_keep, f_ret_y, f_ret_x, f_sum_x, f_sum_y),
        one_hop,
        moved,
        after=(last,),
    )
    bwd_block = local_call(
        functools.partial(hop_bwd_end_kernel, top_count),
        shaped(tok_rows, features),
        (grad_in, saved, gain_here, own, *b_keep, b_ret_y, b_ret_x, b_sum_x, b_sum_y),
        one_hop,
        moved,
    )
    return (fwd_block[None], bwd_block[None])


def per_device(*arrays):
    if lax.axis_size("expert") == 4:
        return per_device_hops(*arrays)
    return per_device_direct(*arrays)


def solution(mesh):
    in_specs = (
        P("section", "expert", None),
        P("section", "expert", None),
        P("section", "expert", None),
        P("section", "expert", None),
        P("section", "expert", None),
        P("section", "expert", None),
        P("section", "expert", None),
        P("section", None),
        P("section", "expert", None, None),
        P("section", "expert", None, None),
    )
    out_specs = (P("section", "expert", None), P("section", "expert", None))
    return jax.shard_map(
        per_device, mesh=mesh, in_specs=in_specs, out_specs=out_specs, check_vma=False
    )
```

```python
import functools

import jax
import jax.numpy as jnp
from jax import lax
from jax.experimental import pallas as pl
from jax.experimental.pallas import tpu as pltpu
from jax.sharding import PartitionSpec as P

EPS = 1e-06
VMEM_LIMIT = 32 * 1024 * 1024


def passed_along(value, axis, steps):
    count = lax.axis_size(axis)
    pairs = [(source, (source + steps) % count) for source in range(count)]
    return lax.ppermute(value, axis, pairs)


def swapped(value, axis, offset):
    count = lax.axis_size(axis)
    pairs = [(source, source ^ offset) for source in range(count)]
    return lax.ppermute(value, axis, pairs)


def exchanged(blocks, axis):
    return [blocks[0]] + [swapped(blocks[d], axis, d) for d in range(1, len(blocks))]


def slot_table(routes, expert_count):
    top_count, tok_rows = routes.shape
    experts = max(8, expert_count)
    wanted = lax.broadcasted_iota(jnp.int32, (experts, tok_rows), 0)
    member = routes[0:1, :] == wanted
    for k in range(1, top_count):
        member = jnp.logical_or(member, routes[k : k + 1, :] == wanted)
    before = lax.broadcasted_iota(jnp.int32, (tok_rows, tok_rows), 0) < lax.broadcasted_iota(
        jnp.int32, (tok_rows, tok_rows), 1
    )
    slots = jnp.dot(
        member.astype(jnp.bfloat16),
        before.astype(jnp.bfloat16),
        preferred_element_type=jnp.float32,
    )
    return jnp.where(member, slots, -1.0)


def placement(slots, expert, capacity):
    tok_rows = slots.shape[1]
    row = lax.broadcasted_iota(jnp.int32, (capacity, tok_rows), 0).astype(jnp.float32)
    return slots[expert : expert + 1, :] == row


def gate_row(routes, gates, expert):
    total = jnp.zeros((1, routes.shape[1]), jnp.float32)
    for k in range(routes.shape[0]):
        total = total + jnp.where(routes[k : k + 1, :] == expert, gates[k : k + 1, :], 0.0)
    return total


def halves(weights):
    high = weights.astype(jnp.bfloat16)
    low = (weights - high.astype(jnp.float32)).astype(jnp.bfloat16)
    return high, low


def normed_kernel(values_ref, routes_ref, gain_ref, *out_refs):
    expert_count = len(out_refs)
    capacity = out_refs[0].shape[0]
    wide = values_ref[...].astype(jnp.float32)
    inv_rms = lax.rsqrt(jnp.mean(wide * wide, axis=-1, keepdims=True) + EPS)
    normed = (wide * inv_rms * gain_ref[...]).astype(jnp.bfloat16)
    slots = slot_table(routes_ref[...], expert_count)
    for e in range(expert_count):
        place = placement(slots, e, capacity).astype(jnp.bfloat16)
        out_refs[e][...] = jnp.dot(place, normed, preferred_element_type=jnp.float32).astype(
            jnp.bfloat16
        )


def grads_kernel(grads_ref, routes_ref, gates_ref, *out_refs):
    expert_count = len(out_refs)
    capacity = out_refs[0].shape[0]
    grads = grads_ref[...]
    routes = routes_ref[...]
    slots = slot_table(routes, expert_count)
    for e in range(expert_count):
        place = placement(slots, e, capacity)
        high, low = halves(jnp.where(place, gate_row(routes, gates_ref[...], e), 0.0))
        out_refs[e][...] = (
            jnp.dot(high, grads, preferred_element_type=jnp.float32)
            + jnp.dot(low, grads, preferred_element_type=jnp.float32)
        ).astype(jnp.bfloat16)


def rows_dot(weights, rows):
    return lax.dot_general(
        weights, rows, (((0,), (0,)), ((), ())), preferred_element_type=jnp.float32
    )


def fwd_end_kernel(layer_ref, routes_ref, gates_ref, *refs):
    row_refs, out_ref = refs[:-1], refs[-1]
    expert_count = len(row_refs)
    capacity = row_refs[0].shape[0]
    routes = routes_ref[...]
    slots = slot_table(routes, expert_count)
    total = layer_ref[...].astype(jnp.float32)
    for e in range(expert_count):
        place = placement(slots, e, capacity)
        high, low = halves(jnp.where(place, gate_row(routes, gates_ref[...], e), 0.0))
        rows = row_refs[e][...]
        total = total + (rows_dot(high, rows) + rows_dot(low, rows))
    out_ref[...] = total.astype(jnp.bfloat16)


def bwd_end_kernel(grads_ref, saved_ref, gain_ref, routes_ref, *refs):
    row_refs, out_ref = refs[:-1], refs[-1]
    expert_count = len(row_refs)
    capacity = row_refs[0].shape[0]
    features = saved_ref.shape[1]
    slots = slot_table(routes_ref[...], expert_count)
    d_normed = None
    for e in range(expert_count):
        place = placement(slots, e, capacity).astype(jnp.bfloat16)
        part = rows_dot(place, row_refs[e][...])
        d_normed = part if d_normed is None else d_normed + part
    wide = saved_ref[...].astype(jnp.float32)
    inv_rms = lax.rsqrt(jnp.mean(wide * wide, axis=-1, keepdims=True) + EPS)
    scaled = d_normed * gain_ref[...]
    cubed = inv_rms * inv_rms * inv_rms
    inner = jnp.sum(scaled * wide, axis=-1, keepdims=True)
    out_ref[...] = (
        grads_ref[...].astype(jnp.float32) + inv_rms * scaled - cubed / features * wide * inner
    ).astype(jnp.bfloat16)


def joined(refs):
    rows = [ref[...] for ref in refs]
    if rows[0].shape[0] % 16 == 0:
        return jnp.concatenate(rows, axis=0)
    return jnp.concatenate([r.astype(jnp.float32) for r in rows], axis=0).astype(jnp.bfloat16)


def tiles(size, step):
    return [(start, min(step, size - start)) for start in range(0, size, step)]


def expert_fwd_kernel(*refs):
    expert_count = (len(refs) - 4) // 2
    row_refs = refs[:expert_count]
    weight_in, weight_out = refs[expert_count : expert_count + 2]
    out_refs = refs[expert_count + 2 : 2 * expert_count + 2]
    rows_ref, hidden_ref = refs[-2:]
    capacity = row_refs[0].shape[0]
    hidden_units, features = weight_out.shape
    rows_ref[...] = joined(row_refs)
    for start, size in tiles(hidden_units, 256):
        gate = jnp.dot(
            rows_ref[...], weight_in[:, start : start + size], preferred_element_type=jnp.float32
        )
        up = jnp.dot(
            rows_ref[...],
            weight_in[:, hidden_units + start : hidden_units + start + size],
            preferred_element_type=jnp.float32,
        )
        hidden_ref[:, start : start + size] = (gate / (1.0 + jnp.exp(-gate)) * up).astype(
            jnp.bfloat16
        )
    for start, size in tiles(features, 512):
        out = jnp.dot(
            hidden_ref[...], weight_out[:, start : start + size], preferred_element_type=jnp.float32
        )
        for d in range(expert_count):
            out_refs[d][:, start : start + size] = out[d * capacity : (d + 1) * capacity].astype(
                jnp.bfloat16
            )


def expert_again_kernel(*refs):
    expert_count = len(refs) - 4
    row_refs = refs[:expert_count]
    weight_in, gate_ref, up_ref, rows_ref = refs[expert_count:]
    hidden_units = gate_ref.shape[1]
    rows_ref[...] = joined(row_refs)
    for start, size in tiles(hidden_units, 256):
        gate_ref[:, start : start + size] = jnp.dot(
            rows_ref[...], weight_in[:, start : start + size], preferred_element_type=jnp.float32
        )
        up_ref[:, start : start + size] = jnp.dot(
            rows_ref[...],
            weight_in[:, hidden_units + start : hidden_units + start + size],
            preferred_element_type=jnp.float32,
        )


def expert_bwd_kernel(*refs):
    expert_count = (len(refs) - 6) // 2
    grad_refs = refs[:expert_count]
    gate_ref, up_ref, weight_in, weight_out = refs[expert_count : expert_count + 4]
    out_refs = refs[expert_count + 4 : 2 * expert_count + 4]
    grads_ref, both_ref = refs[-2:]
    capacity = grad_refs[0].shape[0]
    hidden_units, features = weight_out.shape
    grads_ref[...] = joined(grad_refs)
    for start, size in tiles(hidden_units, 256):
        gate = gate_ref[:, start : start + size]
        up = up_ref[:, start : start + size]
        d_hidden = lax.dot_general(
            grads_ref[...],
            weight_out[start : start + size, :],
            (((1,), (1,)), ((), ())),
            preferred_element_type=jnp.float32,
        )
        sig = 1.0 / (1.0 + jnp.exp(-gate))
        both_ref[:, start : start + size] = (
            d_hidden * up * sig * (1.0 + gate * (1.0 - sig))
        ).astype(jnp.bfloat16)
        both_ref[:, hidden_units + start : hidden_units + start + size] = (
            d_hidden * gate * sig
        ).astype(jnp.bfloat16)
    for start, size in tiles(features, 512):
        out = lax.dot_general(
            both_ref[...],
            weight_in[start : start + size, :],
            (((1,), (1,)), ((), ())),
            preferred_element_type=jnp.float32,
        )
        for d in range(expert_count):
            out_refs[d][:, start : start + size] = out[d * capacity : (d + 1) * capacity].astype(
                jnp.bfloat16
            )


def local_call(kernel, out_shapes, inputs, flops, moved, scratch=(), after=()):
    in_specs = [pl.BlockSpec(memory_space=pltpu.VMEM)] * len(inputs)
    held = len(inputs)

    def body(*refs):
        kernel(*refs[:held], *refs[held + len(after) :])

    return pl.pallas_call(
        body if after else kernel,
        out_shape=out_shapes,
        in_specs=in_specs + [pl.BlockSpec(memory_space=pl.ANY)] * len(after),
        scratch_shapes=list(scratch),
        compiler_params=pltpu.CompilerParams(vmem_limit_bytes=VMEM_LIMIT),
        cost_estimate=pl.CostEstimate(flops=flops, bytes_accessed=moved, transcendentals=0),
    )(*inputs, *after)


def per_device_direct(
    fwd_prev,
    bwd_prev,
    bwd_saved,
    fwd_routes,
    fwd_gates,
    bwd_routes,
    bwd_gates,
    norm_gain,
    w_in,
    w_out,
):
    expert_count = lax.axis_size("expert")
    tok_rows = fwd_prev.shape[1]
    features = fwd_prev.shape[2]
    top_count = fwd_routes.shape[2]
    hidden_units = w_in.shape[3] // 2
    capacity = 3 * tok_rows * top_count // (2 * expert_count)
    gain_row = norm_gain
    weight_in = w_in[0, 0]
    weight_out = w_out[0, 0]
    me = lax.axis_index("expert")
    f_routes = (fwd_routes[0] ^ me).T
    b_routes = (bwd_routes[0] ^ me).T
    f_gates = fwd_gates[0].T
    b_gates = bwd_gates[0].T
    saved = bwd_saved[0]
    layer_in = passed_along(fwd_prev[0], "section", 1)
    grad_in = passed_along(bwd_prev[0], "section", -1)

    block = jax.ShapeDtypeStruct((capacity, features), jnp.bfloat16)
    whole = jax.ShapeDtypeStruct((tok_rows, features), jnp.bfloat16)
    one_dot = 2 * expert_count * capacity * tok_rows * features
    moved = 2 * features * (tok_rows + expert_count * capacity)
    slot_total = expert_count * capacity
    blocks = [block] * expert_count
    expert_flops = 2 * slot_total * features * hidden_units
    expert_moved = 2 * features * (3 * hidden_units + 3 * slot_total)
    rows_scratch = pltpu.VMEM((slot_total, features), jnp.bfloat16)

    b_sent = local_call(normed_kernel, blocks, (saved, b_routes, gain_row), one_dot, moved)
    b_rows = exchanged(b_sent, "expert")
    f_sent = local_call(
        normed_kernel, blocks, (layer_in, f_routes, gain_row), one_dot, moved, after=(b_sent[0],)
    )
    f_rows = exchanged(f_sent, "expert")
    g_sent = local_call(
        grads_kernel, blocks, (grad_in, b_routes, b_gates), 2 * one_dot, moved, after=(f_sent[0],)
    )
    g_rows = exchanged(g_sent, "expert")
    projected = jax.ShapeDtypeStruct((slot_total, hidden_units), jnp.float32)
    gate_pre, up_pre = local_call(
        expert_again_kernel,
        [projected, projected],
        (*b_rows, weight_in),
        2 * expert_flops,
        expert_moved,
        scratch=(rows_scratch,),
        after=(g_sent[0],),
    )
    f_done = local_call(
        expert_fwd_kernel,
        blocks,
        (*f_rows, weight_in, weight_out),
        3 * expert_flops,
        expert_moved,
        scratch=(rows_scratch, pltpu.VMEM((slot_total, hidden_units), jnp.bfloat16)),
        after=(gate_pre,),
    )
    f_back = exchanged(f_done, "expert")
    b_done = local_call(
        expert_bwd_kernel,
        blocks,
        (*g_rows, gate_pre, up_pre, weight_in, weight_out),
        3 * expert_flops,
        expert_moved,
        scratch=(rows_scratch, pltpu.VMEM((slot_total, 2 * hidden_units), jnp.bfloat16)),
        after=(f_back[1],),
    )
    b_back = exchanged(b_done, "expert")
    fwd_block = local_call(
        fwd_end_kernel,
        whole,
        (layer_in, f_routes, f_gates, *f_back),
        2 * one_dot,
        moved,
        after=(b_done[0],),
    )
    bwd_block = local_call(
        bwd_end_kernel,
        whole,
        (grad_in, saved, gain_row, b_routes, *b_back),
        one_dot,
        moved,
    )
    return (fwd_block[None], bwd_block[None])


def pick(table, expert, capacity, kind, top_count):
    first = 0 if kind[0] == "f" else 2 * top_count
    routes = table[first : first + top_count]
    gates = table[first + top_count : first + 2 * top_count]
    tok_rows = table.shape[1]
    member = routes == float(expert)
    held = jnp.sum(member.astype(jnp.float32), axis=0, keepdims=True)
    before = lax.broadcasted_iota(jnp.int32, (tok_rows, tok_rows), 0) < lax.broadcasted_iota(
        jnp.int32, (tok_rows, tok_rows), 1
    )
    slots = jnp.dot(
        jnp.broadcast_to(held, (8, tok_rows)).astype(jnp.bfloat16),
        before.astype(jnp.bfloat16),
        preferred_element_type=jnp.float32,
    )[0:1]
    place = placement(jnp.where(held > 0.0, slots, -1.0), 0, capacity)
    if len(kind) == 1:
        return (place.astype(jnp.bfloat16),)
    gate = jnp.sum(jnp.where(member, gates, 0.0), axis=0, keepdims=True)
    return halves(jnp.where(place, gate, 0.0))


def to_slots(weights, values):
    total = None
    for part in weights:
        term = jnp.dot(part, values, preferred_element_type=jnp.float32)
        total = term if total is None else total + term
    return total.astype(jnp.bfloat16)


def to_tokens(weights, rows):
    total = None
    for part in weights:
        term = rows_dot(part, rows)
        total = term if total is None else total + term
    return total


def three_parts(values):
    high = values.astype(jnp.bfloat16)
    rest = values - high.astype(jnp.float32)
    mid = rest.astype(jnp.bfloat16)
    low = (rest - mid.astype(jnp.float32)).astype(jnp.bfloat16)
    return high, mid, low


def normed_halves(wide, gain):
    inv_rms = lax.rsqrt(jnp.mean(wide * wide, axis=-1, keepdims=True) + EPS)
    return (wide * inv_rms * gain).astype(jnp.bfloat16)


def first_kernel(top_count, me_ref, *refs):
    sources, refs = refs[:6], refs[6:]
    (left_ref, right_ref, table_ref, gain_out), refs = refs[:4], refs[4:]
    held, sems = refs[:6], refs[6]
    copies = [pltpu.make_async_copy(sources[i], held[i], sems.at[i]) for i in range(6)]
    for copy in copies:
        copy.start()
    for copy in copies[1:]:
        copy.wait()
    saved, gain, f_routes, f_gates, b_routes, b_gates = held
    me = me_ref[0]
    fr = (f_routes[...] ^ me).astype(jnp.float32)
    br = (b_routes[...] ^ me).astype(jnp.float32)
    fg = f_gates[...]
    bg = b_gates[...]
    table = jnp.concatenate([fr, fg, br, bg], axis=0)
    table_ref[...] = table
    packed = [fr.astype(jnp.bfloat16), br.astype(jnp.bfloat16), *three_parts(fg), *three_parts(bg)]
    packed = jnp.concatenate([part.astype(jnp.float32) for part in packed], axis=0)
    gain_out[...] = gain[...]
    tok_rows, features = saved.shape
    half = features // 2
    copies[0].wait()
    normed = normed_halves(saved[...].astype(jnp.float32), gain[...])
    capacity = left_ref.shape[0] - tok_rows - packed.shape[0]
    near = tok_rows + packed.shape[0]
    for half_ref, start, expert in ((left_ref, 0, 1), (right_ref, half, 2)):
        half_ref[:tok_rows, :] = normed[:, start : start + half]
        half_ref[tok_rows:near, :] = jnp.zeros((near - tok_rows, half), jnp.bfloat16)
        half_ref[tok_rows:near, :tok_rows] = packed.astype(jnp.bfloat16)
        other = half - start
        half_ref[near:, :] = to_slots(
            pick(table, expert, capacity, "b", top_count), normed[:, other : other + half]
        )


def unpacked(block, tok_rows, top_count):
    rows = block[tok_rows : tok_rows + 8 * top_count, :tok_rows].astype(jnp.float32)
    k = top_count
    fr, br = rows[0:k], rows[k : 2 * k]
    fg = (rows[2 * k : 3 * k] + rows[3 * k : 4 * k]) + rows[4 * k : 5 * k]
    bg = (rows[5 * k : 6 * k] + rows[6 * k : 7 * k]) + rows[7 * k : 8 * k]
    return jnp.concatenate([fr, fg, br, bg], axis=0)


def normed_kernel_halves(values_ref, gain_ref, left_ref, right_ref):
    half = left_ref.shape[1]
    normed = normed_halves(values_ref[...].astype(jnp.float32), gain_ref[...])
    left_ref[...] = normed[:, :half]
    right_ref[...] = normed[:, half:]


def split_kernel(values_ref, left_ref, right_ref):
    half = left_ref.shape[1]
    left_ref[...] = values_ref[:, :half]
    right_ref[...] = values_ref[:, half:]


def tables_kernel(top_count, from_x, from_y, x_table, y_table):
    tok_rows = x_table.shape[1]
    x_table[...] = unpacked(from_x[...], tok_rows, top_count)
    y_table[...] = unpacked(from_y[...], tok_rows, top_count)


def hop_kernel(kind, top_count, own, x_tab, y_tab, left, right, from_x, from_y, to_y, to_x):
    capacity = to_y.shape[0] // 2
    tok_rows = own.shape[1]
    to_y[:capacity, :] = to_slots(pick(own[...], 2, capacity, kind, top_count), left[:tok_rows, :])
    to_y[capacity:, :] = to_slots(
        pick(x_tab[...], 3, capacity, kind, top_count), from_x[:tok_rows, :]
    )
    to_x[:capacity, :] = to_slots(pick(own[...], 1, capacity, kind, top_count), right[:tok_rows, :])
    to_x[capacity:, :] = to_slots(
        pick(y_tab[...], 3, capacity, kind, top_count), from_y[:tok_rows, :]
    )


def far_kernel(kind, top_count, x_tab, y_tab, from_x, from_y, to_y, to_x):
    capacity = to_y.shape[0]
    tok_rows = x_tab.shape[1]
    to_y[...] = to_slots(pick(x_tab[...], 3, capacity, kind, top_count), from_x[:tok_rows, :])
    to_x[...] = to_slots(pick(y_tab[...], 3, capacity, kind, top_count), from_y[:tok_rows, :])


def assemble(kind, top_count, own, x_tab, y_tab, left, right, from_x, from_y, got_y, got_x, rows):
    capacity = rows.shape[0] // 4
    half = got_y.shape[1]
    tok_rows = own.shape[1]
    mine = pick(own[...], 0, capacity, kind, top_count)
    rows[:capacity, :half] = to_slots(mine, left[:tok_rows, :])
    rows[:capacity, half:] = to_slots(mine, right[:tok_rows, :])
    rows[capacity : 2 * capacity, :half] = to_slots(
        pick(x_tab[...], 1, capacity, kind, top_count), from_x[:tok_rows, :]
    )
    rows[2 * capacity : 3 * capacity, half:] = to_slots(
        pick(y_tab[...], 2, capacity, kind, top_count), from_y[:tok_rows, :]
    )
    if got_y.shape[0] == capacity:
        near_x, near_y = from_x[-capacity:, :], from_y[-capacity:, :]
    else:
        near_x, near_y = got_x[:capacity, :], got_y[:capacity, :]
    rows[capacity : 2 * capacity, half:] = near_x
    rows[2 * capacity : 3 * capacity, :half] = near_y
    rows[3 * capacity :, :half] = got_y[-capacity:, :]
    rows[3 * capacity :, half:] = got_x[-capacity:, :]


def hand_out(out, at, capacity, to_left, keep, near, onward):
    size = out.shape[1]
    rows = out.astype(jnp.bfloat16)
    mine, from_x, from_y, far = [rows[d * capacity : (d + 1) * capacity] for d in range(4)]
    keep[:, at : at + size] = mine
    near[:, at : at + size] = from_x if to_left else from_y
    onward[:capacity, at : at + size] = from_y if to_left else from_x
    onward[capacity:, at : at + size] = far


def fwd_half(hidden_ref, weight_out, to_left, keep, near, onward):
    capacity, half = keep.shape
    first = 0 if to_left else half
    for at, size in tiles(half, 512):
        out = jnp.dot(
            hidden_ref[...],
            weight_out[:, first + at : first + at + size],
            preferred_element_type=jnp.float32,
        )
        hand_out(out, at, capacity, to_left, keep, near, onward)


def bwd_half(both_ref, weight_in, to_left, keep, near, onward):
    capacity, half = keep.shape
    first = 0 if to_left else half
    for at, size in tiles(half, 512):
        out = lax.dot_general(
            both_ref[...],
            weight_in[first + at : first + at + size, :],
            (((1,), (1,)), ((), ())),
            preferred_element_type=jnp.float32,
        )
        hand_out(out, at, capacity, to_left, keep, near, onward)


def fwd_right_kernel(hidden_ref, weight_out, keep, near, onward):
    fwd_half(hidden_ref, weight_out, False, keep, near, onward)


def bwd_right_kernel(both_ref, weight_in, keep, near, onward):
    bwd_half(both_ref, weight_in, False, keep, near, onward)


def hop_again_kernel(top_count, *refs):
    dispatch, (weight_in, gate_ref, up_ref, rows_ref) = refs[:9], refs[9:]
    assemble("b", top_count, *dispatch, rows_ref)
    hidden_units = gate_ref.shape[1]
    for start, size in tiles(hidden_units, 256):
        gate_ref[:, start : start + size] = jnp.dot(
            rows_ref[...], weight_in[:, start : start + size], preferred_element_type=jnp.float32
        )
        up_ref[:, start : start + size] = jnp.dot(
            rows_ref[...],
            weight_in[:, hidden_units + start : hidden_units + start + size],
            preferred_element_type=jnp.float32,
        )


def hop_fwd_kernel(top_count, *refs):
    dispatch, refs = refs[:9], refs[9:]
    weight_in, weight_out = refs[:2]
    outs, hidden_ref, rows_ref = refs[2:5], refs[5], refs[6]
    hidden_units = weight_out.shape[0]
    assemble("f", top_count, *dispatch, rows_ref)
    for start, size in tiles(hidden_units, 256):
        gate = jnp.dot(
            rows_ref[...], weight_in[:, start : start + size], preferred_element_type=jnp.float32
        )
        up = jnp.dot(
            rows_ref[...],
            weight_in[:, hidden_units + start : hidden_units + start + size],
            preferred_element_type=jnp.float32,
        )
        hidden_ref[:, start : start + size] = (gate / (1.0 + jnp.exp(-gate)) * up).astype(
            jnp.bfloat16
        )
    fwd_half(hidden_ref, weight_out, True, *outs)


def hop_bwd_kernel(top_count, *refs):
    dispatch, refs = refs[:9], refs[9:]
    gate_ref, up_ref, weight_in, weight_out = refs[:4]
    outs, both_ref, grads_ref = refs[4:7], refs[7], refs[8]
    hidden_units = weight_out.shape[0]
    assemble("bg", top_count, *dispatch, grads_ref)
    for start, size in tiles(hidden_units, 256):
        gate = gate_ref[:, start : start + size]
        up = up_ref[:, start : start + size]
        d_hidden = lax.dot_general(
            grads_ref[...],
            weight_out[start : start + size, :],
            (((1,), (1,)), ((), ())),
            preferred_element_type=jnp.float32,
        )
        sig = 1.0 / (1.0 + jnp.exp(-gate))
        both_ref[:, start : start + size] = (
            d_hidden * up * sig * (1.0 + gate * (1.0 - sig))
        ).astype(jnp.bfloat16)
        both_ref[:, hidden_units + start : hidden_units + start + size] = (
            d_hidden * gate * sig
        ).astype(jnp.bfloat16)
    bwd_half(both_ref, weight_in, True, *outs)


def sums_kernel(kind, top_count, here, table_ref, near, far, out):
    capacity = near.shape[0]
    table = table_ref[...]
    out[...] = (
        to_tokens(pick(table, here, capacity, kind, top_count), near[...])
        + to_tokens(pick(table, 3, capacity, kind, top_count), far[capacity:, :])
    ).astype(jnp.bfloat16)


def summed(kind, top_count, own, keep_left, keep_right, got_y, got_x, sum_x, sum_y):
    capacity = keep_left.shape[0]
    mine = pick(own[...], 0, capacity, kind, top_count)
    near_y = pick(own[...], 2, capacity, kind, top_count)
    near_x = pick(own[...], 1, capacity, kind, top_count)
    left = to_tokens(mine, keep_left[...]) + to_tokens(near_y, got_y[:capacity, :])
    right = to_tokens(mine, keep_right[...]) + to_tokens(near_x, got_x[:capacity, :])
    return left + sum_x[...].astype(jnp.float32), right + sum_y[...].astype(jnp.float32)


def hop_fwd_end_kernel(top_count, layer_ref, *refs):
    out_ref, order_ref = refs[-2:]
    order_ref[...] = jnp.zeros_like(order_ref)
    half = layer_ref.shape[1] // 2
    left, right = summed("fg", top_count, *refs[:-2])
    out_ref[:, :half] = (layer_ref[:, :half].astype(jnp.float32) + left).astype(jnp.bfloat16)
    out_ref[:, half:] = (layer_ref[:, half:].astype(jnp.float32) + right).astype(jnp.bfloat16)


def hop_bwd_end_kernel(top_count, grads_ref, saved_ref, gain_ref, *refs):
    out_ref = refs[-1]
    features = saved_ref.shape[1]
    left, right = summed("b", top_count, *refs[:-1])
    wide = saved_ref[...].astype(jnp.float32)
    inv_rms = lax.rsqrt(jnp.mean(wide * wide, axis=-1, keepdims=True) + EPS)
    scaled = jnp.concatenate([left, right], axis=1) * gain_ref[...]
    cubed = inv_rms * inv_rms * inv_rms
    inner = jnp.sum(scaled * wide, axis=-1, keepdims=True)
    out_ref[...] = (
        grads_ref[...].astype(jnp.float32) + inv_rms * scaled - cubed / features * wide * inner
    ).astype(jnp.bfloat16)


def per_device_hops(
    fwd_prev,
    bwd_prev,
    bwd_saved,
    fwd_routes,
    fwd_gates,
    bwd_routes,
    bwd_gates,
    norm_gain,
    w_in,
    w_out,
):
    tok_rows, features = fwd_prev.shape[1:]
    top_count = fwd_routes.shape[2]
    hidden_units = w_in.shape[3] // 2
    capacity = 3 * tok_rows * top_count // 8
    half = features // 2
    gain_row = norm_gain
    weight_in = w_in[0, 0]
    weight_out = w_out[0, 0]
    me = lax.axis_index("expert").astype(jnp.int32).reshape(1)
    saved = bwd_saved[0]
    layer_in = passed_along(fwd_prev[0], "section", 1)
    grad_in = passed_along(bwd_prev[0], "section", -1)

    def shaped(rows, columns, dtype=jnp.bfloat16):
        return jax.ShapeDtypeStruct((rows, columns), dtype)

    def crossed(left, right):
        return swapped(left, "expert", 1), swapped(right, "expert", 2)

    slot_total = 4 * capacity
    table_rows = 4 * top_count
    one_hop = moved = 1024
    expert_flops = 2 * slot_total * features * hidden_units
    expert_moved = 2 * features * (3 * hidden_units + 3 * slot_total)
    rows_scratch = pltpu.VMEM((slot_total, features), jnp.bfloat16)
    halves_out = [shaped(tok_rows, half)] * 2
    hop_out = [shaped(2 * capacity, half)] * 2
    half_out = [shaped(capacity, half), shaped(capacity, half), shaped(2 * capacity, half)]
    hidden_shape = shaped(slot_total, hidden_units)
    both_shape = shaped(slot_total, 2 * hidden_units)
    table_shape = shaped(table_rows, tok_rows, jnp.float32)
    first_rows = tok_rows + 8 * top_count + capacity

    b_left, b_right, own, gain_here = pl.pallas_call(
        functools.partial(first_kernel, top_count),
        out_shape=[
            shaped(first_rows, half),
            shaped(first_rows, half),
            table_shape,
            shaped(1, features, jnp.float32),
        ],
        in_specs=[pl.BlockSpec(memory_space=pltpu.SMEM)]
        + [pl.BlockSpec(memory_space=pltpu.HBM)] * 6,
        scratch_shapes=[
            pltpu.VMEM((tok_rows, features), jnp.bfloat16),
            pltpu.VMEM((1, features), jnp.float32),
            pltpu.VMEM((top_count, tok_rows), jnp.int32),
            pltpu.VMEM((top_count, tok_rows), jnp.float32),
            pltpu.VMEM((top_count, tok_rows), jnp.int32),
            pltpu.VMEM((top_count, tok_rows), jnp.float32),
            pltpu.SemaphoreType.DMA((6,)),
        ],
        compiler_params=pltpu.CompilerParams(vmem_limit_bytes=VMEM_LIMIT),
        cost_estimate=pl.CostEstimate(flops=one_hop, bytes_accessed=moved, transcendentals=0),
    )(
        me,
        *[
            pltpu.with_memory_space_constraint(value, pltpu.HBM)
            for value in (
                saved,
                gain_row,
                fwd_routes[0].T,
                fwd_gates[0].T,
                bwd_routes[0].T,
                bwd_gates[0].T,
            )
        ],
    )
    b_from_x, b_from_y = crossed(b_left, b_right)
    x_tab, y_tab = local_call(
        functools.partial(tables_kernel, top_count),
        [table_shape] * 2,
        (b_from_x, b_from_y),
        1024,
        1024,
    )
    tabs = (own, x_tab, y_tab)

    def onward(kind, sent, got, after):
        to_y, to_x = local_call(
            functools.partial(hop_kernel, kind, top_count),
            hop_out,
            (*tabs, *sent, *got),
            one_hop,
            moved,
            after=after,
        )
        return swapped(to_y, "expert", 2), swapped(to_x, "expert", 1), to_y

    f_left, f_right = local_call(
        normed_kernel_halves, halves_out, (layer_in, gain_here), one_hop, moved, after=(x_tab,)
    )
    f_from_x, f_from_y = crossed(f_left, f_right)
    g_left, g_right = local_call(split_kernel, halves_out, (grad_in,), 1024, moved, after=(f_left,))
    g_from_x, g_from_y = crossed(g_left, g_right)
    b_to_y, b_to_x = local_call(
        functools.partial(far_kernel, "b", top_count),
        [shaped(capacity, half)] * 2,
        (x_tab, y_tab, b_from_x, b_from_y),
        one_hop,
        moved,
        after=(g_left,),
    )
    b_got_y, b_got_x = swapped(b_to_y, "expert", 2), swapped(b_to_x, "expert", 1)
    f_got_y, f_got_x, f_to_y = onward("f", (f_left, f_right), (f_from_x, f_from_y), (g_left,))
    g_got_y, g_got_x, g_to_y = onward("bg", (g_left, g_right), (g_from_x, g_from_y), (f_to_y,))
    f_keep_l, f_near_l, f_on_l, hidden = local_call(
        functools.partial(hop_fwd_kernel, top_count),
        half_out + [hidden_shape],
        (*tabs, f_left, f_right, f_from_x, f_from_y, f_got_y, f_got_x, weight_in, weight_out),
        5 * expert_flops // 2,
        expert_moved,
        scratch=(rows_scratch,),
        after=(g_to_y,),
    )
    f_ret_y = swapped(f_on_l, "expert", 2)
    f_keep_r, f_near_r, f_on_r = local_call(
        fwd_right_kernel, half_out, (hidden, weight_out), 1024, 1024
    )
    f_ret_x = swapped(f_on_r, "expert", 1)
    gate_pre, up_pre = local_call(
        functools.partial(hop_again_kernel, top_count),
        [shaped(slot_total, hidden_units, jnp.float32)] * 2,
        (*tabs, b_left, b_right, b_from_x, b_from_y, b_got_y, b_got_x, weight_in),
        2 * expert_flops,
        expert_moved,
        scratch=(rows_scratch,),
        after=(f_keep_r,),
    )
    b_keep_l, b_near_l, b_on_l, both = local_call(
        functools.partial(hop_bwd_kernel, top_count),
        half_out + [both_shape],
        (
            *tabs,
            g_left,
            g_right,
            g_from_x,
            g_from_y,
            g_got_y,
            g_got_x,
            gate_pre,
            up_pre,
            weight_in,
            weight_out,
        ),
        2 * expert_flops,
        expert_moved,
        scratch=(rows_scratch,),
        after=(f_keep_r,),
    )
    b_ret_y = swapped(b_on_l, "expert", 2)
    b_keep_r, b_near_r, b_on_r = local_call(
        bwd_right_kernel, half_out, (both, weight_in), 1024, 1024
    )
    b_ret_x = swapped(b_on_r, "expert", 1)

    def summed_call(kind, here, table, near, far, after):
        part = local_call(
            functools.partial(sums_kernel, kind, top_count, here),
            shaped(tok_rows, half),
            (table, near, far),
            one_hop,
            moved,
            after=after,
        )
        return swapped(part, "expert", here), part

    f_sum_x, last = summed_call("fg", 1, x_tab, f_near_l, f_ret_y, (b_keep_r,))
    f_sum_y, last = summed_call("fg", 2, y_tab, f_near_r, f_ret_x, (last,))
    b_sum_x, last = summed_call("b", 1, x_tab, b_near_l, b_ret_y, (last,))
    b_sum_y, last = summed_call("b", 2, y_tab, b_near_r, b_ret_x, (last,))
    f_keep = (f_keep_l, f_keep_r)
    b_keep = (b_keep_l, b_keep_r)
    fwd_block, order = local_call(
        functools.partial(hop_fwd_end_kernel, top_count),
        [shaped(tok_rows, features), shaped(8, 128, jnp.float32)],
        (layer_in, own, *f_keep, f_ret_y, f_ret_x, f_sum_x, f_sum_y),
        one_hop,
        moved,
        after=(last,),
    )
    bwd_block = local_call(
        functools.partial(hop_bwd_end_kernel, top_count),
        shaped(tok_rows, features),
        (grad_in, saved, gain_here, own, *b_keep, b_ret_y, b_ret_x, b_sum_x, b_sum_y),
        one_hop,
        moved,
        after=(order,),
    )
    return (fwd_block[None], bwd_block[None])


def per_device(*arrays):
    if lax.axis_size("expert") == 4:
        return per_device_hops(*arrays)
    return per_device_direct(*arrays)


def solution(mesh):
    in_specs = (
        P("section", "expert", None),
        P("section", "expert", None),
        P("section", "expert", None),
        P("section", "expert", None),
        P("section", "expert", None),
        P("section", "expert", None),
        P("section", "expert", None),
        P("section", None),
        P("section", "expert", None, None),
        P("section", "expert", None, None),
    )
    out_specs = (P("section", "expert", None), P("section", "expert", None))
    return jax.shard_map(
        per_device, mesh=mesh, in_specs=in_specs, out_specs=out_specs, check_vma=False
    )
```

```python
import functools

import jax
import jax.numpy as jnp
from jax import lax
from jax.experimental import pallas as pl
from jax.experimental.pallas import tpu as pltpu
from jax.sharding import PartitionSpec as P

EPS = 1e-06
VMEM_LIMIT = 32 * 1024 * 1024


def passed_along(value, axis, steps):
    count = lax.axis_size(axis)
    pairs = [(source, (source + steps) % count) for source in range(count)]
    return lax.ppermute(value, axis, pairs)


def swapped(value, axis, offset):
    count = lax.axis_size(axis)
    pairs = [(source, source ^ offset) for source in range(count)]
    return lax.ppermute(value, axis, pairs)


def exchanged(blocks, axis):
    return [blocks[0]] + [swapped(blocks[d], axis, d) for d in range(1, len(blocks))]


def slot_table(routes, expert_count):
    top_count, tok_rows = routes.shape
    experts = max(8, expert_count)
    wanted = lax.broadcasted_iota(jnp.int32, (experts, tok_rows), 0)
    member = routes[0:1, :] == wanted
    for k in range(1, top_count):
        member = jnp.logical_or(member, routes[k : k + 1, :] == wanted)
    before = lax.broadcasted_iota(jnp.int32, (tok_rows, tok_rows), 0) < lax.broadcasted_iota(
        jnp.int32, (tok_rows, tok_rows), 1
    )
    slots = jnp.dot(
        member.astype(jnp.bfloat16),
        before.astype(jnp.bfloat16),
        preferred_element_type=jnp.float32,
    )
    return jnp.where(member, slots, -1.0)


def placement(slots, expert, capacity):
    tok_rows = slots.shape[1]
    row = lax.broadcasted_iota(jnp.int32, (capacity, tok_rows), 0).astype(jnp.float32)
    return slots[expert : expert + 1, :] == row


def gate_row(routes, gates, expert):
    total = jnp.zeros((1, routes.shape[1]), jnp.float32)
    for k in range(routes.shape[0]):
        total = total + jnp.where(routes[k : k + 1, :] == expert, gates[k : k + 1, :], 0.0)
    return total


def halves(weights):
    high = weights.astype(jnp.bfloat16)
    low = (weights - high.astype(jnp.float32)).astype(jnp.bfloat16)
    return high, low


def normed_kernel(values_ref, routes_ref, gain_ref, *out_refs):
    expert_count = len(out_refs)
    capacity = out_refs[0].shape[0]
    wide = values_ref[...].astype(jnp.float32)
    inv_rms = lax.rsqrt(jnp.mean(wide * wide, axis=-1, keepdims=True) + EPS)
    normed = (wide * inv_rms * gain_ref[...]).astype(jnp.bfloat16)
    slots = slot_table(routes_ref[...], expert_count)
    for e in range(expert_count):
        place = placement(slots, e, capacity).astype(jnp.bfloat16)
        out_refs[e][...] = jnp.dot(place, normed, preferred_element_type=jnp.float32).astype(
            jnp.bfloat16
        )


def grads_kernel(grads_ref, routes_ref, gates_ref, *out_refs):
    expert_count = len(out_refs)
    capacity = out_refs[0].shape[0]
    grads = grads_ref[...]
    routes = routes_ref[...]
    slots = slot_table(routes, expert_count)
    for e in range(expert_count):
        place = placement(slots, e, capacity)
        high, low = halves(jnp.where(place, gate_row(routes, gates_ref[...], e), 0.0))
        out_refs[e][...] = (
            jnp.dot(high, grads, preferred_element_type=jnp.float32)
            + jnp.dot(low, grads, preferred_element_type=jnp.float32)
        ).astype(jnp.bfloat16)


def rows_dot(weights, rows):
    return lax.dot_general(
        weights, rows, (((0,), (0,)), ((), ())), preferred_element_type=jnp.float32
    )


def fwd_end_kernel(layer_ref, routes_ref, gates_ref, *refs):
    row_refs, out_ref = refs[:-1], refs[-1]
    expert_count = len(row_refs)
    capacity = row_refs[0].shape[0]
    routes = routes_ref[...]
    slots = slot_table(routes, expert_count)
    total = layer_ref[...].astype(jnp.float32)
    for e in range(expert_count):
        place = placement(slots, e, capacity)
        high, low = halves(jnp.where(place, gate_row(routes, gates_ref[...], e), 0.0))
        rows = row_refs[e][...]
        total = total + (rows_dot(high, rows) + rows_dot(low, rows))
    out_ref[...] = total.astype(jnp.bfloat16)


def bwd_end_kernel(grads_ref, saved_ref, gain_ref, routes_ref, *refs):
    row_refs, out_ref = refs[:-1], refs[-1]
    expert_count = len(row_refs)
    capacity = row_refs[0].shape[0]
    features = saved_ref.shape[1]
    slots = slot_table(routes_ref[...], expert_count)
    d_normed = None
    for e in range(expert_count):
        place = placement(slots, e, capacity).astype(jnp.bfloat16)
        part = rows_dot(place, row_refs[e][...])
        d_normed = part if d_normed is None else d_normed + part
    wide = saved_ref[...].astype(jnp.float32)
    inv_rms = lax.rsqrt(jnp.mean(wide * wide, axis=-1, keepdims=True) + EPS)
    scaled = d_normed * gain_ref[...]
    cubed = inv_rms * inv_rms * inv_rms
    inner = jnp.sum(scaled * wide, axis=-1, keepdims=True)
    out_ref[...] = (
        grads_ref[...].astype(jnp.float32) + inv_rms * scaled - cubed / features * wide * inner
    ).astype(jnp.bfloat16)


def joined(refs):
    rows = [ref[...] for ref in refs]
    if rows[0].shape[0] % 16 == 0:
        return jnp.concatenate(rows, axis=0)
    return jnp.concatenate([r.astype(jnp.float32) for r in rows], axis=0).astype(jnp.bfloat16)


def tiles(size, step):
    return [(start, min(step, size - start)) for start in range(0, size, step)]


def expert_fwd_kernel(*refs):
    expert_count = (len(refs) - 4) // 2
    row_refs = refs[:expert_count]
    weight_in, weight_out = refs[expert_count : expert_count + 2]
    out_refs = refs[expert_count + 2 : 2 * expert_count + 2]
    rows_ref, hidden_ref = refs[-2:]
    capacity = row_refs[0].shape[0]
    hidden_units, features = weight_out.shape
    rows_ref[...] = joined(row_refs)
    for start, size in tiles(hidden_units, 256):
        gate = jnp.dot(
            rows_ref[...], weight_in[:, start : start + size], preferred_element_type=jnp.float32
        )
        up = jnp.dot(
            rows_ref[...],
            weight_in[:, hidden_units + start : hidden_units + start + size],
            preferred_element_type=jnp.float32,
        )
        hidden_ref[:, start : start + size] = (gate / (1.0 + jnp.exp(-gate)) * up).astype(
            jnp.bfloat16
        )
    for start, size in tiles(features, 512):
        out = jnp.dot(
            hidden_ref[...], weight_out[:, start : start + size], preferred_element_type=jnp.float32
        )
        for d in range(expert_count):
            out_refs[d][:, start : start + size] = out[d * capacity : (d + 1) * capacity].astype(
                jnp.bfloat16
            )


def expert_again_kernel(*refs):
    expert_count = len(refs) - 4
    row_refs = refs[:expert_count]
    weight_in, gate_ref, up_ref, rows_ref = refs[expert_count:]
    hidden_units = gate_ref.shape[1]
    rows_ref[...] = joined(row_refs)
    for start, size in tiles(hidden_units, 256):
        gate_ref[:, start : start + size] = jnp.dot(
            rows_ref[...], weight_in[:, start : start + size], preferred_element_type=jnp.float32
        )
        up_ref[:, start : start + size] = jnp.dot(
            rows_ref[...],
            weight_in[:, hidden_units + start : hidden_units + start + size],
            preferred_element_type=jnp.float32,
        )


def expert_bwd_kernel(*refs):
    expert_count = (len(refs) - 6) // 2
    grad_refs = refs[:expert_count]
    gate_ref, up_ref, weight_in, weight_out = refs[expert_count : expert_count + 4]
    out_refs = refs[expert_count + 4 : 2 * expert_count + 4]
    grads_ref, both_ref = refs[-2:]
    capacity = grad_refs[0].shape[0]
    hidden_units, features = weight_out.shape
    grads_ref[...] = joined(grad_refs)
    for start, size in tiles(hidden_units, 256):
        gate = gate_ref[:, start : start + size]
        up = up_ref[:, start : start + size]
        d_hidden = lax.dot_general(
            grads_ref[...],
            weight_out[start : start + size, :],
            (((1,), (1,)), ((), ())),
            preferred_element_type=jnp.float32,
        )
        sig = 1.0 / (1.0 + jnp.exp(-gate))
        both_ref[:, start : start + size] = (
            d_hidden * up * sig * (1.0 + gate * (1.0 - sig))
        ).astype(jnp.bfloat16)
        both_ref[:, hidden_units + start : hidden_units + start + size] = (
            d_hidden * gate * sig
        ).astype(jnp.bfloat16)
    for start, size in tiles(features, 512):
        out = lax.dot_general(
            both_ref[...],
            weight_in[start : start + size, :],
            (((1,), (1,)), ((), ())),
            preferred_element_type=jnp.float32,
        )
        for d in range(expert_count):
            out_refs[d][:, start : start + size] = out[d * capacity : (d + 1) * capacity].astype(
                jnp.bfloat16
            )


def local_call(kernel, out_shapes, inputs, flops, moved, scratch=(), after=()):
    in_specs = [pl.BlockSpec(memory_space=pltpu.VMEM)] * len(inputs)
    held = len(inputs)

    def body(*refs):
        kernel(*refs[:held], *refs[held + len(after) :])

    return pl.pallas_call(
        body if after else kernel,
        out_shape=out_shapes,
        in_specs=in_specs + [pl.BlockSpec(memory_space=pl.ANY)] * len(after),
        scratch_shapes=list(scratch),
        compiler_params=pltpu.CompilerParams(vmem_limit_bytes=VMEM_LIMIT),
        cost_estimate=pl.CostEstimate(flops=flops, bytes_accessed=moved, transcendentals=0),
    )(*inputs, *after)


def per_device_direct(
    fwd_prev,
    bwd_prev,
    bwd_saved,
    fwd_routes,
    fwd_gates,
    bwd_routes,
    bwd_gates,
    norm_gain,
    w_in,
    w_out,
):
    expert_count = lax.axis_size("expert")
    tok_rows = fwd_prev.shape[1]
    features = fwd_prev.shape[2]
    top_count = fwd_routes.shape[2]
    hidden_units = w_in.shape[3] // 2
    capacity = 3 * tok_rows * top_count // (2 * expert_count)
    gain_row = norm_gain
    weight_in = w_in[0, 0]
    weight_out = w_out[0, 0]
    me = lax.axis_index("expert")
    f_routes = (fwd_routes[0] ^ me).T
    b_routes = (bwd_routes[0] ^ me).T
    f_gates = fwd_gates[0].T
    b_gates = bwd_gates[0].T
    saved = bwd_saved[0]
    layer_in = passed_along(fwd_prev[0], "section", 1)
    grad_in = passed_along(bwd_prev[0], "section", -1)

    block = jax.ShapeDtypeStruct((capacity, features), jnp.bfloat16)
    whole = jax.ShapeDtypeStruct((tok_rows, features), jnp.bfloat16)
    one_dot = 2 * expert_count * capacity * tok_rows * features
    moved = 2 * features * (tok_rows + expert_count * capacity)
    slot_total = expert_count * capacity
    blocks = [block] * expert_count
    expert_flops = 2 * slot_total * features * hidden_units
    expert_moved = 2 * features * (3 * hidden_units + 3 * slot_total)
    rows_scratch = pltpu.VMEM((slot_total, features), jnp.bfloat16)

    b_sent = local_call(normed_kernel, blocks, (saved, b_routes, gain_row), one_dot, moved)
    b_rows = exchanged(b_sent, "expert")
    f_sent = local_call(
        normed_kernel, blocks, (layer_in, f_routes, gain_row), one_dot, moved, after=(b_sent[0],)
    )
    f_rows = exchanged(f_sent, "expert")
    g_sent = local_call(
        grads_kernel, blocks, (grad_in, b_routes, b_gates), 2 * one_dot, moved, after=(f_sent[0],)
    )
    g_rows = exchanged(g_sent, "expert")
    projected = jax.ShapeDtypeStruct((slot_total, hidden_units), jnp.float32)
    gate_pre, up_pre = local_call(
        expert_again_kernel,
        [projected, projected],
        (*b_rows, weight_in),
        2 * expert_flops,
        expert_moved,
        scratch=(rows_scratch,),
        after=(g_sent[0],),
    )
    f_done = local_call(
        expert_fwd_kernel,
        blocks,
        (*f_rows, weight_in, weight_out),
        3 * expert_flops,
        expert_moved,
        scratch=(rows_scratch, pltpu.VMEM((slot_total, hidden_units), jnp.bfloat16)),
        after=(gate_pre,),
    )
    f_back = exchanged(f_done, "expert")
    b_done = local_call(
        expert_bwd_kernel,
        blocks,
        (*g_rows, gate_pre, up_pre, weight_in, weight_out),
        3 * expert_flops,
        expert_moved,
        scratch=(rows_scratch, pltpu.VMEM((slot_total, 2 * hidden_units), jnp.bfloat16)),
        after=(f_back[1],),
    )
    b_back = exchanged(b_done, "expert")
    fwd_block = local_call(
        fwd_end_kernel,
        whole,
        (layer_in, f_routes, f_gates, *f_back),
        2 * one_dot,
        moved,
        after=(b_done[0],),
    )
    bwd_block = local_call(
        bwd_end_kernel,
        whole,
        (grad_in, saved, gain_row, b_routes, *b_back),
        one_dot,
        moved,
    )
    return (fwd_block[None], bwd_block[None])


def pick(table, expert, capacity, kind, top_count):
    first = 0 if kind[0] == "f" else 2 * top_count
    routes = table[first : first + top_count]
    gates = table[first + top_count : first + 2 * top_count]
    tok_rows = table.shape[1]
    member = routes == float(expert)
    held = jnp.sum(member.astype(jnp.float32), axis=0, keepdims=True)
    before = lax.broadcasted_iota(jnp.int32, (tok_rows, tok_rows), 0) < lax.broadcasted_iota(
        jnp.int32, (tok_rows, tok_rows), 1
    )
    slots = jnp.dot(
        jnp.broadcast_to(held, (8, tok_rows)).astype(jnp.bfloat16),
        before.astype(jnp.bfloat16),
        preferred_element_type=jnp.float32,
    )[0:1]
    place = placement(jnp.where(held > 0.0, slots, -1.0), 0, capacity)
    if len(kind) == 1:
        return (place.astype(jnp.bfloat16),)
    gate = jnp.sum(jnp.where(member, gates, 0.0), axis=0, keepdims=True)
    return halves(jnp.where(place, gate, 0.0))


def to_slots(weights, values):
    total = None
    for part in weights:
        term = jnp.dot(part, values, preferred_element_type=jnp.float32)
        total = term if total is None else total + term
    return total.astype(jnp.bfloat16)


def to_tokens(weights, rows):
    total = None
    for part in weights:
        term = rows_dot(part, rows)
        total = term if total is None else total + term
    return total


def three_parts(values):
    high = values.astype(jnp.bfloat16)
    rest = values - high.astype(jnp.float32)
    mid = rest.astype(jnp.bfloat16)
    low = (rest - mid.astype(jnp.float32)).astype(jnp.bfloat16)
    return high, mid, low


def normed_halves(wide, gain):
    inv_rms = lax.rsqrt(jnp.mean(wide * wide, axis=-1, keepdims=True) + EPS)
    return (wide * inv_rms * gain).astype(jnp.bfloat16)


def first_kernel(top_count, me_ref, *refs):
    sources, refs = refs[:6], refs[6:]
    (left_ref, right_ref, table_ref, gain_out), refs = refs[:4], refs[4:]
    held, sems = refs[:6], refs[6]
    copies = [pltpu.make_async_copy(sources[i], held[i], sems.at[i]) for i in range(6)]
    for copy in copies:
        copy.start()
    for copy in copies[1:]:
        copy.wait()
    saved, gain, f_routes, f_gates, b_routes, b_gates = held
    me = me_ref[0]
    fr = (f_routes[...] ^ me).astype(jnp.float32)
    br = (b_routes[...] ^ me).astype(jnp.float32)
    fg = f_gates[...]
    bg = b_gates[...]
    table = jnp.concatenate([fr, fg, br, bg], axis=0)
    table_ref[...] = table
    packed = [fr.astype(jnp.bfloat16), br.astype(jnp.bfloat16), *three_parts(fg), *three_parts(bg)]
    packed = jnp.concatenate([part.astype(jnp.float32) for part in packed], axis=0)
    gain_out[...] = gain[...]
    tok_rows, features = saved.shape
    half = features // 2
    copies[0].wait()
    normed = normed_halves(saved[...].astype(jnp.float32), gain[...])
    capacity = left_ref.shape[0] - tok_rows - packed.shape[0]
    near = tok_rows + packed.shape[0]
    for half_ref, start, expert in ((left_ref, 0, 1), (right_ref, half, 2)):
        half_ref[:tok_rows, :] = normed[:, start : start + half]
        half_ref[tok_rows:near, :] = jnp.zeros((near - tok_rows, half), jnp.bfloat16)
        half_ref[tok_rows:near, :tok_rows] = packed.astype(jnp.bfloat16)
        other = half - start
        half_ref[near:, :] = to_slots(
            pick(table, expert, capacity, "b", top_count), normed[:, other : other + half]
        )


def unpacked(block, tok_rows, top_count):
    rows = block[tok_rows : tok_rows + 8 * top_count, :tok_rows].astype(jnp.float32)
    k = top_count
    fr, br = rows[0:k], rows[k : 2 * k]
    fg = (rows[2 * k : 3 * k] + rows[3 * k : 4 * k]) + rows[4 * k : 5 * k]
    bg = (rows[5 * k : 6 * k] + rows[6 * k : 7 * k]) + rows[7 * k : 8 * k]
    return jnp.concatenate([fr, fg, br, bg], axis=0)


def normed_kernel_halves(values_ref, gain_ref, left_ref, right_ref):
    half = left_ref.shape[1]
    normed = normed_halves(values_ref[...].astype(jnp.float32), gain_ref[...])
    left_ref[...] = normed[:, :half]
    right_ref[...] = normed[:, half:]


def split_kernel(values_ref, left_ref, right_ref):
    half = left_ref.shape[1]
    left_ref[...] = values_ref[:, :half]
    right_ref[...] = values_ref[:, half:]


def tables_kernel(top_count, from_x, from_y, x_table, y_table):
    tok_rows = x_table.shape[1]
    x_table[...] = unpacked(from_x[...], tok_rows, top_count)
    y_table[...] = unpacked(from_y[...], tok_rows, top_count)


def hop_kernel(kind, top_count, own, x_tab, y_tab, left, right, from_x, from_y, to_y, to_x):
    capacity = to_y.shape[0] // 2
    tok_rows = own.shape[1]
    to_y[:capacity, :] = to_slots(pick(own[...], 2, capacity, kind, top_count), left[:tok_rows, :])
    to_y[capacity:, :] = to_slots(
        pick(x_tab[...], 3, capacity, kind, top_count), from_x[:tok_rows, :]
    )
    to_x[:capacity, :] = to_slots(pick(own[...], 1, capacity, kind, top_count), right[:tok_rows, :])
    to_x[capacity:, :] = to_slots(
        pick(y_tab[...], 3, capacity, kind, top_count), from_y[:tok_rows, :]
    )


def far_kernel(kind, top_count, x_tab, y_tab, from_x, from_y, to_y, to_x):
    capacity = to_y.shape[0]
    tok_rows = x_tab.shape[1]
    to_y[...] = to_slots(pick(x_tab[...], 3, capacity, kind, top_count), from_x[:tok_rows, :])
    to_x[...] = to_slots(pick(y_tab[...], 3, capacity, kind, top_count), from_y[:tok_rows, :])


def assemble(kind, top_count, own, x_tab, y_tab, left, right, from_x, from_y, got_y, got_x, rows):
    capacity = rows.shape[0] // 4
    half = got_y.shape[1]
    tok_rows = own.shape[1]
    mine = pick(own[...], 0, capacity, kind, top_count)
    rows[:capacity, :half] = to_slots(mine, left[:tok_rows, :])
    rows[:capacity, half:] = to_slots(mine, right[:tok_rows, :])
    rows[capacity : 2 * capacity, :half] = to_slots(
        pick(x_tab[...], 1, capacity, kind, top_count), from_x[:tok_rows, :]
    )
    rows[2 * capacity : 3 * capacity, half:] = to_slots(
        pick(y_tab[...], 2, capacity, kind, top_count), from_y[:tok_rows, :]
    )
    if got_y.shape[0] == capacity:
        near_x, near_y = from_x[-capacity:, :], from_y[-capacity:, :]
    else:
        near_x, near_y = got_x[:capacity, :], got_y[:capacity, :]
    rows[capacity : 2 * capacity, half:] = near_x
    rows[2 * capacity : 3 * capacity, :half] = near_y
    rows[3 * capacity :, :half] = got_y[-capacity:, :]
    rows[3 * capacity :, half:] = got_x[-capacity:, :]


def hand_out(out, at, capacity, to_left, keep, near, onward):
    size = out.shape[1]
    rows = out.astype(jnp.bfloat16)
    mine, from_x, from_y, far = [rows[d * capacity : (d + 1) * capacity] for d in range(4)]
    keep[:, at : at + size] = mine
    near[:, at : at + size] = from_x if to_left else from_y
    onward[:capacity, at : at + size] = from_y if to_left else from_x
    onward[capacity:, at : at + size] = far


def fwd_half(hidden_ref, weight_out, to_left, keep, near, onward):
    capacity, half = keep.shape
    first = 0 if to_left else half
    for at, size in tiles(half, 512):
        out = jnp.dot(
            hidden_ref[...],
            weight_out[:, first + at : first + at + size],
            preferred_element_type=jnp.float32,
        )
        hand_out(out, at, capacity, to_left, keep, near, onward)


def bwd_half(both_ref, weight_in, to_left, keep, near, onward):
    capacity, half = keep.shape
    first = 0 if to_left else half
    for at, size in tiles(half, 512):
        out = lax.dot_general(
            both_ref[...],
            weight_in[first + at : first + at + size, :],
            (((1,), (1,)), ((), ())),
            preferred_element_type=jnp.float32,
        )
        hand_out(out, at, capacity, to_left, keep, near, onward)


def fwd_right_kernel(hidden_ref, weight_out, keep, near, onward):
    fwd_half(hidden_ref, weight_out, False, keep, near, onward)


def bwd_right_kernel(both_ref, weight_in, keep, near, onward):
    bwd_half(both_ref, weight_in, False, keep, near, onward)


def hop_again_kernel(top_count, *refs):
    dispatch, (weight_in, gate_ref, up_ref, rows_ref) = refs[:9], refs[9:]
    assemble("b", top_count, *dispatch, rows_ref)
    hidden_units = gate_ref.shape[1]
    for start, size in tiles(hidden_units, 256):
        gate_ref[:, start : start + size] = jnp.dot(
            rows_ref[...], weight_in[:, start : start + size], preferred_element_type=jnp.float32
        )
        up_ref[:, start : start + size] = jnp.dot(
            rows_ref[...],
            weight_in[:, hidden_units + start : hidden_units + start + size],
            preferred_element_type=jnp.float32,
        )


def hop_fwd_kernel(top_count, *refs):
    dispatch, refs = refs[:9], refs[9:]
    weight_in, weight_out = refs[:2]
    outs, hidden_ref, rows_ref = refs[2:5], refs[5], refs[6]
    hidden_units = weight_out.shape[0]
    assemble("f", top_count, *dispatch, rows_ref)
    for start, size in tiles(hidden_units, 256):
        gate = jnp.dot(
            rows_ref[...], weight_in[:, start : start + size], preferred_element_type=jnp.float32
        )
        up = jnp.dot(
            rows_ref[...],
            weight_in[:, hidden_units + start : hidden_units + start + size],
            preferred_element_type=jnp.float32,
        )
        hidden_ref[:, start : start + size] = (gate / (1.0 + jnp.exp(-gate)) * up).astype(
            jnp.bfloat16
        )
    fwd_half(hidden_ref, weight_out, True, *outs)


def hop_bwd_kernel(top_count, *refs):
    dispatch, refs = refs[:9], refs[9:]
    gate_ref, up_ref, weight_in, weight_out = refs[:4]
    outs, both_ref, grads_ref = refs[4:7], refs[7], refs[8]
    hidden_units = weight_out.shape[0]
    assemble("bg", top_count, *dispatch, grads_ref)
    for start, size in tiles(hidden_units, 256):
        gate = gate_ref[:, start : start + size]
        up = up_ref[:, start : start + size]
        d_hidden = lax.dot_general(
            grads_ref[...],
            weight_out[start : start + size, :],
            (((1,), (1,)), ((), ())),
            preferred_element_type=jnp.float32,
        )
        sig = 1.0 / (1.0 + jnp.exp(-gate))
        both_ref[:, start : start + size] = (
            d_hidden * up * sig * (1.0 + gate * (1.0 - sig))
        ).astype(jnp.bfloat16)
        both_ref[:, hidden_units + start : hidden_units + start + size] = (
            d_hidden * gate * sig
        ).astype(jnp.bfloat16)
    bwd_half(both_ref, weight_in, True, *outs)


def sums_kernel(kind, top_count, here, table_ref, near, far, out):
    capacity = near.shape[0]
    table = table_ref[...]
    out[...] = (
        to_tokens(pick(table, here, capacity, kind, top_count), near[...])
        + to_tokens(pick(table, 3, capacity, kind, top_count), far[capacity:, :])
    ).astype(jnp.bfloat16)


def summed(kind, top_count, own, keep_left, keep_right, got_y, got_x, sum_x, sum_y):
    capacity = keep_left.shape[0]
    mine = pick(own[...], 0, capacity, kind, top_count)
    near_y = pick(own[...], 2, capacity, kind, top_count)
    near_x = pick(own[...], 1, capacity, kind, top_count)
    left = to_tokens(mine, keep_left[...]) + to_tokens(near_y, got_y[:capacity, :])
    right = to_tokens(mine, keep_right[...]) + to_tokens(near_x, got_x[:capacity, :])
    return left + sum_x[...].astype(jnp.float32), right + sum_y[...].astype(jnp.float32)


def hop_fwd_end_kernel(top_count, layer_ref, *refs):
    out_ref, order_ref = refs[-2:]
    order_ref[...] = jnp.zeros_like(order_ref)
    half = layer_ref.shape[1] // 2
    left, right = summed("fg", top_count, *refs[:-2])
    out_ref[:, :half] = (layer_ref[:, :half].astype(jnp.float32) + left).astype(jnp.bfloat16)
    out_ref[:, half:] = (layer_ref[:, half:].astype(jnp.float32) + right).astype(jnp.bfloat16)


def hop_bwd_end_kernel(top_count, grads_ref, saved_ref, gain_ref, *refs):
    out_ref = refs[-1]
    features = saved_ref.shape[1]
    left, right = summed("b", top_count, *refs[:-1])
    wide = saved_ref[...].astype(jnp.float32)
    inv_rms = lax.rsqrt(jnp.mean(wide * wide, axis=-1, keepdims=True) + EPS)
    scaled = jnp.concatenate([left, right], axis=1) * gain_ref[...]
    cubed = inv_rms * inv_rms * inv_rms
    inner = jnp.sum(scaled * wide, axis=-1, keepdims=True)
    out_ref[...] = (
        grads_ref[...].astype(jnp.float32) + inv_rms * scaled - cubed / features * wide * inner
    ).astype(jnp.bfloat16)


def per_device_hops(
    fwd_prev,
    bwd_prev,
    bwd_saved,
    fwd_routes,
    fwd_gates,
    bwd_routes,
    bwd_gates,
    norm_gain,
    w_in,
    w_out,
):
    tok_rows, features = fwd_prev.shape[1:]
    top_count = fwd_routes.shape[2]
    hidden_units = w_in.shape[3] // 2
    capacity = 3 * tok_rows * top_count // 8
    half = features // 2
    gain_row = norm_gain
    weight_in = w_in[0, 0]
    weight_out = w_out[0, 0]
    me = lax.axis_index("expert").astype(jnp.int32).reshape(1)
    saved = bwd_saved[0]
    layer_in = passed_along(fwd_prev[0], "section", 1)
    grad_in = passed_along(bwd_prev[0], "section", -1)

    def shaped(rows, columns, dtype=jnp.bfloat16):
        return jax.ShapeDtypeStruct((rows, columns), dtype)

    def crossed(left, right):
        return swapped(left, "expert", 1), swapped(right, "expert", 2)

    slot_total = 4 * capacity
    table_rows = 4 * top_count
    one_hop = moved = 1024
    expert_flops = 2 * slot_total * features * hidden_units
    expert_moved = 2 * features * (3 * hidden_units + 3 * slot_total)
    rows_scratch = pltpu.VMEM((slot_total, features), jnp.bfloat16)
    halves_out = [shaped(tok_rows, half)] * 2
    hop_out = [shaped(2 * capacity, half)] * 2
    half_out = [shaped(capacity, half), shaped(capacity, half), shaped(2 * capacity, half)]
    hidden_shape = shaped(slot_total, hidden_units)
    both_shape = shaped(slot_total, 2 * hidden_units)
    table_shape = shaped(table_rows, tok_rows, jnp.float32)
    first_rows = tok_rows + 8 * top_count + capacity

    b_left, b_right, own, gain_here = pl.pallas_call(
        functools.partial(first_kernel, top_count),
        out_shape=[
            shaped(first_rows, half),
            shaped(first_rows, half),
            table_shape,
            shaped(1, features, jnp.float32),
        ],
        in_specs=[pl.BlockSpec(memory_space=pltpu.SMEM)]
        + [pl.BlockSpec(memory_space=pltpu.HBM)] * 6,
        scratch_shapes=[
            pltpu.VMEM((tok_rows, features), jnp.bfloat16),
            pltpu.VMEM((1, features), jnp.float32),
            pltpu.VMEM((top_count, tok_rows), jnp.int32),
            pltpu.VMEM((top_count, tok_rows), jnp.float32),
            pltpu.VMEM((top_count, tok_rows), jnp.int32),
            pltpu.VMEM((top_count, tok_rows), jnp.float32),
            pltpu.SemaphoreType.DMA((6,)),
        ],
        compiler_params=pltpu.CompilerParams(vmem_limit_bytes=VMEM_LIMIT),
        cost_estimate=pl.CostEstimate(flops=one_hop, bytes_accessed=moved, transcendentals=0),
    )(
        me,
        *[
            pltpu.with_memory_space_constraint(value, pltpu.HBM)
            for value in (
                saved,
                gain_row,
                fwd_routes[0].T,
                fwd_gates[0].T,
                bwd_routes[0].T,
                bwd_gates[0].T,
            )
        ],
    )
    b_from_x, b_from_y = crossed(b_left, b_right)

    def onward(kind, sent, got, after):
        to_y, to_x = local_call(
            functools.partial(hop_kernel, kind, top_count),
            hop_out,
            (*tabs, *sent, *got),
            one_hop,
            moved,
            after=after,
        )
        return swapped(to_y, "expert", 2), swapped(to_x, "expert", 1), to_y

    f_left, f_right = local_call(
        normed_kernel_halves, halves_out, (layer_in, gain_here), one_hop, moved, after=(b_left,)
    )
    f_from_x, f_from_y = crossed(f_left, f_right)
    g_left, g_right = local_call(split_kernel, halves_out, (grad_in,), 1024, moved, after=(f_left,))
    g_from_x, g_from_y = crossed(g_left, g_right)
    x_tab, y_tab = local_call(
        functools.partial(tables_kernel, top_count),
        [table_shape] * 2,
        (b_from_x, b_from_y),
        1024,
        1024,
        after=(g_left,),
    )
    tabs = (own, x_tab, y_tab)
    b_to_y, b_to_x = local_call(
        functools.partial(far_kernel, "b", top_count),
        [shaped(capacity, half)] * 2,
        (x_tab, y_tab, b_from_x, b_from_y),
        one_hop,
        moved,
        after=(g_left,),
    )
    b_got_y, b_got_x = swapped(b_to_y, "expert", 2), swapped(b_to_x, "expert", 1)
    f_got_y, f_got_x, f_to_y = onward("f", (f_left, f_right), (f_from_x, f_from_y), (b_to_y,))
    g_got_y, g_got_x, g_to_y = onward("bg", (g_left, g_right), (g_from_x, g_from_y), (f_to_y,))
    gate_pre, up_pre = local_call(
        functools.partial(hop_again_kernel, top_count),
        [shaped(slot_total, hidden_units, jnp.float32)] * 2,
        (*tabs, b_left, b_right, b_from_x, b_from_y, b_got_y, b_got_x, weight_in),
        2 * expert_flops,
        expert_moved,
        scratch=(rows_scratch,),
        after=(g_to_y,),
    )
    f_keep_l, f_near_l, f_on_l, hidden = local_call(
        functools.partial(hop_fwd_kernel, top_count),
        half_out + [hidden_shape],
        (*tabs, f_left, f_right, f_from_x, f_from_y, f_got_y, f_got_x, weight_in, weight_out),
        5 * expert_flops // 2,
        expert_moved,
        scratch=(rows_scratch,),
        after=(gate_pre,),
    )
    f_ret_y = swapped(f_on_l, "expert", 2)
    f_keep_r, f_near_r, f_on_r = local_call(
        fwd_right_kernel, half_out, (hidden, weight_out), 1024, 1024
    )
    f_ret_x = swapped(f_on_r, "expert", 1)
    b_keep_l, b_near_l, b_on_l, both = local_call(
        functools.partial(hop_bwd_kernel, top_count),
        half_out + [both_shape],
        (
            *tabs,
            g_left,
            g_right,
            g_from_x,
            g_from_y,
            g_got_y,
            g_got_x,
            gate_pre,
            up_pre,
            weight_in,
            weight_out,
        ),
        2 * expert_flops,
        expert_moved,
        scratch=(rows_scratch,),
        after=(f_keep_r,),
    )
    b_ret_y = swapped(b_on_l, "expert", 2)
    b_keep_r, b_near_r, b_on_r = local_call(
        bwd_right_kernel, half_out, (both, weight_in), 1024, 1024
    )
    b_ret_x = swapped(b_on_r, "expert", 1)

    def summed_call(kind, here, table, near, far, after):
        part = local_call(
            functools.partial(sums_kernel, kind, top_count, here),
            shaped(tok_rows, half),
            (table, near, far),
            one_hop,
            moved,
            after=after,
        )
        return swapped(part, "expert", here), part

    f_sum_x, last = summed_call("fg", 1, x_tab, f_near_l, f_ret_y, (b_keep_r,))
    f_sum_y, last = summed_call("fg", 2, y_tab, f_near_r, f_ret_x, (last,))
    b_sum_x, last = summed_call("b", 1, x_tab, b_near_l, b_ret_y, (last,))
    b_sum_y, last = summed_call("b", 2, y_tab, b_near_r, b_ret_x, (last,))
    f_keep = (f_keep_l, f_keep_r)
    b_keep = (b_keep_l, b_keep_r)
    fwd_block, order = local_call(
        functools.partial(hop_fwd_end_kernel, top_count),
        [shaped(tok_rows, features), shaped(8, 128, jnp.float32)],
        (layer_in, own, *f_keep, f_ret_y, f_ret_x, f_sum_x, f_sum_y),
        one_hop,
        moved,
        after=(last,),
    )
    bwd_block = local_call(
        functools.partial(hop_bwd_end_kernel, top_count),
        shaped(tok_rows, features),
        (grad_in, saved, gain_here, own, *b_keep, b_ret_y, b_ret_x, b_sum_x, b_sum_y),
        one_hop,
        moved,
        after=(order,),
    )
    return (fwd_block[None], bwd_block[None])


def per_device(*arrays):
    if lax.axis_size("expert") == 4:
        return per_device_hops(*arrays)
    return per_device_direct(*arrays)


def solution(mesh):
    in_specs = (
        P("section", "expert", None),
        P("section", "expert", None),
        P("section", "expert", None),
        P("section", "expert", None),
        P("section", "expert", None),
        P("section", "expert", None),
        P("section", "expert", None),
        P("section", None),
        P("section", "expert", None, None),
        P("section", "expert", None, None),
    )
    out_specs = (P("section", "expert", None), P("section", "expert", None))
    return jax.shard_map(
        per_device, mesh=mesh, in_specs=in_specs, out_specs=out_specs, check_vma=False
    )
```

```python
import functools

import jax
import jax.numpy as jnp
from jax import lax
from jax.experimental import pallas as pl
from jax.experimental.pallas import tpu as pltpu
from jax.sharding import PartitionSpec as P

EPS = 1e-06
VMEM_LIMIT = 32 * 1024 * 1024


def passed_along(value, axis, steps):
    count = lax.axis_size(axis)
    pairs = [(source, (source + steps) % count) for source in range(count)]
    return lax.ppermute(value, axis, pairs)


def swapped(value, axis, offset):
    count = lax.axis_size(axis)
    pairs = [(source, source ^ offset) for source in range(count)]
    return lax.ppermute(value, axis, pairs)


def exchanged(blocks, axis):
    return [blocks[0]] + [swapped(blocks[d], axis, d) for d in range(1, len(blocks))]


def slot_table(routes, expert_count):
    top_count, tok_rows = routes.shape
    experts = max(8, expert_count)
    wanted = lax.broadcasted_iota(jnp.int32, (experts, tok_rows), 0)
    member = routes[0:1, :] == wanted
    for k in range(1, top_count):
        member = jnp.logical_or(member, routes[k : k + 1, :] == wanted)
    before = lax.broadcasted_iota(jnp.int32, (tok_rows, tok_rows), 0) < lax.broadcasted_iota(
        jnp.int32, (tok_rows, tok_rows), 1
    )
    slots = jnp.dot(
        member.astype(jnp.bfloat16),
        before.astype(jnp.bfloat16),
        preferred_element_type=jnp.float32,
    )
    return jnp.where(member, slots, -1.0)


def placement(slots, expert, capacity):
    tok_rows = slots.shape[1]
    row = lax.broadcasted_iota(jnp.int32, (capacity, tok_rows), 0).astype(jnp.float32)
    return slots[expert : expert + 1, :] == row


def gate_row(routes, gates, expert):
    total = jnp.zeros((1, routes.shape[1]), jnp.float32)
    for k in range(routes.shape[0]):
        total = total + jnp.where(routes[k : k + 1, :] == expert, gates[k : k + 1, :], 0.0)
    return total


def halves(weights):
    high = weights.astype(jnp.bfloat16)
    low = (weights - high.astype(jnp.float32)).astype(jnp.bfloat16)
    return high, low


def normed_kernel(values_ref, routes_ref, gain_ref, *out_refs):
    expert_count = len(out_refs)
    capacity = out_refs[0].shape[0]
    wide = values_ref[...].astype(jnp.float32)
    inv_rms = lax.rsqrt(jnp.mean(wide * wide, axis=-1, keepdims=True) + EPS)
    normed = (wide * inv_rms * gain_ref[...]).astype(jnp.bfloat16)
    slots = slot_table(routes_ref[...], expert_count)
    for e in range(expert_count):
        place = placement(slots, e, capacity).astype(jnp.bfloat16)
        out_refs[e][...] = jnp.dot(place, normed, preferred_element_type=jnp.float32).astype(
            jnp.bfloat16
        )


def grads_kernel(grads_ref, routes_ref, gates_ref, *out_refs):
    expert_count = len(out_refs)
    capacity = out_refs[0].shape[0]
    grads = grads_ref[...]
    routes = routes_ref[...]
    slots = slot_table(routes, expert_count)
    for e in range(expert_count):
        place = placement(slots, e, capacity)
        high, low = halves(jnp.where(place, gate_row(routes, gates_ref[...], e), 0.0))
        out_refs[e][...] = (
            jnp.dot(high, grads, preferred_element_type=jnp.float32)
            + jnp.dot(low, grads, preferred_element_type=jnp.float32)
        ).astype(jnp.bfloat16)


def rows_dot(weights, rows):
    return lax.dot_general(
        weights, rows, (((0,), (0,)), ((), ())), preferred_element_type=jnp.float32
    )


def fwd_end_kernel(layer_ref, routes_ref, gates_ref, *refs):
    row_refs, out_ref = refs[:-1], refs[-1]
    expert_count = len(row_refs)
    capacity = row_refs[0].shape[0]
    routes = routes_ref[...]
    slots = slot_table(routes, expert_count)
    total = layer_ref[...].astype(jnp.float32)
    for e in range(expert_count):
        place = placement(slots, e, capacity)
        high, low = halves(jnp.where(place, gate_row(routes, gates_ref[...], e), 0.0))
        rows = row_refs[e][...]
        total = total + (rows_dot(high, rows) + rows_dot(low, rows))
    out_ref[...] = total.astype(jnp.bfloat16)


def bwd_end_kernel(grads_ref, saved_ref, gain_ref, routes_ref, *refs):
    row_refs, out_ref = refs[:-1], refs[-1]
    expert_count = len(row_refs)
    capacity = row_refs[0].shape[0]
    features = saved_ref.shape[1]
    slots = slot_table(routes_ref[...], expert_count)
    d_normed = None
    for e in range(expert_count):
        place = placement(slots, e, capacity).astype(jnp.bfloat16)
        part = rows_dot(place, row_refs[e][...])
        d_normed = part if d_normed is None else d_normed + part
    wide = saved_ref[...].astype(jnp.float32)
    inv_rms = lax.rsqrt(jnp.mean(wide * wide, axis=-1, keepdims=True) + EPS)
    scaled = d_normed * gain_ref[...]
    cubed = inv_rms * inv_rms * inv_rms
    inner = jnp.sum(scaled * wide, axis=-1, keepdims=True)
    out_ref[...] = (
        grads_ref[...].astype(jnp.float32) + inv_rms * scaled - cubed / features * wide * inner
    ).astype(jnp.bfloat16)


def joined(refs):
    rows = [ref[...] for ref in refs]
    if rows[0].shape[0] % 16 == 0:
        return jnp.concatenate(rows, axis=0)
    return jnp.concatenate([r.astype(jnp.float32) for r in rows], axis=0).astype(jnp.bfloat16)


def tiles(size, step):
    return [(start, min(step, size - start)) for start in range(0, size, step)]


def expert_fwd_kernel(*refs):
    expert_count = (len(refs) - 4) // 2
    row_refs = refs[:expert_count]
    weight_in, weight_out = refs[expert_count : expert_count + 2]
    out_refs = refs[expert_count + 2 : 2 * expert_count + 2]
    rows_ref, hidden_ref = refs[-2:]
    capacity = row_refs[0].shape[0]
    hidden_units, features = weight_out.shape
    rows_ref[...] = joined(row_refs)
    for start, size in tiles(hidden_units, 256):
        gate = jnp.dot(
            rows_ref[...], weight_in[:, start : start + size], preferred_element_type=jnp.float32
        )
        up = jnp.dot(
            rows_ref[...],
            weight_in[:, hidden_units + start : hidden_units + start + size],
            preferred_element_type=jnp.float32,
        )
        hidden_ref[:, start : start + size] = (gate / (1.0 + jnp.exp(-gate)) * up).astype(
            jnp.bfloat16
        )
    for start, size in tiles(features, 512):
        out = jnp.dot(
            hidden_ref[...], weight_out[:, start : start + size], preferred_element_type=jnp.float32
        )
        for d in range(expert_count):
            out_refs[d][:, start : start + size] = out[d * capacity : (d + 1) * capacity].astype(
                jnp.bfloat16
            )


def expert_again_kernel(*refs):
    expert_count = len(refs) - 4
    row_refs = refs[:expert_count]
    weight_in, gate_ref, up_ref, rows_ref = refs[expert_count:]
    hidden_units = gate_ref.shape[1]
    rows_ref[...] = joined(row_refs)
    for start, size in tiles(hidden_units, 256):
        gate_ref[:, start : start + size] = jnp.dot(
            rows_ref[...], weight_in[:, start : start + size], preferred_element_type=jnp.float32
        )
        up_ref[:, start : start + size] = jnp.dot(
            rows_ref[...],
            weight_in[:, hidden_units + start : hidden_units + start + size],
            preferred_element_type=jnp.float32,
        )


def expert_bwd_kernel(*refs):
    expert_count = (len(refs) - 6) // 2
    grad_refs = refs[:expert_count]
    gate_ref, up_ref, weight_in, weight_out = refs[expert_count : expert_count + 4]
    out_refs = refs[expert_count + 4 : 2 * expert_count + 4]
    grads_ref, both_ref = refs[-2:]
    capacity = grad_refs[0].shape[0]
    hidden_units, features = weight_out.shape
    grads_ref[...] = joined(grad_refs)
    for start, size in tiles(hidden_units, 256):
        gate = gate_ref[:, start : start + size]
        up = up_ref[:, start : start + size]
        d_hidden = lax.dot_general(
            grads_ref[...],
            weight_out[start : start + size, :],
            (((1,), (1,)), ((), ())),
            preferred_element_type=jnp.float32,
        )
        sig = 1.0 / (1.0 + jnp.exp(-gate))
        both_ref[:, start : start + size] = (
            d_hidden * up * sig * (1.0 + gate * (1.0 - sig))
        ).astype(jnp.bfloat16)
        both_ref[:, hidden_units + start : hidden_units + start + size] = (
            d_hidden * gate * sig
        ).astype(jnp.bfloat16)
    for start, size in tiles(features, 512):
        out = lax.dot_general(
            both_ref[...],
            weight_in[start : start + size, :],
            (((1,), (1,)), ((), ())),
            preferred_element_type=jnp.float32,
        )
        for d in range(expert_count):
            out_refs[d][:, start : start + size] = out[d * capacity : (d + 1) * capacity].astype(
                jnp.bfloat16
            )


def local_call(kernel, out_shapes, inputs, flops, moved, scratch=(), after=()):
    in_specs = [pl.BlockSpec(memory_space=pltpu.VMEM)] * len(inputs)
    held = len(inputs)

    def body(*refs):
        kernel(*refs[:held], *refs[held + len(after) :])

    return pl.pallas_call(
        body if after else kernel,
        out_shape=out_shapes,
        in_specs=in_specs + [pl.BlockSpec(memory_space=pl.ANY)] * len(after),
        scratch_shapes=list(scratch),
        compiler_params=pltpu.CompilerParams(vmem_limit_bytes=VMEM_LIMIT),
        cost_estimate=pl.CostEstimate(flops=flops, bytes_accessed=moved, transcendentals=0),
    )(*inputs, *after)


def per_device_direct(
    fwd_prev,
    bwd_prev,
    bwd_saved,
    fwd_routes,
    fwd_gates,
    bwd_routes,
    bwd_gates,
    norm_gain,
    w_in,
    w_out,
):
    expert_count = lax.axis_size("expert")
    tok_rows = fwd_prev.shape[1]
    features = fwd_prev.shape[2]
    top_count = fwd_routes.shape[2]
    hidden_units = w_in.shape[3] // 2
    capacity = 3 * tok_rows * top_count // (2 * expert_count)
    gain_row = norm_gain
    weight_in = w_in[0, 0]
    weight_out = w_out[0, 0]
    me = lax.axis_index("expert")
    f_routes = (fwd_routes[0] ^ me).T
    b_routes = (bwd_routes[0] ^ me).T
    f_gates = fwd_gates[0].T
    b_gates = bwd_gates[0].T
    saved = bwd_saved[0]
    layer_in = passed_along(fwd_prev[0], "section", 1)
    grad_in = passed_along(bwd_prev[0], "section", -1)

    block = jax.ShapeDtypeStruct((capacity, features), jnp.bfloat16)
    whole = jax.ShapeDtypeStruct((tok_rows, features), jnp.bfloat16)
    one_dot = 2 * expert_count * capacity * tok_rows * features
    moved = 2 * features * (tok_rows + expert_count * capacity)
    slot_total = expert_count * capacity
    blocks = [block] * expert_count
    expert_flops = 2 * slot_total * features * hidden_units
    expert_moved = 2 * features * (3 * hidden_units + 3 * slot_total)
    rows_scratch = pltpu.VMEM((slot_total, features), jnp.bfloat16)

    b_sent = local_call(normed_kernel, blocks, (saved, b_routes, gain_row), one_dot, moved)
    b_rows = exchanged(b_sent, "expert")
    f_sent = local_call(
        normed_kernel, blocks, (layer_in, f_routes, gain_row), one_dot, moved, after=(b_sent[0],)
    )
    f_rows = exchanged(f_sent, "expert")
    g_sent = local_call(
        grads_kernel, blocks, (grad_in, b_routes, b_gates), 2 * one_dot, moved, after=(f_sent[0],)
    )
    g_rows = exchanged(g_sent, "expert")
    projected = jax.ShapeDtypeStruct((slot_total, hidden_units), jnp.float32)
    gate_pre, up_pre = local_call(
        expert_again_kernel,
        [projected, projected],
        (*b_rows, weight_in),
        2 * expert_flops,
        expert_moved,
        scratch=(rows_scratch,),
        after=(g_sent[0],),
    )
    f_done = local_call(
        expert_fwd_kernel,
        blocks,
        (*f_rows, weight_in, weight_out),
        3 * expert_flops,
        expert_moved,
        scratch=(rows_scratch, pltpu.VMEM((slot_total, hidden_units), jnp.bfloat16)),
        after=(gate_pre,),
    )
    f_back = exchanged(f_done, "expert")
    b_done = local_call(
        expert_bwd_kernel,
        blocks,
        (*g_rows, gate_pre, up_pre, weight_in, weight_out),
        3 * expert_flops,
        expert_moved,
        scratch=(rows_scratch, pltpu.VMEM((slot_total, 2 * hidden_units), jnp.bfloat16)),
        after=(f_back[1],),
    )
    b_back = exchanged(b_done, "expert")
    fwd_block = local_call(
        fwd_end_kernel,
        whole,
        (layer_in, f_routes, f_gates, *f_back),
        2 * one_dot,
        moved,
        after=(b_done[0],),
    )
    bwd_block = local_call(
        bwd_end_kernel,
        whole,
        (grad_in, saved, gain_row, b_routes, *b_back),
        one_dot,
        moved,
    )
    return (fwd_block[None], bwd_block[None])


def pick(table, expert, capacity, kind, top_count):
    first = 0 if kind[0] == "f" else 2 * top_count
    routes = table[first : first + top_count]
    gates = table[first + top_count : first + 2 * top_count]
    tok_rows = table.shape[1]
    member = routes == float(expert)
    held = jnp.sum(member.astype(jnp.float32), axis=0, keepdims=True)
    before = lax.broadcasted_iota(jnp.int32, (tok_rows, tok_rows), 0) < lax.broadcasted_iota(
        jnp.int32, (tok_rows, tok_rows), 1
    )
    slots = jnp.dot(
        jnp.broadcast_to(held, (8, tok_rows)).astype(jnp.bfloat16),
        before.astype(jnp.bfloat16),
        preferred_element_type=jnp.float32,
    )[0:1]
    place = placement(jnp.where(held > 0.0, slots, -1.0), 0, capacity)
    if len(kind) == 1:
        return (place.astype(jnp.bfloat16),)
    gate = jnp.sum(jnp.where(member, gates, 0.0), axis=0, keepdims=True)
    return halves(jnp.where(place, gate, 0.0))


def to_slots(weights, values):
    total = None
    for part in weights:
        term = jnp.dot(part, values, preferred_element_type=jnp.float32)
        total = term if total is None else total + term
    return total.astype(jnp.bfloat16)


def to_tokens(weights, rows):
    total = None
    for part in weights:
        term = rows_dot(part, rows)
        total = term if total is None else total + term
    return total


def three_parts(values):
    high = values.astype(jnp.bfloat16)
    rest = values - high.astype(jnp.float32)
    mid = rest.astype(jnp.bfloat16)
    low = (rest - mid.astype(jnp.float32)).astype(jnp.bfloat16)
    return high, mid, low


def normed_halves(wide, gain):
    inv_rms = lax.rsqrt(jnp.mean(wide * wide, axis=-1, keepdims=True) + EPS)
    return (wide * inv_rms * gain).astype(jnp.bfloat16)


def first_kernel(top_count, me_ref, *refs):
    sources, refs = refs[:6], refs[6:]
    (left_ref, right_ref, table_ref, gain_out), refs = refs[:4], refs[4:]
    held, sems = refs[:6], refs[6]
    copies = [pltpu.make_async_copy(sources[i], held[i], sems.at[i]) for i in range(6)]
    for copy in copies:
        copy.start()
    for copy in copies[1:]:
        copy.wait()
    saved, gain, f_routes, f_gates, b_routes, b_gates = held
    me = me_ref[0]
    fr = (f_routes[...] ^ me).astype(jnp.float32)
    br = (b_routes[...] ^ me).astype(jnp.float32)
    fg = f_gates[...]
    bg = b_gates[...]
    table = jnp.concatenate([fr, fg, br, bg], axis=0)
    table_ref[...] = table
    packed = [fr.astype(jnp.bfloat16), br.astype(jnp.bfloat16), *three_parts(fg), *three_parts(bg)]
    packed = jnp.concatenate([part.astype(jnp.float32) for part in packed], axis=0)
    gain_out[...] = gain[...]
    tok_rows, features = saved.shape
    half = features // 2
    copies[0].wait()
    normed = normed_halves(saved[...].astype(jnp.float32), gain[...])
    capacity = left_ref.shape[0] - tok_rows - packed.shape[0]
    near = tok_rows + packed.shape[0]
    for half_ref, start, expert in ((left_ref, 0, 1), (right_ref, half, 2)):
        half_ref[:tok_rows, :] = normed[:, start : start + half]
        half_ref[tok_rows:near, :] = jnp.zeros((near - tok_rows, half), jnp.bfloat16)
        half_ref[tok_rows:near, :tok_rows] = packed.astype(jnp.bfloat16)
        other = half - start
        half_ref[near:, :] = to_slots(
            pick(table, expert, capacity, "b", top_count), normed[:, other : other + half]
        )


def unpacked(block, tok_rows, top_count):
    rows = block[tok_rows : tok_rows + 8 * top_count, :tok_rows].astype(jnp.float32)
    k = top_count
    fr, br = rows[0:k], rows[k : 2 * k]
    fg = (rows[2 * k : 3 * k] + rows[3 * k : 4 * k]) + rows[4 * k : 5 * k]
    bg = (rows[5 * k : 6 * k] + rows[6 * k : 7 * k]) + rows[7 * k : 8 * k]
    return jnp.concatenate([fr, fg, br, bg], axis=0)


def normed_kernel_halves(values_ref, gain_ref, left_ref, right_ref):
    half = left_ref.shape[1]
    normed = normed_halves(values_ref[...].astype(jnp.float32), gain_ref[...])
    left_ref[...] = normed[:, :half]
    right_ref[...] = normed[:, half:]


def split_kernel(values_ref, left_ref, right_ref):
    half = left_ref.shape[1]
    left_ref[...] = values_ref[:, :half]
    right_ref[...] = values_ref[:, half:]


def tables_kernel(top_count, from_x, from_y, x_table, y_table):
    tok_rows = x_table.shape[1]
    x_table[...] = unpacked(from_x[...], tok_rows, top_count)
    y_table[...] = unpacked(from_y[...], tok_rows, top_count)


def hop_kernel(kind, top_count, own, x_tab, y_tab, left, right, from_x, from_y, to_y, to_x):
    capacity = to_y.shape[0] // 2
    tok_rows = own.shape[1]
    to_y[:capacity, :] = to_slots(pick(own[...], 2, capacity, kind, top_count), left[:tok_rows, :])
    to_y[capacity:, :] = to_slots(
        pick(x_tab[...], 3, capacity, kind, top_count), from_x[:tok_rows, :]
    )
    to_x[:capacity, :] = to_slots(pick(own[...], 1, capacity, kind, top_count), right[:tok_rows, :])
    to_x[capacity:, :] = to_slots(
        pick(y_tab[...], 3, capacity, kind, top_count), from_y[:tok_rows, :]
    )


def far_kernel(kind, top_count, x_tab, y_tab, from_x, from_y, to_y, to_x):
    capacity = to_y.shape[0]
    tok_rows = x_tab.shape[1]
    to_y[...] = to_slots(pick(x_tab[...], 3, capacity, kind, top_count), from_x[:tok_rows, :])
    to_x[...] = to_slots(pick(y_tab[...], 3, capacity, kind, top_count), from_y[:tok_rows, :])


def assemble(kind, top_count, own, x_tab, y_tab, left, right, from_x, from_y, got_y, got_x, rows):
    capacity = rows.shape[0] // 4
    half = got_y.shape[1]
    tok_rows = own.shape[1]
    mine = pick(own[...], 0, capacity, kind, top_count)
    rows[:capacity, :half] = to_slots(mine, left[:tok_rows, :])
    rows[:capacity, half:] = to_slots(mine, right[:tok_rows, :])
    rows[capacity : 2 * capacity, :half] = to_slots(
        pick(x_tab[...], 1, capacity, kind, top_count), from_x[:tok_rows, :]
    )
    rows[2 * capacity : 3 * capacity, half:] = to_slots(
        pick(y_tab[...], 2, capacity, kind, top_count), from_y[:tok_rows, :]
    )
    if got_y.shape[0] == capacity:
        near_x, near_y = from_x[-capacity:, :], from_y[-capacity:, :]
    else:
        near_x, near_y = got_x[:capacity, :], got_y[:capacity, :]
    rows[capacity : 2 * capacity, half:] = near_x
    rows[2 * capacity : 3 * capacity, :half] = near_y
    rows[3 * capacity :, :half] = got_y[-capacity:, :]
    rows[3 * capacity :, half:] = got_x[-capacity:, :]


def hand_out(out, at, capacity, to_left, keep, near, onward):
    size = out.shape[1]
    rows = out.astype(jnp.bfloat16)
    mine, from_x, from_y, far = [rows[d * capacity : (d + 1) * capacity] for d in range(4)]
    keep[:, at : at + size] = mine
    near[:, at : at + size] = from_x if to_left else from_y
    onward[:capacity, at : at + size] = from_y if to_left else from_x
    onward[capacity:, at : at + size] = far


def fwd_half(hidden_ref, weight_out, to_left, keep, near, onward):
    capacity, half = keep.shape
    first = 0 if to_left else half
    for at, size in tiles(half, 512):
        out = jnp.dot(
            hidden_ref[...],
            weight_out[:, first + at : first + at + size],
            preferred_element_type=jnp.float32,
        )
        hand_out(out, at, capacity, to_left, keep, near, onward)


def bwd_half(both_ref, weight_in, to_left, keep, near, onward):
    capacity, half = keep.shape
    first = 0 if to_left else half
    for at, size in tiles(half, 512):
        out = lax.dot_general(
            both_ref[...],
            weight_in[first + at : first + at + size, :],
            (((1,), (1,)), ((), ())),
            preferred_element_type=jnp.float32,
        )
        hand_out(out, at, capacity, to_left, keep, near, onward)


def fwd_right_kernel(hidden_ref, weight_out, keep, near, onward):
    fwd_half(hidden_ref, weight_out, False, keep, near, onward)


def bwd_right_kernel(both_ref, weight_in, keep, near, onward):
    bwd_half(both_ref, weight_in, False, keep, near, onward)


def hop_again_kernel(top_count, *refs):
    dispatch, (weight_in, gate_ref, up_ref, rows_ref) = refs[:9], refs[9:]
    assemble("b", top_count, *dispatch, rows_ref)
    hidden_units = gate_ref.shape[1]
    for start, size in tiles(hidden_units, 256):
        gate_ref[:, start : start + size] = jnp.dot(
            rows_ref[...], weight_in[:, start : start + size], preferred_element_type=jnp.float32
        )
        up_ref[:, start : start + size] = jnp.dot(
            rows_ref[...],
            weight_in[:, hidden_units + start : hidden_units + start + size],
            preferred_element_type=jnp.float32,
        )


def hop_fwd_kernel(top_count, *refs):
    dispatch, refs = refs[:9], refs[9:]
    weight_in, weight_out = refs[:2]
    outs, hidden_ref, rows_ref = refs[2:5], refs[5], refs[6]
    hidden_units = weight_out.shape[0]
    assemble("f", top_count, *dispatch, rows_ref)
    for start, size in tiles(hidden_units, 256):
        gate = jnp.dot(
            rows_ref[...], weight_in[:, start : start + size], preferred_element_type=jnp.float32
        )
        up = jnp.dot(
            rows_ref[...],
            weight_in[:, hidden_units + start : hidden_units + start + size],
            preferred_element_type=jnp.float32,
        )
        hidden_ref[:, start : start + size] = (gate / (1.0 + jnp.exp(-gate)) * up).astype(
            jnp.bfloat16
        )
    fwd_half(hidden_ref, weight_out, True, *outs)


def hop_bwd_kernel(top_count, *refs):
    dispatch, refs = refs[:9], refs[9:]
    gate_ref, up_ref, weight_in, weight_out = refs[:4]
    outs, both_ref, grads_ref = refs[4:7], refs[7], refs[8]
    hidden_units = weight_out.shape[0]
    assemble("bg", top_count, *dispatch, grads_ref)
    for start, size in tiles(hidden_units, 256):
        gate = gate_ref[:, start : start + size]
        up = up_ref[:, start : start + size]
        d_hidden = lax.dot_general(
            grads_ref[...],
            weight_out[start : start + size, :],
            (((1,), (1,)), ((), ())),
            preferred_element_type=jnp.float32,
        )
        sig = 1.0 / (1.0 + jnp.exp(-gate))
        both_ref[:, start : start + size] = (
            d_hidden * up * sig * (1.0 + gate * (1.0 - sig))
        ).astype(jnp.bfloat16)
        both_ref[:, hidden_units + start : hidden_units + start + size] = (
            d_hidden * gate * sig
        ).astype(jnp.bfloat16)
    bwd_half(both_ref, weight_in, True, *outs)


def sums_kernel(kind, top_count, here, table_ref, near, far, out):
    capacity = near.shape[0]
    table = table_ref[...]
    out[...] = (
        to_tokens(pick(table, here, capacity, kind, top_count), near[...])
        + to_tokens(pick(table, 3, capacity, kind, top_count), far[capacity:, :])
    ).astype(jnp.bfloat16)


def summed(kind, top_count, own, keep_left, keep_right, got_y, got_x, sum_x, sum_y):
    capacity = keep_left.shape[0]
    mine = pick(own[...], 0, capacity, kind, top_count)
    near_y = pick(own[...], 2, capacity, kind, top_count)
    near_x = pick(own[...], 1, capacity, kind, top_count)
    left = to_tokens(mine, keep_left[...]) + to_tokens(near_y, got_y[:capacity, :])
    right = to_tokens(mine, keep_right[...]) + to_tokens(near_x, got_x[:capacity, :])
    return left + sum_x[...].astype(jnp.float32), right + sum_y[...].astype(jnp.float32)


def hop_fwd_end_kernel(top_count, layer_ref, *refs):
    out_ref, order_ref = refs[-2:]
    order_ref[...] = jnp.zeros_like(order_ref)
    half = layer_ref.shape[1] // 2
    left, right = summed("fg", top_count, *refs[:-2])
    out_ref[:, :half] = (layer_ref[:, :half].astype(jnp.float32) + left).astype(jnp.bfloat16)
    out_ref[:, half:] = (layer_ref[:, half:].astype(jnp.float32) + right).astype(jnp.bfloat16)


def hop_bwd_near_kernel(top_count, own, keep_left, keep_right, got_y, got_x, left_ref, right_ref):
    capacity = keep_left.shape[0]
    mine = pick(own[...], 0, capacity, "b", top_count)
    near_y = pick(own[...], 2, capacity, "b", top_count)
    near_x = pick(own[...], 1, capacity, "b", top_count)
    left_ref[...] = to_tokens(mine, keep_left[...]) + to_tokens(near_y, got_y[:capacity, :])
    right_ref[...] = to_tokens(mine, keep_right[...]) + to_tokens(near_x, got_x[:capacity, :])


def hop_bwd_end_kernel(grads_ref, saved_ref, gain_ref, left_ref, right_ref, sum_x, sum_y, out_ref):
    features = saved_ref.shape[1]
    half = features // 2
    parts = []
    for start, near, far in ((0, left_ref, sum_x), (half, right_ref, sum_y)):
        wide = saved_ref[:, start : start + half].astype(jnp.float32)
        scaled = (near[...] + far[...].astype(jnp.float32)) * gain_ref[:, start : start + half]
        parts.append((start, wide, scaled))
    square = sum(jnp.sum(wide * wide, axis=-1, keepdims=True) for _, wide, _ in parts)
    inner = sum(jnp.sum(scaled * wide, axis=-1, keepdims=True) for _, wide, scaled in parts)
    inv_rms = lax.rsqrt(square / features + EPS)
    factor = inv_rms * inv_rms * inv_rms / features * inner
    for start, wide, scaled in parts:
        out_ref[:, start : start + half] = (
            grads_ref[:, start : start + half].astype(jnp.float32)
            + inv_rms * scaled
            - factor * wide
        ).astype(jnp.bfloat16)


def per_device_hops(
    fwd_prev,
    bwd_prev,
    bwd_saved,
    fwd_routes,
    fwd_gates,
    bwd_routes,
    bwd_gates,
    norm_gain,
    w_in,
    w_out,
):
    tok_rows, features = fwd_prev.shape[1:]
    top_count = fwd_routes.shape[2]
    hidden_units = w_in.shape[3] // 2
    capacity = 3 * tok_rows * top_count // 8
    half = features // 2
    gain_row = norm_gain
    weight_in = w_in[0, 0]
    weight_out = w_out[0, 0]
    me = lax.axis_index("expert").astype(jnp.int32).reshape(1)
    saved = bwd_saved[0]
    layer_in = passed_along(fwd_prev[0], "section", 1)
    grad_in = passed_along(bwd_prev[0], "section", -1)

    def shaped(rows, columns, dtype=jnp.bfloat16):
        return jax.ShapeDtypeStruct((rows, columns), dtype)

    def crossed(left, right):
        return swapped(left, "expert", 1), swapped(right, "expert", 2)

    slot_total = 4 * capacity
    table_rows = 4 * top_count
    one_hop = moved = 1024
    expert_flops = 2 * slot_total * features * hidden_units
    expert_moved = 2 * features * (3 * hidden_units + 3 * slot_total)
    rows_scratch = pltpu.VMEM((slot_total, features), jnp.bfloat16)
    halves_out = [shaped(tok_rows, half)] * 2
    hop_out = [shaped(2 * capacity, half)] * 2
    half_out = [shaped(capacity, half), shaped(capacity, half), shaped(2 * capacity, half)]
    hidden_shape = shaped(slot_total, hidden_units)
    both_shape = shaped(slot_total, 2 * hidden_units)
    table_shape = shaped(table_rows, tok_rows, jnp.float32)
    first_rows = tok_rows + 8 * top_count + capacity

    b_left, b_right, own, gain_here = pl.pallas_call(
        functools.partial(first_kernel, top_count),
        out_shape=[
            shaped(first_rows, half),
            shaped(first_rows, half),
            table_shape,
            shaped(1, features, jnp.float32),
        ],
        in_specs=[pl.BlockSpec(memory_space=pltpu.SMEM)]
        + [pl.BlockSpec(memory_space=pltpu.HBM)] * 6,
        scratch_shapes=[
            pltpu.VMEM((tok_rows, features), jnp.bfloat16),
            pltpu.VMEM((1, features), jnp.float32),
            pltpu.VMEM((top_count, tok_rows), jnp.int32),
            pltpu.VMEM((top_count, tok_rows), jnp.float32),
            pltpu.VMEM((top_count, tok_rows), jnp.int32),
            pltpu.VMEM((top_count, tok_rows), jnp.float32),
            pltpu.SemaphoreType.DMA((6,)),
        ],
        compiler_params=pltpu.CompilerParams(vmem_limit_bytes=VMEM_LIMIT),
        cost_estimate=pl.CostEstimate(flops=one_hop, bytes_accessed=moved, transcendentals=0),
    )(
        me,
        *[
            pltpu.with_memory_space_constraint(value, pltpu.HBM)
            for value in (
                saved,
                gain_row,
                fwd_routes[0].T,
                fwd_gates[0].T,
                bwd_routes[0].T,
                bwd_gates[0].T,
            )
        ],
    )
    b_from_x, b_from_y = crossed(b_left, b_right)

    def onward(kind, sent, got, after):
        to_y, to_x = local_call(
            functools.partial(hop_kernel, kind, top_count),
            hop_out,
            (*tabs, *sent, *got),
            one_hop,
            moved,
            after=after,
        )
        return swapped(to_y, "expert", 2), swapped(to_x, "expert", 1), to_y

    f_left, f_right = local_call(
        normed_kernel_halves, halves_out, (layer_in, gain_here), one_hop, moved, after=(b_left,)
    )
    f_from_x, f_from_y = crossed(f_left, f_right)
    g_left, g_right = local_call(split_kernel, halves_out, (grad_in,), 1024, moved, after=(f_left,))
    g_from_x, g_from_y = crossed(g_left, g_right)
    x_tab, y_tab = local_call(
        functools.partial(tables_kernel, top_count),
        [table_shape] * 2,
        (b_from_x, b_from_y),
        1024,
        1024,
        after=(g_left,),
    )
    tabs = (own, x_tab, y_tab)
    b_to_y, b_to_x = local_call(
        functools.partial(far_kernel, "b", top_count),
        [shaped(capacity, half)] * 2,
        (x_tab, y_tab, b_from_x, b_from_y),
        one_hop,
        moved,
        after=(g_left,),
    )
    b_got_y, b_got_x = swapped(b_to_y, "expert", 2), swapped(b_to_x, "expert", 1)
    f_got_y, f_got_x, f_to_y = onward("f", (f_left, f_right), (f_from_x, f_from_y), (b_to_y,))
    g_got_y, g_got_x, g_to_y = onward("bg", (g_left, g_right), (g_from_x, g_from_y), (f_to_y,))
    gate_pre, up_pre = local_call(
        functools.partial(hop_again_kernel, top_count),
        [shaped(slot_total, hidden_units, jnp.float32)] * 2,
        (*tabs, b_left, b_right, b_from_x, b_from_y, b_got_y, b_got_x, weight_in),
        2 * expert_flops,
        expert_moved,
        scratch=(rows_scratch,),
        after=(g_to_y,),
    )
    f_keep_l, f_near_l, f_on_l, hidden = local_call(
        functools.partial(hop_fwd_kernel, top_count),
        half_out + [hidden_shape],
        (*tabs, f_left, f_right, f_from_x, f_from_y, f_got_y, f_got_x, weight_in, weight_out),
        5 * expert_flops // 2,
        expert_moved,
        scratch=(rows_scratch,),
        after=(gate_pre,),
    )
    f_ret_y = swapped(f_on_l, "expert", 2)
    f_keep_r, f_near_r, f_on_r = local_call(
        fwd_right_kernel, half_out, (hidden, weight_out), 1024, 1024
    )
    f_ret_x = swapped(f_on_r, "expert", 1)
    b_keep_l, b_near_l, b_on_l, both = local_call(
        functools.partial(hop_bwd_kernel, top_count),
        half_out + [both_shape],
        (
            *tabs,
            g_left,
            g_right,
            g_from_x,
            g_from_y,
            g_got_y,
            g_got_x,
            gate_pre,
            up_pre,
            weight_in,
            weight_out,
        ),
        2 * expert_flops,
        expert_moved,
        scratch=(rows_scratch,),
        after=(f_keep_r,),
    )
    b_ret_y = swapped(b_on_l, "expert", 2)
    b_keep_r, b_near_r, b_on_r = local_call(
        bwd_right_kernel, half_out, (both, weight_in), 1024, 1024
    )
    b_ret_x = swapped(b_on_r, "expert", 1)

    def summed_call(kind, here, table, near, far, after):
        part = local_call(
            functools.partial(sums_kernel, kind, top_count, here),
            shaped(tok_rows, half),
            (table, near, far),
            one_hop,
            moved,
            after=after,
        )
        return swapped(part, "expert", here), part

    f_sum_x, last = summed_call("fg", 1, x_tab, f_near_l, f_ret_y, (b_keep_r,))
    f_sum_y, last = summed_call("fg", 2, y_tab, f_near_r, f_ret_x, (last,))
    b_sum_x, last = summed_call("b", 1, x_tab, b_near_l, b_ret_y, (last,))
    b_sum_y, last = summed_call("b", 2, y_tab, b_near_r, b_ret_x, (last,))
    f_keep = (f_keep_l, f_keep_r)
    b_keep = (b_keep_l, b_keep_r)
    fwd_block, order = local_call(
        functools.partial(hop_fwd_end_kernel, top_count),
        [shaped(tok_rows, features), shaped(8, 128, jnp.float32)],
        (layer_in, own, *f_keep, f_ret_y, f_ret_x, f_sum_x, f_sum_y),
        one_hop,
        moved,
        after=(last,),
    )
    b_near = local_call(
        functools.partial(hop_bwd_near_kernel, top_count),
        [shaped(tok_rows, half, jnp.float32)] * 2,
        (own, *b_keep, b_ret_y, b_ret_x),
        one_hop,
        moved,
        after=(last,),
    )
    bwd_block = local_call(
        hop_bwd_end_kernel,
        shaped(tok_rows, features),
        (grad_in, saved, gain_here, *b_near, b_sum_x, b_sum_y),
        one_hop,
        moved,
        after=(order,),
    )
    return (fwd_block[None], bwd_block[None])


def per_device(*arrays):
    if lax.axis_size("expert") == 4:
        return per_device_hops(*arrays)
    return per_device_direct(*arrays)


def solution(mesh):
    in_specs = (
        P("section", "expert", None),
        P("section", "expert", None),
        P("section", "expert", None),
        P("section", "expert", None),
        P("section", "expert", None),
        P("section", "expert", None),
        P("section", "expert", None),
        P("section", None),
        P("section", "expert", None, None),
        P("section", "expert", None, None),
    )
    out_specs = (P("section", "expert", None), P("section", "expert", None))
    return jax.shard_map(
        per_device, mesh=mesh, in_specs=in_specs, out_specs=out_specs, check_vma=False
    )
```

```python
import functools

import jax
import jax.numpy as jnp
from jax import lax
from jax.experimental import pallas as pl
from jax.experimental.pallas import tpu as pltpu
from jax.sharding import PartitionSpec as P

EPS = 1e-06
VMEM_LIMIT = 32 * 1024 * 1024
TABLES_COST = 6_000_000_000


def passed_along(value, axis, steps):
    count = lax.axis_size(axis)
    pairs = [(source, (source + steps) % count) for source in range(count)]
    return lax.ppermute(value, axis, pairs)


def swapped(value, axis, offset):
    count = lax.axis_size(axis)
    pairs = [(source, source ^ offset) for source in range(count)]
    return lax.ppermute(value, axis, pairs)


def exchanged(blocks, axis):
    return [blocks[0]] + [swapped(blocks[d], axis, d) for d in range(1, len(blocks))]


def slot_table(routes, expert_count):
    top_count, tok_rows = routes.shape
    experts = max(8, expert_count)
    wanted = lax.broadcasted_iota(jnp.int32, (experts, tok_rows), 0)
    member = routes[0:1, :] == wanted
    for k in range(1, top_count):
        member = jnp.logical_or(member, routes[k : k + 1, :] == wanted)
    before = lax.broadcasted_iota(jnp.int32, (tok_rows, tok_rows), 0) < lax.broadcasted_iota(
        jnp.int32, (tok_rows, tok_rows), 1
    )
    slots = jnp.dot(
        member.astype(jnp.bfloat16),
        before.astype(jnp.bfloat16),
        preferred_element_type=jnp.float32,
    )
    return jnp.where(member, slots, -1.0)


def placement(slots, expert, capacity):
    tok_rows = slots.shape[1]
    row = lax.broadcasted_iota(jnp.int32, (capacity, tok_rows), 0).astype(jnp.float32)
    return slots[expert : expert + 1, :] == row


def gate_row(routes, gates, expert):
    total = jnp.zeros((1, routes.shape[1]), jnp.float32)
    for k in range(routes.shape[0]):
        total = total + jnp.where(routes[k : k + 1, :] == expert, gates[k : k + 1, :], 0.0)
    return total


def halves(weights):
    high = weights.astype(jnp.bfloat16)
    low = (weights - high.astype(jnp.float32)).astype(jnp.bfloat16)
    return high, low


def normed_kernel(values_ref, routes_ref, gain_ref, *out_refs):
    expert_count = len(out_refs)
    capacity = out_refs[0].shape[0]
    wide = values_ref[...].astype(jnp.float32)
    inv_rms = lax.rsqrt(jnp.mean(wide * wide, axis=-1, keepdims=True) + EPS)
    normed = (wide * inv_rms * gain_ref[...]).astype(jnp.bfloat16)
    slots = slot_table(routes_ref[...], expert_count)
    for e in range(expert_count):
        place = placement(slots, e, capacity).astype(jnp.bfloat16)
        out_refs[e][...] = jnp.dot(place, normed, preferred_element_type=jnp.float32).astype(
            jnp.bfloat16
        )


def grads_kernel(grads_ref, routes_ref, gates_ref, *out_refs):
    expert_count = len(out_refs)
    capacity = out_refs[0].shape[0]
    grads = grads_ref[...]
    routes = routes_ref[...]
    slots = slot_table(routes, expert_count)
    for e in range(expert_count):
        place = placement(slots, e, capacity)
        high, low = halves(jnp.where(place, gate_row(routes, gates_ref[...], e), 0.0))
        out_refs[e][...] = (
            jnp.dot(high, grads, preferred_element_type=jnp.float32)
            + jnp.dot(low, grads, preferred_element_type=jnp.float32)
        ).astype(jnp.bfloat16)


def rows_dot(weights, rows):
    return lax.dot_general(
        weights, rows, (((0,), (0,)), ((), ())), preferred_element_type=jnp.float32
    )


def fwd_end_kernel(layer_ref, routes_ref, gates_ref, *refs):
    row_refs, out_ref = refs[:-1], refs[-1]
    expert_count = len(row_refs)
    capacity = row_refs[0].shape[0]
    routes = routes_ref[...]
    slots = slot_table(routes, expert_count)
    total = layer_ref[...].astype(jnp.float32)
    for e in range(expert_count):
        place = placement(slots, e, capacity)
        high, low = halves(jnp.where(place, gate_row(routes, gates_ref[...], e), 0.0))
        rows = row_refs[e][...]
        total = total + (rows_dot(high, rows) + rows_dot(low, rows))
    out_ref[...] = total.astype(jnp.bfloat16)


def bwd_end_kernel(grads_ref, saved_ref, gain_ref, routes_ref, *refs):
    row_refs, out_ref = refs[:-1], refs[-1]
    expert_count = len(row_refs)
    capacity = row_refs[0].shape[0]
    features = saved_ref.shape[1]
    slots = slot_table(routes_ref[...], expert_count)
    d_normed = None
    for e in range(expert_count):
        place = placement(slots, e, capacity).astype(jnp.bfloat16)
        part = rows_dot(place, row_refs[e][...])
        d_normed = part if d_normed is None else d_normed + part
    wide = saved_ref[...].astype(jnp.float32)
    inv_rms = lax.rsqrt(jnp.mean(wide * wide, axis=-1, keepdims=True) + EPS)
    scaled = d_normed * gain_ref[...]
    cubed = inv_rms * inv_rms * inv_rms
    inner = jnp.sum(scaled * wide, axis=-1, keepdims=True)
    out_ref[...] = (
        grads_ref[...].astype(jnp.float32) + inv_rms * scaled - cubed / features * wide * inner
    ).astype(jnp.bfloat16)


def joined(refs):
    rows = [ref[...] for ref in refs]
    if rows[0].shape[0] % 16 == 0:
        return jnp.concatenate(rows, axis=0)
    return jnp.concatenate([r.astype(jnp.float32) for r in rows], axis=0).astype(jnp.bfloat16)


def tiles(size, step):
    return [(start, min(step, size - start)) for start in range(0, size, step)]


def expert_fwd_kernel(*refs):
    expert_count = (len(refs) - 4) // 2
    row_refs = refs[:expert_count]
    weight_in, weight_out = refs[expert_count : expert_count + 2]
    out_refs = refs[expert_count + 2 : 2 * expert_count + 2]
    rows_ref, hidden_ref = refs[-2:]
    capacity = row_refs[0].shape[0]
    hidden_units, features = weight_out.shape
    rows_ref[...] = joined(row_refs)
    for start, size in tiles(hidden_units, 256):
        gate = jnp.dot(
            rows_ref[...], weight_in[:, start : start + size], preferred_element_type=jnp.float32
        )
        up = jnp.dot(
            rows_ref[...],
            weight_in[:, hidden_units + start : hidden_units + start + size],
            preferred_element_type=jnp.float32,
        )
        hidden_ref[:, start : start + size] = (gate / (1.0 + jnp.exp(-gate)) * up).astype(
            jnp.bfloat16
        )
    for start, size in tiles(features, 512):
        out = jnp.dot(
            hidden_ref[...], weight_out[:, start : start + size], preferred_element_type=jnp.float32
        )
        for d in range(expert_count):
            out_refs[d][:, start : start + size] = out[d * capacity : (d + 1) * capacity].astype(
                jnp.bfloat16
            )


def expert_again_kernel(*refs):
    expert_count = len(refs) - 4
    row_refs = refs[:expert_count]
    weight_in, gate_ref, up_ref, rows_ref = refs[expert_count:]
    hidden_units = gate_ref.shape[1]
    rows_ref[...] = joined(row_refs)
    for start, size in tiles(hidden_units, 256):
        gate_ref[:, start : start + size] = jnp.dot(
            rows_ref[...], weight_in[:, start : start + size], preferred_element_type=jnp.float32
        )
        up_ref[:, start : start + size] = jnp.dot(
            rows_ref[...],
            weight_in[:, hidden_units + start : hidden_units + start + size],
            preferred_element_type=jnp.float32,
        )


def expert_bwd_kernel(*refs):
    expert_count = (len(refs) - 6) // 2
    grad_refs = refs[:expert_count]
    gate_ref, up_ref, weight_in, weight_out = refs[expert_count : expert_count + 4]
    out_refs = refs[expert_count + 4 : 2 * expert_count + 4]
    grads_ref, both_ref = refs[-2:]
    capacity = grad_refs[0].shape[0]
    hidden_units, features = weight_out.shape
    grads_ref[...] = joined(grad_refs)
    for start, size in tiles(hidden_units, 256):
        gate = gate_ref[:, start : start + size]
        up = up_ref[:, start : start + size]
        d_hidden = lax.dot_general(
            grads_ref[...],
            weight_out[start : start + size, :],
            (((1,), (1,)), ((), ())),
            preferred_element_type=jnp.float32,
        )
        sig = 1.0 / (1.0 + jnp.exp(-gate))
        both_ref[:, start : start + size] = (
            d_hidden * up * sig * (1.0 + gate * (1.0 - sig))
        ).astype(jnp.bfloat16)
        both_ref[:, hidden_units + start : hidden_units + start + size] = (
            d_hidden * gate * sig
        ).astype(jnp.bfloat16)
    for start, size in tiles(features, 512):
        out = lax.dot_general(
            both_ref[...],
            weight_in[start : start + size, :],
            (((1,), (1,)), ((), ())),
            preferred_element_type=jnp.float32,
        )
        for d in range(expert_count):
            out_refs[d][:, start : start + size] = out[d * capacity : (d + 1) * capacity].astype(
                jnp.bfloat16
            )


def local_call(kernel, out_shapes, inputs, flops, moved, scratch=(), after=()):
    in_specs = [pl.BlockSpec(memory_space=pltpu.VMEM)] * len(inputs)
    held = len(inputs)

    def body(*refs):
        kernel(*refs[:held], *refs[held + len(after) :])

    return pl.pallas_call(
        body if after else kernel,
        out_shape=out_shapes,
        in_specs=in_specs + [pl.BlockSpec(memory_space=pl.ANY)] * len(after),
        scratch_shapes=list(scratch),
        compiler_params=pltpu.CompilerParams(vmem_limit_bytes=VMEM_LIMIT),
        cost_estimate=pl.CostEstimate(flops=flops, bytes_accessed=moved, transcendentals=0),
    )(*inputs, *after)


def per_device_direct(
    fwd_prev,
    bwd_prev,
    bwd_saved,
    fwd_routes,
    fwd_gates,
    bwd_routes,
    bwd_gates,
    norm_gain,
    w_in,
    w_out,
):
    expert_count = lax.axis_size("expert")
    tok_rows = fwd_prev.shape[1]
    features = fwd_prev.shape[2]
    top_count = fwd_routes.shape[2]
    hidden_units = w_in.shape[3] // 2
    capacity = 3 * tok_rows * top_count // (2 * expert_count)
    gain_row = norm_gain
    weight_in = w_in[0, 0]
    weight_out = w_out[0, 0]
    me = lax.axis_index("expert")
    f_routes = (fwd_routes[0] ^ me).T
    b_routes = (bwd_routes[0] ^ me).T
    f_gates = fwd_gates[0].T
    b_gates = bwd_gates[0].T
    saved = bwd_saved[0]
    layer_in = passed_along(fwd_prev[0], "section", 1)
    grad_in = passed_along(bwd_prev[0], "section", -1)

    block = jax.ShapeDtypeStruct((capacity, features), jnp.bfloat16)
    whole = jax.ShapeDtypeStruct((tok_rows, features), jnp.bfloat16)
    one_dot = 2 * expert_count * capacity * tok_rows * features
    moved = 2 * features * (tok_rows + expert_count * capacity)
    slot_total = expert_count * capacity
    blocks = [block] * expert_count
    expert_flops = 2 * slot_total * features * hidden_units
    expert_moved = 2 * features * (3 * hidden_units + 3 * slot_total)
    rows_scratch = pltpu.VMEM((slot_total, features), jnp.bfloat16)

    b_sent = local_call(normed_kernel, blocks, (saved, b_routes, gain_row), one_dot, moved)
    b_rows = exchanged(b_sent, "expert")
    f_sent = local_call(
        normed_kernel, blocks, (layer_in, f_routes, gain_row), one_dot, moved, after=(b_sent[0],)
    )
    f_rows = exchanged(f_sent, "expert")
    g_sent = local_call(
        grads_kernel, blocks, (grad_in, b_routes, b_gates), 2 * one_dot, moved, after=(f_sent[0],)
    )
    g_rows = exchanged(g_sent, "expert")
    projected = jax.ShapeDtypeStruct((slot_total, hidden_units), jnp.float32)
    gate_pre, up_pre = local_call(
        expert_again_kernel,
        [projected, projected],
        (*b_rows, weight_in),
        2 * expert_flops,
        expert_moved,
        scratch=(rows_scratch,),
        after=(g_sent[0],),
    )
    f_done = local_call(
        expert_fwd_kernel,
        blocks,
        (*f_rows, weight_in, weight_out),
        3 * expert_flops,
        expert_moved,
        scratch=(rows_scratch, pltpu.VMEM((slot_total, hidden_units), jnp.bfloat16)),
        after=(gate_pre,),
    )
    f_back = exchanged(f_done, "expert")
    b_done = local_call(
        expert_bwd_kernel,
        blocks,
        (*g_rows, gate_pre, up_pre, weight_in, weight_out),
        3 * expert_flops,
        expert_moved,
        scratch=(rows_scratch, pltpu.VMEM((slot_total, 2 * hidden_units), jnp.bfloat16)),
        after=(f_back[1],),
    )
    b_back = exchanged(b_done, "expert")
    fwd_block = local_call(
        fwd_end_kernel,
        whole,
        (layer_in, f_routes, f_gates, *f_back),
        2 * one_dot,
        moved,
        after=(b_done[0],),
    )
    bwd_block = local_call(
        bwd_end_kernel,
        whole,
        (grad_in, saved, gain_row, b_routes, *b_back),
        one_dot,
        moved,
    )
    return (fwd_block[None], bwd_block[None])


def pick(table, expert, capacity, kind, top_count):
    first = 0 if kind[0] == "f" else 2 * top_count
    routes = table[first : first + top_count]
    gates = table[first + top_count : first + 2 * top_count]
    tok_rows = table.shape[1]
    member = routes == float(expert)
    held = jnp.sum(member.astype(jnp.float32), axis=0, keepdims=True)
    before = lax.broadcasted_iota(jnp.int32, (tok_rows, tok_rows), 0) < lax.broadcasted_iota(
        jnp.int32, (tok_rows, tok_rows), 1
    )
    slots = jnp.dot(
        jnp.broadcast_to(held, (8, tok_rows)).astype(jnp.bfloat16),
        before.astype(jnp.bfloat16),
        preferred_element_type=jnp.float32,
    )[0:1]
    place = placement(jnp.where(held > 0.0, slots, -1.0), 0, capacity)
    if len(kind) == 1:
        return (place.astype(jnp.bfloat16),)
    gate = jnp.sum(jnp.where(member, gates, 0.0), axis=0, keepdims=True)
    return halves(jnp.where(place, gate, 0.0))


def to_slots(weights, values):
    total = None
    for part in weights:
        term = jnp.dot(part, values, preferred_element_type=jnp.float32)
        total = term if total is None else total + term
    return total.astype(jnp.bfloat16)


def to_tokens(weights, rows):
    total = None
    for part in weights:
        term = rows_dot(part, rows)
        total = term if total is None else total + term
    return total


def three_parts(values):
    high = values.astype(jnp.bfloat16)
    rest = values - high.astype(jnp.float32)
    mid = rest.astype(jnp.bfloat16)
    low = (rest - mid.astype(jnp.float32)).astype(jnp.bfloat16)
    return high, mid, low


def normed_halves(wide, gain):
    inv_rms = lax.rsqrt(jnp.mean(wide * wide, axis=-1, keepdims=True) + EPS)
    return (wide * inv_rms * gain).astype(jnp.bfloat16)


def first_kernel(top_count, me_ref, *refs):
    sources, refs = refs[:6], refs[6:]
    (left_ref, right_ref, table_ref, gain_out), refs = refs[:4], refs[4:]
    held, sems = refs[:6], refs[6]
    copies = [pltpu.make_async_copy(sources[i], held[i], sems.at[i]) for i in range(6)]
    for copy in copies:
        copy.start()
    for copy in copies[1:]:
        copy.wait()
    saved, gain, f_routes, f_gates, b_routes, b_gates = held
    me = me_ref[0]
    fr = (f_routes[...] ^ me).astype(jnp.float32)
    br = (b_routes[...] ^ me).astype(jnp.float32)
    fg = f_gates[...]
    bg = b_gates[...]
    table = jnp.concatenate([fr, fg, br, bg], axis=0)
    table_ref[...] = table
    packed = [fr.astype(jnp.bfloat16), br.astype(jnp.bfloat16), *three_parts(fg), *three_parts(bg)]
    packed = jnp.concatenate([part.astype(jnp.float32) for part in packed], axis=0)
    gain_out[...] = gain[...]
    tok_rows, features = saved.shape
    half = features // 2
    copies[0].wait()
    normed = normed_halves(saved[...].astype(jnp.float32), gain[...])
    capacity = left_ref.shape[0] - tok_rows - packed.shape[0]
    near = tok_rows + packed.shape[0]
    for half_ref, start, expert in ((left_ref, 0, 1), (right_ref, half, 2)):
        half_ref[:tok_rows, :] = normed[:, start : start + half]
        half_ref[tok_rows:near, :] = jnp.zeros((near - tok_rows, half), jnp.bfloat16)
        half_ref[tok_rows:near, :tok_rows] = packed.astype(jnp.bfloat16)
        other = half - start
        half_ref[near:, :] = to_slots(
            pick(table, expert, capacity, "b", top_count), normed[:, other : other + half]
        )


def unpacked(block, tok_rows, top_count):
    rows = block[tok_rows : tok_rows + 8 * top_count, :tok_rows].astype(jnp.float32)
    k = top_count
    fr, br = rows[0:k], rows[k : 2 * k]
    fg = (rows[2 * k : 3 * k] + rows[3 * k : 4 * k]) + rows[4 * k : 5 * k]
    bg = (rows[5 * k : 6 * k] + rows[6 * k : 7 * k]) + rows[7 * k : 8 * k]
    return jnp.concatenate([fr, fg, br, bg], axis=0)


def normed_kernel_halves(values_ref, gain_ref, left_ref, right_ref):
    half = left_ref.shape[1]
    normed = normed_halves(values_ref[...].astype(jnp.float32), gain_ref[...])
    left_ref[...] = normed[:, :half]
    right_ref[...] = normed[:, half:]


def split_kernel(values_ref, left_ref, right_ref):
    half = left_ref.shape[1]
    left_ref[...] = values_ref[:, :half]
    right_ref[...] = values_ref[:, half:]


def tables_kernel(top_count, from_x, from_y, x_table, y_table):
    tok_rows = x_table.shape[1]
    x_table[...] = unpacked(from_x[...], tok_rows, top_count)
    y_table[...] = unpacked(from_y[...], tok_rows, top_count)


def hop_kernel(kind, top_count, own, x_tab, y_tab, left, right, from_x, from_y, to_y, to_x):
    capacity = to_y.shape[0] // 2
    tok_rows = own.shape[1]
    to_y[:capacity, :] = to_slots(pick(own[...], 2, capacity, kind, top_count), left[:tok_rows, :])
    to_y[capacity:, :] = to_slots(
        pick(x_tab[...], 3, capacity, kind, top_count), from_x[:tok_rows, :]
    )
    to_x[:capacity, :] = to_slots(pick(own[...], 1, capacity, kind, top_count), right[:tok_rows, :])
    to_x[capacity:, :] = to_slots(
        pick(y_tab[...], 3, capacity, kind, top_count), from_y[:tok_rows, :]
    )


def far_kernel(kind, top_count, x_tab, y_tab, from_x, from_y, to_y, to_x):
    capacity = to_y.shape[0]
    tok_rows = x_tab.shape[1]
    to_y[...] = to_slots(pick(x_tab[...], 3, capacity, kind, top_count), from_x[:tok_rows, :])
    to_x[...] = to_slots(pick(y_tab[...], 3, capacity, kind, top_count), from_y[:tok_rows, :])


def assemble(kind, top_count, own, x_tab, y_tab, left, right, from_x, from_y, got_y, got_x, rows):
    capacity = rows.shape[0] // 4
    half = got_y.shape[1]
    tok_rows = own.shape[1]
    mine = pick(own[...], 0, capacity, kind, top_count)
    rows[:capacity, :half] = to_slots(mine, left[:tok_rows, :])
    rows[:capacity, half:] = to_slots(mine, right[:tok_rows, :])
    rows[capacity : 2 * capacity, :half] = to_slots(
        pick(x_tab[...], 1, capacity, kind, top_count), from_x[:tok_rows, :]
    )
    rows[2 * capacity : 3 * capacity, half:] = to_slots(
        pick(y_tab[...], 2, capacity, kind, top_count), from_y[:tok_rows, :]
    )
    if got_y.shape[0] == capacity:
        near_x, near_y = from_x[-capacity:, :], from_y[-capacity:, :]
    else:
        near_x, near_y = got_x[:capacity, :], got_y[:capacity, :]
    rows[capacity : 2 * capacity, half:] = near_x
    rows[2 * capacity : 3 * capacity, :half] = near_y
    rows[3 * capacity :, :half] = got_y[-capacity:, :]
    rows[3 * capacity :, half:] = got_x[-capacity:, :]


def hand_out(out, at, capacity, to_left, keep, near, onward):
    size = out.shape[1]
    rows = out.astype(jnp.bfloat16)
    mine, from_x, from_y, far = [rows[d * capacity : (d + 1) * capacity] for d in range(4)]
    keep[:, at : at + size] = mine
    near[:, at : at + size] = from_x if to_left else from_y
    onward[:capacity, at : at + size] = from_y if to_left else from_x
    onward[capacity:, at : at + size] = far


def fwd_half(hidden_ref, weight_out, to_left, keep, near, onward):
    capacity, half = keep.shape
    first = 0 if to_left else half
    for at, size in tiles(half, 512):
        out = jnp.dot(
            hidden_ref[...],
            weight_out[:, first + at : first + at + size],
            preferred_element_type=jnp.float32,
        )
        hand_out(out, at, capacity, to_left, keep, near, onward)


def bwd_half(both_ref, weight_in, to_left, keep, near, onward):
    capacity, half = keep.shape
    first = 0 if to_left else half
    for at, size in tiles(half, 512):
        out = lax.dot_general(
            both_ref[...],
            weight_in[first + at : first + at + size, :],
            (((1,), (1,)), ((), ())),
            preferred_element_type=jnp.float32,
        )
        hand_out(out, at, capacity, to_left, keep, near, onward)


def fwd_right_kernel(hidden_ref, weight_out, keep, near, onward):
    fwd_half(hidden_ref, weight_out, False, keep, near, onward)


def bwd_right_kernel(both_ref, weight_in, keep, near, onward):
    bwd_half(both_ref, weight_in, False, keep, near, onward)


def hop_again_kernel(top_count, *refs):
    dispatch, (weight_in, gate_ref, up_ref, rows_ref) = refs[:9], refs[9:]
    assemble("b", top_count, *dispatch, rows_ref)
    hidden_units = gate_ref.shape[1]
    for start, size in tiles(hidden_units, 256):
        gate_ref[:, start : start + size] = jnp.dot(
            rows_ref[...], weight_in[:, start : start + size], preferred_element_type=jnp.float32
        )
        up_ref[:, start : start + size] = jnp.dot(
            rows_ref[...],
            weight_in[:, hidden_units + start : hidden_units + start + size],
            preferred_element_type=jnp.float32,
        )


def hop_fwd_kernel(top_count, *refs):
    dispatch, refs = refs[:9], refs[9:]
    weight_in, weight_out = refs[:2]
    outs, hidden_ref, rows_ref = refs[2:5], refs[5], refs[6]
    hidden_units = weight_out.shape[0]
    assemble("f", top_count, *dispatch, rows_ref)
    for start, size in tiles(hidden_units, 256):
        gate = jnp.dot(
            rows_ref[...], weight_in[:, start : start + size], preferred_element_type=jnp.float32
        )
        up = jnp.dot(
            rows_ref[...],
            weight_in[:, hidden_units + start : hidden_units + start + size],
            preferred_element_type=jnp.float32,
        )
        hidden_ref[:, start : start + size] = (gate / (1.0 + jnp.exp(-gate)) * up).astype(
            jnp.bfloat16
        )
    fwd_half(hidden_ref, weight_out, True, *outs)


def hop_bwd_kernel(top_count, *refs):
    dispatch, refs = refs[:9], refs[9:]
    gate_ref, up_ref, weight_in, weight_out = refs[:4]
    outs, both_ref, grads_ref = refs[4:7], refs[7], refs[8]
    hidden_units = weight_out.shape[0]
    assemble("bg", top_count, *dispatch, grads_ref)
    for start, size in tiles(hidden_units, 256):
        gate = gate_ref[:, start : start + size]
        up = up_ref[:, start : start + size]
        d_hidden = lax.dot_general(
            grads_ref[...],
            weight_out[start : start + size, :],
            (((1,), (1,)), ((), ())),
            preferred_element_type=jnp.float32,
        )
        sig = 1.0 / (1.0 + jnp.exp(-gate))
        both_ref[:, start : start + size] = (
            d_hidden * up * sig * (1.0 + gate * (1.0 - sig))
        ).astype(jnp.bfloat16)
        both_ref[:, hidden_units + start : hidden_units + start + size] = (
            d_hidden * gate * sig
        ).astype(jnp.bfloat16)
    bwd_half(both_ref, weight_in, True, *outs)


def sums_kernel(kind, top_count, here, table_ref, near, far, out):
    capacity = near.shape[0]
    table = table_ref[...]
    out[...] = (
        to_tokens(pick(table, here, capacity, kind, top_count), near[...])
        + to_tokens(pick(table, 3, capacity, kind, top_count), far[capacity:, :])
    ).astype(jnp.bfloat16)


def summed(kind, top_count, own, keep_left, keep_right, got_y, got_x, sum_x, sum_y):
    capacity = keep_left.shape[0]
    mine = pick(own[...], 0, capacity, kind, top_count)
    near_y = pick(own[...], 2, capacity, kind, top_count)
    near_x = pick(own[...], 1, capacity, kind, top_count)
    left = to_tokens(mine, keep_left[...]) + to_tokens(near_y, got_y[:capacity, :])
    right = to_tokens(mine, keep_right[...]) + to_tokens(near_x, got_x[:capacity, :])
    return left + sum_x[...].astype(jnp.float32), right + sum_y[...].astype(jnp.float32)


def hop_fwd_end_kernel(top_count, layer_ref, *refs):
    out_ref, order_ref = refs[-2:]
    order_ref[...] = jnp.zeros_like(order_ref)
    half = layer_ref.shape[1] // 2
    left, right = summed("fg", top_count, *refs[:-2])
    out_ref[:, :half] = (layer_ref[:, :half].astype(jnp.float32) + left).astype(jnp.bfloat16)
    out_ref[:, half:] = (layer_ref[:, half:].astype(jnp.float32) + right).astype(jnp.bfloat16)


def hop_bwd_near_kernel(
    top_count, own, keep_left, keep_right, got_y, got_x, sum_x, left_ref, right_ref
):
    capacity = keep_left.shape[0]
    mine = pick(own[...], 0, capacity, "b", top_count)
    near_y = pick(own[...], 2, capacity, "b", top_count)
    near_x = pick(own[...], 1, capacity, "b", top_count)
    left = to_tokens(mine, keep_left[...]) + to_tokens(near_y, got_y[:capacity, :])
    left_ref[...] = left + sum_x[...].astype(jnp.float32)
    right_ref[...] = to_tokens(mine, keep_right[...]) + to_tokens(near_x, got_x[:capacity, :])


def hop_bwd_end_kernel(grads_ref, saved_ref, gain_ref, left_ref, right_ref, sum_y, out_ref):
    features = saved_ref.shape[1]
    half = features // 2
    parts = []
    right = right_ref[...] + sum_y[...].astype(jnp.float32)
    for start, d_normed in ((0, left_ref[...]), (half, right)):
        wide = saved_ref[:, start : start + half].astype(jnp.float32)
        scaled = d_normed * gain_ref[:, start : start + half]
        parts.append((start, wide, scaled))
    square = sum(jnp.sum(wide * wide, axis=-1, keepdims=True) for _, wide, _ in parts)
    inner = sum(jnp.sum(scaled * wide, axis=-1, keepdims=True) for _, wide, scaled in parts)
    inv_rms = lax.rsqrt(square / features + EPS)
    factor = inv_rms * inv_rms * inv_rms / features * inner
    for start, wide, scaled in parts:
        out_ref[:, start : start + half] = (
            grads_ref[:, start : start + half].astype(jnp.float32)
            + inv_rms * scaled
            - factor * wide
        ).astype(jnp.bfloat16)


def per_device_hops(
    fwd_prev,
    bwd_prev,
    bwd_saved,
    fwd_routes,
    fwd_gates,
    bwd_routes,
    bwd_gates,
    norm_gain,
    w_in,
    w_out,
):
    tok_rows, features = fwd_prev.shape[1:]
    top_count = fwd_routes.shape[2]
    hidden_units = w_in.shape[3] // 2
    capacity = 3 * tok_rows * top_count // 8
    half = features // 2
    gain_row = norm_gain
    weight_in = w_in[0, 0]
    weight_out = w_out[0, 0]
    me = lax.axis_index("expert").astype(jnp.int32).reshape(1)
    saved = bwd_saved[0]
    layer_in = passed_along(fwd_prev[0], "section", 1)
    grad_in = passed_along(bwd_prev[0], "section", -1)

    def shaped(rows, columns, dtype=jnp.bfloat16):
        return jax.ShapeDtypeStruct((rows, columns), dtype)

    def crossed(left, right):
        return swapped(left, "expert", 1), swapped(right, "expert", 2)

    slot_total = 4 * capacity
    table_rows = 4 * top_count
    one_hop = moved = 1024
    expert_flops = 2 * slot_total * features * hidden_units
    expert_moved = 2 * features * (3 * hidden_units + 3 * slot_total)
    rows_scratch = pltpu.VMEM((slot_total, features), jnp.bfloat16)
    halves_out = [shaped(tok_rows, half)] * 2
    hop_out = [shaped(2 * capacity, half)] * 2
    half_out = [shaped(capacity, half), shaped(capacity, half), shaped(2 * capacity, half)]
    hidden_shape = shaped(slot_total, hidden_units)
    both_shape = shaped(slot_total, 2 * hidden_units)
    table_shape = shaped(table_rows, tok_rows, jnp.float32)
    first_rows = tok_rows + 8 * top_count + capacity

    b_left, b_right, own, gain_here = pl.pallas_call(
        functools.partial(first_kernel, top_count),
        out_shape=[
            shaped(first_rows, half),
            shaped(first_rows, half),
            table_shape,
            shaped(1, features, jnp.float32),
        ],
        in_specs=[pl.BlockSpec(memory_space=pltpu.SMEM)]
        + [pl.BlockSpec(memory_space=pltpu.HBM)] * 6,
        scratch_shapes=[
            pltpu.VMEM((tok_rows, features), jnp.bfloat16),
            pltpu.VMEM((1, features), jnp.float32),
            pltpu.VMEM((top_count, tok_rows), jnp.int32),
            pltpu.VMEM((top_count, tok_rows), jnp.float32),
            pltpu.VMEM((top_count, tok_rows), jnp.int32),
            pltpu.VMEM((top_count, tok_rows), jnp.float32),
            pltpu.SemaphoreType.DMA((6,)),
        ],
        compiler_params=pltpu.CompilerParams(vmem_limit_bytes=VMEM_LIMIT),
        cost_estimate=pl.CostEstimate(flops=one_hop, bytes_accessed=moved, transcendentals=0),
    )(
        me,
        *[
            pltpu.with_memory_space_constraint(value, pltpu.HBM)
            for value in (
                saved,
                gain_row,
                fwd_routes[0].T,
                fwd_gates[0].T,
                bwd_routes[0].T,
                bwd_gates[0].T,
            )
        ],
    )
    b_from_x, b_from_y = crossed(b_left, b_right)

    def onward(kind, sent, got, after):
        to_y, to_x = local_call(
            functools.partial(hop_kernel, kind, top_count),
            hop_out,
            (*tabs, *sent, *got),
            one_hop,
            moved,
            after=after,
        )
        return swapped(to_y, "expert", 2), swapped(to_x, "expert", 1), to_y

    f_left, f_right = local_call(
        normed_kernel_halves, halves_out, (layer_in, gain_here), one_hop, moved, after=(b_left,)
    )
    f_from_x, f_from_y = crossed(f_left, f_right)
    x_tab, y_tab = local_call(
        functools.partial(tables_kernel, top_count),
        [table_shape] * 2,
        (b_from_x, b_from_y),
        TABLES_COST,
        1024,
        after=(f_left,),
    )
    g_left, g_right = local_call(split_kernel, halves_out, (grad_in,), 1024, moved, after=(x_tab,))
    g_from_x, g_from_y = crossed(g_left, g_right)
    tabs = (own, x_tab, y_tab)
    b_to_y, b_to_x = local_call(
        functools.partial(far_kernel, "b", top_count),
        [shaped(capacity, half)] * 2,
        (x_tab, y_tab, b_from_x, b_from_y),
        one_hop,
        moved,
        after=(g_left,),
    )
    b_got_y, b_got_x = swapped(b_to_y, "expert", 2), swapped(b_to_x, "expert", 1)
    f_got_y, f_got_x, f_to_y = onward("f", (f_left, f_right), (f_from_x, f_from_y), (b_to_y,))
    g_got_y, g_got_x, g_to_y = onward("bg", (g_left, g_right), (g_from_x, g_from_y), (f_to_y,))
    gate_pre, up_pre = local_call(
        functools.partial(hop_again_kernel, top_count),
        [shaped(slot_total, hidden_units, jnp.float32)] * 2,
        (*tabs, b_left, b_right, b_from_x, b_from_y, b_got_y, b_got_x, weight_in),
        2 * expert_flops,
        expert_moved,
        scratch=(rows_scratch,),
        after=(g_to_y,),
    )
    f_keep_l, f_near_l, f_on_l, hidden = local_call(
        functools.partial(hop_fwd_kernel, top_count),
        half_out + [hidden_shape],
        (*tabs, f_left, f_right, f_from_x, f_from_y, f_got_y, f_got_x, weight_in, weight_out),
        5 * expert_flops // 2,
        expert_moved,
        scratch=(rows_scratch,),
        after=(gate_pre,),
    )
    f_ret_y = swapped(f_on_l, "expert", 2)
    f_keep_r, f_near_r, f_on_r = local_call(
        fwd_right_kernel, half_out, (hidden, weight_out), 1024, 1024
    )
    f_ret_x = swapped(f_on_r, "expert", 1)
    b_keep_l, b_near_l, b_on_l, both = local_call(
        functools.partial(hop_bwd_kernel, top_count),
        half_out + [both_shape],
        (
            *tabs,
            g_left,
            g_right,
            g_from_x,
            g_from_y,
            g_got_y,
            g_got_x,
            gate_pre,
            up_pre,
            weight_in,
            weight_out,
        ),
        2 * expert_flops,
        expert_moved,
        scratch=(rows_scratch,),
        after=(f_keep_r,),
    )
    b_ret_y = swapped(b_on_l, "expert", 2)
    b_keep_r, b_near_r, b_on_r = local_call(
        bwd_right_kernel, half_out, (both, weight_in), 1024, 1024
    )
    b_ret_x = swapped(b_on_r, "expert", 1)

    def summed_call(kind, here, table, near, far, after):
        part = local_call(
            functools.partial(sums_kernel, kind, top_count, here),
            shaped(tok_rows, half),
            (table, near, far),
            one_hop,
            moved,
            after=after,
        )
        return swapped(part, "expert", here), part

    f_sum_x, last = summed_call("fg", 1, x_tab, f_near_l, f_ret_y, (b_keep_r,))
    f_sum_y, last = summed_call("fg", 2, y_tab, f_near_r, f_ret_x, (last,))
    b_sum_x, last = summed_call("b", 1, x_tab, b_near_l, b_ret_y, (last,))
    b_sum_y, last = summed_call("b", 2, y_tab, b_near_r, b_ret_x, (last,))
    f_keep = (f_keep_l, f_keep_r)
    b_keep = (b_keep_l, b_keep_r)
    fwd_block, order = local_call(
        functools.partial(hop_fwd_end_kernel, top_count),
        [shaped(tok_rows, features), shaped(8, 128, jnp.float32)],
        (layer_in, own, *f_keep, f_ret_y, f_ret_x, f_sum_x, f_sum_y),
        one_hop,
        moved,
        after=(last,),
    )
    b_near = local_call(
        functools.partial(hop_bwd_near_kernel, top_count),
        [shaped(tok_rows, half, jnp.float32)] * 2,
        (own, *b_keep, b_ret_y, b_ret_x, b_sum_x),
        one_hop,
        moved,
        after=(order,),
    )
    bwd_block = local_call(
        hop_bwd_end_kernel,
        shaped(tok_rows, features),
        (grad_in, saved, gain_here, *b_near, b_sum_y),
        one_hop,
        moved,
    )
    return (fwd_block[None], bwd_block[None])


def per_device(*arrays):
    if lax.axis_size("expert") == 4:
        return per_device_hops(*arrays)
    return per_device_direct(*arrays)


def solution(mesh):
    in_specs = (
        P("section", "expert", None),
        P("section", "expert", None),
        P("section", "expert", None),
        P("section", "expert", None),
        P("section", "expert", None),
        P("section", "expert", None),
        P("section", "expert", None),
        P("section", None),
        P("section", "expert", None, None),
        P("section", "expert", None, None),
    )
    out_specs = (P("section", "expert", None), P("section", "expert", None))
    return jax.shard_map(
        per_device, mesh=mesh, in_specs=in_specs, out_specs=out_specs, check_vma=False
    )
```

```python
import functools

import jax
import jax.numpy as jnp
from jax import lax
from jax.experimental import pallas as pl
from jax.experimental.pallas import tpu as pltpu
from jax.sharding import PartitionSpec as P

EPS = 1e-06
VMEM_LIMIT = 32 * 1024 * 1024
TABLES_COST = 6_000_000_000


def passed_along(value, axis, steps):
    count = lax.axis_size(axis)
    pairs = [(source, (source + steps) % count) for source in range(count)]
    return lax.ppermute(value, axis, pairs)


def swapped(value, axis, offset):
    count = lax.axis_size(axis)
    pairs = [(source, source ^ offset) for source in range(count)]
    return lax.ppermute(value, axis, pairs)


def exchanged(blocks, axis):
    return [blocks[0]] + [swapped(blocks[d], axis, d) for d in range(1, len(blocks))]


def slot_table(routes, expert_count):
    top_count, tok_rows = routes.shape
    experts = max(8, expert_count)
    wanted = lax.broadcasted_iota(jnp.int32, (experts, tok_rows), 0)
    member = routes[0:1, :] == wanted
    for k in range(1, top_count):
        member = jnp.logical_or(member, routes[k : k + 1, :] == wanted)
    before = lax.broadcasted_iota(jnp.int32, (tok_rows, tok_rows), 0) < lax.broadcasted_iota(
        jnp.int32, (tok_rows, tok_rows), 1
    )
    slots = jnp.dot(
        member.astype(jnp.bfloat16),
        before.astype(jnp.bfloat16),
        preferred_element_type=jnp.float32,
    )
    return jnp.where(member, slots, -1.0)


def placement(slots, expert, capacity):
    tok_rows = slots.shape[1]
    row = lax.broadcasted_iota(jnp.int32, (capacity, tok_rows), 0).astype(jnp.float32)
    return slots[expert : expert + 1, :] == row


def gate_row(routes, gates, expert):
    total = jnp.zeros((1, routes.shape[1]), jnp.float32)
    for k in range(routes.shape[0]):
        total = total + jnp.where(routes[k : k + 1, :] == expert, gates[k : k + 1, :], 0.0)
    return total


def halves(weights):
    high = weights.astype(jnp.bfloat16)
    low = (weights - high.astype(jnp.float32)).astype(jnp.bfloat16)
    return high, low


def normed_kernel(values_ref, routes_ref, gain_ref, *out_refs):
    expert_count = len(out_refs)
    capacity = out_refs[0].shape[0]
    wide = values_ref[...].astype(jnp.float32)
    inv_rms = lax.rsqrt(jnp.mean(wide * wide, axis=-1, keepdims=True) + EPS)
    normed = (wide * inv_rms * gain_ref[...]).astype(jnp.bfloat16)
    slots = slot_table(routes_ref[...], expert_count)
    for e in range(expert_count):
        place = placement(slots, e, capacity).astype(jnp.bfloat16)
        out_refs[e][...] = jnp.dot(place, normed, preferred_element_type=jnp.float32).astype(
            jnp.bfloat16
        )


def grads_kernel(grads_ref, routes_ref, gates_ref, *out_refs):
    expert_count = len(out_refs)
    capacity = out_refs[0].shape[0]
    grads = grads_ref[...]
    routes = routes_ref[...]
    slots = slot_table(routes, expert_count)
    for e in range(expert_count):
        place = placement(slots, e, capacity)
        high, low = halves(jnp.where(place, gate_row(routes, gates_ref[...], e), 0.0))
        out_refs[e][...] = (
            jnp.dot(high, grads, preferred_element_type=jnp.float32)
            + jnp.dot(low, grads, preferred_element_type=jnp.float32)
        ).astype(jnp.bfloat16)


def rows_dot(weights, rows):
    return lax.dot_general(
        weights, rows, (((0,), (0,)), ((), ())), preferred_element_type=jnp.float32
    )


def fwd_end_kernel(layer_ref, routes_ref, gates_ref, *refs):
    row_refs, out_ref = refs[:-1], refs[-1]
    expert_count = len(row_refs)
    capacity = row_refs[0].shape[0]
    routes = routes_ref[...]
    slots = slot_table(routes, expert_count)
    total = layer_ref[...].astype(jnp.float32)
    for e in range(expert_count):
        place = placement(slots, e, capacity)
        high, low = halves(jnp.where(place, gate_row(routes, gates_ref[...], e), 0.0))
        rows = row_refs[e][...]
        total = total + (rows_dot(high, rows) + rows_dot(low, rows))
    out_ref[...] = total.astype(jnp.bfloat16)


def bwd_end_kernel(grads_ref, saved_ref, gain_ref, routes_ref, *refs):
    row_refs, out_ref = refs[:-1], refs[-1]
    expert_count = len(row_refs)
    capacity = row_refs[0].shape[0]
    features = saved_ref.shape[1]
    slots = slot_table(routes_ref[...], expert_count)
    d_normed = None
    for e in range(expert_count):
        place = placement(slots, e, capacity).astype(jnp.bfloat16)
        part = rows_dot(place, row_refs[e][...])
        d_normed = part if d_normed is None else d_normed + part
    wide = saved_ref[...].astype(jnp.float32)
    inv_rms = lax.rsqrt(jnp.mean(wide * wide, axis=-1, keepdims=True) + EPS)
    scaled = d_normed * gain_ref[...]
    cubed = inv_rms * inv_rms * inv_rms
    inner = jnp.sum(scaled * wide, axis=-1, keepdims=True)
    out_ref[...] = (
        grads_ref[...].astype(jnp.float32) + inv_rms * scaled - cubed / features * wide * inner
    ).astype(jnp.bfloat16)


def joined(refs):
    rows = [ref[...] for ref in refs]
    if rows[0].shape[0] % 16 == 0:
        return jnp.concatenate(rows, axis=0)
    return jnp.concatenate([r.astype(jnp.float32) for r in rows], axis=0).astype(jnp.bfloat16)


def tiles(size, step):
    return [(start, min(step, size - start)) for start in range(0, size, step)]


def expert_fwd_kernel(*refs):
    expert_count = (len(refs) - 4) // 2
    row_refs = refs[:expert_count]
    weight_in, weight_out = refs[expert_count : expert_count + 2]
    out_refs = refs[expert_count + 2 : 2 * expert_count + 2]
    rows_ref, hidden_ref = refs[-2:]
    capacity = row_refs[0].shape[0]
    hidden_units, features = weight_out.shape
    rows_ref[...] = joined(row_refs)
    for start, size in tiles(hidden_units, 256):
        gate = jnp.dot(
            rows_ref[...], weight_in[:, start : start + size], preferred_element_type=jnp.float32
        )
        up = jnp.dot(
            rows_ref[...],
            weight_in[:, hidden_units + start : hidden_units + start + size],
            preferred_element_type=jnp.float32,
        )
        hidden_ref[:, start : start + size] = (gate / (1.0 + jnp.exp(-gate)) * up).astype(
            jnp.bfloat16
        )
    for start, size in tiles(features, 512):
        out = jnp.dot(
            hidden_ref[...], weight_out[:, start : start + size], preferred_element_type=jnp.float32
        )
        for d in range(expert_count):
            out_refs[d][:, start : start + size] = out[d * capacity : (d + 1) * capacity].astype(
                jnp.bfloat16
            )


def expert_again_kernel(*refs):
    expert_count = len(refs) - 4
    row_refs = refs[:expert_count]
    weight_in, gate_ref, up_ref, rows_ref = refs[expert_count:]
    hidden_units = gate_ref.shape[1]
    rows_ref[...] = joined(row_refs)
    for start, size in tiles(hidden_units, 256):
        gate_ref[:, start : start + size] = jnp.dot(
            rows_ref[...], weight_in[:, start : start + size], preferred_element_type=jnp.float32
        )
        up_ref[:, start : start + size] = jnp.dot(
            rows_ref[...],
            weight_in[:, hidden_units + start : hidden_units + start + size],
            preferred_element_type=jnp.float32,
        )


def expert_bwd_kernel(*refs):
    expert_count = (len(refs) - 6) // 2
    grad_refs = refs[:expert_count]
    gate_ref, up_ref, weight_in, weight_out = refs[expert_count : expert_count + 4]
    out_refs = refs[expert_count + 4 : 2 * expert_count + 4]
    grads_ref, both_ref = refs[-2:]
    capacity = grad_refs[0].shape[0]
    hidden_units, features = weight_out.shape
    grads_ref[...] = joined(grad_refs)
    for start, size in tiles(hidden_units, 256):
        gate = gate_ref[:, start : start + size]
        up = up_ref[:, start : start + size]
        d_hidden = lax.dot_general(
            grads_ref[...],
            weight_out[start : start + size, :],
            (((1,), (1,)), ((), ())),
            preferred_element_type=jnp.float32,
        )
        sig = 1.0 / (1.0 + jnp.exp(-gate))
        both_ref[:, start : start + size] = (
            d_hidden * up * sig * (1.0 + gate * (1.0 - sig))
        ).astype(jnp.bfloat16)
        both_ref[:, hidden_units + start : hidden_units + start + size] = (
            d_hidden * gate * sig
        ).astype(jnp.bfloat16)
    for start, size in tiles(features, 512):
        out = lax.dot_general(
            both_ref[...],
            weight_in[start : start + size, :],
            (((1,), (1,)), ((), ())),
            preferred_element_type=jnp.float32,
        )
        for d in range(expert_count):
            out_refs[d][:, start : start + size] = out[d * capacity : (d + 1) * capacity].astype(
                jnp.bfloat16
            )


def local_call(kernel, out_shapes, inputs, flops, moved, scratch=(), after=()):
    in_specs = [pl.BlockSpec(memory_space=pltpu.VMEM)] * len(inputs)
    held = len(inputs)

    def body(*refs):
        kernel(*refs[:held], *refs[held + len(after) :])

    return pl.pallas_call(
        body if after else kernel,
        out_shape=out_shapes,
        in_specs=in_specs + [pl.BlockSpec(memory_space=pl.ANY)] * len(after),
        scratch_shapes=list(scratch),
        compiler_params=pltpu.CompilerParams(vmem_limit_bytes=VMEM_LIMIT),
        cost_estimate=pl.CostEstimate(flops=flops, bytes_accessed=moved, transcendentals=0),
    )(*inputs, *after)


def per_device_direct(
    fwd_prev,
    bwd_prev,
    bwd_saved,
    fwd_routes,
    fwd_gates,
    bwd_routes,
    bwd_gates,
    norm_gain,
    w_in,
    w_out,
):
    expert_count = lax.axis_size("expert")
    tok_rows = fwd_prev.shape[1]
    features = fwd_prev.shape[2]
    top_count = fwd_routes.shape[2]
    hidden_units = w_in.shape[3] // 2
    capacity = 3 * tok_rows * top_count // (2 * expert_count)
    gain_row = norm_gain
    weight_in = w_in[0, 0]
    weight_out = w_out[0, 0]
    me = lax.axis_index("expert")
    f_routes = (fwd_routes[0] ^ me).T
    b_routes = (bwd_routes[0] ^ me).T
    f_gates = fwd_gates[0].T
    b_gates = bwd_gates[0].T
    saved = bwd_saved[0]
    layer_in = passed_along(fwd_prev[0], "section", 1)
    grad_in = passed_along(bwd_prev[0], "section", -1)

    block = jax.ShapeDtypeStruct((capacity, features), jnp.bfloat16)
    whole = jax.ShapeDtypeStruct((tok_rows, features), jnp.bfloat16)
    one_dot = 2 * expert_count * capacity * tok_rows * features
    moved = 2 * features * (tok_rows + expert_count * capacity)
    slot_total = expert_count * capacity
    blocks = [block] * expert_count
    expert_flops = 2 * slot_total * features * hidden_units
    expert_moved = 2 * features * (3 * hidden_units + 3 * slot_total)
    rows_scratch = pltpu.VMEM((slot_total, features), jnp.bfloat16)

    b_sent = local_call(normed_kernel, blocks, (saved, b_routes, gain_row), one_dot, moved)
    b_rows = exchanged(b_sent, "expert")
    f_sent = local_call(
        normed_kernel, blocks, (layer_in, f_routes, gain_row), one_dot, moved, after=(b_sent[0],)
    )
    f_rows = exchanged(f_sent, "expert")
    g_sent = local_call(
        grads_kernel, blocks, (grad_in, b_routes, b_gates), 2 * one_dot, moved, after=(f_sent[0],)
    )
    g_rows = exchanged(g_sent, "expert")
    projected = jax.ShapeDtypeStruct((slot_total, hidden_units), jnp.float32)
    gate_pre, up_pre = local_call(
        expert_again_kernel,
        [projected, projected],
        (*b_rows, weight_in),
        2 * expert_flops,
        expert_moved,
        scratch=(rows_scratch,),
        after=(g_sent[0],),
    )
    f_done = local_call(
        expert_fwd_kernel,
        blocks,
        (*f_rows, weight_in, weight_out),
        3 * expert_flops,
        expert_moved,
        scratch=(rows_scratch, pltpu.VMEM((slot_total, hidden_units), jnp.bfloat16)),
        after=(gate_pre,),
    )
    f_back = exchanged(f_done, "expert")
    b_done = local_call(
        expert_bwd_kernel,
        blocks,
        (*g_rows, gate_pre, up_pre, weight_in, weight_out),
        3 * expert_flops,
        expert_moved,
        scratch=(rows_scratch, pltpu.VMEM((slot_total, 2 * hidden_units), jnp.bfloat16)),
        after=(f_back[1],),
    )
    b_back = exchanged(b_done, "expert")
    fwd_block = local_call(
        fwd_end_kernel,
        whole,
        (layer_in, f_routes, f_gates, *f_back),
        2 * one_dot,
        moved,
        after=(b_done[0],),
    )
    bwd_block = local_call(
        bwd_end_kernel,
        whole,
        (grad_in, saved, gain_row, b_routes, *b_back),
        one_dot,
        moved,
    )
    return (fwd_block[None], bwd_block[None])


def pick(table, expert, capacity, kind, top_count):
    first = 0 if kind[0] == "f" else 2 * top_count
    routes = table[first : first + top_count]
    gates = table[first + top_count : first + 2 * top_count]
    tok_rows = table.shape[1]
    member = routes == float(expert)
    held = jnp.sum(member.astype(jnp.float32), axis=0, keepdims=True)
    before = lax.broadcasted_iota(jnp.int32, (tok_rows, tok_rows), 0) < lax.broadcasted_iota(
        jnp.int32, (tok_rows, tok_rows), 1
    )
    slots = jnp.dot(
        jnp.broadcast_to(held, (8, tok_rows)).astype(jnp.bfloat16),
        before.astype(jnp.bfloat16),
        preferred_element_type=jnp.float32,
    )[0:1]
    place = placement(jnp.where(held > 0.0, slots, -1.0), 0, capacity)
    if len(kind) == 1:
        return (place.astype(jnp.bfloat16),)
    gate = jnp.sum(jnp.where(member, gates, 0.0), axis=0, keepdims=True)
    return halves(jnp.where(place, gate, 0.0))


def to_slots(weights, values):
    total = None
    for part in weights:
        term = jnp.dot(part, values, preferred_element_type=jnp.float32)
        total = term if total is None else total + term
    return total.astype(jnp.bfloat16)


def to_tokens(weights, rows):
    total = None
    for part in weights:
        term = rows_dot(part, rows)
        total = term if total is None else total + term
    return total


def three_parts(values):
    high = values.astype(jnp.bfloat16)
    rest = values - high.astype(jnp.float32)
    mid = rest.astype(jnp.bfloat16)
    low = (rest - mid.astype(jnp.float32)).astype(jnp.bfloat16)
    return high, mid, low


def normed_halves(wide, gain):
    inv_rms = lax.rsqrt(jnp.mean(wide * wide, axis=-1, keepdims=True) + EPS)
    return (wide * inv_rms * gain).astype(jnp.bfloat16)


def first_kernel(top_count, me_ref, *refs):
    sources, refs = refs[:6], refs[6:]
    (left_ref, right_ref, table_ref, gain_out), refs = refs[:4], refs[4:]
    held, sems = refs[:6], refs[6]
    copies = [pltpu.make_async_copy(sources[i], held[i], sems.at[i]) for i in range(6)]
    for copy in copies:
        copy.start()
    for copy in copies[1:]:
        copy.wait()
    saved, gain, f_routes, f_gates, b_routes, b_gates = held
    me = me_ref[0]
    fr = (f_routes[...] ^ me).astype(jnp.float32)
    br = (b_routes[...] ^ me).astype(jnp.float32)
    fg = f_gates[...]
    bg = b_gates[...]
    table = jnp.concatenate([fr, fg, br, bg], axis=0)
    table_ref[...] = table
    packed = [fr.astype(jnp.bfloat16), br.astype(jnp.bfloat16), *three_parts(fg), *three_parts(bg)]
    packed = jnp.concatenate([part.astype(jnp.float32) for part in packed], axis=0)
    gain_out[...] = gain[...]
    tok_rows, features = saved.shape
    half = features // 2
    copies[0].wait()
    normed = normed_halves(saved[...].astype(jnp.float32), gain[...])
    capacity = left_ref.shape[0] - tok_rows - packed.shape[0]
    near = tok_rows + packed.shape[0]
    for half_ref, start, expert in ((left_ref, 0, 1), (right_ref, half, 2)):
        half_ref[:tok_rows, :] = normed[:, start : start + half]
        half_ref[tok_rows:near, :] = jnp.zeros((near - tok_rows, half), jnp.bfloat16)
        half_ref[tok_rows:near, :tok_rows] = packed.astype(jnp.bfloat16)
        other = half - start
        half_ref[near:, :] = to_slots(
            pick(table, expert, capacity, "b", top_count), normed[:, other : other + half]
        )


def unpacked(block, tok_rows, top_count):
    rows = block[tok_rows : tok_rows + 8 * top_count, :tok_rows].astype(jnp.float32)
    k = top_count
    fr, br = rows[0:k], rows[k : 2 * k]
    fg = (rows[2 * k : 3 * k] + rows[3 * k : 4 * k]) + rows[4 * k : 5 * k]
    bg = (rows[5 * k : 6 * k] + rows[6 * k : 7 * k]) + rows[7 * k : 8 * k]
    return jnp.concatenate([fr, fg, br, bg], axis=0)


def normed_kernel_halves(values_ref, gain_ref, left_ref, right_ref):
    half = left_ref.shape[1]
    normed = normed_halves(values_ref[...].astype(jnp.float32), gain_ref[...])
    left_ref[...] = normed[:, :half]
    right_ref[...] = normed[:, half:]


def split_kernel(values_ref, left_ref, right_ref):
    half = left_ref.shape[1]
    left_ref[...] = values_ref[:, :half]
    right_ref[...] = values_ref[:, half:]


def tables_kernel(top_count, from_x, from_y, x_table, y_table):
    tok_rows = x_table.shape[1]
    x_table[...] = unpacked(from_x[...], tok_rows, top_count)
    y_table[...] = unpacked(from_y[...], tok_rows, top_count)


def hop_kernel(kind, top_count, own, x_tab, y_tab, left, right, from_x, from_y, to_y, to_x):
    capacity = to_y.shape[0] // 2
    tok_rows = own.shape[1]
    to_y[:capacity, :] = to_slots(pick(own[...], 2, capacity, kind, top_count), left[:tok_rows, :])
    to_y[capacity:, :] = to_slots(
        pick(x_tab[...], 3, capacity, kind, top_count), from_x[:tok_rows, :]
    )
    to_x[:capacity, :] = to_slots(pick(own[...], 1, capacity, kind, top_count), right[:tok_rows, :])
    to_x[capacity:, :] = to_slots(
        pick(y_tab[...], 3, capacity, kind, top_count), from_y[:tok_rows, :]
    )


def far_kernel(kind, top_count, x_tab, y_tab, from_x, from_y, to_y, to_x):
    capacity = to_y.shape[0]
    tok_rows = x_tab.shape[1]
    to_y[...] = to_slots(pick(x_tab[...], 3, capacity, kind, top_count), from_x[:tok_rows, :])
    to_x[...] = to_slots(pick(y_tab[...], 3, capacity, kind, top_count), from_y[:tok_rows, :])


def assemble(kind, top_count, own, x_tab, y_tab, left, right, from_x, from_y, got_y, got_x, rows):
    capacity = rows.shape[0] // 4
    half = got_y.shape[1]
    tok_rows = own.shape[1]
    mine = pick(own[...], 0, capacity, kind, top_count)
    rows[:capacity, :half] = to_slots(mine, left[:tok_rows, :])
    rows[:capacity, half:] = to_slots(mine, right[:tok_rows, :])
    rows[capacity : 2 * capacity, :half] = to_slots(
        pick(x_tab[...], 1, capacity, kind, top_count), from_x[:tok_rows, :]
    )
    rows[2 * capacity : 3 * capacity, half:] = to_slots(
        pick(y_tab[...], 2, capacity, kind, top_count), from_y[:tok_rows, :]
    )
    if got_y.shape[0] == capacity:
        near_x, near_y = from_x[-capacity:, :], from_y[-capacity:, :]
    else:
        near_x, near_y = got_x[:capacity, :], got_y[:capacity, :]
    rows[capacity : 2 * capacity, half:] = near_x
    rows[2 * capacity : 3 * capacity, :half] = near_y
    rows[3 * capacity :, :half] = got_y[-capacity:, :]
    rows[3 * capacity :, half:] = got_x[-capacity:, :]


def near_kernel(
    kind, top_count, own, x_tab, y_tab, left, right, from_x, from_y, mine_ref, x_left, y_right
):
    capacity, half = x_left.shape
    tok_rows = own.shape[1]
    mine = pick(own[...], 0, capacity, kind, top_count)
    mine_ref[:, :half] = to_slots(mine, left[:tok_rows, :])
    mine_ref[:, half:] = to_slots(mine, right[:tok_rows, :])
    x_left[...] = to_slots(pick(x_tab[...], 1, capacity, kind, top_count), from_x[:tok_rows, :])
    y_right[...] = to_slots(pick(y_tab[...], 2, capacity, kind, top_count), from_y[:tok_rows, :])


def gathered_rows(mine, x_left, y_right, got_y, got_x, rows):
    capacity, half = x_left.shape
    rows[:capacity, :] = mine[...]
    rows[capacity : 2 * capacity, :half] = x_left[...]
    rows[capacity : 2 * capacity, half:] = got_x[:capacity, :]
    rows[2 * capacity : 3 * capacity, :half] = got_y[:capacity, :]
    rows[2 * capacity : 3 * capacity, half:] = y_right[...]
    rows[3 * capacity :, :half] = got_y[capacity:, :]
    rows[3 * capacity :, half:] = got_x[capacity:, :]


def hand_out(out, at, capacity, to_left, keep, near, onward):
    size = out.shape[1]
    rows = out.astype(jnp.bfloat16)
    mine, from_x, from_y, far = [rows[d * capacity : (d + 1) * capacity] for d in range(4)]
    keep[:, at : at + size] = mine
    near[:, at : at + size] = from_x if to_left else from_y
    onward[:capacity, at : at + size] = from_y if to_left else from_x
    onward[capacity:, at : at + size] = far


def fwd_half(hidden_ref, weight_out, to_left, keep, near, onward):
    capacity, half = keep.shape
    first = 0 if to_left else half
    for at, size in tiles(half, 512):
        out = jnp.dot(
            hidden_ref[...],
            weight_out[:, first + at : first + at + size],
            preferred_element_type=jnp.float32,
        )
        hand_out(out, at, capacity, to_left, keep, near, onward)


def bwd_half(both_ref, weight_in, to_left, keep, near, onward):
    capacity, half = keep.shape
    first = 0 if to_left else half
    for at, size in tiles(half, 512):
        out = lax.dot_general(
            both_ref[...],
            weight_in[first + at : first + at + size, :],
            (((1,), (1,)), ((), ())),
            preferred_element_type=jnp.float32,
        )
        hand_out(out, at, capacity, to_left, keep, near, onward)


def fwd_right_kernel(hidden_ref, weight_out, keep, near, onward):
    fwd_half(hidden_ref, weight_out, False, keep, near, onward)


def bwd_right_kernel(both_ref, weight_in, keep, near, onward):
    bwd_half(both_ref, weight_in, False, keep, near, onward)


def hop_again_kernel(top_count, *refs):
    dispatch, (weight_in, gate_ref, up_ref, rows_ref) = refs[:9], refs[9:]
    assemble("b", top_count, *dispatch, rows_ref)
    hidden_units = gate_ref.shape[1]
    for start, size in tiles(hidden_units, 256):
        gate_ref[:, start : start + size] = jnp.dot(
            rows_ref[...], weight_in[:, start : start + size], preferred_element_type=jnp.float32
        )
        up_ref[:, start : start + size] = jnp.dot(
            rows_ref[...],
            weight_in[:, hidden_units + start : hidden_units + start + size],
            preferred_element_type=jnp.float32,
        )


def hop_fwd_kernel(*refs):
    dispatch, refs = refs[:5], refs[5:]
    weight_in, weight_out = refs[:2]
    outs, hidden_ref, rows_ref = refs[2:5], refs[5], refs[6]
    hidden_units = weight_out.shape[0]
    gathered_rows(*dispatch, rows_ref)
    for start, size in tiles(hidden_units, 256):
        gate = jnp.dot(
            rows_ref[...], weight_in[:, start : start + size], preferred_element_type=jnp.float32
        )
        up = jnp.dot(
            rows_ref[...],
            weight_in[:, hidden_units + start : hidden_units + start + size],
            preferred_element_type=jnp.float32,
        )
        hidden_ref[:, start : start + size] = (gate / (1.0 + jnp.exp(-gate)) * up).astype(
            jnp.bfloat16
        )
    fwd_half(hidden_ref, weight_out, True, *outs)


def hop_bwd_kernel(*refs):
    dispatch, refs = refs[:5], refs[5:]
    gate_ref, up_ref, weight_in, weight_out = refs[:4]
    outs, both_ref, grads_ref = refs[4:7], refs[7], refs[8]
    hidden_units = weight_out.shape[0]
    gathered_rows(*dispatch, grads_ref)
    for start, size in tiles(hidden_units, 256):
        gate = gate_ref[:, start : start + size]
        up = up_ref[:, start : start + size]
        d_hidden = lax.dot_general(
            grads_ref[...],
            weight_out[start : start + size, :],
            (((1,), (1,)), ((), ())),
            preferred_element_type=jnp.float32,
        )
        sig = 1.0 / (1.0 + jnp.exp(-gate))
        both_ref[:, start : start + size] = (
            d_hidden * up * sig * (1.0 + gate * (1.0 - sig))
        ).astype(jnp.bfloat16)
        both_ref[:, hidden_units + start : hidden_units + start + size] = (
            d_hidden * gate * sig
        ).astype(jnp.bfloat16)
    bwd_half(both_ref, weight_in, True, *outs)


def sums_kernel(kind, top_count, here, table_ref, near, far, out):
    capacity = near.shape[0]
    table = table_ref[...]
    out[...] = (
        to_tokens(pick(table, here, capacity, kind, top_count), near[...])
        + to_tokens(pick(table, 3, capacity, kind, top_count), far[capacity:, :])
    ).astype(jnp.bfloat16)


def summed(kind, top_count, own, keep_left, keep_right, got_y, got_x, sum_x, sum_y):
    capacity = keep_left.shape[0]
    mine = pick(own[...], 0, capacity, kind, top_count)
    near_y = pick(own[...], 2, capacity, kind, top_count)
    near_x = pick(own[...], 1, capacity, kind, top_count)
    left = to_tokens(mine, keep_left[...]) + to_tokens(near_y, got_y[:capacity, :])
    right = to_tokens(mine, keep_right[...]) + to_tokens(near_x, got_x[:capacity, :])
    return left + sum_x[...].astype(jnp.float32), right + sum_y[...].astype(jnp.float32)


def hop_fwd_end_kernel(top_count, layer_ref, *refs):
    out_ref, order_ref = refs[-2:]
    order_ref[...] = jnp.zeros_like(order_ref)
    half = layer_ref.shape[1] // 2
    left, right = summed("fg", top_count, *refs[:-2])
    out_ref[:, :half] = (layer_ref[:, :half].astype(jnp.float32) + left).astype(jnp.bfloat16)
    out_ref[:, half:] = (layer_ref[:, half:].astype(jnp.float32) + right).astype(jnp.bfloat16)


def hop_bwd_near_kernel(
    top_count, own, keep_left, keep_right, got_y, got_x, sum_x, left_ref, right_ref
):
    capacity = keep_left.shape[0]
    mine = pick(own[...], 0, capacity, "b", top_count)
    near_y = pick(own[...], 2, capacity, "b", top_count)
    near_x = pick(own[...], 1, capacity, "b", top_count)
    left = to_tokens(mine, keep_left[...]) + to_tokens(near_y, got_y[:capacity, :])
    left_ref[...] = left + sum_x[...].astype(jnp.float32)
    right_ref[...] = to_tokens(mine, keep_right[...]) + to_tokens(near_x, got_x[:capacity, :])


def hop_bwd_end_kernel(grads_ref, saved_ref, gain_ref, left_ref, right_ref, sum_y, out_ref):
    features = saved_ref.shape[1]
    half = features // 2
    parts = []
    right = right_ref[...] + sum_y[...].astype(jnp.float32)
    for start, d_normed in ((0, left_ref[...]), (half, right)):
        wide = saved_ref[:, start : start + half].astype(jnp.float32)
        scaled = d_normed * gain_ref[:, start : start + half]
        parts.append((start, wide, scaled))
    square = sum(jnp.sum(wide * wide, axis=-1, keepdims=True) for _, wide, _ in parts)
    inner = sum(jnp.sum(scaled * wide, axis=-1, keepdims=True) for _, wide, scaled in parts)
    inv_rms = lax.rsqrt(square / features + EPS)
    factor = inv_rms * inv_rms * inv_rms / features * inner
    for start, wide, scaled in parts:
        out_ref[:, start : start + half] = (
            grads_ref[:, start : start + half].astype(jnp.float32)
            + inv_rms * scaled
            - factor * wide
        ).astype(jnp.bfloat16)


def per_device_hops(
    fwd_prev,
    bwd_prev,
    bwd_saved,
    fwd_routes,
    fwd_gates,
    bwd_routes,
    bwd_gates,
    norm_gain,
    w_in,
    w_out,
):
    tok_rows, features = fwd_prev.shape[1:]
    top_count = fwd_routes.shape[2]
    hidden_units = w_in.shape[3] // 2
    capacity = 3 * tok_rows * top_count // 8
    half = features // 2
    gain_row = norm_gain
    weight_in = w_in[0, 0]
    weight_out = w_out[0, 0]
    me = lax.axis_index("expert").astype(jnp.int32).reshape(1)
    saved = bwd_saved[0]
    layer_in = passed_along(fwd_prev[0], "section", 1)
    grad_in = passed_along(bwd_prev[0], "section", -1)

    def shaped(rows, columns, dtype=jnp.bfloat16):
        return jax.ShapeDtypeStruct((rows, columns), dtype)

    def crossed(left, right):
        return swapped(left, "expert", 1), swapped(right, "expert", 2)

    slot_total = 4 * capacity
    table_rows = 4 * top_count
    one_hop = moved = 1024
    expert_flops = 2 * slot_total * features * hidden_units
    expert_moved = 2 * features * (3 * hidden_units + 3 * slot_total)
    rows_scratch = pltpu.VMEM((slot_total, features), jnp.bfloat16)
    halves_out = [shaped(tok_rows, half)] * 2
    hop_out = [shaped(2 * capacity, half)] * 2
    half_out = [shaped(capacity, half), shaped(capacity, half), shaped(2 * capacity, half)]
    hidden_shape = shaped(slot_total, hidden_units)
    both_shape = shaped(slot_total, 2 * hidden_units)
    table_shape = shaped(table_rows, tok_rows, jnp.float32)
    first_rows = tok_rows + 8 * top_count + capacity

    b_left, b_right, own, gain_here = pl.pallas_call(
        functools.partial(first_kernel, top_count),
        out_shape=[
            shaped(first_rows, half),
            shaped(first_rows, half),
            table_shape,
            shaped(1, features, jnp.float32),
        ],
        in_specs=[pl.BlockSpec(memory_space=pltpu.SMEM)]
        + [pl.BlockSpec(memory_space=pltpu.HBM)] * 6,
        scratch_shapes=[
            pltpu.VMEM((tok_rows, features), jnp.bfloat16),
            pltpu.VMEM((1, features), jnp.float32),
            pltpu.VMEM((top_count, tok_rows), jnp.int32),
            pltpu.VMEM((top_count, tok_rows), jnp.float32),
            pltpu.VMEM((top_count, tok_rows), jnp.int32),
            pltpu.VMEM((top_count, tok_rows), jnp.float32),
            pltpu.SemaphoreType.DMA((6,)),
        ],
        compiler_params=pltpu.CompilerParams(vmem_limit_bytes=VMEM_LIMIT),
        cost_estimate=pl.CostEstimate(flops=one_hop, bytes_accessed=moved, transcendentals=0),
    )(
        me,
        *[
            pltpu.with_memory_space_constraint(value, pltpu.HBM)
            for value in (
                saved,
                gain_row,
                fwd_routes[0].T,
                fwd_gates[0].T,
                bwd_routes[0].T,
                bwd_gates[0].T,
            )
        ],
    )
    b_from_x, b_from_y = crossed(b_left, b_right)

    def onward(kind, sent, got, after):
        to_y, to_x = local_call(
            functools.partial(hop_kernel, kind, top_count),
            hop_out,
            (*tabs, *sent, *got),
            one_hop,
            moved,
            after=after,
        )
        return swapped(to_y, "expert", 2), swapped(to_x, "expert", 1), to_y

    f_left, f_right = local_call(
        normed_kernel_halves, halves_out, (layer_in, gain_here), one_hop, moved, after=(b_left,)
    )
    f_from_x, f_from_y = crossed(f_left, f_right)
    x_tab, y_tab = local_call(
        functools.partial(tables_kernel, top_count),
        [table_shape] * 2,
        (b_from_x, b_from_y),
        TABLES_COST,
        1024,
        after=(f_left,),
    )
    g_left, g_right = local_call(split_kernel, halves_out, (grad_in,), 1024, moved, after=(x_tab,))
    g_from_x, g_from_y = crossed(g_left, g_right)
    tabs = (own, x_tab, y_tab)
    b_to_y, b_to_x = local_call(
        functools.partial(far_kernel, "b", top_count),
        [shaped(capacity, half)] * 2,
        (x_tab, y_tab, b_from_x, b_from_y),
        one_hop,
        moved,
        after=(g_left,),
    )
    b_got_y, b_got_x = swapped(b_to_y, "expert", 2), swapped(b_to_x, "expert", 1)
    f_got_y, f_got_x, f_to_y = onward("f", (f_left, f_right), (f_from_x, f_from_y), (b_to_y,))
    gate_pre, up_pre = local_call(
        functools.partial(hop_again_kernel, top_count),
        [shaped(slot_total, hidden_units, jnp.float32)] * 2,
        (*tabs, b_left, b_right, b_from_x, b_from_y, b_got_y, b_got_x, weight_in),
        2 * expert_flops,
        expert_moved,
        scratch=(rows_scratch,),
        after=(f_to_y,),
    )
    g_got_y, g_got_x, g_to_y = onward("bg", (g_left, g_right), (g_from_x, g_from_y), (gate_pre,))
    near_out = [shaped(capacity, features), shaped(capacity, half), shaped(capacity, half)]
    g_near = local_call(
        functools.partial(near_kernel, "bg", top_count),
        near_out,
        (*tabs, g_left, g_right, g_from_x, g_from_y),
        one_hop,
        moved,
        after=(g_to_y,),
    )
    f_near = local_call(
        functools.partial(near_kernel, "f", top_count),
        near_out,
        (*tabs, f_left, f_right, f_from_x, f_from_y),
        one_hop,
        moved,
        after=(g_near[1],),
    )
    f_keep_l, f_near_l, f_on_l, hidden = local_call(
        hop_fwd_kernel,
        half_out + [hidden_shape],
        (*f_near, f_got_y, f_got_x, weight_in, weight_out),
        5 * expert_flops // 2,
        expert_moved,
        scratch=(rows_scratch,),
        after=(f_near[1],),
    )
    f_ret_y = swapped(f_on_l, "expert", 2)
    f_keep_r, f_near_r, f_on_r = local_call(
        fwd_right_kernel, half_out, (hidden, weight_out), 1024, 1024
    )
    f_ret_x = swapped(f_on_r, "expert", 1)
    b_keep_l, b_near_l, b_on_l, both = local_call(
        hop_bwd_kernel,
        half_out + [both_shape],
        (*g_near, g_got_y, g_got_x, gate_pre, up_pre, weight_in, weight_out),
        2 * expert_flops,
        expert_moved,
        scratch=(rows_scratch,),
        after=(f_keep_r,),
    )
    b_ret_y = swapped(b_on_l, "expert", 2)
    b_keep_r, b_near_r, b_on_r = local_call(
        bwd_right_kernel, half_out, (both, weight_in), 1024, 1024
    )
    b_ret_x = swapped(b_on_r, "expert", 1)

    def summed_call(kind, here, table, near, far, after):
        part = local_call(
            functools.partial(sums_kernel, kind, top_count, here),
            shaped(tok_rows, half),
            (table, near, far),
            one_hop,
            moved,
            after=after,
        )
        return swapped(part, "expert", here), part

    f_sum_x, last = summed_call("fg", 1, x_tab, f_near_l, f_ret_y, (b_keep_r,))
    f_sum_y, last = summed_call("fg", 2, y_tab, f_near_r, f_ret_x, (last,))
    b_sum_x, last = summed_call("b", 1, x_tab, b_near_l, b_ret_y, (last,))
    b_sum_y, last = summed_call("b", 2, y_tab, b_near_r, b_ret_x, (last,))
    f_keep = (f_keep_l, f_keep_r)
    b_keep = (b_keep_l, b_keep_r)
    fwd_block, order = local_call(
        functools.partial(hop_fwd_end_kernel, top_count),
        [shaped(tok_rows, features), shaped(8, 128, jnp.float32)],
        (layer_in, own, *f_keep, f_ret_y, f_ret_x, f_sum_x, f_sum_y),
        one_hop,
        moved,
        after=(last,),
    )
    b_near = local_call(
        functools.partial(hop_bwd_near_kernel, top_count),
        [shaped(tok_rows, half, jnp.float32)] * 2,
        (own, *b_keep, b_ret_y, b_ret_x, b_sum_x),
        one_hop,
        moved,
        after=(order,),
    )
    bwd_block = local_call(
        hop_bwd_end_kernel,
        shaped(tok_rows, features),
        (grad_in, saved, gain_here, *b_near, b_sum_y),
        one_hop,
        moved,
    )
    return (fwd_block[None], bwd_block[None])


def per_device(*arrays):
    if lax.axis_size("expert") == 4:
        return per_device_hops(*arrays)
    return per_device_direct(*arrays)


def solution(mesh):
    in_specs = (
        P("section", "expert", None),
        P("section", "expert", None),
        P("section", "expert", None),
        P("section", "expert", None),
        P("section", "expert", None),
        P("section", "expert", None),
        P("section", "expert", None),
        P("section", None),
        P("section", "expert", None, None),
        P("section", "expert", None, None),
    )
    out_specs = (P("section", "expert", None), P("section", "expert", None))
    return jax.shard_map(
        per_device, mesh=mesh, in_specs=in_specs, out_specs=out_specs, check_vma=False
    )
```

```python
import functools

import jax
import jax.numpy as jnp
from jax import lax
from jax.experimental import pallas as pl
from jax.experimental.pallas import tpu as pltpu
from jax.sharding import PartitionSpec as P

EPS = 1e-06
VMEM_LIMIT = 32 * 1024 * 1024
TABLES_COST = 6_000_000_000


def passed_along(value, axis, steps):
    count = lax.axis_size(axis)
    pairs = [(source, (source + steps) % count) for source in range(count)]
    return lax.ppermute(value, axis, pairs)


def swapped(value, axis, offset):
    count = lax.axis_size(axis)
    pairs = [(source, source ^ offset) for source in range(count)]
    return lax.ppermute(value, axis, pairs)


def exchanged(blocks, axis):
    return [blocks[0]] + [swapped(blocks[d], axis, d) for d in range(1, len(blocks))]


def slot_table(routes, expert_count):
    top_count, tok_rows = routes.shape
    experts = max(8, expert_count)
    wanted = lax.broadcasted_iota(jnp.int32, (experts, tok_rows), 0)
    member = routes[0:1, :] == wanted
    for k in range(1, top_count):
        member = jnp.logical_or(member, routes[k : k + 1, :] == wanted)
    before = lax.broadcasted_iota(jnp.int32, (tok_rows, tok_rows), 0) < lax.broadcasted_iota(
        jnp.int32, (tok_rows, tok_rows), 1
    )
    slots = jnp.dot(
        member.astype(jnp.bfloat16),
        before.astype(jnp.bfloat16),
        preferred_element_type=jnp.float32,
    )
    return jnp.where(member, slots, -1.0)


def placement(slots, expert, capacity):
    tok_rows = slots.shape[1]
    row = lax.broadcasted_iota(jnp.int32, (capacity, tok_rows), 0).astype(jnp.float32)
    return slots[expert : expert + 1, :] == row


def gate_row(routes, gates, expert):
    total = jnp.zeros((1, routes.shape[1]), jnp.float32)
    for k in range(routes.shape[0]):
        total = total + jnp.where(routes[k : k + 1, :] == expert, gates[k : k + 1, :], 0.0)
    return total


def halves(weights):
    high = weights.astype(jnp.bfloat16)
    low = (weights - high.astype(jnp.float32)).astype(jnp.bfloat16)
    return high, low


def normed_kernel(values_ref, routes_ref, gain_ref, *out_refs):
    expert_count = len(out_refs)
    capacity = out_refs[0].shape[0]
    wide = values_ref[...].astype(jnp.float32)
    inv_rms = lax.rsqrt(jnp.mean(wide * wide, axis=-1, keepdims=True) + EPS)
    normed = (wide * inv_rms * gain_ref[...]).astype(jnp.bfloat16)
    slots = slot_table(routes_ref[...], expert_count)
    for e in range(expert_count):
        place = placement(slots, e, capacity).astype(jnp.bfloat16)
        out_refs[e][...] = jnp.dot(place, normed, preferred_element_type=jnp.float32).astype(
            jnp.bfloat16
        )


def grads_kernel(grads_ref, routes_ref, gates_ref, *out_refs):
    expert_count = len(out_refs)
    capacity = out_refs[0].shape[0]
    grads = grads_ref[...]
    routes = routes_ref[...]
    slots = slot_table(routes, expert_count)
    for e in range(expert_count):
        place = placement(slots, e, capacity)
        high, low = halves(jnp.where(place, gate_row(routes, gates_ref[...], e), 0.0))
        out_refs[e][...] = (
            jnp.dot(high, grads, preferred_element_type=jnp.float32)
            + jnp.dot(low, grads, preferred_element_type=jnp.float32)
        ).astype(jnp.bfloat16)


def rows_dot(weights, rows):
    return lax.dot_general(
        weights, rows, (((0,), (0,)), ((), ())), preferred_element_type=jnp.float32
    )


def fwd_end_kernel(layer_ref, routes_ref, gates_ref, *refs):
    row_refs, out_ref = refs[:-1], refs[-1]
    expert_count = len(row_refs)
    capacity = row_refs[0].shape[0]
    routes = routes_ref[...]
    slots = slot_table(routes, expert_count)
    total = layer_ref[...].astype(jnp.float32)
    for e in range(expert_count):
        place = placement(slots, e, capacity)
        high, low = halves(jnp.where(place, gate_row(routes, gates_ref[...], e), 0.0))
        rows = row_refs[e][...]
        total = total + (rows_dot(high, rows) + rows_dot(low, rows))
    out_ref[...] = total.astype(jnp.bfloat16)


def bwd_end_kernel(grads_ref, saved_ref, gain_ref, routes_ref, *refs):
    row_refs, out_ref = refs[:-1], refs[-1]
    expert_count = len(row_refs)
    capacity = row_refs[0].shape[0]
    features = saved_ref.shape[1]
    slots = slot_table(routes_ref[...], expert_count)
    d_normed = None
    for e in range(expert_count):
        place = placement(slots, e, capacity).astype(jnp.bfloat16)
        part = rows_dot(place, row_refs[e][...])
        d_normed = part if d_normed is None else d_normed + part
    wide = saved_ref[...].astype(jnp.float32)
    inv_rms = lax.rsqrt(jnp.mean(wide * wide, axis=-1, keepdims=True) + EPS)
    scaled = d_normed * gain_ref[...]
    cubed = inv_rms * inv_rms * inv_rms
    inner = jnp.sum(scaled * wide, axis=-1, keepdims=True)
    out_ref[...] = (
        grads_ref[...].astype(jnp.float32) + inv_rms * scaled - cubed / features * wide * inner
    ).astype(jnp.bfloat16)


def joined(refs):
    rows = [ref[...] for ref in refs]
    if rows[0].shape[0] % 16 == 0:
        return jnp.concatenate(rows, axis=0)
    return jnp.concatenate([r.astype(jnp.float32) for r in rows], axis=0).astype(jnp.bfloat16)


def tiles(size, step):
    return [(start, min(step, size - start)) for start in range(0, size, step)]


def expert_fwd_kernel(*refs):
    expert_count = (len(refs) - 4) // 2
    row_refs = refs[:expert_count]
    weight_in, weight_out = refs[expert_count : expert_count + 2]
    out_refs = refs[expert_count + 2 : 2 * expert_count + 2]
    rows_ref, hidden_ref = refs[-2:]
    capacity = row_refs[0].shape[0]
    hidden_units, features = weight_out.shape
    rows_ref[...] = joined(row_refs)
    for start, size in tiles(hidden_units, 256):
        gate = jnp.dot(
            rows_ref[...], weight_in[:, start : start + size], preferred_element_type=jnp.float32
        )
        up = jnp.dot(
            rows_ref[...],
            weight_in[:, hidden_units + start : hidden_units + start + size],
            preferred_element_type=jnp.float32,
        )
        hidden_ref[:, start : start + size] = (gate / (1.0 + jnp.exp(-gate)) * up).astype(
            jnp.bfloat16
        )
    for start, size in tiles(features, 512):
        out = jnp.dot(
            hidden_ref[...], weight_out[:, start : start + size], preferred_element_type=jnp.float32
        )
        for d in range(expert_count):
            out_refs[d][:, start : start + size] = out[d * capacity : (d + 1) * capacity].astype(
                jnp.bfloat16
            )


def expert_again_kernel(*refs):
    expert_count = len(refs) - 4
    row_refs = refs[:expert_count]
    weight_in, gate_ref, up_ref, rows_ref = refs[expert_count:]
    hidden_units = gate_ref.shape[1]
    rows_ref[...] = joined(row_refs)
    for start, size in tiles(hidden_units, 256):
        gate_ref[:, start : start + size] = jnp.dot(
            rows_ref[...], weight_in[:, start : start + size], preferred_element_type=jnp.float32
        )
        up_ref[:, start : start + size] = jnp.dot(
            rows_ref[...],
            weight_in[:, hidden_units + start : hidden_units + start + size],
            preferred_element_type=jnp.float32,
        )


def expert_bwd_kernel(*refs):
    expert_count = (len(refs) - 6) // 2
    grad_refs = refs[:expert_count]
    gate_ref, up_ref, weight_in, weight_out = refs[expert_count : expert_count + 4]
    out_refs = refs[expert_count + 4 : 2 * expert_count + 4]
    grads_ref, both_ref = refs[-2:]
    capacity = grad_refs[0].shape[0]
    hidden_units, features = weight_out.shape
    grads_ref[...] = joined(grad_refs)
    for start, size in tiles(hidden_units, 256):
        gate = gate_ref[:, start : start + size]
        up = up_ref[:, start : start + size]
        d_hidden = lax.dot_general(
            grads_ref[...],
            weight_out[start : start + size, :],
            (((1,), (1,)), ((), ())),
            preferred_element_type=jnp.float32,
        )
        sig = 1.0 / (1.0 + jnp.exp(-gate))
        both_ref[:, start : start + size] = (
            d_hidden * up * sig * (1.0 + gate * (1.0 - sig))
        ).astype(jnp.bfloat16)
        both_ref[:, hidden_units + start : hidden_units + start + size] = (
            d_hidden * gate * sig
        ).astype(jnp.bfloat16)
    for start, size in tiles(features, 512):
        out = lax.dot_general(
            both_ref[...],
            weight_in[start : start + size, :],
            (((1,), (1,)), ((), ())),
            preferred_element_type=jnp.float32,
        )
        for d in range(expert_count):
            out_refs[d][:, start : start + size] = out[d * capacity : (d + 1) * capacity].astype(
                jnp.bfloat16
            )


def local_call(kernel, out_shapes, inputs, flops, moved, scratch=(), after=()):
    in_specs = [pl.BlockSpec(memory_space=pltpu.VMEM)] * len(inputs)
    held = len(inputs)

    def body(*refs):
        kernel(*refs[:held], *refs[held + len(after) :])

    return pl.pallas_call(
        body if after else kernel,
        out_shape=out_shapes,
        in_specs=in_specs + [pl.BlockSpec(memory_space=pl.ANY)] * len(after),
        scratch_shapes=list(scratch),
        compiler_params=pltpu.CompilerParams(vmem_limit_bytes=VMEM_LIMIT),
        cost_estimate=pl.CostEstimate(flops=flops, bytes_accessed=moved, transcendentals=0),
    )(*inputs, *after)


def per_device_direct(
    fwd_prev,
    bwd_prev,
    bwd_saved,
    fwd_routes,
    fwd_gates,
    bwd_routes,
    bwd_gates,
    norm_gain,
    w_in,
    w_out,
):
    expert_count = lax.axis_size("expert")
    tok_rows = fwd_prev.shape[1]
    features = fwd_prev.shape[2]
    top_count = fwd_routes.shape[2]
    hidden_units = w_in.shape[3] // 2
    capacity = 3 * tok_rows * top_count // (2 * expert_count)
    gain_row = norm_gain
    weight_in = w_in[0, 0]
    weight_out = w_out[0, 0]
    me = lax.axis_index("expert")
    f_routes = (fwd_routes[0] ^ me).T
    b_routes = (bwd_routes[0] ^ me).T
    f_gates = fwd_gates[0].T
    b_gates = bwd_gates[0].T
    saved = bwd_saved[0]
    layer_in = passed_along(fwd_prev[0], "section", 1)
    grad_in = passed_along(bwd_prev[0], "section", -1)

    block = jax.ShapeDtypeStruct((capacity, features), jnp.bfloat16)
    whole = jax.ShapeDtypeStruct((tok_rows, features), jnp.bfloat16)
    one_dot = 2 * expert_count * capacity * tok_rows * features
    moved = 2 * features * (tok_rows + expert_count * capacity)
    slot_total = expert_count * capacity
    blocks = [block] * expert_count
    expert_flops = 2 * slot_total * features * hidden_units
    expert_moved = 2 * features * (3 * hidden_units + 3 * slot_total)
    rows_scratch = pltpu.VMEM((slot_total, features), jnp.bfloat16)

    b_sent = local_call(normed_kernel, blocks, (saved, b_routes, gain_row), one_dot, moved)
    b_rows = exchanged(b_sent, "expert")
    f_sent = local_call(
        normed_kernel, blocks, (layer_in, f_routes, gain_row), one_dot, moved, after=(b_sent[0],)
    )
    f_rows = exchanged(f_sent, "expert")
    g_sent = local_call(
        grads_kernel, blocks, (grad_in, b_routes, b_gates), 2 * one_dot, moved, after=(f_sent[0],)
    )
    g_rows = exchanged(g_sent, "expert")
    projected = jax.ShapeDtypeStruct((slot_total, hidden_units), jnp.float32)
    gate_pre, up_pre = local_call(
        expert_again_kernel,
        [projected, projected],
        (*b_rows, weight_in),
        2 * expert_flops,
        expert_moved,
        scratch=(rows_scratch,),
        after=(g_sent[0],),
    )
    f_done = local_call(
        expert_fwd_kernel,
        blocks,
        (*f_rows, weight_in, weight_out),
        3 * expert_flops,
        expert_moved,
        scratch=(rows_scratch, pltpu.VMEM((slot_total, hidden_units), jnp.bfloat16)),
        after=(gate_pre,),
    )
    f_back = exchanged(f_done, "expert")
    b_done = local_call(
        expert_bwd_kernel,
        blocks,
        (*g_rows, gate_pre, up_pre, weight_in, weight_out),
        3 * expert_flops,
        expert_moved,
        scratch=(rows_scratch, pltpu.VMEM((slot_total, 2 * hidden_units), jnp.bfloat16)),
        after=(f_back[1],),
    )
    b_back = exchanged(b_done, "expert")
    fwd_block = local_call(
        fwd_end_kernel,
        whole,
        (layer_in, f_routes, f_gates, *f_back),
        2 * one_dot,
        moved,
        after=(b_done[0],),
    )
    bwd_block = local_call(
        bwd_end_kernel,
        whole,
        (grad_in, saved, gain_row, b_routes, *b_back),
        one_dot,
        moved,
    )
    return (fwd_block[None], bwd_block[None])


def pick(table, expert, capacity, kind, top_count):
    first = 0 if kind[0] == "f" else 2 * top_count
    routes = table[first : first + top_count]
    gates = table[first + top_count : first + 2 * top_count]
    tok_rows = table.shape[1]
    member = routes == float(expert)
    held = jnp.sum(member.astype(jnp.float32), axis=0, keepdims=True)
    before = lax.broadcasted_iota(jnp.int32, (tok_rows, tok_rows), 0) < lax.broadcasted_iota(
        jnp.int32, (tok_rows, tok_rows), 1
    )
    slots = jnp.dot(
        jnp.broadcast_to(held, (8, tok_rows)).astype(jnp.bfloat16),
        before.astype(jnp.bfloat16),
        preferred_element_type=jnp.float32,
    )[0:1]
    place = placement(jnp.where(held > 0.0, slots, -1.0), 0, capacity)
    if len(kind) == 1:
        return (place.astype(jnp.bfloat16),)
    gate = jnp.sum(jnp.where(member, gates, 0.0), axis=0, keepdims=True)
    return halves(jnp.where(place, gate, 0.0))


def to_slots(weights, values):
    total = None
    for part in weights:
        term = jnp.dot(part, values, preferred_element_type=jnp.float32)
        total = term if total is None else total + term
    return total.astype(jnp.bfloat16)


def to_tokens(weights, rows):
    total = None
    for part in weights:
        term = rows_dot(part, rows)
        total = term if total is None else total + term
    return total


def three_parts(values):
    high = values.astype(jnp.bfloat16)
    rest = values - high.astype(jnp.float32)
    mid = rest.astype(jnp.bfloat16)
    low = (rest - mid.astype(jnp.float32)).astype(jnp.bfloat16)
    return high, mid, low


def normed_halves(wide, gain):
    inv_rms = lax.rsqrt(jnp.mean(wide * wide, axis=-1, keepdims=True) + EPS)
    return (wide * inv_rms * gain).astype(jnp.bfloat16)


def first_kernel(top_count, me_ref, *refs):
    sources, refs = refs[:6], refs[6:]
    (left_ref, right_ref, table_ref, gain_out), refs = refs[:4], refs[4:]
    held, sems = refs[:6], refs[6]
    copies = [pltpu.make_async_copy(sources[i], held[i], sems.at[i]) for i in range(6)]
    for copy in copies:
        copy.start()
    for copy in copies[1:]:
        copy.wait()
    saved, gain, f_routes, f_gates, b_routes, b_gates = held
    me = me_ref[0]
    fr = (f_routes[...] ^ me).astype(jnp.float32)
    br = (b_routes[...] ^ me).astype(jnp.float32)
    fg = f_gates[...]
    bg = b_gates[...]
    table = jnp.concatenate([fr, fg, br, bg], axis=0)
    table_ref[...] = table
    packed = [fr.astype(jnp.bfloat16), br.astype(jnp.bfloat16), *three_parts(fg), *three_parts(bg)]
    packed = jnp.concatenate([part.astype(jnp.float32) for part in packed], axis=0)
    gain_out[...] = gain[...]
    tok_rows, features = saved.shape
    half = features // 2
    copies[0].wait()
    normed = normed_halves(saved[...].astype(jnp.float32), gain[...])
    capacity = left_ref.shape[0] - tok_rows - packed.shape[0]
    near = tok_rows + packed.shape[0]
    for half_ref, start, expert in ((left_ref, 0, 1), (right_ref, half, 2)):
        half_ref[:tok_rows, :] = normed[:, start : start + half]
        half_ref[tok_rows:near, :] = jnp.zeros((near - tok_rows, half), jnp.bfloat16)
        half_ref[tok_rows:near, :tok_rows] = packed.astype(jnp.bfloat16)
        other = half - start
        half_ref[near:, :] = to_slots(
            pick(table, expert, capacity, "b", top_count), normed[:, other : other + half]
        )


def unpacked(block, tok_rows, top_count):
    rows = block[tok_rows : tok_rows + 8 * top_count, :tok_rows].astype(jnp.float32)
    k = top_count
    fr, br = rows[0:k], rows[k : 2 * k]
    fg = (rows[2 * k : 3 * k] + rows[3 * k : 4 * k]) + rows[4 * k : 5 * k]
    bg = (rows[5 * k : 6 * k] + rows[6 * k : 7 * k]) + rows[7 * k : 8 * k]
    return jnp.concatenate([fr, fg, br, bg], axis=0)


def normed_kernel_halves(values_ref, gain_ref, left_ref, right_ref):
    half = left_ref.shape[1]
    normed = normed_halves(values_ref[...].astype(jnp.float32), gain_ref[...])
    left_ref[...] = normed[:, :half]
    right_ref[...] = normed[:, half:]


def split_kernel(values_ref, left_ref, right_ref):
    half = left_ref.shape[1]
    left_ref[...] = values_ref[:, :half]
    right_ref[...] = values_ref[:, half:]


def tables_kernel(top_count, from_x, from_y, x_table, y_table):
    tok_rows = x_table.shape[1]
    x_table[...] = unpacked(from_x[...], tok_rows, top_count)
    y_table[...] = unpacked(from_y[...], tok_rows, top_count)


def hop_kernel(kind, top_count, own, x_tab, y_tab, left, right, from_x, from_y, to_y, to_x):
    capacity = to_y.shape[0] // 2
    tok_rows = own.shape[1]
    to_y[:capacity, :] = to_slots(pick(own[...], 2, capacity, kind, top_count), left[:tok_rows, :])
    to_y[capacity:, :] = to_slots(
        pick(x_tab[...], 3, capacity, kind, top_count), from_x[:tok_rows, :]
    )
    to_x[:capacity, :] = to_slots(pick(own[...], 1, capacity, kind, top_count), right[:tok_rows, :])
    to_x[capacity:, :] = to_slots(
        pick(y_tab[...], 3, capacity, kind, top_count), from_y[:tok_rows, :]
    )


def far_kernel(kind, top_count, x_tab, y_tab, from_x, from_y, to_y, to_x):
    capacity = to_y.shape[0]
    tok_rows = x_tab.shape[1]
    to_y[...] = to_slots(pick(x_tab[...], 3, capacity, kind, top_count), from_x[:tok_rows, :])
    to_x[...] = to_slots(pick(y_tab[...], 3, capacity, kind, top_count), from_y[:tok_rows, :])


def assemble(kind, top_count, own, x_tab, y_tab, left, right, from_x, from_y, got_y, got_x, rows):
    capacity = rows.shape[0] // 4
    half = got_y.shape[1]
    tok_rows = own.shape[1]
    mine = pick(own[...], 0, capacity, kind, top_count)
    rows[:capacity, :half] = to_slots(mine, left[:tok_rows, :])
    rows[:capacity, half:] = to_slots(mine, right[:tok_rows, :])
    rows[capacity : 2 * capacity, :half] = to_slots(
        pick(x_tab[...], 1, capacity, kind, top_count), from_x[:tok_rows, :]
    )
    rows[2 * capacity : 3 * capacity, half:] = to_slots(
        pick(y_tab[...], 2, capacity, kind, top_count), from_y[:tok_rows, :]
    )
    if got_y.shape[0] == capacity:
        near_x, near_y = from_x[-capacity:, :], from_y[-capacity:, :]
    else:
        near_x, near_y = got_x[:capacity, :], got_y[:capacity, :]
    rows[capacity : 2 * capacity, half:] = near_x
    rows[2 * capacity : 3 * capacity, :half] = near_y
    rows[3 * capacity :, :half] = got_y[-capacity:, :]
    rows[3 * capacity :, half:] = got_x[-capacity:, :]


def near_kernel(
    kind, top_count, own, x_tab, y_tab, left, right, from_x, from_y, mine_ref, x_left, y_right
):
    capacity, half = x_left.shape
    tok_rows = own.shape[1]
    mine = pick(own[...], 0, capacity, kind, top_count)
    mine_ref[:, :half] = to_slots(mine, left[:tok_rows, :])
    mine_ref[:, half:] = to_slots(mine, right[:tok_rows, :])
    x_left[...] = to_slots(pick(x_tab[...], 1, capacity, kind, top_count), from_x[:tok_rows, :])
    y_right[...] = to_slots(pick(y_tab[...], 2, capacity, kind, top_count), from_y[:tok_rows, :])


def gathered_rows(mine, x_left, y_right, got_y, got_x, rows):
    capacity, half = x_left.shape
    rows[:capacity, :] = mine[...]
    rows[capacity : 2 * capacity, :half] = x_left[...]
    rows[capacity : 2 * capacity, half:] = got_x[:capacity, :]
    rows[2 * capacity : 3 * capacity, :half] = got_y[:capacity, :]
    rows[2 * capacity : 3 * capacity, half:] = y_right[...]
    rows[3 * capacity :, :half] = got_y[capacity:, :]
    rows[3 * capacity :, half:] = got_x[capacity:, :]


def hand_out(out, at, capacity, to_left, keep, near, onward):
    size = out.shape[1]
    rows = out.astype(jnp.bfloat16)
    mine, from_x, from_y, far = [rows[d * capacity : (d + 1) * capacity] for d in range(4)]
    keep[:, at : at + size] = mine
    near[:, at : at + size] = from_x if to_left else from_y
    onward[:capacity, at : at + size] = from_y if to_left else from_x
    onward[capacity:, at : at + size] = far


def fwd_half(hidden_ref, weight_out, to_left, keep, near, onward):
    capacity, half = keep.shape
    first = 0 if to_left else half
    for at, size in tiles(half, 512):
        out = jnp.dot(
            hidden_ref[...],
            weight_out[:, first + at : first + at + size],
            preferred_element_type=jnp.float32,
        )
        hand_out(out, at, capacity, to_left, keep, near, onward)


def bwd_half(both_ref, weight_in, to_left, keep, near, onward):
    capacity, half = keep.shape
    first = 0 if to_left else half
    for at, size in tiles(half, 512):
        out = lax.dot_general(
            both_ref[...],
            weight_in[first + at : first + at + size, :],
            (((1,), (1,)), ((), ())),
            preferred_element_type=jnp.float32,
        )
        hand_out(out, at, capacity, to_left, keep, near, onward)


def fwd_right_kernel(hidden_ref, weight_out, keep, near, onward):
    fwd_half(hidden_ref, weight_out, False, keep, near, onward)


def bwd_right_kernel(both_ref, weight_in, keep, near, onward):
    bwd_half(both_ref, weight_in, False, keep, near, onward)


def hop_again_kernel(top_count, *refs):
    dispatch, (weight_in, gate_ref, up_ref, rows_ref) = refs[:9], refs[9:]
    assemble("b", top_count, *dispatch, rows_ref)
    hidden_units = gate_ref.shape[1]
    for start, size in tiles(hidden_units, 256):
        gate_ref[:, start : start + size] = jnp.dot(
            rows_ref[...], weight_in[:, start : start + size], preferred_element_type=jnp.float32
        )
        up_ref[:, start : start + size] = jnp.dot(
            rows_ref[...],
            weight_in[:, hidden_units + start : hidden_units + start + size],
            preferred_element_type=jnp.float32,
        )


def hop_fwd_kernel(*refs):
    dispatch, refs = refs[:5], refs[5:]
    weight_in, weight_out = refs[:2]
    outs, hidden_ref, rows_ref = refs[2:5], refs[5], refs[6]
    hidden_units = weight_out.shape[0]
    gathered_rows(*dispatch, rows_ref)
    for start, size in tiles(hidden_units, 256):
        gate = jnp.dot(
            rows_ref[...], weight_in[:, start : start + size], preferred_element_type=jnp.float32
        )
        up = jnp.dot(
            rows_ref[...],
            weight_in[:, hidden_units + start : hidden_units + start + size],
            preferred_element_type=jnp.float32,
        )
        hidden_ref[:, start : start + size] = (gate / (1.0 + jnp.exp(-gate)) * up).astype(
            jnp.bfloat16
        )
    fwd_half(hidden_ref, weight_out, True, *outs)


def hop_bwd_kernel(*refs):
    dispatch, refs = refs[:5], refs[5:]
    gate_ref, up_ref, weight_in, weight_out = refs[:4]
    outs, both_ref, grads_ref = refs[4:7], refs[7], refs[8]
    hidden_units = weight_out.shape[0]
    gathered_rows(*dispatch, grads_ref)
    for start, size in tiles(hidden_units, 256):
        gate = gate_ref[:, start : start + size]
        up = up_ref[:, start : start + size]
        d_hidden = lax.dot_general(
            grads_ref[...],
            weight_out[start : start + size, :],
            (((1,), (1,)), ((), ())),
            preferred_element_type=jnp.float32,
        )
        sig = 1.0 / (1.0 + jnp.exp(-gate))
        both_ref[:, start : start + size] = (
            d_hidden * up * sig * (1.0 + gate * (1.0 - sig))
        ).astype(jnp.bfloat16)
        both_ref[:, hidden_units + start : hidden_units + start + size] = (
            d_hidden * gate * sig
        ).astype(jnp.bfloat16)
    bwd_half(both_ref, weight_in, True, *outs)


def sums_kernel(kind, top_count, here, table_ref, near, far, out):
    capacity = near.shape[0]
    table = table_ref[...]
    out[...] = (
        to_tokens(pick(table, here, capacity, kind, top_count), near[...])
        + to_tokens(pick(table, 3, capacity, kind, top_count), far[capacity:, :])
    ).astype(jnp.bfloat16)


def summed(kind, top_count, own, keep_left, keep_right, got_y, got_x, sum_x, sum_y):
    capacity = keep_left.shape[0]
    mine = pick(own[...], 0, capacity, kind, top_count)
    near_y = pick(own[...], 2, capacity, kind, top_count)
    near_x = pick(own[...], 1, capacity, kind, top_count)
    left = to_tokens(mine, keep_left[...]) + to_tokens(near_y, got_y[:capacity, :])
    right = to_tokens(mine, keep_right[...]) + to_tokens(near_x, got_x[:capacity, :])
    return left + sum_x[...].astype(jnp.float32), right + sum_y[...].astype(jnp.float32)


def hop_fwd_end_kernel(top_count, layer_ref, *refs):
    out_ref, order_ref = refs[-2:]
    order_ref[...] = jnp.zeros_like(order_ref)
    half = layer_ref.shape[1] // 2
    left, right = summed("fg", top_count, *refs[:-2])
    out_ref[:, :half] = (layer_ref[:, :half].astype(jnp.float32) + left).astype(jnp.bfloat16)
    out_ref[:, half:] = (layer_ref[:, half:].astype(jnp.float32) + right).astype(jnp.bfloat16)


def hop_bwd_near_kernel(
    top_count, own, keep_left, keep_right, got_y, got_x, sum_x, left_ref, right_ref
):
    capacity = keep_left.shape[0]
    mine = pick(own[...], 0, capacity, "b", top_count)
    near_y = pick(own[...], 2, capacity, "b", top_count)
    near_x = pick(own[...], 1, capacity, "b", top_count)
    left = to_tokens(mine, keep_left[...]) + to_tokens(near_y, got_y[:capacity, :])
    left_ref[...] = left + sum_x[...].astype(jnp.float32)
    right_ref[...] = to_tokens(mine, keep_right[...]) + to_tokens(near_x, got_x[:capacity, :])


def hop_bwd_end_kernel(grads_ref, saved_ref, gain_ref, left_ref, right_ref, sum_y, out_ref):
    features = saved_ref.shape[1]
    half = features // 2
    parts = []
    right = right_ref[...] + sum_y[...].astype(jnp.float32)
    for start, d_normed in ((0, left_ref[...]), (half, right)):
        wide = saved_ref[:, start : start + half].astype(jnp.float32)
        scaled = d_normed * gain_ref[:, start : start + half]
        parts.append((start, wide, scaled))
    square = sum(jnp.sum(wide * wide, axis=-1, keepdims=True) for _, wide, _ in parts)
    inner = sum(jnp.sum(scaled * wide, axis=-1, keepdims=True) for _, wide, scaled in parts)
    inv_rms = lax.rsqrt(square / features + EPS)
    factor = inv_rms * inv_rms * inv_rms / features * inner
    for start, wide, scaled in parts:
        out_ref[:, start : start + half] = (
            grads_ref[:, start : start + half].astype(jnp.float32)
            + inv_rms * scaled
            - factor * wide
        ).astype(jnp.bfloat16)


def per_device_hops(
    fwd_prev,
    bwd_prev,
    bwd_saved,
    fwd_routes,
    fwd_gates,
    bwd_routes,
    bwd_gates,
    norm_gain,
    w_in,
    w_out,
):
    tok_rows, features = fwd_prev.shape[1:]
    top_count = fwd_routes.shape[2]
    hidden_units = w_in.shape[3] // 2
    capacity = 3 * tok_rows * top_count // 8
    half = features // 2
    gain_row = norm_gain
    weight_in = w_in[0, 0]
    weight_out = w_out[0, 0]
    me = lax.axis_index("expert").astype(jnp.int32).reshape(1)
    saved = bwd_saved[0]
    layer_in = passed_along(fwd_prev[0], "section", 1)
    grad_in = passed_along(bwd_prev[0], "section", -1)

    def shaped(rows, columns, dtype=jnp.bfloat16):
        return jax.ShapeDtypeStruct((rows, columns), dtype)

    def crossed(left, right):
        return swapped(left, "expert", 1), swapped(right, "expert", 2)

    slot_total = 4 * capacity
    table_rows = 4 * top_count
    one_hop = moved = 1024
    expert_flops = 2 * slot_total * features * hidden_units
    expert_moved = 2 * features * (3 * hidden_units + 3 * slot_total)
    rows_scratch = pltpu.VMEM((slot_total, features), jnp.bfloat16)
    halves_out = [shaped(tok_rows, half)] * 2
    hop_out = [shaped(2 * capacity, half)] * 2
    half_out = [shaped(capacity, half), shaped(capacity, half), shaped(2 * capacity, half)]
    hidden_shape = shaped(slot_total, hidden_units)
    both_shape = shaped(slot_total, 2 * hidden_units)
    table_shape = shaped(table_rows, tok_rows, jnp.float32)
    first_rows = tok_rows + 8 * top_count + capacity

    b_left, b_right, own, gain_here = pl.pallas_call(
        functools.partial(first_kernel, top_count),
        out_shape=[
            shaped(first_rows, half),
            shaped(first_rows, half),
            table_shape,
            shaped(1, features, jnp.float32),
        ],
        in_specs=[pl.BlockSpec(memory_space=pltpu.SMEM)]
        + [pl.BlockSpec(memory_space=pltpu.HBM)] * 6,
        scratch_shapes=[
            pltpu.VMEM((tok_rows, features), jnp.bfloat16),
            pltpu.VMEM((1, features), jnp.float32),
            pltpu.VMEM((top_count, tok_rows), jnp.int32),
            pltpu.VMEM((top_count, tok_rows), jnp.float32),
            pltpu.VMEM((top_count, tok_rows), jnp.int32),
            pltpu.VMEM((top_count, tok_rows), jnp.float32),
            pltpu.SemaphoreType.DMA((6,)),
        ],
        compiler_params=pltpu.CompilerParams(vmem_limit_bytes=VMEM_LIMIT),
        cost_estimate=pl.CostEstimate(flops=one_hop, bytes_accessed=moved, transcendentals=0),
    )(
        me,
        *[
            pltpu.with_memory_space_constraint(value, pltpu.HBM)
            for value in (
                saved,
                gain_row,
                fwd_routes[0].T,
                fwd_gates[0].T,
                bwd_routes[0].T,
                bwd_gates[0].T,
            )
        ],
    )
    b_from_x, b_from_y = crossed(b_left, b_right)

    def onward(kind, sent, got, after):
        to_y, to_x = local_call(
            functools.partial(hop_kernel, kind, top_count),
            hop_out,
            (*tabs, *sent, *got),
            one_hop,
            moved,
            after=after,
        )
        return swapped(to_y, "expert", 2), swapped(to_x, "expert", 1), to_y

    f_left, f_right = local_call(
        normed_kernel_halves, halves_out, (layer_in, gain_here), one_hop, moved, after=(b_left,)
    )
    f_from_x, f_from_y = crossed(f_left, f_right)
    x_tab, y_tab = local_call(
        functools.partial(tables_kernel, top_count),
        [table_shape] * 2,
        (b_from_x, b_from_y),
        TABLES_COST,
        1024,
        after=(f_left,),
    )
    g_left, g_right = local_call(split_kernel, halves_out, (grad_in,), 1024, moved, after=(x_tab,))
    g_from_x, g_from_y = crossed(g_left, g_right)
    tabs = (own, x_tab, y_tab)
    b_to_y, b_to_x = local_call(
        functools.partial(far_kernel, "b", top_count),
        [shaped(capacity, half)] * 2,
        (x_tab, y_tab, b_from_x, b_from_y),
        one_hop,
        moved,
        after=(g_left,),
    )
    b_got_y, b_got_x = swapped(b_to_y, "expert", 2), swapped(b_to_x, "expert", 1)
    f_got_y, f_got_x, f_to_y = onward("f", (f_left, f_right), (f_from_x, f_from_y), (b_to_y,))
    g_got_y, g_got_x, g_to_y = onward("bg", (g_left, g_right), (g_from_x, g_from_y), (f_to_y,))
    gate_pre, up_pre = local_call(
        functools.partial(hop_again_kernel, top_count),
        [shaped(slot_total, hidden_units, jnp.float32)] * 2,
        (*tabs, b_left, b_right, b_from_x, b_from_y, b_got_y, b_got_x, weight_in),
        2 * expert_flops,
        expert_moved,
        scratch=(rows_scratch,),
        after=(g_to_y,),
    )
    near_out = [shaped(capacity, features), shaped(capacity, half), shaped(capacity, half)]
    g_near = local_call(
        functools.partial(near_kernel, "bg", top_count),
        near_out,
        (*tabs, g_left, g_right, g_from_x, g_from_y),
        one_hop,
        moved,
        after=(gate_pre,),
    )
    f_near = local_call(
        functools.partial(near_kernel, "f", top_count),
        near_out,
        (*tabs, f_left, f_right, f_from_x, f_from_y),
        one_hop,
        moved,
        after=(g_near[1],),
    )
    f_keep_l, f_near_l, f_on_l, hidden = local_call(
        hop_fwd_kernel,
        half_out + [hidden_shape],
        (*f_near, f_got_y, f_got_x, weight_in, weight_out),
        5 * expert_flops // 2,
        expert_moved,
        scratch=(rows_scratch,),
        after=(f_near[1],),
    )
    f_ret_y = swapped(f_on_l, "expert", 2)
    f_keep_r, f_near_r, f_on_r = local_call(
        fwd_right_kernel, half_out, (hidden, weight_out), 1024, 1024
    )
    f_ret_x = swapped(f_on_r, "expert", 1)
    b_keep_l, b_near_l, b_on_l, both = local_call(
        hop_bwd_kernel,
        half_out + [both_shape],
        (*g_near, g_got_y, g_got_x, gate_pre, up_pre, weight_in, weight_out),
        2 * expert_flops,
        expert_moved,
        scratch=(rows_scratch,),
        after=(f_keep_r,),
    )
    b_ret_y = swapped(b_on_l, "expert", 2)
    b_keep_r, b_near_r, b_on_r = local_call(
        bwd_right_kernel, half_out, (both, weight_in), 1024, 1024
    )
    b_ret_x = swapped(b_on_r, "expert", 1)

    def summed_call(kind, here, table, near, far, after):
        part = local_call(
            functools.partial(sums_kernel, kind, top_count, here),
            shaped(tok_rows, half),
            (table, near, far),
            one_hop,
            moved,
            after=after,
        )
        return swapped(part, "expert", here), part

    f_sum_x, last = summed_call("fg", 1, x_tab, f_near_l, f_ret_y, (b_keep_r,))
    f_sum_y, last = summed_call("fg", 2, y_tab, f_near_r, f_ret_x, (last,))
    b_sum_x, last = summed_call("b", 1, x_tab, b_near_l, b_ret_y, (last,))
    b_sum_y, last = summed_call("b", 2, y_tab, b_near_r, b_ret_x, (last,))
    f_keep = (f_keep_l, f_keep_r)
    b_keep = (b_keep_l, b_keep_r)
    fwd_block, order = local_call(
        functools.partial(hop_fwd_end_kernel, top_count),
        [shaped(tok_rows, features), shaped(8, 128, jnp.float32)],
        (layer_in, own, *f_keep, f_ret_y, f_ret_x, f_sum_x, f_sum_y),
        one_hop,
        moved,
        after=(last,),
    )
    b_near = local_call(
        functools.partial(hop_bwd_near_kernel, top_count),
        [shaped(tok_rows, half, jnp.float32)] * 2,
        (own, *b_keep, b_ret_y, b_ret_x, b_sum_x),
        one_hop,
        moved,
        after=(order,),
    )
    bwd_block = local_call(
        hop_bwd_end_kernel,
        shaped(tok_rows, features),
        (grad_in, saved, gain_here, *b_near, b_sum_y),
        one_hop,
        moved,
    )
    return (fwd_block[None], bwd_block[None])


def per_device(*arrays):
    if lax.axis_size("expert") == 4:
        return per_device_hops(*arrays)
    return per_device_direct(*arrays)


def solution(mesh):
    in_specs = (
        P("section", "expert", None),
        P("section", "expert", None),
        P("section", "expert", None),
        P("section", "expert", None),
        P("section", "expert", None),
        P("section", "expert", None),
        P("section", "expert", None),
        P("section", None),
        P("section", "expert", None, None),
        P("section", "expert", None, None),
    )
    out_specs = (P("section", "expert", None), P("section", "expert", None))
    return jax.shard_map(
        per_device, mesh=mesh, in_specs=in_specs, out_specs=out_specs, check_vma=False
    )
```

```python
import functools

import jax
import jax.numpy as jnp
from jax import lax
from jax.experimental import pallas as pl
from jax.experimental.pallas import tpu as pltpu
from jax.sharding import PartitionSpec as P

EPS = 1e-06
VMEM_LIMIT = 32 * 1024 * 1024
TABLES_COST = 6_000_000_000


def passed_along(value, axis, steps):
    count = lax.axis_size(axis)
    pairs = [(source, (source + steps) % count) for source in range(count)]
    return lax.ppermute(value, axis, pairs)


def swapped(value, axis, offset):
    count = lax.axis_size(axis)
    pairs = [(source, source ^ offset) for source in range(count)]
    return lax.ppermute(value, axis, pairs)


def exchanged(blocks, axis):
    return [blocks[0]] + [swapped(blocks[d], axis, d) for d in range(1, len(blocks))]


def slot_table(routes, expert_count):
    top_count, tok_rows = routes.shape
    experts = max(8, expert_count)
    wanted = lax.broadcasted_iota(jnp.int32, (experts, tok_rows), 0)
    member = routes[0:1, :] == wanted
    for k in range(1, top_count):
        member = jnp.logical_or(member, routes[k : k + 1, :] == wanted)
    before = lax.broadcasted_iota(jnp.int32, (tok_rows, tok_rows), 0) < lax.broadcasted_iota(
        jnp.int32, (tok_rows, tok_rows), 1
    )
    slots = jnp.dot(
        member.astype(jnp.bfloat16),
        before.astype(jnp.bfloat16),
        preferred_element_type=jnp.float32,
    )
    return jnp.where(member, slots, -1.0)


def placement(slots, expert, capacity):
    tok_rows = slots.shape[1]
    row = lax.broadcasted_iota(jnp.int32, (capacity, tok_rows), 0).astype(jnp.float32)
    return slots[expert : expert + 1, :] == row


def gate_row(routes, gates, expert):
    total = jnp.zeros((1, routes.shape[1]), jnp.float32)
    for k in range(routes.shape[0]):
        total = total + jnp.where(routes[k : k + 1, :] == expert, gates[k : k + 1, :], 0.0)
    return total


def halves(weights):
    high = weights.astype(jnp.bfloat16)
    low = (weights - high.astype(jnp.float32)).astype(jnp.bfloat16)
    return high, low


def normed_kernel(values_ref, routes_ref, gain_ref, *out_refs):
    expert_count = len(out_refs)
    capacity = out_refs[0].shape[0]
    wide = values_ref[...].astype(jnp.float32)
    inv_rms = lax.rsqrt(jnp.mean(wide * wide, axis=-1, keepdims=True) + EPS)
    normed = (wide * inv_rms * gain_ref[...]).astype(jnp.bfloat16)
    slots = slot_table(routes_ref[...], expert_count)
    for e in range(expert_count):
        place = placement(slots, e, capacity).astype(jnp.bfloat16)
        out_refs[e][...] = jnp.dot(place, normed, preferred_element_type=jnp.float32).astype(
            jnp.bfloat16
        )


def grads_kernel(grads_ref, routes_ref, gates_ref, *out_refs):
    expert_count = len(out_refs)
    capacity = out_refs[0].shape[0]
    grads = grads_ref[...]
    routes = routes_ref[...]
    slots = slot_table(routes, expert_count)
    for e in range(expert_count):
        place = placement(slots, e, capacity)
        high, low = halves(jnp.where(place, gate_row(routes, gates_ref[...], e), 0.0))
        out_refs[e][...] = (
            jnp.dot(high, grads, preferred_element_type=jnp.float32)
            + jnp.dot(low, grads, preferred_element_type=jnp.float32)
        ).astype(jnp.bfloat16)


def rows_dot(weights, rows):
    return lax.dot_general(
        weights, rows, (((0,), (0,)), ((), ())), preferred_element_type=jnp.float32
    )


def fwd_end_kernel(layer_ref, routes_ref, gates_ref, *refs):
    row_refs, out_ref = refs[:-1], refs[-1]
    expert_count = len(row_refs)
    capacity = row_refs[0].shape[0]
    routes = routes_ref[...]
    slots = slot_table(routes, expert_count)
    total = layer_ref[...].astype(jnp.float32)
    for e in range(expert_count):
        place = placement(slots, e, capacity)
        high, low = halves(jnp.where(place, gate_row(routes, gates_ref[...], e), 0.0))
        rows = row_refs[e][...]
        total = total + (rows_dot(high, rows) + rows_dot(low, rows))
    out_ref[...] = total.astype(jnp.bfloat16)


def bwd_end_kernel(grads_ref, saved_ref, gain_ref, routes_ref, *refs):
    row_refs, out_ref = refs[:-1], refs[-1]
    expert_count = len(row_refs)
    capacity = row_refs[0].shape[0]
    features = saved_ref.shape[1]
    slots = slot_table(routes_ref[...], expert_count)
    d_normed = None
    for e in range(expert_count):
        place = placement(slots, e, capacity).astype(jnp.bfloat16)
        part = rows_dot(place, row_refs[e][...])
        d_normed = part if d_normed is None else d_normed + part
    wide = saved_ref[...].astype(jnp.float32)
    inv_rms = lax.rsqrt(jnp.mean(wide * wide, axis=-1, keepdims=True) + EPS)
    scaled = d_normed * gain_ref[...]
    cubed = inv_rms * inv_rms * inv_rms
    inner = jnp.sum(scaled * wide, axis=-1, keepdims=True)
    out_ref[...] = (
        grads_ref[...].astype(jnp.float32) + inv_rms * scaled - cubed / features * wide * inner
    ).astype(jnp.bfloat16)


def joined(refs):
    rows = [ref[...] for ref in refs]
    if rows[0].shape[0] % 16 == 0:
        return jnp.concatenate(rows, axis=0)
    return jnp.concatenate([r.astype(jnp.float32) for r in rows], axis=0).astype(jnp.bfloat16)


def tiles(size, step):
    return [(start, min(step, size - start)) for start in range(0, size, step)]


def expert_fwd_kernel(*refs):
    expert_count = (len(refs) - 4) // 2
    row_refs = refs[:expert_count]
    weight_in, weight_out = refs[expert_count : expert_count + 2]
    out_refs = refs[expert_count + 2 : 2 * expert_count + 2]
    rows_ref, hidden_ref = refs[-2:]
    capacity = row_refs[0].shape[0]
    hidden_units, features = weight_out.shape
    rows_ref[...] = joined(row_refs)
    for start, size in tiles(hidden_units, 256):
        gate = jnp.dot(
            rows_ref[...], weight_in[:, start : start + size], preferred_element_type=jnp.float32
        )
        up = jnp.dot(
            rows_ref[...],
            weight_in[:, hidden_units + start : hidden_units + start + size],
            preferred_element_type=jnp.float32,
        )
        hidden_ref[:, start : start + size] = (gate / (1.0 + jnp.exp(-gate)) * up).astype(
            jnp.bfloat16
        )
    for start, size in tiles(features, 512):
        out = jnp.dot(
            hidden_ref[...], weight_out[:, start : start + size], preferred_element_type=jnp.float32
        )
        for d in range(expert_count):
            out_refs[d][:, start : start + size] = out[d * capacity : (d + 1) * capacity].astype(
                jnp.bfloat16
            )


def expert_again_kernel(*refs):
    expert_count = len(refs) - 4
    row_refs = refs[:expert_count]
    weight_in, gate_ref, up_ref, rows_ref = refs[expert_count:]
    hidden_units = gate_ref.shape[1]
    rows_ref[...] = joined(row_refs)
    for start, size in tiles(hidden_units, 256):
        gate_ref[:, start : start + size] = jnp.dot(
            rows_ref[...], weight_in[:, start : start + size], preferred_element_type=jnp.float32
        )
        up_ref[:, start : start + size] = jnp.dot(
            rows_ref[...],
            weight_in[:, hidden_units + start : hidden_units + start + size],
            preferred_element_type=jnp.float32,
        )


def expert_bwd_kernel(*refs):
    expert_count = (len(refs) - 6) // 2
    grad_refs = refs[:expert_count]
    gate_ref, up_ref, weight_in, weight_out = refs[expert_count : expert_count + 4]
    out_refs = refs[expert_count + 4 : 2 * expert_count + 4]
    grads_ref, both_ref = refs[-2:]
    capacity = grad_refs[0].shape[0]
    hidden_units, features = weight_out.shape
    grads_ref[...] = joined(grad_refs)
    for start, size in tiles(hidden_units, 256):
        gate = gate_ref[:, start : start + size]
        up = up_ref[:, start : start + size]
        d_hidden = lax.dot_general(
            grads_ref[...],
            weight_out[start : start + size, :],
            (((1,), (1,)), ((), ())),
            preferred_element_type=jnp.float32,
        )
        sig = 1.0 / (1.0 + jnp.exp(-gate))
        both_ref[:, start : start + size] = (
            d_hidden * up * sig * (1.0 + gate * (1.0 - sig))
        ).astype(jnp.bfloat16)
        both_ref[:, hidden_units + start : hidden_units + start + size] = (
            d_hidden * gate * sig
        ).astype(jnp.bfloat16)
    for start, size in tiles(features, 512):
        out = lax.dot_general(
            both_ref[...],
            weight_in[start : start + size, :],
            (((1,), (1,)), ((), ())),
            preferred_element_type=jnp.float32,
        )
        for d in range(expert_count):
            out_refs[d][:, start : start + size] = out[d * capacity : (d + 1) * capacity].astype(
                jnp.bfloat16
            )


def local_call(kernel, out_shapes, inputs, flops, moved, scratch=(), after=()):
    in_specs = [pl.BlockSpec(memory_space=pltpu.VMEM)] * len(inputs)
    held = len(inputs)

    def body(*refs):
        kernel(*refs[:held], *refs[held + len(after) :])

    return pl.pallas_call(
        body if after else kernel,
        out_shape=out_shapes,
        in_specs=in_specs + [pl.BlockSpec(memory_space=pl.ANY)] * len(after),
        scratch_shapes=list(scratch),
        compiler_params=pltpu.CompilerParams(vmem_limit_bytes=VMEM_LIMIT),
        cost_estimate=pl.CostEstimate(flops=flops, bytes_accessed=moved, transcendentals=0),
    )(*inputs, *after)


def per_device_direct(
    fwd_prev,
    bwd_prev,
    bwd_saved,
    fwd_routes,
    fwd_gates,
    bwd_routes,
    bwd_gates,
    norm_gain,
    w_in,
    w_out,
):
    expert_count = lax.axis_size("expert")
    tok_rows = fwd_prev.shape[1]
    features = fwd_prev.shape[2]
    top_count = fwd_routes.shape[2]
    hidden_units = w_in.shape[3] // 2
    capacity = 3 * tok_rows * top_count // (2 * expert_count)
    gain_row = norm_gain
    weight_in = w_in[0, 0]
    weight_out = w_out[0, 0]
    me = lax.axis_index("expert")
    f_routes = (fwd_routes[0] ^ me).T
    b_routes = (bwd_routes[0] ^ me).T
    f_gates = fwd_gates[0].T
    b_gates = bwd_gates[0].T
    saved = bwd_saved[0]
    layer_in = passed_along(fwd_prev[0], "section", 1)
    grad_in = passed_along(bwd_prev[0], "section", -1)

    block = jax.ShapeDtypeStruct((capacity, features), jnp.bfloat16)
    whole = jax.ShapeDtypeStruct((tok_rows, features), jnp.bfloat16)
    one_dot = 2 * expert_count * capacity * tok_rows * features
    moved = 2 * features * (tok_rows + expert_count * capacity)
    slot_total = expert_count * capacity
    blocks = [block] * expert_count
    expert_flops = 2 * slot_total * features * hidden_units
    expert_moved = 2 * features * (3 * hidden_units + 3 * slot_total)
    rows_scratch = pltpu.VMEM((slot_total, features), jnp.bfloat16)

    b_sent = local_call(normed_kernel, blocks, (saved, b_routes, gain_row), one_dot, moved)
    b_rows = exchanged(b_sent, "expert")
    f_sent = local_call(
        normed_kernel, blocks, (layer_in, f_routes, gain_row), one_dot, moved, after=(b_sent[0],)
    )
    f_rows = exchanged(f_sent, "expert")
    g_sent = local_call(
        grads_kernel, blocks, (grad_in, b_routes, b_gates), 2 * one_dot, moved, after=(f_sent[0],)
    )
    g_rows = exchanged(g_sent, "expert")
    projected = jax.ShapeDtypeStruct((slot_total, hidden_units), jnp.float32)
    gate_pre, up_pre = local_call(
        expert_again_kernel,
        [projected, projected],
        (*b_rows, weight_in),
        2 * expert_flops,
        expert_moved,
        scratch=(rows_scratch,),
        after=(g_sent[0],),
    )
    f_done = local_call(
        expert_fwd_kernel,
        blocks,
        (*f_rows, weight_in, weight_out),
        3 * expert_flops,
        expert_moved,
        scratch=(rows_scratch, pltpu.VMEM((slot_total, hidden_units), jnp.bfloat16)),
        after=(gate_pre,),
    )
    f_back = exchanged(f_done, "expert")
    b_done = local_call(
        expert_bwd_kernel,
        blocks,
        (*g_rows, gate_pre, up_pre, weight_in, weight_out),
        3 * expert_flops,
        expert_moved,
        scratch=(rows_scratch, pltpu.VMEM((slot_total, 2 * hidden_units), jnp.bfloat16)),
        after=(f_back[1],),
    )
    b_back = exchanged(b_done, "expert")
    fwd_block = local_call(
        fwd_end_kernel,
        whole,
        (layer_in, f_routes, f_gates, *f_back),
        2 * one_dot,
        moved,
        after=(b_done[0],),
    )
    bwd_block = local_call(
        bwd_end_kernel,
        whole,
        (grad_in, saved, gain_row, b_routes, *b_back),
        one_dot,
        moved,
    )
    return (fwd_block[None], bwd_block[None])


def pick(table, expert, capacity, kind, top_count):
    first = 0 if kind[0] == "f" else 2 * top_count
    routes = table[first : first + top_count]
    gates = table[first + top_count : first + 2 * top_count]
    tok_rows = table.shape[1]
    member = routes == float(expert)
    held = jnp.sum(member.astype(jnp.float32), axis=0, keepdims=True)
    before = lax.broadcasted_iota(jnp.int32, (tok_rows, tok_rows), 0) < lax.broadcasted_iota(
        jnp.int32, (tok_rows, tok_rows), 1
    )
    slots = jnp.dot(
        jnp.broadcast_to(held, (8, tok_rows)).astype(jnp.bfloat16),
        before.astype(jnp.bfloat16),
        preferred_element_type=jnp.float32,
    )[0:1]
    place = placement(jnp.where(held > 0.0, slots, -1.0), 0, capacity)
    if len(kind) == 1:
        return (place.astype(jnp.bfloat16),)
    gate = jnp.sum(jnp.where(member, gates, 0.0), axis=0, keepdims=True)
    return halves(jnp.where(place, gate, 0.0))


def to_slots(weights, values):
    total = None
    for part in weights:
        term = jnp.dot(part, values, preferred_element_type=jnp.float32)
        total = term if total is None else total + term
    return total.astype(jnp.bfloat16)


def to_tokens(weights, rows):
    total = None
    for part in weights:
        term = rows_dot(part, rows)
        total = term if total is None else total + term
    return total


def three_parts(values):
    high = values.astype(jnp.bfloat16)
    rest = values - high.astype(jnp.float32)
    mid = rest.astype(jnp.bfloat16)
    low = (rest - mid.astype(jnp.float32)).astype(jnp.bfloat16)
    return high, mid, low


def normed_halves(wide, gain):
    inv_rms = lax.rsqrt(jnp.mean(wide * wide, axis=-1, keepdims=True) + EPS)
    return (wide * inv_rms * gain).astype(jnp.bfloat16)


def first_kernel(top_count, me_ref, *refs):
    sources, refs = refs[:6], refs[6:]
    (left_ref, right_ref, table_ref, gain_out), refs = refs[:4], refs[4:]
    held, sems = refs[:6], refs[6]
    copies = [pltpu.make_async_copy(sources[i], held[i], sems.at[i]) for i in range(6)]
    for copy in copies:
        copy.start()
    for copy in copies[1:]:
        copy.wait()
    saved, gain, f_routes, f_gates, b_routes, b_gates = held
    me = me_ref[0]
    fr = (f_routes[...] ^ me).astype(jnp.float32)
    br = (b_routes[...] ^ me).astype(jnp.float32)
    fg = f_gates[...]
    bg = b_gates[...]
    table = jnp.concatenate([fr, fg, br, bg], axis=0)
    table_ref[...] = table
    packed = [fr.astype(jnp.bfloat16), br.astype(jnp.bfloat16), *three_parts(fg), *three_parts(bg)]
    packed = jnp.concatenate([part.astype(jnp.float32) for part in packed], axis=0)
    gain_out[...] = gain[...]
    tok_rows, features = saved.shape
    half = features // 2
    copies[0].wait()
    normed = normed_halves(saved[...].astype(jnp.float32), gain[...])
    capacity = left_ref.shape[0] - tok_rows - packed.shape[0]
    near = tok_rows + packed.shape[0]
    for half_ref, start, expert in ((left_ref, 0, 1), (right_ref, half, 2)):
        half_ref[:tok_rows, :] = normed[:, start : start + half]
        half_ref[tok_rows:near, :] = jnp.zeros((near - tok_rows, half), jnp.bfloat16)
        half_ref[tok_rows:near, :tok_rows] = packed.astype(jnp.bfloat16)
        other = half - start
        half_ref[near:, :] = to_slots(
            pick(table, expert, capacity, "b", top_count), normed[:, other : other + half]
        )


def unpacked(block, tok_rows, top_count):
    rows = block[tok_rows : tok_rows + 8 * top_count, :tok_rows].astype(jnp.float32)
    k = top_count
    fr, br = rows[0:k], rows[k : 2 * k]
    fg = (rows[2 * k : 3 * k] + rows[3 * k : 4 * k]) + rows[4 * k : 5 * k]
    bg = (rows[5 * k : 6 * k] + rows[6 * k : 7 * k]) + rows[7 * k : 8 * k]
    return jnp.concatenate([fr, fg, br, bg], axis=0)


def normed_kernel_halves(values_ref, gain_ref, left_ref, right_ref):
    half = left_ref.shape[1]
    normed = normed_halves(values_ref[...].astype(jnp.float32), gain_ref[...])
    left_ref[...] = normed[:, :half]
    right_ref[...] = normed[:, half:]


def split_kernel(values_ref, left_ref, right_ref):
    half = left_ref.shape[1]
    left_ref[...] = values_ref[:, :half]
    right_ref[...] = values_ref[:, half:]


def tables_kernel(top_count, from_x, from_y, x_table, y_table):
    tok_rows = x_table.shape[1]
    x_table[...] = unpacked(from_x[...], tok_rows, top_count)
    y_table[...] = unpacked(from_y[...], tok_rows, top_count)


def hop_kernel(kind, top_count, own, x_tab, y_tab, left, right, from_x, from_y, to_y, to_x):
    capacity = to_y.shape[0] // 2
    tok_rows = own.shape[1]
    to_y[:capacity, :] = to_slots(pick(own[...], 2, capacity, kind, top_count), left[:tok_rows, :])
    to_y[capacity:, :] = to_slots(
        pick(x_tab[...], 3, capacity, kind, top_count), from_x[:tok_rows, :]
    )
    to_x[:capacity, :] = to_slots(pick(own[...], 1, capacity, kind, top_count), right[:tok_rows, :])
    to_x[capacity:, :] = to_slots(
        pick(y_tab[...], 3, capacity, kind, top_count), from_y[:tok_rows, :]
    )


def far_kernel(kind, top_count, x_tab, y_tab, from_x, from_y, to_y, to_x):
    capacity = to_y.shape[0]
    tok_rows = x_tab.shape[1]
    to_y[...] = to_slots(pick(x_tab[...], 3, capacity, kind, top_count), from_x[:tok_rows, :])
    to_x[...] = to_slots(pick(y_tab[...], 3, capacity, kind, top_count), from_y[:tok_rows, :])


def assemble(kind, top_count, own, x_tab, y_tab, left, right, from_x, from_y, got_y, got_x, rows):
    capacity = rows.shape[0] // 4
    half = got_y.shape[1]
    tok_rows = own.shape[1]
    mine = pick(own[...], 0, capacity, kind, top_count)
    rows[:capacity, :half] = to_slots(mine, left[:tok_rows, :])
    rows[:capacity, half:] = to_slots(mine, right[:tok_rows, :])
    rows[capacity : 2 * capacity, :half] = to_slots(
        pick(x_tab[...], 1, capacity, kind, top_count), from_x[:tok_rows, :]
    )
    rows[2 * capacity : 3 * capacity, half:] = to_slots(
        pick(y_tab[...], 2, capacity, kind, top_count), from_y[:tok_rows, :]
    )
    if got_y.shape[0] == capacity:
        near_x, near_y = from_x[-capacity:, :], from_y[-capacity:, :]
    else:
        near_x, near_y = got_x[:capacity, :], got_y[:capacity, :]
    rows[capacity : 2 * capacity, half:] = near_x
    rows[2 * capacity : 3 * capacity, :half] = near_y
    rows[3 * capacity :, :half] = got_y[-capacity:, :]
    rows[3 * capacity :, half:] = got_x[-capacity:, :]


def near_kernel(
    kind, top_count, own, x_tab, y_tab, left, right, from_x, from_y, mine_ref, x_left, y_right
):
    capacity, half = x_left.shape
    tok_rows = own.shape[1]
    mine = pick(own[...], 0, capacity, kind, top_count)
    mine_ref[:, :half] = to_slots(mine, left[:tok_rows, :])
    mine_ref[:, half:] = to_slots(mine, right[:tok_rows, :])
    x_left[...] = to_slots(pick(x_tab[...], 1, capacity, kind, top_count), from_x[:tok_rows, :])
    y_right[...] = to_slots(pick(y_tab[...], 2, capacity, kind, top_count), from_y[:tok_rows, :])


def gathered_rows(mine, x_left, y_right, got_y, got_x, rows):
    capacity, half = x_left.shape
    rows[:capacity, :] = mine[...]
    rows[capacity : 2 * capacity, :half] = x_left[...]
    rows[capacity : 2 * capacity, half:] = got_x[:capacity, :]
    rows[2 * capacity : 3 * capacity, :half] = got_y[:capacity, :]
    rows[2 * capacity : 3 * capacity, half:] = y_right[...]
    rows[3 * capacity :, :half] = got_y[capacity:, :]
    rows[3 * capacity :, half:] = got_x[capacity:, :]


def hand_out(out, at, capacity, to_left, keep, near, onward):
    size = out.shape[1]
    rows = out.astype(jnp.bfloat16)
    mine, from_x, from_y, far = [rows[d * capacity : (d + 1) * capacity] for d in range(4)]
    keep[:, at : at + size] = mine
    near[:, at : at + size] = from_x if to_left else from_y
    onward[:capacity, at : at + size] = from_y if to_left else from_x
    onward[capacity:, at : at + size] = far


def fwd_half(hidden_ref, weight_out, to_left, keep, near, onward):
    capacity, half = keep.shape
    first = 0 if to_left else half
    for at, size in tiles(half, 512):
        out = jnp.dot(
            hidden_ref[...],
            weight_out[:, first + at : first + at + size],
            preferred_element_type=jnp.float32,
        )
        hand_out(out, at, capacity, to_left, keep, near, onward)


def bwd_half(both_ref, weight_in, to_left, keep, near, onward):
    capacity, half = keep.shape
    first = 0 if to_left else half
    for at, size in tiles(half, 512):
        out = lax.dot_general(
            both_ref[...],
            weight_in[first + at : first + at + size, :],
            (((1,), (1,)), ((), ())),
            preferred_element_type=jnp.float32,
        )
        hand_out(out, at, capacity, to_left, keep, near, onward)


def fwd_right_kernel(hidden_ref, weight_out, keep, near, onward):
    fwd_half(hidden_ref, weight_out, False, keep, near, onward)


def bwd_right_kernel(both_ref, weight_in, keep, near, onward):
    bwd_half(both_ref, weight_in, False, keep, near, onward)


def hop_again_kernel(top_count, *refs):
    dispatch, (weight_in, gate_ref, up_ref, rows_ref) = refs[:9], refs[9:]
    assemble("b", top_count, *dispatch, rows_ref)
    hidden_units = gate_ref.shape[1]
    for start, size in tiles(hidden_units, 256):
        gate_ref[:, start : start + size] = jnp.dot(
            rows_ref[...], weight_in[:, start : start + size], preferred_element_type=jnp.float32
        )
        up_ref[:, start : start + size] = jnp.dot(
            rows_ref[...],
            weight_in[:, hidden_units + start : hidden_units + start + size],
            preferred_element_type=jnp.float32,
        )


def hop_fwd_kernel(*refs):
    dispatch, refs = refs[:5], refs[5:]
    weight_in, weight_out = refs[:2]
    outs, hidden_ref, rows_ref = refs[2:5], refs[5], refs[6]
    hidden_units = weight_out.shape[0]
    gathered_rows(*dispatch, rows_ref)
    for start, size in tiles(hidden_units, 256):
        gate = jnp.dot(
            rows_ref[...], weight_in[:, start : start + size], preferred_element_type=jnp.float32
        )
        up = jnp.dot(
            rows_ref[...],
            weight_in[:, hidden_units + start : hidden_units + start + size],
            preferred_element_type=jnp.float32,
        )
        hidden_ref[:, start : start + size] = (gate / (1.0 + jnp.exp(-gate)) * up).astype(
            jnp.bfloat16
        )
    fwd_half(hidden_ref, weight_out, True, *outs)


def hop_bwd_kernel(*refs):
    dispatch, refs = refs[:5], refs[5:]
    gate_ref, up_ref, weight_in, weight_out = refs[:4]
    outs, both_ref, grads_ref = refs[4:7], refs[7], refs[8]
    hidden_units = weight_out.shape[0]
    gathered_rows(*dispatch, grads_ref)
    for start, size in tiles(hidden_units, 256):
        gate = gate_ref[:, start : start + size]
        up = up_ref[:, start : start + size]
        d_hidden = lax.dot_general(
            grads_ref[...],
            weight_out[start : start + size, :],
            (((1,), (1,)), ((), ())),
            preferred_element_type=jnp.float32,
        )
        sig = 1.0 / (1.0 + jnp.exp(-gate))
        both_ref[:, start : start + size] = (
            d_hidden * up * sig * (1.0 + gate * (1.0 - sig))
        ).astype(jnp.bfloat16)
        both_ref[:, hidden_units + start : hidden_units + start + size] = (
            d_hidden * gate * sig
        ).astype(jnp.bfloat16)
    bwd_half(both_ref, weight_in, True, *outs)


def sums_kernel(kind, top_count, here, table_ref, near, far, out):
    capacity = near.shape[0]
    table = table_ref[...]
    out[...] = (
        to_tokens(pick(table, here, capacity, kind, top_count), near[...])
        + to_tokens(pick(table, 3, capacity, kind, top_count), far[capacity:, :])
    ).astype(jnp.bfloat16)


def summed(kind, top_count, own, keep_left, keep_right, got_y, got_x, sum_x, sum_y):
    capacity = keep_left.shape[0]
    mine = pick(own[...], 0, capacity, kind, top_count)
    near_y = pick(own[...], 2, capacity, kind, top_count)
    near_x = pick(own[...], 1, capacity, kind, top_count)
    left = to_tokens(mine, keep_left[...]) + to_tokens(near_y, got_y[:capacity, :])
    right = to_tokens(mine, keep_right[...]) + to_tokens(near_x, got_x[:capacity, :])
    return left + sum_x[...].astype(jnp.float32), right + sum_y[...].astype(jnp.float32)


def hop_fwd_end_kernel(top_count, layer_ref, *refs):
    out_ref, order_ref = refs[-2:]
    order_ref[...] = jnp.zeros_like(order_ref)
    half = layer_ref.shape[1] // 2
    left, right = summed("fg", top_count, *refs[:-2])
    out_ref[:, :half] = (layer_ref[:, :half].astype(jnp.float32) + left).astype(jnp.bfloat16)
    out_ref[:, half:] = (layer_ref[:, half:].astype(jnp.float32) + right).astype(jnp.bfloat16)


def hop_bwd_near_kernel(
    top_count, own, keep_left, keep_right, got_y, got_x, left_ref, right_ref
):
    capacity = keep_left.shape[0]
    mine = pick(own[...], 0, capacity, "b", top_count)
    near_y = pick(own[...], 2, capacity, "b", top_count)
    near_x = pick(own[...], 1, capacity, "b", top_count)
    left_ref[...] = to_tokens(mine, keep_left[...]) + to_tokens(near_y, got_y[:capacity, :])
    right_ref[...] = to_tokens(mine, keep_right[...]) + to_tokens(near_x, got_x[:capacity, :])


def order_kernel(order_ref):
    order_ref[...] = jnp.zeros_like(order_ref)


def hop_bwd_end_kernel(grads_ref, saved_ref, gain_ref, left_ref, right_ref, sum_x, sum_y, out_ref):
    features = saved_ref.shape[1]
    half = features // 2
    parts = []
    left = left_ref[...] + sum_x[...].astype(jnp.float32)
    right = right_ref[...] + sum_y[...].astype(jnp.float32)
    for start, d_normed in ((0, left), (half, right)):
        wide = saved_ref[:, start : start + half].astype(jnp.float32)
        scaled = d_normed * gain_ref[:, start : start + half]
        parts.append((start, wide, scaled))
    square = sum(jnp.sum(wide * wide, axis=-1, keepdims=True) for _, wide, _ in parts)
    inner = sum(jnp.sum(scaled * wide, axis=-1, keepdims=True) for _, wide, scaled in parts)
    inv_rms = lax.rsqrt(square / features + EPS)
    factor = inv_rms * inv_rms * inv_rms / features * inner
    for start, wide, scaled in parts:
        out_ref[:, start : start + half] = (
            grads_ref[:, start : start + half].astype(jnp.float32)
            + inv_rms * scaled
            - factor * wide
        ).astype(jnp.bfloat16)


def per_device_hops(
    fwd_prev,
    bwd_prev,
    bwd_saved,
    fwd_routes,
    fwd_gates,
    bwd_routes,
    bwd_gates,
    norm_gain,
    w_in,
    w_out,
):
    tok_rows, features = fwd_prev.shape[1:]
    top_count = fwd_routes.shape[2]
    hidden_units = w_in.shape[3] // 2
    capacity = 3 * tok_rows * top_count // 8
    half = features // 2
    gain_row = norm_gain
    weight_in = w_in[0, 0]
    weight_out = w_out[0, 0]
    me = lax.axis_index("expert").astype(jnp.int32).reshape(1)
    saved = bwd_saved[0]
    layer_in = passed_along(fwd_prev[0], "section", 1)
    grad_in = passed_along(bwd_prev[0], "section", -1)

    def shaped(rows, columns, dtype=jnp.bfloat16):
        return jax.ShapeDtypeStruct((rows, columns), dtype)

    def crossed(left, right):
        return swapped(left, "expert", 1), swapped(right, "expert", 2)

    slot_total = 4 * capacity
    table_rows = 4 * top_count
    one_hop = moved = 1024
    expert_flops = 2 * slot_total * features * hidden_units
    expert_moved = 2 * features * (3 * hidden_units + 3 * slot_total)
    rows_scratch = pltpu.VMEM((slot_total, features), jnp.bfloat16)
    halves_out = [shaped(tok_rows, half)] * 2
    hop_out = [shaped(2 * capacity, half)] * 2
    half_out = [shaped(capacity, half), shaped(capacity, half), shaped(2 * capacity, half)]
    hidden_shape = shaped(slot_total, hidden_units)
    both_shape = shaped(slot_total, 2 * hidden_units)
    table_shape = shaped(table_rows, tok_rows, jnp.float32)
    first_rows = tok_rows + 8 * top_count + capacity

    b_left, b_right, own, gain_here = pl.pallas_call(
        functools.partial(first_kernel, top_count),
        out_shape=[
            shaped(first_rows, half),
            shaped(first_rows, half),
            table_shape,
            shaped(1, features, jnp.float32),
        ],
        in_specs=[pl.BlockSpec(memory_space=pltpu.SMEM)]
        + [pl.BlockSpec(memory_space=pltpu.HBM)] * 6,
        scratch_shapes=[
            pltpu.VMEM((tok_rows, features), jnp.bfloat16),
            pltpu.VMEM((1, features), jnp.float32),
            pltpu.VMEM((top_count, tok_rows), jnp.int32),
            pltpu.VMEM((top_count, tok_rows), jnp.float32),
            pltpu.VMEM((top_count, tok_rows), jnp.int32),
            pltpu.VMEM((top_count, tok_rows), jnp.float32),
            pltpu.SemaphoreType.DMA((6,)),
        ],
        compiler_params=pltpu.CompilerParams(vmem_limit_bytes=VMEM_LIMIT),
        cost_estimate=pl.CostEstimate(flops=one_hop, bytes_accessed=moved, transcendentals=0),
    )(
        me,
        *[
            pltpu.with_memory_space_constraint(value, pltpu.HBM)
            for value in (
                saved,
                gain_row,
                fwd_routes[0].T,
                fwd_gates[0].T,
                bwd_routes[0].T,
                bwd_gates[0].T,
            )
        ],
    )
    b_from_x, b_from_y = crossed(b_left, b_right)

    def onward(kind, sent, got, after):
        to_y, to_x = local_call(
            functools.partial(hop_kernel, kind, top_count),
            hop_out,
            (*tabs, *sent, *got),
            one_hop,
            moved,
            after=after,
        )
        return swapped(to_y, "expert", 2), swapped(to_x, "expert", 1), to_y

    f_left, f_right = local_call(
        normed_kernel_halves, halves_out, (layer_in, gain_here), one_hop, moved, after=(b_left,)
    )
    f_from_x, f_from_y = crossed(f_left, f_right)
    x_tab, y_tab = local_call(
        functools.partial(tables_kernel, top_count),
        [table_shape] * 2,
        (b_from_x, b_from_y),
        TABLES_COST,
        1024,
        after=(f_left,),
    )
    g_left, g_right = local_call(split_kernel, halves_out, (grad_in,), 1024, moved, after=(x_tab,))
    g_from_x, g_from_y = crossed(g_left, g_right)
    tabs = (own, x_tab, y_tab)
    b_to_y, b_to_x = local_call(
        functools.partial(far_kernel, "b", top_count),
        [shaped(capacity, half)] * 2,
        (x_tab, y_tab, b_from_x, b_from_y),
        one_hop,
        moved,
        after=(g_left,),
    )
    b_got_y, b_got_x = swapped(b_to_y, "expert", 2), swapped(b_to_x, "expert", 1)
    f_got_y, f_got_x, f_to_y = onward("f", (f_left, f_right), (f_from_x, f_from_y), (b_to_y,))
    g_got_y, g_got_x, g_to_y = onward("bg", (g_left, g_right), (g_from_x, g_from_y), (f_to_y,))
    gate_pre, up_pre = local_call(
        functools.partial(hop_again_kernel, top_count),
        [shaped(slot_total, hidden_units, jnp.float32)] * 2,
        (*tabs, b_left, b_right, b_from_x, b_from_y, b_got_y, b_got_x, weight_in),
        2 * expert_flops,
        expert_moved,
        scratch=(rows_scratch,),
        after=(g_to_y,),
    )
    near_out = [shaped(capacity, features), shaped(capacity, half), shaped(capacity, half)]
    g_near = local_call(
        functools.partial(near_kernel, "bg", top_count),
        near_out,
        (*tabs, g_left, g_right, g_from_x, g_from_y),
        one_hop,
        moved,
        after=(gate_pre,),
    )
    f_near = local_call(
        functools.partial(near_kernel, "f", top_count),
        near_out,
        (*tabs, f_left, f_right, f_from_x, f_from_y),
        one_hop,
        moved,
        after=(g_near[1],),
    )
    f_keep_l, f_near_l, f_on_l, hidden = local_call(
        hop_fwd_kernel,
        half_out + [hidden_shape],
        (*f_near, f_got_y, f_got_x, weight_in, weight_out),
        5 * expert_flops // 2,
        expert_moved,
        scratch=(rows_scratch,),
        after=(f_near[1],),
    )
    f_ret_y = swapped(f_on_l, "expert", 2)
    f_keep_r, f_near_r, f_on_r = local_call(
        fwd_right_kernel, half_out, (hidden, weight_out), 1024, 1024
    )
    f_ret_x = swapped(f_on_r, "expert", 1)
    b_keep_l, b_near_l, b_on_l, both = local_call(
        hop_bwd_kernel,
        half_out + [both_shape],
        (*g_near, g_got_y, g_got_x, gate_pre, up_pre, weight_in, weight_out),
        2 * expert_flops,
        expert_moved,
        scratch=(rows_scratch,),
        after=(f_keep_r,),
    )
    b_ret_y = swapped(b_on_l, "expert", 2)
    b_keep_r, b_near_r, b_on_r = local_call(
        bwd_right_kernel, half_out, (both, weight_in), 1024, 1024
    )
    b_ret_x = swapped(b_on_r, "expert", 1)

    def summed_call(kind, here, table, near, far, after):
        part = local_call(
            functools.partial(sums_kernel, kind, top_count, here),
            shaped(tok_rows, half),
            (table, near, far),
            one_hop,
            moved,
            after=after,
        )
        return swapped(part, "expert", here), part

    f_sum_x, last = summed_call("fg", 1, x_tab, f_near_l, f_ret_y, (b_keep_r,))
    f_sum_y, last = summed_call("fg", 2, y_tab, f_near_r, f_ret_x, (last,))
    b_sum_x, last = summed_call("b", 1, x_tab, b_near_l, b_ret_y, (last,))
    b_sum_y, last = summed_call("b", 2, y_tab, b_near_r, b_ret_x, (last,))
    f_keep = (f_keep_l, f_keep_r)
    b_keep = (b_keep_l, b_keep_r)
    fwd_block, order = local_call(
        functools.partial(hop_fwd_end_kernel, top_count),
        [shaped(tok_rows, features), shaped(8, 128, jnp.float32)],
        (layer_in, own, *f_keep, f_ret_y, f_ret_x, f_sum_x, f_sum_y),
        one_hop,
        moved,
        after=(last,),
    )
    b_near = local_call(
        functools.partial(hop_bwd_near_kernel, top_count),
        [shaped(tok_rows, half, jnp.float32)] * 2,
        (own, *b_keep, b_ret_y, b_ret_x),
        one_hop,
        moved,
        after=(last,),
    )
    x_there = local_call(
        order_kernel,
        shaped(8, 128, jnp.float32),
        (),
        one_hop,
        moved,
        after=(order, b_near[0], b_sum_x),
    )
    bwd_block = local_call(
        hop_bwd_end_kernel,
        shaped(tok_rows, features),
        (grad_in, saved, gain_here, *b_near, b_sum_x, b_sum_y),
        one_hop,
        moved,
        after=(x_there,),
    )
    return (fwd_block[None], bwd_block[None])


def per_device(*arrays):
    if lax.axis_size("expert") == 4:
        return per_device_hops(*arrays)
    return per_device_direct(*arrays)


def solution(mesh):
    in_specs = (
        P("section", "expert", None),
        P("section", "expert", None),
        P("section", "expert", None),
        P("section", "expert", None),
        P("section", "expert", None),
        P("section", "expert", None),
        P("section", "expert", None),
        P("section", None),
        P("section", "expert", None, None),
        P("section", "expert", None, None),
    )
    out_specs = (P("section", "expert", None), P("section", "expert", None))
    return jax.shard_map(
        per_device, mesh=mesh, in_specs=in_specs, out_specs=out_specs, check_vma=False
    )
```

```python
import functools

import jax
import jax.numpy as jnp
from jax import lax
from jax.experimental import pallas as pl
from jax.experimental.pallas import tpu as pltpu
from jax.sharding import PartitionSpec as P

EPS = 1e-06
VMEM_LIMIT = 32 * 1024 * 1024
TABLES_COST = 6_000_000_000


def passed_along(value, axis, steps):
    count = lax.axis_size(axis)
    pairs = [(source, (source + steps) % count) for source in range(count)]
    return lax.ppermute(value, axis, pairs)


def swapped(value, axis, offset):
    count = lax.axis_size(axis)
    pairs = [(source, source ^ offset) for source in range(count)]
    return lax.ppermute(value, axis, pairs)


def exchanged(blocks, axis):
    return [blocks[0]] + [swapped(blocks[d], axis, d) for d in range(1, len(blocks))]


def slot_table(routes, expert_count):
    top_count, tok_rows = routes.shape
    experts = max(8, expert_count)
    wanted = lax.broadcasted_iota(jnp.int32, (experts, tok_rows), 0)
    member = routes[0:1, :] == wanted
    for k in range(1, top_count):
        member = jnp.logical_or(member, routes[k : k + 1, :] == wanted)
    before = lax.broadcasted_iota(jnp.int32, (tok_rows, tok_rows), 0) < lax.broadcasted_iota(
        jnp.int32, (tok_rows, tok_rows), 1
    )
    slots = jnp.dot(
        member.astype(jnp.bfloat16),
        before.astype(jnp.bfloat16),
        preferred_element_type=jnp.float32,
    )
    return jnp.where(member, slots, -1.0)


def placement(slots, expert, capacity):
    tok_rows = slots.shape[1]
    row = lax.broadcasted_iota(jnp.int32, (capacity, tok_rows), 0).astype(jnp.float32)
    return slots[expert : expert + 1, :] == row


def gate_row(routes, gates, expert):
    total = jnp.zeros((1, routes.shape[1]), jnp.float32)
    for k in range(routes.shape[0]):
        total = total + jnp.where(routes[k : k + 1, :] == expert, gates[k : k + 1, :], 0.0)
    return total


def halves(weights):
    high = weights.astype(jnp.bfloat16)
    low = (weights - high.astype(jnp.float32)).astype(jnp.bfloat16)
    return high, low


def normed_kernel(values_ref, routes_ref, gain_ref, *out_refs):
    expert_count = len(out_refs)
    capacity = out_refs[0].shape[0]
    wide = values_ref[...].astype(jnp.float32)
    inv_rms = lax.rsqrt(jnp.mean(wide * wide, axis=-1, keepdims=True) + EPS)
    normed = (wide * inv_rms * gain_ref[...]).astype(jnp.bfloat16)
    slots = slot_table(routes_ref[...], expert_count)
    for e in range(expert_count):
        place = placement(slots, e, capacity).astype(jnp.bfloat16)
        out_refs[e][...] = jnp.dot(place, normed, preferred_element_type=jnp.float32).astype(
            jnp.bfloat16
        )


def grads_kernel(grads_ref, routes_ref, gates_ref, *out_refs):
    expert_count = len(out_refs)
    capacity = out_refs[0].shape[0]
    grads = grads_ref[...]
    routes = routes_ref[...]
    slots = slot_table(routes, expert_count)
    for e in range(expert_count):
        place = placement(slots, e, capacity)
        high, low = halves(jnp.where(place, gate_row(routes, gates_ref[...], e), 0.0))
        out_refs[e][...] = (
            jnp.dot(high, grads, preferred_element_type=jnp.float32)
            + jnp.dot(low, grads, preferred_element_type=jnp.float32)
        ).astype(jnp.bfloat16)


def rows_dot(weights, rows):
    return lax.dot_general(
        weights, rows, (((0,), (0,)), ((), ())), preferred_element_type=jnp.float32
    )


def fwd_end_kernel(layer_ref, routes_ref, gates_ref, *refs):
    row_refs, out_ref = refs[:-1], refs[-1]
    expert_count = len(row_refs)
    capacity = row_refs[0].shape[0]
    routes = routes_ref[...]
    slots = slot_table(routes, expert_count)
    total = layer_ref[...].astype(jnp.float32)
    for e in range(expert_count):
        place = placement(slots, e, capacity)
        high, low = halves(jnp.where(place, gate_row(routes, gates_ref[...], e), 0.0))
        rows = row_refs[e][...]
        total = total + (rows_dot(high, rows) + rows_dot(low, rows))
    out_ref[...] = total.astype(jnp.bfloat16)


def bwd_end_kernel(grads_ref, saved_ref, gain_ref, routes_ref, *refs):
    row_refs, out_ref = refs[:-1], refs[-1]
    expert_count = len(row_refs)
    capacity = row_refs[0].shape[0]
    features = saved_ref.shape[1]
    slots = slot_table(routes_ref[...], expert_count)
    d_normed = None
    for e in range(expert_count):
        place = placement(slots, e, capacity).astype(jnp.bfloat16)
        part = rows_dot(place, row_refs[e][...])
        d_normed = part if d_normed is None else d_normed + part
    wide = saved_ref[...].astype(jnp.float32)
    inv_rms = lax.rsqrt(jnp.mean(wide * wide, axis=-1, keepdims=True) + EPS)
    scaled = d_normed * gain_ref[...]
    cubed = inv_rms * inv_rms * inv_rms
    inner = jnp.sum(scaled * wide, axis=-1, keepdims=True)
    out_ref[...] = (
        grads_ref[...].astype(jnp.float32) + inv_rms * scaled - cubed / features * wide * inner
    ).astype(jnp.bfloat16)


def joined(refs):
    rows = [ref[...] for ref in refs]
    if rows[0].shape[0] % 16 == 0:
        return jnp.concatenate(rows, axis=0)
    return jnp.concatenate([r.astype(jnp.float32) for r in rows], axis=0).astype(jnp.bfloat16)


def tiles(size, step):
    return [(start, min(step, size - start)) for start in range(0, size, step)]


def expert_fwd_kernel(*refs):
    expert_count = (len(refs) - 4) // 2
    row_refs = refs[:expert_count]
    weight_in, weight_out = refs[expert_count : expert_count + 2]
    out_refs = refs[expert_count + 2 : 2 * expert_count + 2]
    rows_ref, hidden_ref = refs[-2:]
    capacity = row_refs[0].shape[0]
    hidden_units, features = weight_out.shape
    rows_ref[...] = joined(row_refs)
    for start, size in tiles(hidden_units, 256):
        gate = jnp.dot(
            rows_ref[...], weight_in[:, start : start + size], preferred_element_type=jnp.float32
        )
        up = jnp.dot(
            rows_ref[...],
            weight_in[:, hidden_units + start : hidden_units + start + size],
            preferred_element_type=jnp.float32,
        )
        hidden_ref[:, start : start + size] = (gate / (1.0 + jnp.exp(-gate)) * up).astype(
            jnp.bfloat16
        )
    for start, size in tiles(features, 512):
        out = jnp.dot(
            hidden_ref[...], weight_out[:, start : start + size], preferred_element_type=jnp.float32
        )
        for d in range(expert_count):
            out_refs[d][:, start : start + size] = out[d * capacity : (d + 1) * capacity].astype(
                jnp.bfloat16
            )


def expert_again_kernel(*refs):
    expert_count = len(refs) - 4
    row_refs = refs[:expert_count]
    weight_in, gate_ref, up_ref, rows_ref = refs[expert_count:]
    hidden_units = gate_ref.shape[1]
    rows_ref[...] = joined(row_refs)
    for start, size in tiles(hidden_units, 256):
        gate_ref[:, start : start + size] = jnp.dot(
            rows_ref[...], weight_in[:, start : start + size], preferred_element_type=jnp.float32
        )
        up_ref[:, start : start + size] = jnp.dot(
            rows_ref[...],
            weight_in[:, hidden_units + start : hidden_units + start + size],
            preferred_element_type=jnp.float32,
        )


def expert_bwd_kernel(*refs):
    expert_count = (len(refs) - 6) // 2
    grad_refs = refs[:expert_count]
    gate_ref, up_ref, weight_in, weight_out = refs[expert_count : expert_count + 4]
    out_refs = refs[expert_count + 4 : 2 * expert_count + 4]
    grads_ref, both_ref = refs[-2:]
    capacity = grad_refs[0].shape[0]
    hidden_units, features = weight_out.shape
    grads_ref[...] = joined(grad_refs)
    for start, size in tiles(hidden_units, 256):
        gate = gate_ref[:, start : start + size]
        up = up_ref[:, start : start + size]
        d_hidden = lax.dot_general(
            grads_ref[...],
            weight_out[start : start + size, :],
            (((1,), (1,)), ((), ())),
            preferred_element_type=jnp.float32,
        )
        sig = 1.0 / (1.0 + jnp.exp(-gate))
        both_ref[:, start : start + size] = (
            d_hidden * up * sig * (1.0 + gate * (1.0 - sig))
        ).astype(jnp.bfloat16)
        both_ref[:, hidden_units + start : hidden_units + start + size] = (
            d_hidden * gate * sig
        ).astype(jnp.bfloat16)
    for start, size in tiles(features, 512):
        out = lax.dot_general(
            both_ref[...],
            weight_in[start : start + size, :],
            (((1,), (1,)), ((), ())),
            preferred_element_type=jnp.float32,
        )
        for d in range(expert_count):
            out_refs[d][:, start : start + size] = out[d * capacity : (d + 1) * capacity].astype(
                jnp.bfloat16
            )


def local_call(kernel, out_shapes, inputs, flops, moved, scratch=(), after=()):
    in_specs = [pl.BlockSpec(memory_space=pltpu.VMEM)] * len(inputs)
    held = len(inputs)

    def body(*refs):
        kernel(*refs[:held], *refs[held + len(after) :])

    return pl.pallas_call(
        body if after else kernel,
        out_shape=out_shapes,
        in_specs=in_specs + [pl.BlockSpec(memory_space=pl.ANY)] * len(after),
        scratch_shapes=list(scratch),
        compiler_params=pltpu.CompilerParams(vmem_limit_bytes=VMEM_LIMIT),
        cost_estimate=pl.CostEstimate(flops=flops, bytes_accessed=moved, transcendentals=0),
    )(*inputs, *after)


def per_device_direct(
    fwd_prev,
    bwd_prev,
    bwd_saved,
    fwd_routes,
    fwd_gates,
    bwd_routes,
    bwd_gates,
    norm_gain,
    w_in,
    w_out,
):
    expert_count = lax.axis_size("expert")
    tok_rows = fwd_prev.shape[1]
    features = fwd_prev.shape[2]
    top_count = fwd_routes.shape[2]
    hidden_units = w_in.shape[3] // 2
    capacity = 3 * tok_rows * top_count // (2 * expert_count)
    gain_row = norm_gain
    weight_in = w_in[0, 0]
    weight_out = w_out[0, 0]
    me = lax.axis_index("expert")
    f_routes = (fwd_routes[0] ^ me).T
    b_routes = (bwd_routes[0] ^ me).T
    f_gates = fwd_gates[0].T
    b_gates = bwd_gates[0].T
    saved = bwd_saved[0]
    layer_in = passed_along(fwd_prev[0], "section", 1)
    grad_in = passed_along(bwd_prev[0], "section", -1)

    block = jax.ShapeDtypeStruct((capacity, features), jnp.bfloat16)
    whole = jax.ShapeDtypeStruct((tok_rows, features), jnp.bfloat16)
    one_dot = 2 * expert_count * capacity * tok_rows * features
    moved = 2 * features * (tok_rows + expert_count * capacity)
    slot_total = expert_count * capacity
    blocks = [block] * expert_count
    expert_flops = 2 * slot_total * features * hidden_units
    expert_moved = 2 * features * (3 * hidden_units + 3 * slot_total)
    rows_scratch = pltpu.VMEM((slot_total, features), jnp.bfloat16)

    b_sent = local_call(normed_kernel, blocks, (saved, b_routes, gain_row), one_dot, moved)
    b_rows = exchanged(b_sent, "expert")
    f_sent = local_call(
        normed_kernel, blocks, (layer_in, f_routes, gain_row), one_dot, moved, after=(b_sent[0],)
    )
    f_rows = exchanged(f_sent, "expert")
    g_sent = local_call(
        grads_kernel, blocks, (grad_in, b_routes, b_gates), 2 * one_dot, moved, after=(f_sent[0],)
    )
    g_rows = exchanged(g_sent, "expert")
    projected = jax.ShapeDtypeStruct((slot_total, hidden_units), jnp.float32)
    gate_pre, up_pre = local_call(
        expert_again_kernel,
        [projected, projected],
        (*b_rows, weight_in),
        2 * expert_flops,
        expert_moved,
        scratch=(rows_scratch,),
        after=(g_sent[0],),
    )
    f_done = local_call(
        expert_fwd_kernel,
        blocks,
        (*f_rows, weight_in, weight_out),
        3 * expert_flops,
        expert_moved,
        scratch=(rows_scratch, pltpu.VMEM((slot_total, hidden_units), jnp.bfloat16)),
        after=(gate_pre,),
    )
    f_back = exchanged(f_done, "expert")
    b_done = local_call(
        expert_bwd_kernel,
        blocks,
        (*g_rows, gate_pre, up_pre, weight_in, weight_out),
        3 * expert_flops,
        expert_moved,
        scratch=(rows_scratch, pltpu.VMEM((slot_total, 2 * hidden_units), jnp.bfloat16)),
        after=(f_back[1],),
    )
    b_back = exchanged(b_done, "expert")
    fwd_block = local_call(
        fwd_end_kernel,
        whole,
        (layer_in, f_routes, f_gates, *f_back),
        2 * one_dot,
        moved,
        after=(b_done[0],),
    )
    bwd_block = local_call(
        bwd_end_kernel,
        whole,
        (grad_in, saved, gain_row, b_routes, *b_back),
        one_dot,
        moved,
    )
    return (fwd_block[None], bwd_block[None])


def pick(table, expert, capacity, kind, top_count):
    first = 0 if kind[0] == "f" else 2 * top_count
    routes = table[first : first + top_count]
    gates = table[first + top_count : first + 2 * top_count]
    tok_rows = table.shape[1]
    member = routes == float(expert)
    held = jnp.sum(member.astype(jnp.float32), axis=0, keepdims=True)
    before = lax.broadcasted_iota(jnp.int32, (tok_rows, tok_rows), 0) < lax.broadcasted_iota(
        jnp.int32, (tok_rows, tok_rows), 1
    )
    slots = jnp.dot(
        jnp.broadcast_to(held, (8, tok_rows)).astype(jnp.bfloat16),
        before.astype(jnp.bfloat16),
        preferred_element_type=jnp.float32,
    )[0:1]
    place = placement(jnp.where(held > 0.0, slots, -1.0), 0, capacity)
    if len(kind) == 1:
        return (place.astype(jnp.bfloat16),)
    gate = jnp.sum(jnp.where(member, gates, 0.0), axis=0, keepdims=True)
    return halves(jnp.where(place, gate, 0.0))


def to_slots(weights, values):
    total = None
    for part in weights:
        term = jnp.dot(part, values, preferred_element_type=jnp.float32)
        total = term if total is None else total + term
    return total.astype(jnp.bfloat16)


def to_tokens(weights, rows):
    total = None
    for part in weights:
        term = rows_dot(part, rows)
        total = term if total is None else total + term
    return total


def three_parts(values):
    high = values.astype(jnp.bfloat16)
    rest = values - high.astype(jnp.float32)
    mid = rest.astype(jnp.bfloat16)
    low = (rest - mid.astype(jnp.float32)).astype(jnp.bfloat16)
    return high, mid, low


def normed_halves(wide, gain):
    inv_rms = lax.rsqrt(jnp.mean(wide * wide, axis=-1, keepdims=True) + EPS)
    return (wide * inv_rms * gain).astype(jnp.bfloat16)


def first_kernel(top_count, me_ref, *refs):
    sources, refs = refs[:6], refs[6:]
    (left_ref, right_ref, table_ref, gain_out), refs = refs[:4], refs[4:]
    held, sems = refs[:6], refs[6]
    copies = [pltpu.make_async_copy(sources[i], held[i], sems.at[i]) for i in range(6)]
    for copy in copies:
        copy.start()
    for copy in copies[1:]:
        copy.wait()
    saved, gain, f_routes, f_gates, b_routes, b_gates = held
    me = me_ref[0]
    fr = (f_routes[...] ^ me).astype(jnp.float32)
    br = (b_routes[...] ^ me).astype(jnp.float32)
    fg = f_gates[...]
    bg = b_gates[...]
    table = jnp.concatenate([fr, fg, br, bg], axis=0)
    table_ref[...] = table
    packed = [fr.astype(jnp.bfloat16), br.astype(jnp.bfloat16), *three_parts(fg), *three_parts(bg)]
    packed = jnp.concatenate([part.astype(jnp.float32) for part in packed], axis=0)
    gain_out[...] = gain[...]
    tok_rows, features = saved.shape
    half = features // 2
    copies[0].wait()
    normed = normed_halves(saved[...].astype(jnp.float32), gain[...])
    capacity = left_ref.shape[0] - tok_rows - packed.shape[0]
    near = tok_rows + packed.shape[0]
    for half_ref, start, expert in ((left_ref, 0, 1), (right_ref, half, 2)):
        half_ref[:tok_rows, :] = normed[:, start : start + half]
        half_ref[tok_rows:near, :] = jnp.zeros((near - tok_rows, half), jnp.bfloat16)
        half_ref[tok_rows:near, :tok_rows] = packed.astype(jnp.bfloat16)
        other = half - start
        half_ref[near:, :] = to_slots(
            pick(table, expert, capacity, "b", top_count), normed[:, other : other + half]
        )


def unpacked(block, tok_rows, top_count):
    rows = block[tok_rows : tok_rows + 8 * top_count, :tok_rows].astype(jnp.float32)
    k = top_count
    fr, br = rows[0:k], rows[k : 2 * k]
    fg = (rows[2 * k : 3 * k] + rows[3 * k : 4 * k]) + rows[4 * k : 5 * k]
    bg = (rows[5 * k : 6 * k] + rows[6 * k : 7 * k]) + rows[7 * k : 8 * k]
    return jnp.concatenate([fr, fg, br, bg], axis=0)


def normed_kernel_halves(values_ref, gain_ref, left_ref, right_ref):
    half = left_ref.shape[1]
    normed = normed_halves(values_ref[...].astype(jnp.float32), gain_ref[...])
    left_ref[...] = normed[:, :half]
    right_ref[...] = normed[:, half:]


def split_kernel(values_ref, left_ref, right_ref):
    half = left_ref.shape[1]
    left_ref[...] = values_ref[:, :half]
    right_ref[...] = values_ref[:, half:]


def tables_kernel(top_count, from_x, from_y, x_table, y_table):
    tok_rows = x_table.shape[1]
    x_table[...] = unpacked(from_x[...], tok_rows, top_count)
    y_table[...] = unpacked(from_y[...], tok_rows, top_count)


def hop_kernel(kind, top_count, own, x_tab, y_tab, left, right, from_x, from_y, to_y, to_x):
    capacity = to_y.shape[0] // 2
    tok_rows = own.shape[1]
    to_y[:capacity, :] = to_slots(pick(own[...], 2, capacity, kind, top_count), left[:tok_rows, :])
    to_y[capacity:, :] = to_slots(
        pick(x_tab[...], 3, capacity, kind, top_count), from_x[:tok_rows, :]
    )
    to_x[:capacity, :] = to_slots(pick(own[...], 1, capacity, kind, top_count), right[:tok_rows, :])
    to_x[capacity:, :] = to_slots(
        pick(y_tab[...], 3, capacity, kind, top_count), from_y[:tok_rows, :]
    )


def far_kernel(kind, top_count, x_tab, y_tab, from_x, from_y, to_y, to_x):
    capacity = to_y.shape[0]
    tok_rows = x_tab.shape[1]
    to_y[...] = to_slots(pick(x_tab[...], 3, capacity, kind, top_count), from_x[:tok_rows, :])
    to_x[...] = to_slots(pick(y_tab[...], 3, capacity, kind, top_count), from_y[:tok_rows, :])


def assemble(kind, top_count, own, x_tab, y_tab, left, right, from_x, from_y, got_y, got_x, rows):
    capacity = rows.shape[0] // 4
    half = got_y.shape[1]
    tok_rows = own.shape[1]
    mine = pick(own[...], 0, capacity, kind, top_count)
    rows[:capacity, :half] = to_slots(mine, left[:tok_rows, :])
    rows[:capacity, half:] = to_slots(mine, right[:tok_rows, :])
    rows[capacity : 2 * capacity, :half] = to_slots(
        pick(x_tab[...], 1, capacity, kind, top_count), from_x[:tok_rows, :]
    )
    rows[2 * capacity : 3 * capacity, half:] = to_slots(
        pick(y_tab[...], 2, capacity, kind, top_count), from_y[:tok_rows, :]
    )
    if got_y.shape[0] == capacity:
        near_x, near_y = from_x[-capacity:, :], from_y[-capacity:, :]
    else:
        near_x, near_y = got_x[:capacity, :], got_y[:capacity, :]
    rows[capacity : 2 * capacity, half:] = near_x
    rows[2 * capacity : 3 * capacity, :half] = near_y
    rows[3 * capacity :, :half] = got_y[-capacity:, :]
    rows[3 * capacity :, half:] = got_x[-capacity:, :]


def near_kernel(
    kind, top_count, own, x_tab, y_tab, left, right, from_x, from_y, mine_ref, x_left, y_right
):
    capacity, half = x_left.shape
    tok_rows = own.shape[1]
    mine = pick(own[...], 0, capacity, kind, top_count)
    mine_ref[:, :half] = to_slots(mine, left[:tok_rows, :])
    mine_ref[:, half:] = to_slots(mine, right[:tok_rows, :])
    x_left[...] = to_slots(pick(x_tab[...], 1, capacity, kind, top_count), from_x[:tok_rows, :])
    y_right[...] = to_slots(pick(y_tab[...], 2, capacity, kind, top_count), from_y[:tok_rows, :])


def gathered_rows(mine, x_left, y_right, got_y, got_x, rows):
    capacity, half = x_left.shape
    rows[:capacity, :] = mine[...]
    rows[capacity : 2 * capacity, :half] = x_left[...]
    rows[capacity : 2 * capacity, half:] = got_x[:capacity, :]
    rows[2 * capacity : 3 * capacity, :half] = got_y[:capacity, :]
    rows[2 * capacity : 3 * capacity, half:] = y_right[...]
    rows[3 * capacity :, :half] = got_y[capacity:, :]
    rows[3 * capacity :, half:] = got_x[capacity:, :]


def hand_out(out, at, capacity, to_left, keep, near, onward):
    size = out.shape[1]
    rows = out.astype(jnp.bfloat16)
    mine, from_x, from_y, far = [rows[d * capacity : (d + 1) * capacity] for d in range(4)]
    keep[:, at : at + size] = mine
    near[:, at : at + size] = from_x if to_left else from_y
    onward[:capacity, at : at + size] = from_y if to_left else from_x
    onward[capacity:, at : at + size] = far


def fwd_half(hidden_ref, weight_out, to_left, keep, near, onward):
    capacity, half = keep.shape
    first = 0 if to_left else half
    for at, size in tiles(half, 512):
        out = jnp.dot(
            hidden_ref[...],
            weight_out[:, first + at : first + at + size],
            preferred_element_type=jnp.float32,
        )
        hand_out(out, at, capacity, to_left, keep, near, onward)


def bwd_half(both_ref, weight_in, to_left, keep, near, onward):
    capacity, half = keep.shape
    first = 0 if to_left else half
    for at, size in tiles(half, 512):
        out = lax.dot_general(
            both_ref[...],
            weight_in[first + at : first + at + size, :],
            (((1,), (1,)), ((), ())),
            preferred_element_type=jnp.float32,
        )
        hand_out(out, at, capacity, to_left, keep, near, onward)


def fwd_right_kernel(hidden_ref, weight_out, keep, near, onward):
    fwd_half(hidden_ref, weight_out, False, keep, near, onward)


def bwd_right_kernel(both_ref, weight_in, keep, near, onward):
    bwd_half(both_ref, weight_in, False, keep, near, onward)


def hop_again_kernel(top_count, *refs):
    dispatch, (weight_in, gate_ref, up_ref, rows_ref) = refs[:9], refs[9:]
    assemble("b", top_count, *dispatch, rows_ref)
    hidden_units = gate_ref.shape[1]
    for start, size in tiles(hidden_units, 256):
        gate_ref[:, start : start + size] = jnp.dot(
            rows_ref[...], weight_in[:, start : start + size], preferred_element_type=jnp.float32
        )
        up_ref[:, start : start + size] = jnp.dot(
            rows_ref[...],
            weight_in[:, hidden_units + start : hidden_units + start + size],
            preferred_element_type=jnp.float32,
        )


def hop_fwd_kernel(*refs):
    dispatch, refs = refs[:5], refs[5:]
    weight_in, weight_out = refs[:2]
    outs, hidden_ref, rows_ref = refs[2:5], refs[5], refs[6]
    hidden_units = weight_out.shape[0]
    gathered_rows(*dispatch, rows_ref)
    for start, size in tiles(hidden_units, 256):
        gate = jnp.dot(
            rows_ref[...], weight_in[:, start : start + size], preferred_element_type=jnp.float32
        )
        up = jnp.dot(
            rows_ref[...],
            weight_in[:, hidden_units + start : hidden_units + start + size],
            preferred_element_type=jnp.float32,
        )
        hidden_ref[:, start : start + size] = (gate / (1.0 + jnp.exp(-gate)) * up).astype(
            jnp.bfloat16
        )
    fwd_half(hidden_ref, weight_out, True, *outs)


def hop_bwd_kernel(*refs):
    dispatch, refs = refs[:5], refs[5:]
    gate_ref, up_ref, weight_in, weight_out = refs[:4]
    outs, both_ref, grads_ref = refs[4:7], refs[7], refs[8]
    hidden_units = weight_out.shape[0]
    gathered_rows(*dispatch, grads_ref)
    for start, size in tiles(hidden_units, 256):
        gate = gate_ref[:, start : start + size]
        up = up_ref[:, start : start + size]
        d_hidden = lax.dot_general(
            grads_ref[...],
            weight_out[start : start + size, :],
            (((1,), (1,)), ((), ())),
            preferred_element_type=jnp.float32,
        )
        sig = 1.0 / (1.0 + jnp.exp(-gate))
        both_ref[:, start : start + size] = (
            d_hidden * up * sig * (1.0 + gate * (1.0 - sig))
        ).astype(jnp.bfloat16)
        both_ref[:, hidden_units + start : hidden_units + start + size] = (
            d_hidden * gate * sig
        ).astype(jnp.bfloat16)
    bwd_half(both_ref, weight_in, True, *outs)


def sums_kernel(kind, top_count, here, table_ref, near, far, out):
    capacity = near.shape[0]
    table = table_ref[...]
    out[...] = (
        to_tokens(pick(table, here, capacity, kind, top_count), near[...])
        + to_tokens(pick(table, 3, capacity, kind, top_count), far[capacity:, :])
    ).astype(jnp.bfloat16)


def hop_fwd_near_kernel(
    top_count, layer_ref, own, keep_left, keep_right, got_y, got_x, sum_y, left_ref, right_ref
):
    capacity, half = keep_left.shape
    mine = pick(own[...], 0, capacity, "fg", top_count)
    near_y = pick(own[...], 2, capacity, "fg", top_count)
    near_x = pick(own[...], 1, capacity, "fg", top_count)
    left = to_tokens(mine, keep_left[...]) + to_tokens(near_y, got_y[:capacity, :])
    right = to_tokens(mine, keep_right[...]) + to_tokens(near_x, got_x[:capacity, :])
    left_ref[...] = layer_ref[:, :half].astype(jnp.float32) + left
    right = right + sum_y[...].astype(jnp.float32)
    right_ref[...] = layer_ref[:, half:].astype(jnp.float32) + right


def hop_fwd_end_kernel(left_ref, right_ref, sum_x, out_ref):
    half = left_ref.shape[1]
    out_ref[:, :half] = (left_ref[...] + sum_x[...].astype(jnp.float32)).astype(jnp.bfloat16)
    out_ref[:, half:] = right_ref[...].astype(jnp.bfloat16)


def hop_bwd_near_kernel(
    top_count, own, keep_left, keep_right, got_y, got_x, left_ref, right_ref
):
    capacity = keep_left.shape[0]
    mine = pick(own[...], 0, capacity, "b", top_count)
    near_y = pick(own[...], 2, capacity, "b", top_count)
    near_x = pick(own[...], 1, capacity, "b", top_count)
    left_ref[...] = to_tokens(mine, keep_left[...]) + to_tokens(near_y, got_y[:capacity, :])
    right_ref[...] = to_tokens(mine, keep_right[...]) + to_tokens(near_x, got_x[:capacity, :])


def order_kernel(order_ref):
    order_ref[...] = jnp.zeros_like(order_ref)


def hop_bwd_end_kernel(
    grads_ref, saved_ref, gain_ref, left_ref, right_ref, sum_x, sum_y, out_ref, order_ref
):
    order_ref[...] = jnp.zeros_like(order_ref)
    features = saved_ref.shape[1]
    half = features // 2
    parts = []
    left = left_ref[...] + sum_x[...].astype(jnp.float32)
    right = right_ref[...] + sum_y[...].astype(jnp.float32)
    for start, d_normed in ((0, left), (half, right)):
        wide = saved_ref[:, start : start + half].astype(jnp.float32)
        scaled = d_normed * gain_ref[:, start : start + half]
        parts.append((start, wide, scaled))
    square = sum(jnp.sum(wide * wide, axis=-1, keepdims=True) for _, wide, _ in parts)
    inner = sum(jnp.sum(scaled * wide, axis=-1, keepdims=True) for _, wide, scaled in parts)
    inv_rms = lax.rsqrt(square / features + EPS)
    factor = inv_rms * inv_rms * inv_rms / features * inner
    for start, wide, scaled in parts:
        out_ref[:, start : start + half] = (
            grads_ref[:, start : start + half].astype(jnp.float32)
            + inv_rms * scaled
            - factor * wide
        ).astype(jnp.bfloat16)


def per_device_hops(
    fwd_prev,
    bwd_prev,
    bwd_saved,
    fwd_routes,
    fwd_gates,
    bwd_routes,
    bwd_gates,
    norm_gain,
    w_in,
    w_out,
):
    tok_rows, features = fwd_prev.shape[1:]
    top_count = fwd_routes.shape[2]
    hidden_units = w_in.shape[3] // 2
    capacity = 3 * tok_rows * top_count // 8
    half = features // 2
    gain_row = norm_gain
    weight_in = w_in[0, 0]
    weight_out = w_out[0, 0]
    me = lax.axis_index("expert").astype(jnp.int32).reshape(1)
    saved = bwd_saved[0]
    layer_in = passed_along(fwd_prev[0], "section", 1)
    grad_in = passed_along(bwd_prev[0], "section", -1)

    def shaped(rows, columns, dtype=jnp.bfloat16):
        return jax.ShapeDtypeStruct((rows, columns), dtype)

    def crossed(left, right):
        return swapped(left, "expert", 1), swapped(right, "expert", 2)

    slot_total = 4 * capacity
    table_rows = 4 * top_count
    one_hop = moved = 1024
    expert_flops = 2 * slot_total * features * hidden_units
    expert_moved = 2 * features * (3 * hidden_units + 3 * slot_total)
    rows_scratch = pltpu.VMEM((slot_total, features), jnp.bfloat16)
    halves_out = [shaped(tok_rows, half)] * 2
    hop_out = [shaped(2 * capacity, half)] * 2
    half_out = [shaped(capacity, half), shaped(capacity, half), shaped(2 * capacity, half)]
    hidden_shape = shaped(slot_total, hidden_units)
    both_shape = shaped(slot_total, 2 * hidden_units)
    table_shape = shaped(table_rows, tok_rows, jnp.float32)
    first_rows = tok_rows + 8 * top_count + capacity

    b_left, b_right, own, gain_here = pl.pallas_call(
        functools.partial(first_kernel, top_count),
        out_shape=[
            shaped(first_rows, half),
            shaped(first_rows, half),
            table_shape,
            shaped(1, features, jnp.float32),
        ],
        in_specs=[pl.BlockSpec(memory_space=pltpu.SMEM)]
        + [pl.BlockSpec(memory_space=pltpu.HBM)] * 6,
        scratch_shapes=[
            pltpu.VMEM((tok_rows, features), jnp.bfloat16),
            pltpu.VMEM((1, features), jnp.float32),
            pltpu.VMEM((top_count, tok_rows), jnp.int32),
            pltpu.VMEM((top_count, tok_rows), jnp.float32),
            pltpu.VMEM((top_count, tok_rows), jnp.int32),
            pltpu.VMEM((top_count, tok_rows), jnp.float32),
            pltpu.SemaphoreType.DMA((6,)),
        ],
        compiler_params=pltpu.CompilerParams(vmem_limit_bytes=VMEM_LIMIT),
        cost_estimate=pl.CostEstimate(flops=one_hop, bytes_accessed=moved, transcendentals=0),
    )(
        me,
        *[
            pltpu.with_memory_space_constraint(value, pltpu.HBM)
            for value in (
                saved,
                gain_row,
                fwd_routes[0].T,
                fwd_gates[0].T,
                bwd_routes[0].T,
                bwd_gates[0].T,
            )
        ],
    )
    b_from_x, b_from_y = crossed(b_left, b_right)

    def onward(kind, sent, got, after):
        to_y, to_x = local_call(
            functools.partial(hop_kernel, kind, top_count),
            hop_out,
            (*tabs, *sent, *got),
            one_hop,
            moved,
            after=after,
        )
        return swapped(to_y, "expert", 2), swapped(to_x, "expert", 1), to_y

    f_left, f_right = local_call(
        normed_kernel_halves, halves_out, (layer_in, gain_here), one_hop, moved, after=(b_left,)
    )
    f_from_x, f_from_y = crossed(f_left, f_right)
    x_tab, y_tab = local_call(
        functools.partial(tables_kernel, top_count),
        [table_shape] * 2,
        (b_from_x, b_from_y),
        TABLES_COST,
        1024,
        after=(f_left,),
    )
    g_left, g_right = local_call(split_kernel, halves_out, (grad_in,), 1024, moved, after=(x_tab,))
    g_from_x, g_from_y = crossed(g_left, g_right)
    tabs = (own, x_tab, y_tab)
    b_to_y, b_to_x = local_call(
        functools.partial(far_kernel, "b", top_count),
        [shaped(capacity, half)] * 2,
        (x_tab, y_tab, b_from_x, b_from_y),
        one_hop,
        moved,
        after=(g_left,),
    )
    b_got_y, b_got_x = swapped(b_to_y, "expert", 2), swapped(b_to_x, "expert", 1)
    f_got_y, f_got_x, f_to_y = onward("f", (f_left, f_right), (f_from_x, f_from_y), (b_to_y,))
    g_got_y, g_got_x, g_to_y = onward("bg", (g_left, g_right), (g_from_x, g_from_y), (f_to_y,))
    gate_pre, up_pre = local_call(
        functools.partial(hop_again_kernel, top_count),
        [shaped(slot_total, hidden_units, jnp.float32)] * 2,
        (*tabs, b_left, b_right, b_from_x, b_from_y, b_got_y, b_got_x, weight_in),
        2 * expert_flops,
        expert_moved,
        scratch=(rows_scratch,),
        after=(g_to_y,),
    )
    near_out = [shaped(capacity, features), shaped(capacity, half), shaped(capacity, half)]
    g_near = local_call(
        functools.partial(near_kernel, "bg", top_count),
        near_out,
        (*tabs, g_left, g_right, g_from_x, g_from_y),
        one_hop,
        moved,
        after=(gate_pre,),
    )
    f_near = local_call(
        functools.partial(near_kernel, "f", top_count),
        near_out,
        (*tabs, f_left, f_right, f_from_x, f_from_y),
        one_hop,
        moved,
        after=(g_near[1],),
    )
    f_keep_l, f_near_l, f_on_l, hidden = local_call(
        hop_fwd_kernel,
        half_out + [hidden_shape],
        (*f_near, f_got_y, f_got_x, weight_in, weight_out),
        5 * expert_flops // 2,
        expert_moved,
        scratch=(rows_scratch,),
        after=(f_near[1],),
    )
    f_ret_y = swapped(f_on_l, "expert", 2)
    f_keep_r, f_near_r, f_on_r = local_call(
        fwd_right_kernel, half_out, (hidden, weight_out), 1024, 1024
    )
    f_ret_x = swapped(f_on_r, "expert", 1)
    b_keep_l, b_near_l, b_on_l, both = local_call(
        hop_bwd_kernel,
        half_out + [both_shape],
        (*g_near, g_got_y, g_got_x, gate_pre, up_pre, weight_in, weight_out),
        2 * expert_flops,
        expert_moved,
        scratch=(rows_scratch,),
        after=(f_keep_r,),
    )
    b_ret_y = swapped(b_on_l, "expert", 2)
    b_keep_r, b_near_r, b_on_r = local_call(
        bwd_right_kernel, half_out, (both, weight_in), 1024, 1024, after=(f_ret_y,)
    )
    b_ret_x = swapped(b_on_r, "expert", 1)

    def summed_call(kind, here, table, near, far, after):
        part = local_call(
            functools.partial(sums_kernel, kind, top_count, here),
            shaped(tok_rows, half),
            (table, near, far),
            one_hop,
            moved,
            after=after,
        )
        return swapped(part, "expert", here), part

    f_sum_y, last = summed_call("fg", 2, y_tab, f_near_r, f_ret_x, (b_keep_r,))
    b_sum_x, last = summed_call("b", 1, x_tab, b_near_l, b_ret_y, (last,))
    b_sum_y, last = summed_call("b", 2, y_tab, b_near_r, b_ret_x, (last,))
    f_sum_x, last = summed_call("fg", 1, x_tab, f_near_l, f_ret_y, (last,))
    order_shape = shaped(8, 128, jnp.float32)
    wide_halves = [shaped(tok_rows, half, jnp.float32)] * 2
    b_part = local_call(
        functools.partial(hop_bwd_near_kernel, top_count),
        wide_halves,
        (own, b_keep_l, b_keep_r, b_ret_y, b_ret_x),
        one_hop,
        moved,
        after=(last,),
    )
    f_part = local_call(
        functools.partial(hop_fwd_near_kernel, top_count),
        wide_halves,
        (layer_in, own, f_keep_l, f_keep_r, f_ret_y, f_ret_x, f_sum_y),
        one_hop,
        moved,
        after=(b_part[0],),
    )
    x_there = local_call(
        order_kernel, order_shape, (), one_hop, moved, after=(f_part[0], b_sum_x)
    )
    bwd_block, order = local_call(
        hop_bwd_end_kernel,
        [shaped(tok_rows, features), order_shape],
        (grad_in, saved, gain_here, *b_part, b_sum_x, b_sum_y),
        one_hop,
        moved,
        after=(x_there,),
    )
    fwd_block = local_call(
        hop_fwd_end_kernel,
        shaped(tok_rows, features),
        (*f_part, f_sum_x),
        one_hop,
        moved,
        after=(order,),
    )
    return (fwd_block[None], bwd_block[None])


def per_device(*arrays):
    if lax.axis_size("expert") == 4:
        return per_device_hops(*arrays)
    return per_device_direct(*arrays)


def solution(mesh):
    in_specs = (
        P("section", "expert", None),
        P("section", "expert", None),
        P("section", "expert", None),
        P("section", "expert", None),
        P("section", "expert", None),
        P("section", "expert", None),
        P("section", "expert", None),
        P("section", None),
        P("section", "expert", None, None),
        P("section", "expert", None, None),
    )
    out_specs = (P("section", "expert", None), P("section", "expert", None))
    return jax.shard_map(
        per_device, mesh=mesh, in_specs=in_specs, out_specs=out_specs, check_vma=False
    )
```

```python
import functools

import jax
import jax.numpy as jnp
from jax import lax
from jax.experimental import pallas as pl
from jax.experimental.pallas import tpu as pltpu
from jax.sharding import PartitionSpec as P

EPS = 1e-06
VMEM_LIMIT = 32 * 1024 * 1024
TABLES_COST = 6_000_000_000


def passed_along(value, axis, steps):
    count = lax.axis_size(axis)
    pairs = [(source, (source + steps) % count) for source in range(count)]
    return lax.ppermute(value, axis, pairs)


def swapped(value, axis, offset):
    count = lax.axis_size(axis)
    pairs = [(source, source ^ offset) for source in range(count)]
    return lax.ppermute(value, axis, pairs)


def exchanged(blocks, axis):
    return [blocks[0]] + [swapped(blocks[d], axis, d) for d in range(1, len(blocks))]


def slot_table(routes, expert_count):
    top_count, tok_rows = routes.shape
    experts = max(8, expert_count)
    wanted = lax.broadcasted_iota(jnp.int32, (experts, tok_rows), 0)
    member = routes[0:1, :] == wanted
    for k in range(1, top_count):
        member = jnp.logical_or(member, routes[k : k + 1, :] == wanted)
    before = lax.broadcasted_iota(jnp.int32, (tok_rows, tok_rows), 0) < lax.broadcasted_iota(
        jnp.int32, (tok_rows, tok_rows), 1
    )
    slots = jnp.dot(
        member.astype(jnp.bfloat16),
        before.astype(jnp.bfloat16),
        preferred_element_type=jnp.float32,
    )
    return jnp.where(member, slots, -1.0)


def placement(slots, expert, capacity):
    tok_rows = slots.shape[1]
    row = lax.broadcasted_iota(jnp.int32, (capacity, tok_rows), 0).astype(jnp.float32)
    return slots[expert : expert + 1, :] == row


def gate_row(routes, gates, expert):
    total = jnp.zeros((1, routes.shape[1]), jnp.float32)
    for k in range(routes.shape[0]):
        total = total + jnp.where(routes[k : k + 1, :] == expert, gates[k : k + 1, :], 0.0)
    return total


def halves(weights):
    high = weights.astype(jnp.bfloat16)
    low = (weights - high.astype(jnp.float32)).astype(jnp.bfloat16)
    return high, low


def normed_kernel(values_ref, routes_ref, gain_ref, *out_refs):
    expert_count = len(out_refs)
    capacity = out_refs[0].shape[0]
    wide = values_ref[...].astype(jnp.float32)
    inv_rms = lax.rsqrt(jnp.mean(wide * wide, axis=-1, keepdims=True) + EPS)
    normed = (wide * inv_rms * gain_ref[...]).astype(jnp.bfloat16)
    slots = slot_table(routes_ref[...], expert_count)
    for e in range(expert_count):
        place = placement(slots, e, capacity).astype(jnp.bfloat16)
        out_refs[e][...] = jnp.dot(place, normed, preferred_element_type=jnp.float32).astype(
            jnp.bfloat16
        )


def grads_kernel(grads_ref, routes_ref, gates_ref, *out_refs):
    expert_count = len(out_refs)
    capacity = out_refs[0].shape[0]
    grads = grads_ref[...]
    routes = routes_ref[...]
    slots = slot_table(routes, expert_count)
    for e in range(expert_count):
        place = placement(slots, e, capacity)
        high, low = halves(jnp.where(place, gate_row(routes, gates_ref[...], e), 0.0))
        out_refs[e][...] = (
            jnp.dot(high, grads, preferred_element_type=jnp.float32)
            + jnp.dot(low, grads, preferred_element_type=jnp.float32)
        ).astype(jnp.bfloat16)


def rows_dot(weights, rows):
    return lax.dot_general(
        weights, rows, (((0,), (0,)), ((), ())), preferred_element_type=jnp.float32
    )


def fwd_end_kernel(layer_ref, routes_ref, gates_ref, *refs):
    row_refs, out_ref = refs[:-1], refs[-1]
    expert_count = len(row_refs)
    capacity = row_refs[0].shape[0]
    routes = routes_ref[...]
    slots = slot_table(routes, expert_count)
    total = layer_ref[...].astype(jnp.float32)
    for e in range(expert_count):
        place = placement(slots, e, capacity)
        high, low = halves(jnp.where(place, gate_row(routes, gates_ref[...], e), 0.0))
        rows = row_refs[e][...]
        total = total + (rows_dot(high, rows) + rows_dot(low, rows))
    out_ref[...] = total.astype(jnp.bfloat16)


def bwd_end_kernel(grads_ref, saved_ref, gain_ref, routes_ref, *refs):
    row_refs, out_ref = refs[:-1], refs[-1]
    expert_count = len(row_refs)
    capacity = row_refs[0].shape[0]
    features = saved_ref.shape[1]
    slots = slot_table(routes_ref[...], expert_count)
    d_normed = None
    for e in range(expert_count):
        place = placement(slots, e, capacity).astype(jnp.bfloat16)
        part = rows_dot(place, row_refs[e][...])
        d_normed = part if d_normed is None else d_normed + part
    wide = saved_ref[...].astype(jnp.float32)
    inv_rms = lax.rsqrt(jnp.mean(wide * wide, axis=-1, keepdims=True) + EPS)
    scaled = d_normed * gain_ref[...]
    cubed = inv_rms * inv_rms * inv_rms
    inner = jnp.sum(scaled * wide, axis=-1, keepdims=True)
    out_ref[...] = (
        grads_ref[...].astype(jnp.float32) + inv_rms * scaled - cubed / features * wide * inner
    ).astype(jnp.bfloat16)


def joined(refs):
    rows = [ref[...] for ref in refs]
    if rows[0].shape[0] % 16 == 0:
        return jnp.concatenate(rows, axis=0)
    return jnp.concatenate([r.astype(jnp.float32) for r in rows], axis=0).astype(jnp.bfloat16)


def tiles(size, step):
    return [(start, min(step, size - start)) for start in range(0, size, step)]


def expert_fwd_kernel(*refs):
    expert_count = (len(refs) - 4) // 2
    row_refs = refs[:expert_count]
    weight_in, weight_out = refs[expert_count : expert_count + 2]
    out_refs = refs[expert_count + 2 : 2 * expert_count + 2]
    rows_ref, hidden_ref = refs[-2:]
    capacity = row_refs[0].shape[0]
    hidden_units, features = weight_out.shape
    rows_ref[...] = joined(row_refs)
    for start, size in tiles(hidden_units, 256):
        gate = jnp.dot(
            rows_ref[...], weight_in[:, start : start + size], preferred_element_type=jnp.float32
        )
        up = jnp.dot(
            rows_ref[...],
            weight_in[:, hidden_units + start : hidden_units + start + size],
            preferred_element_type=jnp.float32,
        )
        hidden_ref[:, start : start + size] = (gate / (1.0 + jnp.exp(-gate)) * up).astype(
            jnp.bfloat16
        )
    for start, size in tiles(features, 512):
        out = jnp.dot(
            hidden_ref[...], weight_out[:, start : start + size], preferred_element_type=jnp.float32
        )
        for d in range(expert_count):
            out_refs[d][:, start : start + size] = out[d * capacity : (d + 1) * capacity].astype(
                jnp.bfloat16
            )


def expert_again_kernel(*refs):
    expert_count = len(refs) - 4
    row_refs = refs[:expert_count]
    weight_in, gate_ref, up_ref, rows_ref = refs[expert_count:]
    hidden_units = gate_ref.shape[1]
    rows_ref[...] = joined(row_refs)
    for start, size in tiles(hidden_units, 256):
        gate_ref[:, start : start + size] = jnp.dot(
            rows_ref[...], weight_in[:, start : start + size], preferred_element_type=jnp.float32
        )
        up_ref[:, start : start + size] = jnp.dot(
            rows_ref[...],
            weight_in[:, hidden_units + start : hidden_units + start + size],
            preferred_element_type=jnp.float32,
        )


def expert_bwd_kernel(*refs):
    expert_count = (len(refs) - 6) // 2
    grad_refs = refs[:expert_count]
    gate_ref, up_ref, weight_in, weight_out = refs[expert_count : expert_count + 4]
    out_refs = refs[expert_count + 4 : 2 * expert_count + 4]
    grads_ref, both_ref = refs[-2:]
    capacity = grad_refs[0].shape[0]
    hidden_units, features = weight_out.shape
    grads_ref[...] = joined(grad_refs)
    for start, size in tiles(hidden_units, 256):
        gate = gate_ref[:, start : start + size]
        up = up_ref[:, start : start + size]
        d_hidden = lax.dot_general(
            grads_ref[...],
            weight_out[start : start + size, :],
            (((1,), (1,)), ((), ())),
            preferred_element_type=jnp.float32,
        )
        sig = 1.0 / (1.0 + jnp.exp(-gate))
        both_ref[:, start : start + size] = (
            d_hidden * up * sig * (1.0 + gate * (1.0 - sig))
        ).astype(jnp.bfloat16)
        both_ref[:, hidden_units + start : hidden_units + start + size] = (
            d_hidden * gate * sig
        ).astype(jnp.bfloat16)
    for start, size in tiles(features, 512):
        out = lax.dot_general(
            both_ref[...],
            weight_in[start : start + size, :],
            (((1,), (1,)), ((), ())),
            preferred_element_type=jnp.float32,
        )
        for d in range(expert_count):
            out_refs[d][:, start : start + size] = out[d * capacity : (d + 1) * capacity].astype(
                jnp.bfloat16
            )


def local_call(kernel, out_shapes, inputs, flops, moved, scratch=(), after=()):
    in_specs = [pl.BlockSpec(memory_space=pltpu.VMEM)] * len(inputs)
    held = len(inputs)

    def body(*refs):
        kernel(*refs[:held], *refs[held + len(after) :])

    return pl.pallas_call(
        body if after else kernel,
        out_shape=out_shapes,
        in_specs=in_specs + [pl.BlockSpec(memory_space=pl.ANY)] * len(after),
        scratch_shapes=list(scratch),
        compiler_params=pltpu.CompilerParams(vmem_limit_bytes=VMEM_LIMIT),
        cost_estimate=pl.CostEstimate(flops=flops, bytes_accessed=moved, transcendentals=0),
    )(*inputs, *after)


def per_device_direct(
    fwd_prev,
    bwd_prev,
    bwd_saved,
    fwd_routes,
    fwd_gates,
    bwd_routes,
    bwd_gates,
    norm_gain,
    w_in,
    w_out,
):
    expert_count = lax.axis_size("expert")
    tok_rows = fwd_prev.shape[1]
    features = fwd_prev.shape[2]
    top_count = fwd_routes.shape[2]
    hidden_units = w_in.shape[3] // 2
    capacity = 3 * tok_rows * top_count // (2 * expert_count)
    gain_row = norm_gain
    weight_in = w_in[0, 0]
    weight_out = w_out[0, 0]
    me = lax.axis_index("expert")
    f_routes = (fwd_routes[0] ^ me).T
    b_routes = (bwd_routes[0] ^ me).T
    f_gates = fwd_gates[0].T
    b_gates = bwd_gates[0].T
    saved = bwd_saved[0]
    layer_in = passed_along(fwd_prev[0], "section", 1)
    grad_in = passed_along(bwd_prev[0], "section", -1)

    block = jax.ShapeDtypeStruct((capacity, features), jnp.bfloat16)
    whole = jax.ShapeDtypeStruct((tok_rows, features), jnp.bfloat16)
    one_dot = 2 * expert_count * capacity * tok_rows * features
    moved = 2 * features * (tok_rows + expert_count * capacity)
    slot_total = expert_count * capacity
    blocks = [block] * expert_count
    expert_flops = 2 * slot_total * features * hidden_units
    expert_moved = 2 * features * (3 * hidden_units + 3 * slot_total)
    rows_scratch = pltpu.VMEM((slot_total, features), jnp.bfloat16)

    b_sent = local_call(normed_kernel, blocks, (saved, b_routes, gain_row), one_dot, moved)
    b_rows = exchanged(b_sent, "expert")
    f_sent = local_call(
        normed_kernel, blocks, (layer_in, f_routes, gain_row), one_dot, moved, after=(b_sent[0],)
    )
    f_rows = exchanged(f_sent, "expert")
    g_sent = local_call(
        grads_kernel, blocks, (grad_in, b_routes, b_gates), 2 * one_dot, moved, after=(f_sent[0],)
    )
    g_rows = exchanged(g_sent, "expert")
    projected = jax.ShapeDtypeStruct((slot_total, hidden_units), jnp.float32)
    gate_pre, up_pre = local_call(
        expert_again_kernel,
        [projected, projected],
        (*b_rows, weight_in),
        2 * expert_flops,
        expert_moved,
        scratch=(rows_scratch,),
        after=(g_sent[0],),
    )
    f_done = local_call(
        expert_fwd_kernel,
        blocks,
        (*f_rows, weight_in, weight_out),
        3 * expert_flops,
        expert_moved,
        scratch=(rows_scratch, pltpu.VMEM((slot_total, hidden_units), jnp.bfloat16)),
        after=(gate_pre,),
    )
    f_back = exchanged(f_done, "expert")
    b_done = local_call(
        expert_bwd_kernel,
        blocks,
        (*g_rows, gate_pre, up_pre, weight_in, weight_out),
        3 * expert_flops,
        expert_moved,
        scratch=(rows_scratch, pltpu.VMEM((slot_total, 2 * hidden_units), jnp.bfloat16)),
        after=(f_back[1],),
    )
    b_back = exchanged(b_done, "expert")
    fwd_block = local_call(
        fwd_end_kernel,
        whole,
        (layer_in, f_routes, f_gates, *f_back),
        2 * one_dot,
        moved,
        after=(b_done[0],),
    )
    bwd_block = local_call(
        bwd_end_kernel,
        whole,
        (grad_in, saved, gain_row, b_routes, *b_back),
        one_dot,
        moved,
    )
    return (fwd_block[None], bwd_block[None])


def pick(table, expert, capacity, kind, top_count):
    first = 0 if kind[0] == "f" else 2 * top_count
    routes = table[first : first + top_count]
    gates = table[first + top_count : first + 2 * top_count]
    tok_rows = table.shape[1]
    member = routes == float(expert)
    held = jnp.sum(member.astype(jnp.float32), axis=0, keepdims=True)
    before = lax.broadcasted_iota(jnp.int32, (tok_rows, tok_rows), 0) < lax.broadcasted_iota(
        jnp.int32, (tok_rows, tok_rows), 1
    )
    slots = jnp.dot(
        jnp.broadcast_to(held, (8, tok_rows)).astype(jnp.bfloat16),
        before.astype(jnp.bfloat16),
        preferred_element_type=jnp.float32,
    )[0:1]
    place = placement(jnp.where(held > 0.0, slots, -1.0), 0, capacity)
    if len(kind) == 1:
        return (place.astype(jnp.bfloat16),)
    gate = jnp.sum(jnp.where(member, gates, 0.0), axis=0, keepdims=True)
    return halves(jnp.where(place, gate, 0.0))


def to_slots(weights, values):
    total = None
    for part in weights:
        term = jnp.dot(part, values, preferred_element_type=jnp.float32)
        total = term if total is None else total + term
    return total.astype(jnp.bfloat16)


def to_tokens(weights, rows):
    total = None
    for part in weights:
        term = rows_dot(part, rows)
        total = term if total is None else total + term
    return total


def three_parts(values):
    high = values.astype(jnp.bfloat16)
    rest = values - high.astype(jnp.float32)
    mid = rest.astype(jnp.bfloat16)
    low = (rest - mid.astype(jnp.float32)).astype(jnp.bfloat16)
    return high, mid, low


def normed_halves(wide, gain):
    inv_rms = lax.rsqrt(jnp.mean(wide * wide, axis=-1, keepdims=True) + EPS)
    return (wide * inv_rms * gain).astype(jnp.bfloat16)


def first_kernel(top_count, me_ref, *refs):
    sources, refs = refs[:6], refs[6:]
    (left_ref, right_ref, table_ref, gain_out), refs = refs[:4], refs[4:]
    held, sems = refs[:6], refs[6]
    copies = [pltpu.make_async_copy(sources[i], held[i], sems.at[i]) for i in range(6)]
    for copy in copies:
        copy.start()
    for copy in copies[1:]:
        copy.wait()
    saved, gain, f_routes, f_gates, b_routes, b_gates = held
    me = me_ref[0]
    fr = (f_routes[...] ^ me).astype(jnp.float32)
    br = (b_routes[...] ^ me).astype(jnp.float32)
    fg = f_gates[...]
    bg = b_gates[...]
    table = jnp.concatenate([fr, fg, br, bg], axis=0)
    table_ref[...] = table
    packed = [fr.astype(jnp.bfloat16), br.astype(jnp.bfloat16), *three_parts(fg), *three_parts(bg)]
    packed = jnp.concatenate([part.astype(jnp.float32) for part in packed], axis=0)
    gain_out[...] = gain[...]
    tok_rows, features = saved.shape
    half = features // 2
    copies[0].wait()
    normed = normed_halves(saved[...].astype(jnp.float32), gain[...])
    capacity = left_ref.shape[0] - tok_rows - packed.shape[0]
    near = tok_rows + packed.shape[0]
    for half_ref, start, expert in ((left_ref, 0, 1), (right_ref, half, 2)):
        half_ref[:tok_rows, :] = normed[:, start : start + half]
        half_ref[tok_rows:near, :] = jnp.zeros((near - tok_rows, half), jnp.bfloat16)
        half_ref[tok_rows:near, :tok_rows] = packed.astype(jnp.bfloat16)
        other = half - start
        half_ref[near:, :] = to_slots(
            pick(table, expert, capacity, "b", top_count), normed[:, other : other + half]
        )


def unpacked(block, tok_rows, top_count):
    rows = block[tok_rows : tok_rows + 8 * top_count, :tok_rows].astype(jnp.float32)
    k = top_count
    fr, br = rows[0:k], rows[k : 2 * k]
    fg = (rows[2 * k : 3 * k] + rows[3 * k : 4 * k]) + rows[4 * k : 5 * k]
    bg = (rows[5 * k : 6 * k] + rows[6 * k : 7 * k]) + rows[7 * k : 8 * k]
    return jnp.concatenate([fr, fg, br, bg], axis=0)


def normed_kernel_halves(values_ref, gain_ref, left_ref, right_ref):
    half = left_ref.shape[1]
    normed = normed_halves(values_ref[...].astype(jnp.float32), gain_ref[...])
    left_ref[...] = normed[:, :half]
    right_ref[...] = normed[:, half:]


def split_kernel(values_ref, left_ref, right_ref):
    half = left_ref.shape[1]
    left_ref[...] = values_ref[:, :half]
    right_ref[...] = values_ref[:, half:]


def tables_kernel(top_count, from_x, from_y, x_table, y_table):
    tok_rows = x_table.shape[1]
    x_table[...] = unpacked(from_x[...], tok_rows, top_count)
    y_table[...] = unpacked(from_y[...], tok_rows, top_count)


def hop_kernel(kind, top_count, own, x_tab, y_tab, left, right, from_x, from_y, to_y, to_x):
    capacity = to_y.shape[0] // 2
    tok_rows = own.shape[1]
    to_y[:capacity, :] = to_slots(pick(own[...], 2, capacity, kind, top_count), left[:tok_rows, :])
    to_y[capacity:, :] = to_slots(
        pick(x_tab[...], 3, capacity, kind, top_count), from_x[:tok_rows, :]
    )
    to_x[:capacity, :] = to_slots(pick(own[...], 1, capacity, kind, top_count), right[:tok_rows, :])
    to_x[capacity:, :] = to_slots(
        pick(y_tab[...], 3, capacity, kind, top_count), from_y[:tok_rows, :]
    )


def far_kernel(kind, top_count, x_tab, y_tab, from_x, from_y, to_y, to_x):
    capacity = to_y.shape[0]
    tok_rows = x_tab.shape[1]
    to_y[...] = to_slots(pick(x_tab[...], 3, capacity, kind, top_count), from_x[:tok_rows, :])
    to_x[...] = to_slots(pick(y_tab[...], 3, capacity, kind, top_count), from_y[:tok_rows, :])


def assemble(kind, top_count, own, x_tab, y_tab, left, right, from_x, from_y, got_y, got_x, rows):
    capacity = rows.shape[0] // 4
    half = got_y.shape[1]
    tok_rows = own.shape[1]
    mine = pick(own[...], 0, capacity, kind, top_count)
    rows[:capacity, :half] = to_slots(mine, left[:tok_rows, :])
    rows[:capacity, half:] = to_slots(mine, right[:tok_rows, :])
    rows[capacity : 2 * capacity, :half] = to_slots(
        pick(x_tab[...], 1, capacity, kind, top_count), from_x[:tok_rows, :]
    )
    rows[2 * capacity : 3 * capacity, half:] = to_slots(
        pick(y_tab[...], 2, capacity, kind, top_count), from_y[:tok_rows, :]
    )
    if got_y.shape[0] == capacity:
        near_x, near_y = from_x[-capacity:, :], from_y[-capacity:, :]
    else:
        near_x, near_y = got_x[:capacity, :], got_y[:capacity, :]
    rows[capacity : 2 * capacity, half:] = near_x
    rows[2 * capacity : 3 * capacity, :half] = near_y
    rows[3 * capacity :, :half] = got_y[-capacity:, :]
    rows[3 * capacity :, half:] = got_x[-capacity:, :]


def near_kernel(
    kind, top_count, own, x_tab, y_tab, left, right, from_x, from_y, mine_ref, x_left, y_right
):
    capacity, half = x_left.shape
    tok_rows = own.shape[1]
    mine = pick(own[...], 0, capacity, kind, top_count)
    mine_ref[:, :half] = to_slots(mine, left[:tok_rows, :])
    mine_ref[:, half:] = to_slots(mine, right[:tok_rows, :])
    x_left[...] = to_slots(pick(x_tab[...], 1, capacity, kind, top_count), from_x[:tok_rows, :])
    y_right[...] = to_slots(pick(y_tab[...], 2, capacity, kind, top_count), from_y[:tok_rows, :])


def gathered_rows(mine, x_left, y_right, got_y, got_x, rows):
    capacity, half = x_left.shape
    rows[:capacity, :] = mine[...]
    rows[capacity : 2 * capacity, :half] = x_left[...]
    rows[capacity : 2 * capacity, half:] = got_x[:capacity, :]
    rows[2 * capacity : 3 * capacity, :half] = got_y[:capacity, :]
    rows[2 * capacity : 3 * capacity, half:] = y_right[...]
    rows[3 * capacity :, :half] = got_y[capacity:, :]
    rows[3 * capacity :, half:] = got_x[capacity:, :]


def hand_out(out, at, capacity, to_left, keep, near, onward):
    size = out.shape[1]
    rows = out.astype(jnp.bfloat16)
    mine, from_x, from_y, far = [rows[d * capacity : (d + 1) * capacity] for d in range(4)]
    keep[:, at : at + size] = mine
    near[:, at : at + size] = from_x if to_left else from_y
    onward[:capacity, at : at + size] = from_y if to_left else from_x
    onward[capacity:, at : at + size] = far


def fwd_half(hidden_ref, weight_out, to_left, keep, near, onward):
    capacity, half = keep.shape
    first = 0 if to_left else half
    for at, size in tiles(half, 512):
        out = jnp.dot(
            hidden_ref[...],
            weight_out[:, first + at : first + at + size],
            preferred_element_type=jnp.float32,
        )
        hand_out(out, at, capacity, to_left, keep, near, onward)


def bwd_half(both_ref, weight_in, to_left, keep, near, onward):
    capacity, half = keep.shape
    first = 0 if to_left else half
    for at, size in tiles(half, 512):
        out = lax.dot_general(
            both_ref[...],
            weight_in[first + at : first + at + size, :],
            (((1,), (1,)), ((), ())),
            preferred_element_type=jnp.float32,
        )
        hand_out(out, at, capacity, to_left, keep, near, onward)


def fwd_right_kernel(hidden_ref, weight_out, keep, near, onward):
    fwd_half(hidden_ref, weight_out, False, keep, near, onward)


def bwd_right_kernel(both_ref, weight_in, keep, near, onward):
    bwd_half(both_ref, weight_in, False, keep, near, onward)


def hop_again_kernel(top_count, *refs):
    dispatch, (weight_in, gate_ref, up_ref, rows_ref) = refs[:9], refs[9:]
    assemble("b", top_count, *dispatch, rows_ref)
    hidden_units = gate_ref.shape[1]
    for start, size in tiles(hidden_units, 256):
        gate_ref[:, start : start + size] = jnp.dot(
            rows_ref[...], weight_in[:, start : start + size], preferred_element_type=jnp.float32
        )
        up_ref[:, start : start + size] = jnp.dot(
            rows_ref[...],
            weight_in[:, hidden_units + start : hidden_units + start + size],
            preferred_element_type=jnp.float32,
        )


def hop_fwd_kernel(*refs):
    dispatch, refs = refs[:5], refs[5:]
    weight_in, weight_out = refs[:2]
    outs, hidden_ref, rows_ref = refs[2:5], refs[5], refs[6]
    hidden_units = weight_out.shape[0]
    gathered_rows(*dispatch, rows_ref)
    for start, size in tiles(hidden_units, 256):
        gate = jnp.dot(
            rows_ref[...], weight_in[:, start : start + size], preferred_element_type=jnp.float32
        )
        up = jnp.dot(
            rows_ref[...],
            weight_in[:, hidden_units + start : hidden_units + start + size],
            preferred_element_type=jnp.float32,
        )
        hidden_ref[:, start : start + size] = (gate / (1.0 + jnp.exp(-gate)) * up).astype(
            jnp.bfloat16
        )
    fwd_half(hidden_ref, weight_out, True, *outs)


def hop_bwd_kernel(*refs):
    dispatch, refs = refs[:5], refs[5:]
    gate_ref, up_ref, weight_in, weight_out = refs[:4]
    outs, both_ref, grads_ref = refs[4:7], refs[7], refs[8]
    hidden_units = weight_out.shape[0]
    gathered_rows(*dispatch, grads_ref)
    for start, size in tiles(hidden_units, 256):
        gate = gate_ref[:, start : start + size]
        up = up_ref[:, start : start + size]
        d_hidden = lax.dot_general(
            grads_ref[...],
            weight_out[start : start + size, :],
            (((1,), (1,)), ((), ())),
            preferred_element_type=jnp.float32,
        )
        sig = 1.0 / (1.0 + jnp.exp(-gate))
        both_ref[:, start : start + size] = (
            d_hidden * up * sig * (1.0 + gate * (1.0 - sig))
        ).astype(jnp.bfloat16)
        both_ref[:, hidden_units + start : hidden_units + start + size] = (
            d_hidden * gate * sig
        ).astype(jnp.bfloat16)
    bwd_half(both_ref, weight_in, True, *outs)


def sums_kernel(kind, top_count, here, table_ref, near, far, out):
    capacity = near.shape[0]
    table = table_ref[...]
    out[...] = (
        to_tokens(pick(table, here, capacity, kind, top_count), near[...])
        + to_tokens(pick(table, 3, capacity, kind, top_count), far[capacity:, :])
    ).astype(jnp.bfloat16)


def summed(kind, top_count, own, keep_left, keep_right, got_y, got_x, sum_x, sum_y):
    capacity = keep_left.shape[0]
    mine = pick(own[...], 0, capacity, kind, top_count)
    near_y = pick(own[...], 2, capacity, kind, top_count)
    near_x = pick(own[...], 1, capacity, kind, top_count)
    left = to_tokens(mine, keep_left[...]) + to_tokens(near_y, got_y[:capacity, :])
    right = to_tokens(mine, keep_right[...]) + to_tokens(near_x, got_x[:capacity, :])
    return left + sum_x[...].astype(jnp.float32), right + sum_y[...].astype(jnp.float32)


def hop_fwd_end_kernel(top_count, layer_ref, *refs):
    out_ref, order_ref = refs[-2:]
    order_ref[...] = jnp.zeros_like(order_ref)
    half = layer_ref.shape[1] // 2
    left, right = summed("fg", top_count, *refs[:-2])
    out_ref[:, :half] = (layer_ref[:, :half].astype(jnp.float32) + left).astype(jnp.bfloat16)
    out_ref[:, half:] = (layer_ref[:, half:].astype(jnp.float32) + right).astype(jnp.bfloat16)


def hop_bwd_near_kernel(
    top_count, own, keep_left, keep_right, got_y, got_x, saved_ref, left_ref, right_ref, inv_ref
):
    wide = saved_ref[...].astype(jnp.float32)
    inv_rms = lax.rsqrt(jnp.mean(wide * wide, axis=-1, keepdims=True) + EPS)
    inv_ref[...] = jnp.broadcast_to(inv_rms, inv_ref.shape)
    capacity = keep_left.shape[0]
    mine = pick(own[...], 0, capacity, "b", top_count)
    near_y = pick(own[...], 2, capacity, "b", top_count)
    near_x = pick(own[...], 1, capacity, "b", top_count)
    left_ref[...] = to_tokens(mine, keep_left[...]) + to_tokens(near_y, got_y[:capacity, :])
    right_ref[...] = to_tokens(mine, keep_right[...]) + to_tokens(near_x, got_x[:capacity, :])


def order_kernel(order_ref):
    order_ref[...] = jnp.zeros_like(order_ref)


def hop_bwd_end_kernel(grads_ref, saved_ref, gain_ref, left_ref, right_ref, inv_ref, sum_x, sum_y, out_ref):
    features = saved_ref.shape[1]
    half = features // 2
    parts = []
    left = left_ref[...] + sum_x[...].astype(jnp.float32)
    right = right_ref[...] + sum_y[...].astype(jnp.float32)
    for start, d_normed in ((0, left), (half, right)):
        wide = saved_ref[:, start : start + half].astype(jnp.float32)
        scaled = d_normed * gain_ref[:, start : start + half]
        parts.append((start, wide, scaled))
    inner = sum(jnp.sum(scaled * wide, axis=-1, keepdims=True) for _, wide, scaled in parts)
    inv_rms = inv_ref[:, :1]
    factor = inv_rms * inv_rms * inv_rms / features * inner
    for start, wide, scaled in parts:
        out_ref[:, start : start + half] = (
            grads_ref[:, start : start + half].astype(jnp.float32)
            + inv_rms * scaled
            - factor * wide
        ).astype(jnp.bfloat16)


def per_device_hops(
    fwd_prev,
    bwd_prev,
    bwd_saved,
    fwd_routes,
    fwd_gates,
    bwd_routes,
    bwd_gates,
    norm_gain,
    w_in,
    w_out,
):
    tok_rows, features = fwd_prev.shape[1:]
    top_count = fwd_routes.shape[2]
    hidden_units = w_in.shape[3] // 2
    capacity = 3 * tok_rows * top_count // 8
    half = features // 2
    gain_row = norm_gain
    weight_in = w_in[0, 0]
    weight_out = w_out[0, 0]
    me = lax.axis_index("expert").astype(jnp.int32).reshape(1)
    saved = bwd_saved[0]
    layer_in = passed_along(fwd_prev[0], "section", 1)
    grad_in = passed_along(bwd_prev[0], "section", -1)

    def shaped(rows, columns, dtype=jnp.bfloat16):
        return jax.ShapeDtypeStruct((rows, columns), dtype)

    def crossed(left, right):
        return swapped(left, "expert", 1), swapped(right, "expert", 2)

    slot_total = 4 * capacity
    table_rows = 4 * top_count
    one_hop = moved = 1024
    expert_flops = 2 * slot_total * features * hidden_units
    expert_moved = 2 * features * (3 * hidden_units + 3 * slot_total)
    rows_scratch = pltpu.VMEM((slot_total, features), jnp.bfloat16)
    halves_out = [shaped(tok_rows, half)] * 2
    hop_out = [shaped(2 * capacity, half)] * 2
    half_out = [shaped(capacity, half), shaped(capacity, half), shaped(2 * capacity, half)]
    hidden_shape = shaped(slot_total, hidden_units)
    both_shape = shaped(slot_total, 2 * hidden_units)
    table_shape = shaped(table_rows, tok_rows, jnp.float32)
    first_rows = tok_rows + 8 * top_count + capacity

    b_left, b_right, own, gain_here = pl.pallas_call(
        functools.partial(first_kernel, top_count),
        out_shape=[
            shaped(first_rows, half),
            shaped(first_rows, half),
            table_shape,
            shaped(1, features, jnp.float32),
        ],
        in_specs=[pl.BlockSpec(memory_space=pltpu.SMEM)]
        + [pl.BlockSpec(memory_space=pltpu.HBM)] * 6,
        scratch_shapes=[
            pltpu.VMEM((tok_rows, features), jnp.bfloat16),
            pltpu.VMEM((1, features), jnp.float32),
            pltpu.VMEM((top_count, tok_rows), jnp.int32),
            pltpu.VMEM((top_count, tok_rows), jnp.float32),
            pltpu.VMEM((top_count, tok_rows), jnp.int32),
            pltpu.VMEM((top_count, tok_rows), jnp.float32),
            pltpu.SemaphoreType.DMA((6,)),
        ],
        compiler_params=pltpu.CompilerParams(vmem_limit_bytes=VMEM_LIMIT),
        cost_estimate=pl.CostEstimate(flops=one_hop, bytes_accessed=moved, transcendentals=0),
    )(
        me,
        *[
            pltpu.with_memory_space_constraint(value, pltpu.HBM)
            for value in (
                saved,
                gain_row,
                fwd_routes[0].T,
                fwd_gates[0].T,
                bwd_routes[0].T,
                bwd_gates[0].T,
            )
        ],
    )
    b_from_x, b_from_y = crossed(b_left, b_right)

    def onward(kind, sent, got, after):
        to_y, to_x = local_call(
            functools.partial(hop_kernel, kind, top_count),
            hop_out,
            (*tabs, *sent, *got),
            one_hop,
            moved,
            after=after,
        )
        return swapped(to_y, "expert", 2), swapped(to_x, "expert", 1), to_y

    f_left, f_right = local_call(
        normed_kernel_halves, halves_out, (layer_in, gain_here), one_hop, moved, after=(b_left,)
    )
    f_from_x, f_from_y = crossed(f_left, f_right)
    x_tab, y_tab = local_call(
        functools.partial(tables_kernel, top_count),
        [table_shape] * 2,
        (b_from_x, b_from_y),
        TABLES_COST,
        1024,
        after=(f_left,),
    )
    g_left, g_right = local_call(split_kernel, halves_out, (grad_in,), 1024, moved, after=(x_tab,))
    g_from_x, g_from_y = crossed(g_left, g_right)
    tabs = (own, x_tab, y_tab)
    b_to_y, b_to_x = local_call(
        functools.partial(far_kernel, "b", top_count),
        [shaped(capacity, half)] * 2,
        (x_tab, y_tab, b_from_x, b_from_y),
        one_hop,
        moved,
        after=(g_left,),
    )
    b_got_y, b_got_x = swapped(b_to_y, "expert", 2), swapped(b_to_x, "expert", 1)
    f_got_y, f_got_x, f_to_y = onward("f", (f_left, f_right), (f_from_x, f_from_y), (b_to_y,))
    g_got_y, g_got_x, g_to_y = onward("bg", (g_left, g_right), (g_from_x, g_from_y), (f_to_y,))
    gate_pre, up_pre = local_call(
        functools.partial(hop_again_kernel, top_count),
        [shaped(slot_total, hidden_units, jnp.float32)] * 2,
        (*tabs, b_left, b_right, b_from_x, b_from_y, b_got_y, b_got_x, weight_in),
        2 * expert_flops,
        expert_moved,
        scratch=(rows_scratch,),
        after=(g_to_y,),
    )
    near_out = [shaped(capacity, features), shaped(capacity, half), shaped(capacity, half)]
    g_near = local_call(
        functools.partial(near_kernel, "bg", top_count),
        near_out,
        (*tabs, g_left, g_right, g_from_x, g_from_y),
        one_hop,
        moved,
        after=(gate_pre,),
    )
    f_near = local_call(
        functools.partial(near_kernel, "f", top_count),
        near_out,
        (*tabs, f_left, f_right, f_from_x, f_from_y),
        one_hop,
        moved,
        after=(g_near[1],),
    )
    f_keep_l, f_near_l, f_on_l, hidden = local_call(
        hop_fwd_kernel,
        half_out + [hidden_shape],
        (*f_near, f_got_y, f_got_x, weight_in, weight_out),
        5 * expert_flops // 2,
        expert_moved,
        scratch=(rows_scratch,),
        after=(f_near[1],),
    )
    f_ret_y = swapped(f_on_l, "expert", 2)
    f_keep_r, f_near_r, f_on_r = local_call(
        fwd_right_kernel, half_out, (hidden, weight_out), 1024, 1024
    )
    f_ret_x = swapped(f_on_r, "expert", 1)
    b_keep_l, b_near_l, b_on_l, both = local_call(
        hop_bwd_kernel,
        half_out + [both_shape],
        (*g_near, g_got_y, g_got_x, gate_pre, up_pre, weight_in, weight_out),
        2 * expert_flops,
        expert_moved,
        scratch=(rows_scratch,),
        after=(f_keep_r,),
    )
    b_ret_y = swapped(b_on_l, "expert", 2)
    b_keep_r, b_near_r, b_on_r = local_call(
        bwd_right_kernel, half_out, (both, weight_in), 1024, 1024
    )
    b_ret_x = swapped(b_on_r, "expert", 1)

    def summed_call(kind, here, table, near, far, after):
        part = local_call(
            functools.partial(sums_kernel, kind, top_count, here),
            shaped(tok_rows, half),
            (table, near, far),
            one_hop,
            moved,
            after=after,
        )
        return swapped(part, "expert", here), part

    f_sum_x, last = summed_call("fg", 1, x_tab, f_near_l, f_ret_y, (b_keep_r,))
    f_sum_y, last = summed_call("fg", 2, y_tab, f_near_r, f_ret_x, (last,))
    b_sum_x, last = summed_call("b", 1, x_tab, b_near_l, b_ret_y, (last,))
    b_sum_y, last = summed_call("b", 2, y_tab, b_near_r, b_ret_x, (last,))
    f_keep = (f_keep_l, f_keep_r)
    b_keep = (b_keep_l, b_keep_r)
    fwd_block, order = local_call(
        functools.partial(hop_fwd_end_kernel, top_count),
        [shaped(tok_rows, features), shaped(8, 128, jnp.float32)],
        (layer_in, own, *f_keep, f_ret_y, f_ret_x, f_sum_x, f_sum_y),
        one_hop,
        moved,
        after=(last,),
    )
    b_near = local_call(
        functools.partial(hop_bwd_near_kernel, top_count),
        [shaped(tok_rows, half, jnp.float32)] * 2 + [shaped(tok_rows, 128, jnp.float32)],
        (own, *b_keep, b_ret_y, b_ret_x, saved),
        one_hop,
        moved,
        after=(last,),
    )
    x_there = local_call(
        order_kernel,
        shaped(8, 128, jnp.float32),
        (),
        one_hop,
        moved,
        after=(order, b_near[0], b_sum_x),
    )
    bwd_block = local_call(
        hop_bwd_end_kernel,
        shaped(tok_rows, features),
        (grad_in, saved, gain_here, *b_near, b_sum_x, b_sum_y),
        one_hop,
        moved,
        after=(x_there,),
    )
    return (fwd_block[None], bwd_block[None])


def per_device(*arrays):
    if lax.axis_size("expert") == 4:
        return per_device_hops(*arrays)
    return per_device_direct(*arrays)


def solution(mesh):
    in_specs = (
        P("section", "expert", None),
        P("section", "expert", None),
        P("section", "expert", None),
        P("section", "expert", None),
        P("section", "expert", None),
        P("section", "expert", None),
        P("section", "expert", None),
        P("section", None),
        P("section", "expert", None, None),
        P("section", "expert", None, None),
    )
    out_specs = (P("section", "expert", None), P("section", "expert", None))
    return jax.shard_map(
        per_device, mesh=mesh, in_specs=in_specs, out_specs=out_specs, check_vma=False
    )
```
